32 devices in a mesh: grp: 2 (over y), store: 4 (over z), layer: 4 (over x, core).
Axes of the slice: x: 2, y: 2, z: 4, core: 2. Of those that a mesh axis runs over, the one named last changes fastest.
Arguments:
- hidden: bfloat16 [4, 288, 8, 8192], P('layer', ('grp', 'store')), parts along dimension 1, may hold values from -6 to 6
- cotangent: bfloat16 [4, 288, 8, 1024], P('layer', ('grp', 'store')), parts along dimension 1, may hold values from -6 to 6
- lengths: int32 [288], P(('grp', 'store')), parts along dimension 0, may hold values from 1 to 8, as said below
- norm_gain: bfloat16 [4, 8192], P('layer'), may hold values from 0.25 to 1.75
- in_projection: bfloat16 [4, 64, 8192], P('layer'), may hold values from -0.0625 to 0.0625
- out_projection: bfloat16 [4, 64, 1024], P('layer'), may hold values from -0.1875 to 0.1875
- store_slab: bfloat16 [4, 7680, 4096], P('layer', ('grp', 'store')), parts along dimension 1, may hold values from -0.0625 to 0.0625
Outputs:
- scores: float32 [7680, 144], P(('grp', 'store', 'layer')), parts along dimension 0
The draws below stay inside these ranges and needn't reach their ends.
There are 2 independent parts, one for each index of `grp`. The reference program is written for one: setup_inputs(seed, part) draws one part's arguments, and reference() takes and returns one part's arrays. A program takes and returns all parts, laid end to end along the dimension named above; an argument that names none is the same for every part. Nothing has to cross between parts.
Inputs may be any that keep to these rules, and one draw needn't show every extreme that they name: Positions s < lengths[q] of query q count; some query has 8 tokens and some has 1.
All inputs are finite; a program needn't handle non-finite values.
Results may differ from the reference program's by a relative error of at most 0.0057.
Values may be sent and summed in bfloat16 or wider, within the bound.
No kernel may reach another device: no remote copies, remote signals or barrier semaphores. Data moves between devices by JAX's collectives and lax.ppermute only.
A program may use at most 64 MiB of HBM per device.

```python
import jax
import jax.numpy as jnp
from jax import lax

D = 8192
DOUT = 1024
R_IN = 64
R_OUT = 64
S = 8
QUERIES = 144
EXAMPLES = 3840
LAYERS = 4
F = 4096


def draw_lengths(key, part):
    key = jax.random.fold_in(key, 7)
    first_key, second_key = jax.random.split(key)
    drawn = jax.random.randint(first_key, (QUERIES,), 1, S + 1)
    order = jax.random.permutation(second_key, QUERIES)
    drawn = drawn.at[order[0]].set(S)
    drawn = drawn.at[order[1]].set(1)
    return drawn.astype(jnp.int32)


def shard_levels(stream_key, extent, cuts, low, top_value):
    loudness = 1.0
    for position, parts in cuts:
        draws = jax.random.uniform(jax.random.fold_in(jax.random.fold_in(stream_key, 6), position), (parts,), jnp.float32, low / len(cuts), top_value / len(cuts))
        loudness = loudness * jnp.repeat(jnp.exp(draws), extent[position] // parts).reshape((-1,) + (1,) * (len(extent) - 1 - position))
    return loudness


def centred(own_key, extent, scale, bound, pieces=(), dtype=jnp.bfloat16):
    gain = shard_levels(own_key, extent, pieces, -0.22, 0.18) if pieces else 1.0
    entries = jax.random.normal(own_key, extent, jnp.float32) * scale * gain
    return jnp.minimum(jnp.maximum(entries, -bound), bound).astype(dtype)


def setup_inputs(seed: int = 0, part: int = 0) -> dict:
    streams_of = jax.random.split(jax.random.key(seed), 8)
    part_keys = jax.random.split(jax.random.fold_in(streams_of[7], part), 8)
    return {
        "hidden": centred(part_keys[0], (LAYERS, QUERIES, S, D), 1.0, 6.0, ((0, 4), (1, 4))),
        "cotangent": centred(part_keys[1], (LAYERS, QUERIES, S, DOUT), 1.0, 6.0, ((0, 4), (1, 4))),
        "lengths": draw_lengths(jax.random.fold_in(jax.random.fold_in(streams_of[7], part), 71), part),
        "norm_gain": jnp.clip(1.0 + 0.15 * jax.random.normal(streams_of[3], (LAYERS, D), jnp.float32), 0.25, 1.75).astype(jnp.bfloat16),
        "in_projection": centred(streams_of[4], (LAYERS, R_IN, D), D ** -0.5, 0.0625, ((0, 4),)),
        "out_projection": centred(streams_of[5], (LAYERS, R_OUT, DOUT), DOUT ** -0.5, 0.1875, ((0, 4),)),
        "store_slab": centred(part_keys[6], (LAYERS, EXAMPLES, F), (1 / 256), 0.0625, ((0, 4), (1, 4))),
    }


norm_epsilon = 1e-05

def contract_last(left, right):
    return lax.dot_general(left, right, (((1,), (1,)), ((), ())), preferred_element_type=jnp.float32)

def layer_grads(hidden, cotangent, lengths, norm_gain, in_projection, out_projection):
    queries, positions, width = hidden.shape
    flat = hidden.reshape(queries * positions, width).astype(jnp.float32)
    mean_square = lax.optimization_barrier(jnp.mean(flat * flat, axis=-1, keepdims=True))
    normed = (flat * lax.rsqrt(mean_square + norm_epsilon) * norm_gain.astype(jnp.float32)).astype(jnp.bfloat16)
    in_factor = contract_last(normed, in_projection).astype(jnp.bfloat16)
    flat_cot = cotangent.reshape(queries * positions, cotangent.shape[2])
    out_factor = contract_last(flat_cot, out_projection).astype(jnp.bfloat16)
    live_mask = lax.broadcasted_iota(jnp.int32, (queries, positions), 1) < lengths[:, None].astype(jnp.int32)
    out_factor = out_factor.reshape(queries, positions, -1) * live_mask[:, :, None].astype(jnp.bfloat16)
    in_factor = in_factor.reshape(queries, positions, -1)
    grads = jnp.einsum('qsi,qsj->qij', out_factor.astype(jnp.float32), in_factor.astype(jnp.float32))
    return grads.astype(jnp.bfloat16).reshape(queries, -1)

def reference(hidden, cotangent, lengths, norm_gain, in_projection, out_projection, store_slab):
    scores = jnp.zeros((store_slab.shape[1], hidden.shape[1]), jnp.float32)
    for layer_index in range(LAYERS):
        query_grads = layer_grads(hidden[layer_index], cotangent[layer_index], lengths, norm_gain[layer_index], in_projection[layer_index], out_projection[layer_index])
        scores = scores + contract_last(store_slab[layer_index], query_grads)
    return scores
```

```python
import functools

import jax
import jax.numpy as jnp
from jax import lax
from jax.experimental import pallas as pl
from jax.experimental.pallas import tpu as pltpu
from jax.sharding import PartitionSpec as P

norm_epsilon = 1e-05
f32 = jnp.float32
bf16 = jnp.bfloat16
S = 8
R = 64
B = 4
A = R // B
G = 8
H = 4


def dot_nt(left, right):
    return lax.dot_general(left, right, (((1,), (1,)), ((), ())), preferred_element_type=f32)


def iota(shape, dim):
    return lax.broadcasted_iota(jnp.int32, shape, dim)


def factors_kernel(
    steps, width, lengths, hidden, cot, gain, inp, outp, packed, in_acc, out_acc, sq_acc, out_t
):
    step = pl.program_id(0)
    queries = lengths.shape[0]
    rows = queries * S
    full = queries // G * G * S
    half = rows - full

    @pl.when(step == 0)
    def _():
        in_acc[...] = jnp.zeros_like(in_acc)
        out_acc[...] = jnp.zeros_like(out_acc)
        sq_acc[...] = jnp.zeros_like(sq_acc)

    block = hidden[...]
    wide = block.astype(f32)
    square = wide * wide
    lanes = sq_acc.shape[1]
    total = square[:, :lanes]
    for at in range(lanes, block.shape[1], lanes):
        total += square[:, at : at + lanes]
    sq_acc[...] += total
    scaled = (inp[...].astype(f32) * gain[...].astype(f32)).astype(bf16)
    in_acc[...] += dot_nt(block, scaled)
    out_acc[...] += dot_nt(cot[...], outp[...])

    @pl.when(step == steps - 1)
    def _():
        mean_square = jnp.sum(sq_acc[...], axis=1, keepdims=True) * (1.0 / width)
        factor = in_acc[...] * lax.rsqrt(mean_square + norm_epsilon)
        position = iota((S, R), 0)
        for q in range(queries):
            in_acc[q * S : (q + 1) * S, :] = jnp.where(
                position < lengths[q], factor[q * S : (q + 1) * S], 0.0
            )
        odd = lax.rem(lax.axis_index("store"), 2)
        at_full = pl.multiple_of(odd * half, half)
        at_half = pl.multiple_of((1 - odd) * full, half)
        in_full = in_acc[pl.ds(at_full, full), :]
        in_half = in_acc[pl.ds(at_half, half), :]
        mid, low = full // 2, half // 2
        packed[:mid, :] = jnp.concatenate([in_full[:mid], in_full[mid:]], axis=1).astype(bf16)
        packed[mid : mid + low, :] = jnp.concatenate(
            [in_half[:low], in_half[low:]], axis=1
        ).astype(bf16)
        turned = out_acc[pl.ds(at_full, full), :].T
        for t in range(full // 128):
            out_t[t * R : (t + 1) * R, :] = turned[:, t * 128 : (t + 1) * 128]
        out_t[full // 128 * R :, :half] = out_acc[pl.ds(at_half, half), :].T

        def part(t, b):
            return out_t[pl.ds(t * R + b, A, stride=B), :]

        row = mid + low
        for m in range(full // (G * S)):
            t, at = divmod(m * G * S, 128)
            for b in range(0, B, 2):
                both = [part(t, b + c)[:, at : at + G * S] for c in range(2)]
                packed[row : row + A, :] = jnp.concatenate(both, axis=1).astype(bf16)
                row += A
        packed[row : row + A, :] = jnp.concatenate(
            [part(full // 128, b)[:, :half] for b in range(B)], axis=1
        ).astype(bf16)


def factors(lengths, hidden, cotangent, gain, in_projection, out_projection):
    rows, width = hidden.shape
    steps = 8
    k_in, k_out = width // steps, cotangent.shape[1] // steps
    column = lambda step: (0, step)
    return pl.pallas_call(
        functools.partial(factors_kernel, steps, width),
        grid=(steps,),
        out_shape=jax.ShapeDtypeStruct((rows, 2 * R), bf16),
        in_specs=[
            pl.BlockSpec(memory_space=pltpu.SMEM),
            pl.BlockSpec((rows, k_in), column),
            pl.BlockSpec((rows, k_out), column),
            pl.BlockSpec((1, k_in), column),
            pl.BlockSpec((R, k_in), column),
            pl.BlockSpec((R, k_out), column),
        ],
        out_specs=pl.BlockSpec((rows, 2 * R), lambda step: (0, 0)),
        scratch_shapes=[
            pltpu.VMEM((rows, R), f32),
            pltpu.VMEM((rows, R), f32),
            pltpu.VMEM((rows, 128), f32),
            pltpu.VMEM((-(-rows // 128) * R, 128), f32),
        ],
        compiler_params=pltpu.CompilerParams(vmem_limit_bytes=16 * 2**20),
        name="factors",
    )(lengths, hidden, cotangent, gain, in_projection, out_projection)


def spread_out(tile, owner):
    lanes = tile.shape[1]
    mine = (owner == iota((G, lanes), 0))[None]
    wide = jnp.where(mine, tile.astype(f32)[:, None, :], 0.0)
    return wide.reshape(A * G, lanes).astype(bf16)


def halves(tile):
    wide = tile.astype(f32)
    turned = jnp.concatenate([wide[:, R:], wide[:, :R]], axis=1)
    low = iota(wide.shape, 1) < R
    return [
        jnp.where(mask, x, 0.0).astype(bf16)
        for x in (wide, turned)
        for mask in (low, jnp.logical_not(low))
    ]


def diagonal(low, high):
    zero = jnp.zeros_like(low)
    left = jnp.concatenate([low, high, zero, zero], axis=0)
    right = jnp.concatenate([zero, zero, low, high], axis=0)
    return jnp.concatenate([left, right], axis=1)


def build_grads(shards, base, row0, full_groups, grads):
    mid = full_groups * G * S // 2
    low = H * S // 2
    lane = iota((G, 2 * 128), 1)
    whole_owner = lax.rem(lane, G * S) // S
    half_owner = lax.rem(lane, H * S) // S + H * (lane // 128)

    def whole(shard):
        found = []
        pairs = {}
        for m in range(full_groups):
            first = m % (full_groups // 2)
            if first not in pairs:
                pairs[first] = halves(
                    shards[base + shard, first * G * S : (first + 1) * G * S, :]
                )
            plain_low, plain_high, turned_low, turned_high = pairs[first]
            weights = (
                diagonal(plain_low, turned_high)
                if m < full_groups // 2
                else diagonal(turned_low, plain_high)
            )
            at = mid + low + m * 2 * A
            tile = jnp.concatenate(
                [shards[base + shard, at : at + A, :], shards[base + shard, at + A : at + 2 * A, :]],
                axis=1,
            )
            found.append((spread_out(tile, whole_owner), weights))
        return found

    def joined(shard):
        tiles, weights = [], []
        for s in (shard, shard + 1):
            plain_low, plain_high, turned_low, turned_high = halves(
                shards[base + s, mid : mid + low, :]
            )
            weights.append(
                diagonal(
                    jnp.concatenate([plain_low, turned_low], axis=0),
                    jnp.concatenate([turned_high, plain_high], axis=0),
                )
            )
            at = mid + low + full_groups * 2 * A
            tiles.append(shards[base + s, at : at + A, :])
        return [
            (
                spread_out(jnp.concatenate(tiles, axis=1), half_owner),
                jnp.concatenate(weights, axis=0),
            )
        ]

    groups = []
    for shard in (0, 2):
        groups += whole(shard) + joined(shard) + whole(shard + 1)
    for at in range(0, len(groups), 2):
        first, second = [jnp.dot(x, w, preferred_element_type=f32) for x, w in groups[at : at + 2]]
        for a in range(A):
            pair = [x[a * G : (a + 1) * G] for x in (first, second)]
            grads[pl.ds(row0 + at * G, 2 * G), a * 256 : (a + 1) * 256] = jnp.concatenate(
                pair, axis=0
            ).astype(bf16)


def scores_kernel(n_store, n_layer, full_groups, *refs):
    gathered = refs[:n_store]
    store = refs[n_store]
    outs = refs[n_store + 1 : n_store + 1 + n_layer]
    shards, grads, slab, sems = refs[n_store + 1 + n_layer :]
    block = slab.shape[1]
    me_layer = lax.axis_index("layer")
    me_store = lax.axis_index("store")
    rows = 16 if block % 16 == 0 else 8
    copies = []
    for place, k in enumerate(reversed(range(n_layer))):
        copies.append(
            pltpu.make_async_copy(
                store.at[pl.ds(pl.multiple_of(partner(me_layer, k, n_layer) * block, rows), block)],
                slab.at[place],
                sems.at[place],
            )
        )
        copies[-1].start()
    for k in range(n_store):
        shards[partner(me_store, k, n_store)] = gathered[k][...]
    four = 4 * (full_groups * G + H)
    if n_store == 4:
        build_grads(shards, 0, 0, full_groups, grads)
    else:

        @pl.loop(0, n_store // 4)
        def _(at):
            build_grads(shards, at * 4, pl.multiple_of(at * four, 16), full_groups, grads)

    for place, k in enumerate(reversed(range(n_layer))):
        copies[place].wait()
        outs[k][...] = dot_nt(grads[...], slab[place]).astype(outs[k].dtype)


def partner(me, k, n):
    return jnp.bitwise_xor(me, k) if n & (n - 1) == 0 else lax.rem(n + k - me, n)


def swap(x, axis, n, k):
    pairs = [(i, i ^ k if n & (n - 1) == 0 else (n + k - i) % n) for i in range(n)]
    return lax.ppermute(x, axis, pairs)


def scores(gathered, store, n_store, n_layer):
    rows, features = store.shape
    queries = gathered[0].shape[0] // S
    block = rows // n_layer
    vmem = pl.BlockSpec(memory_space=pltpu.VMEM)
    return pl.pallas_call(
        functools.partial(scores_kernel, n_store, n_layer, queries // G),
        out_shape=[
            jax.ShapeDtypeStruct((n_store * queries, block), f32 if k == 0 else bf16)
            for k in range(n_layer)
        ],
        in_specs=[vmem] * n_store + [pl.BlockSpec(memory_space=pl.ANY)],
        out_specs=[vmem] * n_layer,
        scratch_shapes=[
            pltpu.VMEM((n_store,) + gathered[0].shape, bf16),
            pltpu.VMEM((n_store * queries, features), bf16),
            pltpu.VMEM((n_layer, block, features), bf16),
            pltpu.SemaphoreType.DMA((n_layer,)),
        ],
        compiler_params=pltpu.CompilerParams(vmem_limit_bytes=32 * 2**20),
        name="scores",
    )(*gathered, store)


def on_device(n_store, n_layer, hidden, cotangent, lengths, norm_gain, in_proj, out_proj, store):
    queries, positions, width = hidden.shape[1:]
    packed = factors(
        lengths,
        hidden.reshape(queries * positions, width),
        cotangent.reshape(queries * positions, cotangent.shape[3]),
        norm_gain,
        in_proj[0],
        out_proj[0],
    )
    gathered = [packed] + [swap(packed, "store", n_store, k) for k in range(1, n_store)]
    partial = scores(gathered, store[0], n_store, n_layer)
    total = partial[0]
    for k in range(1, n_layer):
        total = total + swap(partial[k], "layer", n_layer, k).astype(f32)
    return total.T


def solution(mesh):
    placed = (
        P("layer", ("grp", "store"), None, None),
        P("layer", ("grp", "store"), None, None),
        P(("grp", "store")),
        P("layer", None),
        P("layer", None, None),
        P("layer", None, None),
        P("layer", ("grp", "store"), None),
    )
    return jax.shard_map(
        functools.partial(on_device, mesh.shape["store"], mesh.shape["layer"]),
        mesh=mesh,
        in_specs=placed,
        out_specs=P(("grp", "store", "layer"), None),
        check_vma=False,
    )
```

```python
import functools

import jax
import jax.numpy as jnp
from jax import lax
from jax.experimental import pallas as pl
from jax.experimental.pallas import tpu as pltpu
from jax.sharding import PartitionSpec as P

norm_epsilon = 1e-05
f32 = jnp.float32
bf16 = jnp.bfloat16
S = 8
R = 64
B = 4
A = R // B
G = 8
H = 4


def dot_nt(left, right):
    return lax.dot_general(left, right, (((1,), (1,)), ((), ())), preferred_element_type=f32)


def iota(shape, dim):
    return lax.broadcasted_iota(jnp.int32, shape, dim)


def factors_kernel(
    columns,
    width,
    hbm_lengths,
    hbm_hidden,
    hbm_cot,
    hbm_gain,
    hbm_inp,
    hbm_outp,
    packed,
    lengths,
    hidden,
    cot,
    gain,
    inp,
    outp,
    in_acc,
    out_acc,
    sq_acc,
    out_t,
    sems,
):
    chunks = width // columns
    queries = lengths.shape[0]
    rows = queries * S
    full = queries // G * G * S
    half = rows - full
    mid, low = full // 2, half // 2

    def start(source, target, at):
        copy = pltpu.make_async_copy(source, target, sems.at[at])
        copy.start()
        return copy

    head = [
        start(hbm_cot, cot, 0),
        start(hbm_outp, outp, 1),
        start(hbm_gain, gain, 2),
        start(hbm_lengths, lengths, 3),
    ]
    body = []
    for c in range(chunks):
        cut = pl.ds(c * columns, columns)
        body.append(
            [
                start(hbm_inp.at[:, cut], inp.at[c], 4 + 2 * c),
                start(hbm_hidden.at[:, cut], hidden.at[c], 5 + 2 * c),
            ]
        )
    for copy in head:
        copy.wait()
    odd = lax.rem(lax.axis_index("store"), 2)
    at_full = pl.multiple_of(odd * half, half)
    at_half = pl.multiple_of((1 - odd) * full, half)

    out_acc[...] = dot_nt(cot[...], outp[...])
    turned = out_acc[pl.ds(at_full, full), :].T
    for t in range(full // 128):
        out_t[t * R : (t + 1) * R, :] = turned[:, t * 128 : (t + 1) * 128]
    out_t[full // 128 * R :, :half] = out_acc[pl.ds(at_half, half), :].T

    def part(t, b):
        return out_t[pl.ds(t * R + b, A, stride=B), :]

    row = mid + low
    for m in range(full // (G * S)):
        t, at = divmod(m * G * S, 128)
        for b in range(0, B, 2):
            both = [part(t, b + c)[:, at : at + G * S] for c in range(2)]
            packed[row : row + A, :] = jnp.concatenate(both, axis=1).astype(bf16)
            row += A
    packed[row : row + A, :] = jnp.concatenate(
        [part(full // 128, b)[:, :half] for b in range(B)], axis=1
    ).astype(bf16)

    for c in range(chunks):
        for copy in body[c]:
            copy.wait()
        scaled = inp[c].astype(f32) * gain[:, c * columns : (c + 1) * columns].astype(f32)
        high = scaled.astype(bf16)
        rest = (scaled - high.astype(f32)).astype(bf16)
        product = dot_nt(hidden[c], jnp.concatenate([high, rest], axis=0))
        in_acc[...] = product if c == 0 else in_acc[...] + product
        for r in range(0, rows, 16):
            total = None if c == 0 else sq_acc[r : r + 16, :]
            for at in range(0, columns, 128):
                wide = hidden[c, r : r + 16, at : at + 128].astype(f32)
                total = wide * wide if total is None else total + wide * wide
            sq_acc[r : r + 16, :] = total

    mean_square = jnp.sum(sq_acc[...], axis=1, keepdims=True) * (1.0 / width)
    factor = in_acc[:, :R] + in_acc[:, R:]
    factor = factor * lax.rsqrt(mean_square + norm_epsilon)
    position = iota((S, R), 0)
    for q in range(queries):
        out_acc[q * S : (q + 1) * S, :] = jnp.where(
            position < lengths[q], factor[q * S : (q + 1) * S], 0.0
        )
    in_full = out_acc[pl.ds(at_full, full), :]
    in_half = out_acc[pl.ds(at_half, half), :]
    packed[:mid, :] = jnp.concatenate([in_full[:mid], in_full[mid:]], axis=1).astype(bf16)
    packed[mid : mid + low, :] = jnp.concatenate([in_half[:low], in_half[low:]], axis=1).astype(
        bf16
    )


def in_hbm(x):
    return pltpu.with_memory_space_constraint(x, pltpu.HBM)


def factors(lengths, hidden, cotangent, gain, in_projection, out_projection):
    rows, width = hidden.shape
    columns = 1024
    chunks = width // columns
    return pl.pallas_call(
        functools.partial(factors_kernel, columns, width),
        out_shape=jax.ShapeDtypeStruct((rows, 2 * R), bf16),
        in_specs=[pl.BlockSpec(memory_space=pl.ANY)] * 6,
        out_specs=pl.BlockSpec(memory_space=pltpu.VMEM),
        scratch_shapes=[
            pltpu.SMEM(lengths.shape, jnp.int32),
            pltpu.VMEM((chunks, rows, columns), bf16),
            pltpu.VMEM(cotangent.shape, bf16),
            pltpu.VMEM(gain.shape, bf16),
            pltpu.VMEM((chunks, R, columns), bf16),
            pltpu.VMEM(out_projection.shape, bf16),
            pltpu.VMEM((rows, 2 * R), f32),
            pltpu.VMEM((rows, R), f32),
            pltpu.VMEM((rows, 128), f32),
            pltpu.VMEM((-(-rows // 128) * R, 128), f32),
            pltpu.SemaphoreType.DMA((4 + 2 * chunks,)),
        ],
        compiler_params=pltpu.CompilerParams(vmem_limit_bytes=24 * 2**20),
        name="factors",
    )(*[in_hbm(x) for x in (lengths, hidden, cotangent, gain, in_projection, out_projection)])


def fetch_kernel(n_layer, after, store, slab, sems):
    block = slab.shape[1]
    rows = 16 if block % 16 == 0 else 8
    me = lax.axis_index("layer")
    copies = []
    for k in range(n_layer):
        at = pl.multiple_of(partner(me, k, n_layer) * block, rows)
        copies.append(pltpu.make_async_copy(store.at[pl.ds(at, block)], slab.at[k], sems.at[k]))
        copies[-1].start()
    for copy in copies:
        copy.wait()


def fetch(after, store, n_layer):
    rows, features = store.shape
    return pl.pallas_call(
        functools.partial(fetch_kernel, n_layer),
        out_shape=jax.ShapeDtypeStruct((n_layer, rows // n_layer, features), bf16),
        in_specs=[pl.BlockSpec(memory_space=pl.ANY)] * 2,
        out_specs=pl.BlockSpec(memory_space=pltpu.VMEM),
        scratch_shapes=[pltpu.SemaphoreType.DMA((n_layer,))],
        compiler_params=pltpu.CompilerParams(vmem_limit_bytes=12 * 2**20),
        cost_estimate=pl.CostEstimate(
            flops=0, bytes_accessed=2 * rows * features, transcendentals=0
        ),
        name="fetch",
    )(after, in_hbm(store))


def spread_out(tile, owner):
    lanes = tile.shape[1]
    mine = (owner == iota((G, lanes), 0))[None]
    wide = jnp.where(mine, tile.astype(f32)[:, None, :], 0.0)
    return wide.reshape(A * G, lanes).astype(bf16)


def halves(tile):
    wide = tile.astype(f32)
    turned = jnp.concatenate([wide[:, R:], wide[:, :R]], axis=1)
    low = iota(wide.shape, 1) < R
    return [
        jnp.where(mask, x, 0.0).astype(bf16)
        for x in (wide, turned)
        for mask in (low, jnp.logical_not(low))
    ]


def diagonal(low, high):
    zero = jnp.zeros_like(low)
    left = jnp.concatenate([low, high, zero, zero], axis=0)
    right = jnp.concatenate([zero, zero, low, high], axis=0)
    return jnp.concatenate([left, right], axis=1)


def build_grads(shards, base, row0, full_groups, grads):
    mid = full_groups * G * S // 2
    low = H * S // 2
    lane = iota((G, 2 * 128), 1)
    whole_owner = lax.rem(lane, G * S) // S
    half_owner = lax.rem(lane, H * S) // S + H * (lane // 128)

    def whole(shard):
        found = []
        pairs = {}
        for m in range(full_groups):
            first = m % (full_groups // 2)
            if first not in pairs:
                pairs[first] = halves(
                    shards[base + shard, first * G * S : (first + 1) * G * S, :]
                )
            plain_low, plain_high, turned_low, turned_high = pairs[first]
            weights = (
                diagonal(plain_low, turned_high)
                if m < full_groups // 2
                else diagonal(turned_low, plain_high)
            )
            at = mid + low + m * 2 * A
            tile = jnp.concatenate(
                [shards[base + shard, at : at + A, :], shards[base + shard, at + A : at + 2 * A, :]],
                axis=1,
            )
            found.append((spread_out(tile, whole_owner), weights))
        return found

    def joined(shard):
        tiles, weights = [], []
        for s in (shard, shard + 1):
            plain_low, plain_high, turned_low, turned_high = halves(
                shards[base + s, mid : mid + low, :]
            )
            weights.append(
                diagonal(
                    jnp.concatenate([plain_low, turned_low], axis=0),
                    jnp.concatenate([turned_high, plain_high], axis=0),
                )
            )
            at = mid + low + full_groups * 2 * A
            tiles.append(shards[base + s, at : at + A, :])
        return [
            (
                spread_out(jnp.concatenate(tiles, axis=1), half_owner),
                jnp.concatenate(weights, axis=0),
            )
        ]

    groups = []
    for shard in (0, 2):
        groups += whole(shard) + joined(shard) + whole(shard + 1)
    for at in range(0, len(groups), 2):
        first, second = [jnp.dot(x, w, preferred_element_type=f32) for x, w in groups[at : at + 2]]
        for a in range(A):
            pair = [x[a * G : (a + 1) * G] for x in (first, second)]
            grads[pl.ds(row0 + at * G, 2 * G), a * 256 : (a + 1) * 256] = jnp.concatenate(
                pair, axis=0
            ).astype(bf16)


def scores_kernel(n_store, n_layer, full_groups, *refs):
    gathered = refs[:n_store]
    slab = refs[n_store]
    outs = refs[n_store + 1 : n_store + 1 + n_layer]
    shards, grads = refs[n_store + 1 + n_layer :]
    me_store = lax.axis_index("store")
    for k in range(n_store):
        shards[partner(me_store, k, n_store)] = gathered[k][...]
    four = 4 * (full_groups * G + H)
    if n_store == 4:
        build_grads(shards, 0, 0, full_groups, grads)
    else:

        @pl.loop(0, n_store // 4)
        def _(at):
            build_grads(shards, at * 4, pl.multiple_of(at * four, 16), full_groups, grads)

    for k in reversed(range(n_layer)):
        outs[k][...] = dot_nt(grads[...], slab[k]).astype(outs[k].dtype)


def partner(me, k, n):
    return jnp.bitwise_xor(me, k) if n & (n - 1) == 0 else lax.rem(n + k - me, n)


def swap(x, axis, n, k):
    pairs = [(i, i ^ k if n & (n - 1) == 0 else (n + k - i) % n) for i in range(n)]
    return lax.ppermute(x, axis, pairs)


def scores(gathered, slab, n_store, n_layer):
    block, features = slab.shape[1:]
    queries = gathered[0].shape[0] // S
    vmem = pl.BlockSpec(memory_space=pltpu.VMEM)
    return pl.pallas_call(
        functools.partial(scores_kernel, n_store, n_layer, queries // G),
        out_shape=[
            jax.ShapeDtypeStruct((n_store * queries, block), f32 if k == 0 else bf16)
            for k in range(n_layer)
        ],
        in_specs=[vmem] * (n_store + 1),
        out_specs=[vmem] * n_layer,
        scratch_shapes=[
            pltpu.VMEM((n_store,) + gathered[0].shape, bf16),
            pltpu.VMEM((n_store * queries, features), bf16),
        ],
        compiler_params=pltpu.CompilerParams(vmem_limit_bytes=24 * 2**20),
        name="scores",
    )(*gathered, slab)


def on_device(n_store, n_layer, hidden, cotangent, lengths, norm_gain, in_proj, out_proj, store):
    queries, positions, width = hidden.shape[1:]
    packed = factors(
        lengths,
        hidden.reshape(queries * positions, width),
        cotangent.reshape(queries * positions, cotangent.shape[3]),
        norm_gain,
        in_proj[0],
        out_proj[0],
    )
    gathered = [packed] + [swap(packed, "store", n_store, k) for k in range(1, n_store)]
    slab = fetch(packed, store[0], n_layer)
    partial = scores(gathered, slab, n_store, n_layer)
    total = partial[0]
    for k in range(1, n_layer):
        total = total + swap(partial[k], "layer", n_layer, k).astype(f32)
    return total.T


def solution(mesh):
    placed = (
        P("layer", ("grp", "store"), None, None),
        P("layer", ("grp", "store"), None, None),
        P(("grp", "store")),
        P("layer", None),
        P("layer", None, None),
        P("layer", None, None),
        P("layer", ("grp", "store"), None),
    )
    return jax.shard_map(
        functools.partial(on_device, mesh.shape["store"], mesh.shape["layer"]),
        mesh=mesh,
        in_specs=placed,
        out_specs=P(("grp", "store", "layer"), None),
        check_vma=False,
    )
```

```python
import functools

import jax
import jax.numpy as jnp
from jax import lax
from jax.experimental import pallas as pl
from jax.experimental.pallas import tpu as pltpu
from jax.sharding import PartitionSpec as P

norm_epsilon = 1e-05
f32 = jnp.float32
bf16 = jnp.bfloat16
S = 8
R = 64
B = 4
A = R // B
G = 8
H = 4


def dot_nt(left, right):
    return lax.dot_general(left, right, (((1,), (1,)), ((), ())), preferred_element_type=f32)


def iota(shape, dim):
    return lax.broadcasted_iota(jnp.int32, shape, dim)


def factors_kernel(
    cuts,
    hbm_lengths,
    hbm_hidden,
    hbm_cot,
    hbm_gain,
    hbm_inp,
    hbm_outp,
    packed,
    lengths,
    hidden,
    cot,
    gain,
    inp,
    outp,
    weights,
    in_acc,
    out_acc,
    sq_acc,
    out_t,
    sems,
):
    width = hidden.shape[1]
    queries = lengths.shape[0]
    rows = queries * S
    full = queries // G * G * S
    half = rows - full
    mid, low = full // 2, half // 2

    def start(source, target, at):
        copy = pltpu.make_async_copy(source, target, sems.at[at])
        copy.start()
        return copy

    copy_gain = start(hbm_gain, gain, 0)
    copy_inp = start(hbm_inp, inp, 1)
    copy_outp = start(hbm_outp, outp, 2)
    copy_cot = start(hbm_cot, cot, 3)
    copy_lengths = start(hbm_lengths, lengths, 4)
    copies = []
    for c in range(len(cuts) - 1):
        cut = pl.ds(cuts[c], cuts[c + 1] - cuts[c])
        copies.append(start(hbm_hidden.at[:, cut], hidden.at[:, cut], 5 + c))
    odd = lax.rem(lax.axis_index("store"), 2)
    at_full = pl.multiple_of(odd * half, half)
    at_half = pl.multiple_of((1 - odd) * full, half)

    copy_gain.wait()
    copy_inp.wait()
    for at in range(0, width, 512):
        cut = slice(at, at + 512)
        scaled = inp[:, cut].astype(f32) * gain[:, cut].astype(f32)
        high = scaled.astype(bf16)
        weights[:R, cut] = high
        weights[R:, cut] = (scaled - high.astype(f32)).astype(bf16)

    copy_outp.wait()
    copy_cot.wait()
    copy_lengths.wait()
    out_acc[...] = dot_nt(cot[...], outp[...])
    turned = out_acc[pl.ds(at_full, full), :].T
    for t in range(full // 128):
        out_t[t * R : (t + 1) * R, :] = turned[:, t * 128 : (t + 1) * 128]
    out_t[full // 128 * R :, :half] = out_acc[pl.ds(at_half, half), :].T

    def part(t, b):
        return out_t[pl.ds(t * R + b, A, stride=B), :]

    row = mid + low
    for m in range(full // (G * S)):
        t, at = divmod(m * G * S, 128)
        for b in range(0, B, 2):
            both = [part(t, b + c)[:, at : at + G * S] for c in range(2)]
            packed[row : row + A, :] = jnp.concatenate(both, axis=1).astype(bf16)
            row += A
    packed[row : row + A, :] = jnp.concatenate(
        [part(full // 128, b)[:, :half] for b in range(B)], axis=1
    ).astype(bf16)

    for c, copy in enumerate(copies):
        copy.wait()
        cut = slice(cuts[c], cuts[c + 1])
        product = dot_nt(hidden[:, cut], weights[:, cut])
        in_acc[...] = product if c == 0 else in_acc[...] + product
        for r in range(0, rows, 16):
            total = None if c == 0 else sq_acc[r : r + 16, :]
            for at in range(cuts[c], cuts[c + 1], 128):
                wide = hidden[r : r + 16, at : at + 128].astype(f32)
                total = wide * wide if total is None else total + wide * wide
            sq_acc[r : r + 16, :] = total

    mean_square = jnp.sum(sq_acc[...], axis=1, keepdims=True) * (1.0 / width)
    factor = in_acc[:, :R] + in_acc[:, R:]
    factor = factor * lax.rsqrt(mean_square + norm_epsilon)
    position = iota((S, R), 0)
    for q in range(queries):
        out_acc[q * S : (q + 1) * S, :] = jnp.where(
            position < lengths[q], factor[q * S : (q + 1) * S], 0.0
        )
    in_full = out_acc[pl.ds(at_full, full), :]
    in_half = out_acc[pl.ds(at_half, half), :]
    packed[:mid, :] = jnp.concatenate([in_full[:mid], in_full[mid:]], axis=1).astype(bf16)
    packed[mid : mid + low, :] = jnp.concatenate([in_half[:low], in_half[low:]], axis=1).astype(
        bf16
    )


def in_hbm(x):
    return pltpu.with_memory_space_constraint(x, pltpu.HBM)


def factors(lengths, hidden, cotangent, gain, in_projection, out_projection):
    rows, width = hidden.shape
    cuts = [width * part // 8 for part in (0, 2, 4, 6, 7, 8)]
    return pl.pallas_call(
        functools.partial(factors_kernel, cuts),
        out_shape=jax.ShapeDtypeStruct((rows, 2 * R), bf16),
        in_specs=[pl.BlockSpec(memory_space=pl.ANY)] * 6,
        out_specs=pl.BlockSpec(memory_space=pltpu.VMEM),
        scratch_shapes=[
            pltpu.SMEM(lengths.shape, jnp.int32),
            pltpu.VMEM(hidden.shape, bf16),
            pltpu.VMEM(cotangent.shape, bf16),
            pltpu.VMEM(gain.shape, bf16),
            pltpu.VMEM(in_projection.shape, bf16),
            pltpu.VMEM(out_projection.shape, bf16),
            pltpu.VMEM((2 * R, width), bf16),
            pltpu.VMEM((rows, 2 * R), f32),
            pltpu.VMEM((rows, R), f32),
            pltpu.VMEM((rows, 128), f32),
            pltpu.VMEM((-(-rows // 128) * R, 128), f32),
            pltpu.SemaphoreType.DMA((4 + len(cuts),)),
        ],
        compiler_params=pltpu.CompilerParams(vmem_limit_bytes=24 * 2**20),
        name="factors",
    )(*[in_hbm(x) for x in (lengths, hidden, cotangent, gain, in_projection, out_projection)])


def fetch_kernel(n_layer, after, store, slab, sems):
    block = slab.shape[1]
    rows = 16 if block % 16 == 0 else 8
    me = lax.axis_index("layer")
    copies = []
    for k in range(n_layer):
        at = pl.multiple_of(partner(me, k, n_layer) * block, rows)
        copies.append(pltpu.make_async_copy(store.at[pl.ds(at, block)], slab.at[k], sems.at[k]))
        copies[-1].start()
    for copy in copies:
        copy.wait()


def fetch(after, store, n_layer):
    rows, features = store.shape
    return pl.pallas_call(
        functools.partial(fetch_kernel, n_layer),
        out_shape=jax.ShapeDtypeStruct((n_layer, rows // n_layer, features), bf16),
        in_specs=[pl.BlockSpec(memory_space=pl.ANY)] * 2,
        out_specs=pl.BlockSpec(memory_space=pltpu.VMEM),
        scratch_shapes=[pltpu.SemaphoreType.DMA((n_layer,))],
        compiler_params=pltpu.CompilerParams(vmem_limit_bytes=12 * 2**20),
        cost_estimate=pl.CostEstimate(
            flops=0, bytes_accessed=2 * rows * features, transcendentals=0
        ),
        name="fetch",
    )(after, in_hbm(store))


def spread_out(tile, owner):
    lanes = tile.shape[1]
    mine = (owner == iota((G, lanes), 0))[None]
    wide = jnp.where(mine, tile.astype(f32)[:, None, :], 0.0)
    return wide.reshape(A * G, lanes).astype(bf16)


def halves(tile):
    wide = tile.astype(f32)
    turned = jnp.concatenate([wide[:, R:], wide[:, :R]], axis=1)
    low = iota(wide.shape, 1) < R
    return [
        jnp.where(mask, x, 0.0).astype(bf16)
        for x in (wide, turned)
        for mask in (low, jnp.logical_not(low))
    ]


def diagonal(low, high):
    zero = jnp.zeros_like(low)
    left = jnp.concatenate([low, high, zero, zero], axis=0)
    right = jnp.concatenate([zero, zero, low, high], axis=0)
    return jnp.concatenate([left, right], axis=1)


def build_grads(shards, base, row0, full_groups, grads):
    mid = full_groups * G * S // 2
    low = H * S // 2
    lane = iota((G, 2 * 128), 1)
    whole_owner = lax.rem(lane, G * S) // S
    half_owner = lax.rem(lane, H * S) // S + H * (lane // 128)

    def whole(shard):
        found = []
        pairs = {}
        for m in range(full_groups):
            first = m % (full_groups // 2)
            if first not in pairs:
                pairs[first] = halves(
                    shards[base + shard, first * G * S : (first + 1) * G * S, :]
                )
            plain_low, plain_high, turned_low, turned_high = pairs[first]
            weights = (
                diagonal(plain_low, turned_high)
                if m < full_groups // 2
                else diagonal(turned_low, plain_high)
            )
            at = mid + low + m * 2 * A
            tile = jnp.concatenate(
                [shards[base + shard, at : at + A, :], shards[base + shard, at + A : at + 2 * A, :]],
                axis=1,
            )
            found.append((spread_out(tile, whole_owner), weights))
        return found

    def joined(shard):
        tiles, weights = [], []
        for s in (shard, shard + 1):
            plain_low, plain_high, turned_low, turned_high = halves(
                shards[base + s, mid : mid + low, :]
            )
            weights.append(
                diagonal(
                    jnp.concatenate([plain_low, turned_low], axis=0),
                    jnp.concatenate([turned_high, plain_high], axis=0),
                )
            )
            at = mid + low + full_groups * 2 * A
            tiles.append(shards[base + s, at : at + A, :])
        return [
            (
                spread_out(jnp.concatenate(tiles, axis=1), half_owner),
                jnp.concatenate(weights, axis=0),
            )
        ]

    groups = []
    for shard in (0, 2):
        groups += whole(shard) + joined(shard) + whole(shard + 1)
    for at in range(0, len(groups), 2):
        first, second = [jnp.dot(x, w, preferred_element_type=f32) for x, w in groups[at : at + 2]]
        for a in range(A):
            pair = [x[a * G : (a + 1) * G] for x in (first, second)]
            grads[pl.ds(row0 + at * G, 2 * G), a * 256 : (a + 1) * 256] = jnp.concatenate(
                pair, axis=0
            ).astype(bf16)


def far_kernel(n_store, full_groups, *refs):
    gathered = refs[:n_store]
    slab, grads = refs[n_store : n_store + 2]
    outs = refs[n_store + 2 : -1]
    shards = refs[-1]
    me_store = lax.axis_index("store")
    for k in range(n_store):
        shards[partner(me_store, k, n_store)] = gathered[k][...]
    four = 4 * (full_groups * G + H)
    if n_store == 4:
        build_grads(shards, 0, 0, full_groups, grads)
    else:

        @pl.loop(0, n_store // 4)
        def _(at):
            build_grads(shards, at * 4, pl.multiple_of(at * four, 16), full_groups, grads)

    for at, out in enumerate(outs):
        out[...] = dot_nt(grads[...], slab[2 + at]).astype(out.dtype)


def near_kernel(grads, slab, *outs):
    for k, out in enumerate(outs):
        out[...] = dot_nt(grads[...], slab[k]).astype(out.dtype)


def partner(me, k, n):
    return jnp.bitwise_xor(me, k) if n & (n - 1) == 0 else lax.rem(n + k - me, n)


def swap(x, axis, n, k):
    pairs = [(i, i ^ k if n & (n - 1) == 0 else (n + k - i) % n) for i in range(n)]
    return lax.ppermute(x, axis, pairs)


def far_scores(gathered, slab, n_store):
    n_layer, block, features = slab.shape
    queries = gathered[0].shape[0] // S
    vmem = pl.BlockSpec(memory_space=pltpu.VMEM)
    return pl.pallas_call(
        functools.partial(far_kernel, n_store, queries // G),
        out_shape=[jax.ShapeDtypeStruct((n_store * queries, features), bf16)]
        + [
            jax.ShapeDtypeStruct((n_store * queries, block), f32 if k % 2 == 0 else bf16)
            for k in range(2, n_layer)
        ],
        in_specs=[vmem] * (n_store + 1),
        out_specs=[vmem] * (n_layer - 1),
        scratch_shapes=[pltpu.VMEM((n_store,) + gathered[0].shape, bf16)],
        compiler_params=pltpu.CompilerParams(vmem_limit_bytes=24 * 2**20),
        name="far_scores",
    )(*gathered, slab)


def near_scores(grads, slab):
    block, features = slab.shape[1:]
    queries = grads.shape[0]
    vmem = pl.BlockSpec(memory_space=pltpu.VMEM)
    return pl.pallas_call(
        near_kernel,
        out_shape=[
            jax.ShapeDtypeStruct((queries, block), f32),
            jax.ShapeDtypeStruct((queries, block), bf16),
        ],
        in_specs=[vmem] * 2,
        out_specs=[vmem] * 2,
        compiler_params=pltpu.CompilerParams(vmem_limit_bytes=24 * 2**20),
        cost_estimate=pl.CostEstimate(
            flops=4 * queries * block * features,
            bytes_accessed=4 * block * features,
            transcendentals=0,
        ),
        name="near_scores",
    )(grads, slab)


def on_device(n_store, n_layer, hidden, cotangent, lengths, norm_gain, in_proj, out_proj, store):
    queries, positions, width = hidden.shape[1:]
    packed = factors(
        lengths,
        hidden.reshape(queries * positions, width),
        cotangent.reshape(queries * positions, cotangent.shape[3]),
        norm_gain,
        in_proj[0],
        out_proj[0],
    )
    gathered = [packed] + [swap(packed, "store", n_store, k) for k in range(1, n_store)]
    slab = fetch(packed, store[0], n_layer)
    grads, *far = far_scores(gathered, slab, n_store)
    crossed = [swap(x, "layer", n_layer, 1) for x in far[1::2]]
    own, other = near_scores(grads, slab)
    joined = [(x + y.astype(f32)).astype(bf16) for x, y in zip(far[::2], crossed)]
    total = own + swap(other, "layer", n_layer, 1).astype(f32)
    for at, x in enumerate(joined):
        total = total + swap(x, "layer", n_layer, 2 + 2 * at).astype(f32)
    return total.T


def solution(mesh):
    placed = (
        P("layer", ("grp", "store"), None, None),
        P("layer", ("grp", "store"), None, None),
        P(("grp", "store")),
        P("layer", None),
        P("layer", None, None),
        P("layer", None, None),
        P("layer", ("grp", "store"), None),
    )
    return jax.shard_map(
        functools.partial(on_device, mesh.shape["store"], mesh.shape["layer"]),
        mesh=mesh,
        in_specs=placed,
        out_specs=P(("grp", "store", "layer"), None),
        check_vma=False,
    )
```

```python
import functools

import jax
import jax.numpy as jnp
from jax import lax
from jax.experimental import pallas as pl
from jax.experimental.pallas import tpu as pltpu
from jax.sharding import PartitionSpec as P

norm_epsilon = 1e-05
f32 = jnp.float32
bf16 = jnp.bfloat16
S = 8
R = 64
B = 4
A = R // B
G = 8
H = 4
LANES = 128


def dot_nt(left, right):
    return lax.dot_general(left, right, (((1,), (1,)), ((), ())), preferred_element_type=f32)


def iota(shape, dim):
    return lax.broadcasted_iota(jnp.int32, shape, dim)


def factors_kernel(
    cuts,
    hbm_lengths,
    hbm_hidden,
    hbm_cot,
    hbm_gain,
    hbm_inp,
    hbm_outp,
    packed,
    lengths,
    hidden,
    cot,
    gain,
    inp,
    outp,
    weights,
    in_acc,
    out_acc,
    sq_acc,
    out_t,
    sems,
):
    width = hbm_hidden.shape[1]
    queries = lengths.shape[0]
    rows = queries * S
    full = queries // G * G * S
    half = rows - full
    mid, low = full // 2, half // 2

    def start(source, target, at):
        copy = pltpu.make_async_copy(source, target, sems.at[at])
        copy.start()
        return copy

    copy_gain = start(hbm_gain, gain, 0)
    copy_inp = start(hbm_inp, inp, 1)
    copy_outp = start(hbm_outp, outp, 2)
    copy_cot = start(hbm_cot, cot, 3)
    copy_lengths = start(hbm_lengths, lengths, 4)
    tiles = hidden.shape[0]
    copies = [
        start(hbm_hidden.at[:, pl.ds(t * LANES, LANES)], hidden.at[t], 5 + t) for t in range(tiles)
    ]
    odd = lax.rem(lax.axis_index("store"), 2)
    at_full = pl.multiple_of(odd * half, half)
    at_half = pl.multiple_of((1 - odd) * full, half)

    copy_gain.wait()
    copy_inp.wait()
    for at in range(0, width, 512):
        cut = slice(at, at + 512)
        scaled = inp[:, cut].astype(f32) * gain[:, cut].astype(f32)
        high = scaled.astype(bf16)
        weights[:R, cut] = high
        weights[R:, cut] = (scaled - high.astype(f32)).astype(bf16)

    copy_outp.wait()
    copy_cot.wait()
    copy_lengths.wait()
    out_acc[...] = dot_nt(cot[...], outp[...])
    turned = out_acc[pl.ds(at_full, full), :].T
    for t in range(full // 128):
        out_t[t * R : (t + 1) * R, :] = turned[:, t * 128 : (t + 1) * 128]
    out_t[full // 128 * R :, :half] = out_acc[pl.ds(at_half, half), :].T

    def part(t, b):
        return out_t[pl.ds(t * R + b, A, stride=B), :]

    row = mid + low
    for m in range(full // (G * S)):
        t, at = divmod(m * G * S, 128)
        for b in range(0, B, 2):
            both = [part(t, b + c)[:, at : at + G * S] for c in range(2)]
            packed[row : row + A, :] = jnp.concatenate(both, axis=1).astype(bf16)
            row += A
    packed[row : row + A, :] = jnp.concatenate(
        [part(full // 128, b)[:, :half] for b in range(B)], axis=1
    ).astype(bf16)

    for c in range(len(cuts) - 1):
        held = range(cuts[c], cuts[c + 1])
        for t in held:
            copies[t].wait()
        product = dot_nt(
            jnp.concatenate([hidden[t] for t in held], axis=1),
            weights[:, cuts[c] * LANES : cuts[c + 1] * LANES],
        )
        in_acc[...] = product if c == 0 else in_acc[...] + product
        for r in range(0, rows, 16):
            total = None if c == 0 else sq_acc[r : r + 16, :]
            for t in held:
                wide = hidden[t, r : r + 16, :].astype(f32)
                total = wide * wide if total is None else total + wide * wide
            sq_acc[r : r + 16, :] = total

    mean_square = jnp.sum(sq_acc[...], axis=1, keepdims=True) * (1.0 / width)
    factor = in_acc[:, :R] + in_acc[:, R:]
    factor = factor * lax.rsqrt(mean_square + norm_epsilon)
    position = iota((S, R), 0)
    for q in range(queries):
        out_acc[q * S : (q + 1) * S, :] = jnp.where(
            position < lengths[q], factor[q * S : (q + 1) * S], 0.0
        )
    in_full = out_acc[pl.ds(at_full, full), :]
    in_half = out_acc[pl.ds(at_half, half), :]
    packed[:mid, :] = jnp.concatenate([in_full[:mid], in_full[mid:]], axis=1).astype(bf16)
    packed[mid : mid + low, :] = jnp.concatenate([in_half[:low], in_half[low:]], axis=1).astype(
        bf16
    )


def in_hbm(x):
    return pltpu.with_memory_space_constraint(x, pltpu.HBM)


def factors(lengths, hidden, cotangent, gain, in_projection, out_projection):
    rows, width = hidden.shape
    tiles = width // LANES
    cuts = [tiles * part // 8 for part in (0, 2, 4, 6, 7, 8)]
    return pl.pallas_call(
        functools.partial(factors_kernel, cuts),
        out_shape=jax.ShapeDtypeStruct((rows, 2 * R), bf16),
        in_specs=[pl.BlockSpec(memory_space=pl.ANY)] * 6,
        out_specs=pl.BlockSpec(memory_space=pltpu.VMEM),
        scratch_shapes=[
            pltpu.SMEM(lengths.shape, jnp.int32),
            pltpu.VMEM((tiles, rows, LANES), bf16),
            pltpu.VMEM(cotangent.shape, bf16),
            pltpu.VMEM(gain.shape, bf16),
            pltpu.VMEM(in_projection.shape, bf16),
            pltpu.VMEM(out_projection.shape, bf16),
            pltpu.VMEM((2 * R, width), bf16),
            pltpu.VMEM((rows, 2 * R), f32),
            pltpu.VMEM((rows, R), f32),
            pltpu.VMEM((rows, 128), f32),
            pltpu.VMEM((-(-rows // 128) * R, 128), f32),
            pltpu.SemaphoreType.DMA((5 + tiles,)),
        ],
        compiler_params=pltpu.CompilerParams(vmem_limit_bytes=24 * 2**20),
        name="factors",
    )(*[in_hbm(x) for x in (lengths, hidden, cotangent, gain, in_projection, out_projection)])


def fetch_kernel(n_layer, after, store, slab, sems):
    block = slab.shape[0] // n_layer
    rows = 16 if block % 16 == 0 else 8
    me = lax.axis_index("layer")
    copies = []
    for k in range(n_layer):
        at = pl.multiple_of(partner(me, k, n_layer) * block, rows)
        to = slab.at[pl.ds(k * block, block)]
        copies.append(pltpu.make_async_copy(store.at[pl.ds(at, block)], to, sems.at[k]))
        copies[-1].start()
    for copy in copies:
        copy.wait()


def fetch(after, store, n_layer):
    rows, features = store.shape
    return pl.pallas_call(
        functools.partial(fetch_kernel, n_layer),
        out_shape=jax.ShapeDtypeStruct((rows, features), bf16),
        in_specs=[pl.BlockSpec(memory_space=pl.ANY)] * 2,
        out_specs=pl.BlockSpec(memory_space=pltpu.VMEM),
        scratch_shapes=[pltpu.SemaphoreType.DMA((n_layer,))],
        compiler_params=pltpu.CompilerParams(vmem_limit_bytes=12 * 2**20),
        cost_estimate=pl.CostEstimate(
            flops=0, bytes_accessed=2 * rows * features, transcendentals=0
        ),
        name="fetch",
    )(after, in_hbm(store))


def spread_out(tile, owner):
    lanes = tile.shape[1]
    mine = (owner == iota((G, lanes), 0))[None]
    wide = jnp.where(mine, tile.astype(f32)[:, None, :], 0.0)
    return wide.reshape(A * G, lanes).astype(bf16)


def halves(tile):
    wide = tile.astype(f32)
    turned = jnp.concatenate([wide[:, R:], wide[:, :R]], axis=1)
    low = iota(wide.shape, 1) < R
    return [
        jnp.where(mask, x, 0.0).astype(bf16)
        for x in (wide, turned)
        for mask in (low, jnp.logical_not(low))
    ]


def diagonal(low, high):
    zero = jnp.zeros_like(low)
    left = jnp.concatenate([low, high, zero, zero], axis=0)
    right = jnp.concatenate([zero, zero, low, high], axis=0)
    return jnp.concatenate([left, right], axis=1)


def build_grads(shards, base, row0, full_groups, grads):
    mid = full_groups * G * S // 2
    low = H * S // 2
    lane = iota((G, 2 * 128), 1)
    whole_owner = lax.rem(lane, G * S) // S
    half_owner = lax.rem(lane, H * S) // S + H * (lane // 128)

    def whole(shard):
        found = []
        pairs = {}
        for m in range(full_groups):
            first = m % (full_groups // 2)
            if first not in pairs:
                pairs[first] = halves(
                    shards[base + shard, first * G * S : (first + 1) * G * S, :]
                )
            plain_low, plain_high, turned_low, turned_high = pairs[first]
            weights = (
                diagonal(plain_low, turned_high)
                if m < full_groups // 2
                else diagonal(turned_low, plain_high)
            )
            at = mid + low + m * 2 * A
            tile = jnp.concatenate(
                [shards[base + shard, at : at + A, :], shards[base + shard, at + A : at + 2 * A, :]],
                axis=1,
            )
            found.append((spread_out(tile, whole_owner), weights))
        return found

    def joined(shard):
        tiles, weights = [], []
        for s in (shard, shard + 1):
            plain_low, plain_high, turned_low, turned_high = halves(
                shards[base + s, mid : mid + low, :]
            )
            weights.append(
                diagonal(
                    jnp.concatenate([plain_low, turned_low], axis=0),
                    jnp.concatenate([turned_high, plain_high], axis=0),
                )
            )
            at = mid + low + full_groups * 2 * A
            tiles.append(shards[base + s, at : at + A, :])
        return [
            (
                spread_out(jnp.concatenate(tiles, axis=1), half_owner),
                jnp.concatenate(weights, axis=0),
            )
        ]

    groups = []
    for shard in (0, 2):
        groups += whole(shard) + joined(shard) + whole(shard + 1)
    for at in range(0, len(groups), 2):
        first, second = [jnp.dot(x, w, preferred_element_type=f32) for x, w in groups[at : at + 2]]
        for a in range(A):
            pair = [x[a * G : (a + 1) * G] for x in (first, second)]
            grads[pl.ds(row0 + at * G, 2 * G), a * 256 : (a + 1) * 256] = jnp.concatenate(
                pair, axis=0
            ).astype(bf16)


def far_kernel(n_store, full_groups, *refs):
    gathered = refs[:n_store]
    slab, grads = refs[n_store : n_store + 2]
    outs = refs[n_store + 2 : -1]
    shards = refs[-1]
    me_store = lax.axis_index("store")
    for k in range(n_store):
        shards[partner(me_store, k, n_store)] = gathered[k][...]
    four = 4 * (full_groups * G + H)
    if n_store == 4:
        build_grads(shards, 0, 0, full_groups, grads)
    else:

        @pl.loop(0, n_store // 4)
        def _(at):
            build_grads(shards, at * 4, pl.multiple_of(at * four, 16), full_groups, grads)

    score(slab, 2, grads, outs)


def score(slab, first, grads, outs):
    block = outs[0].shape[1]
    rows = slab[first * block : (first + len(outs)) * block, :]
    product = dot_nt(rows, grads[...])
    for at, out in enumerate(outs):
        out[...] = product[at * block : (at + 1) * block].T.astype(out.dtype)


def near_kernel(grads, slab, *outs):
    score(slab, 0, grads, outs)


def partner(me, k, n):
    return jnp.bitwise_xor(me, k) if n & (n - 1) == 0 else lax.rem(n + k - me, n)


def swap(x, axis, n, k):
    pairs = [(i, i ^ k if n & (n - 1) == 0 else (n + k - i) % n) for i in range(n)]
    return lax.ppermute(x, axis, pairs)


def far_scores(gathered, slab, n_store, n_layer):
    rows, features = slab.shape
    block = rows // n_layer
    queries = gathered[0].shape[0] // S
    vmem = pl.BlockSpec(memory_space=pltpu.VMEM)
    return pl.pallas_call(
        functools.partial(far_kernel, n_store, queries // G),
        out_shape=[jax.ShapeDtypeStruct((n_store * queries, features), bf16)]
        + [
            jax.ShapeDtypeStruct((n_store * queries, block), f32 if k % 2 == 0 else bf16)
            for k in range(2, n_layer)
        ],
        in_specs=[vmem] * (n_store + 1),
        out_specs=[vmem] * (n_layer - 1),
        scratch_shapes=[pltpu.VMEM((n_store,) + gathered[0].shape, bf16)],
        compiler_params=pltpu.CompilerParams(vmem_limit_bytes=24 * 2**20),
        name="far_scores",
    )(*gathered, slab)


def near_scores(grads, slab, n_layer):
    rows, features = slab.shape
    block = rows // n_layer
    queries = grads.shape[0]
    vmem = pl.BlockSpec(memory_space=pltpu.VMEM)
    return pl.pallas_call(
        near_kernel,
        out_shape=[
            jax.ShapeDtypeStruct((queries, block), f32),
            jax.ShapeDtypeStruct((queries, block), bf16),
        ],
        in_specs=[vmem] * 2,
        out_specs=[vmem] * 2,
        compiler_params=pltpu.CompilerParams(vmem_limit_bytes=24 * 2**20),
        cost_estimate=pl.CostEstimate(
            flops=4 * queries * block * features,
            bytes_accessed=4 * block * features,
            transcendentals=0,
        ),
        name="near_scores",
    )(grads, slab)


def on_device(n_store, n_layer, hidden, cotangent, lengths, norm_gain, in_proj, out_proj, store):
    queries, positions, width = hidden.shape[1:]
    packed = factors(
        lengths,
        hidden.reshape(queries * positions, width),
        cotangent.reshape(queries * positions, cotangent.shape[3]),
        norm_gain,
        in_proj[0],
        out_proj[0],
    )
    gathered = [packed] + [swap(packed, "store", n_store, k) for k in range(1, n_store)]
    slab = fetch(packed, store[0], n_layer)
    grads, *far = far_scores(gathered, slab, n_store, n_layer)
    crossed = [swap(x, "layer", n_layer, 1) for x in far[1::2]]
    own, other = near_scores(grads, slab, n_layer)
    joined = [(x + y.astype(f32)).astype(bf16) for x, y in zip(far[::2], crossed)]
    total = own + swap(other, "layer", n_layer, 1).astype(f32)
    for at, x in enumerate(joined):
        total = total + swap(x, "layer", n_layer, 2 + 2 * at).astype(f32)
    return total.T


def solution(mesh):
    placed = (
        P("layer", ("grp", "store"), None, None),
        P("layer", ("grp", "store"), None, None),
        P(("grp", "store")),
        P("layer", None),
        P("layer", None, None),
        P("layer", None, None),
        P("layer", ("grp", "store"), None),
    )
    return jax.shard_map(
        functools.partial(on_device, mesh.shape["store"], mesh.shape["layer"]),
        mesh=mesh,
        in_specs=placed,
        out_specs=P(("grp", "store", "layer"), None),
        check_vma=False,
    )
```

```python
import functools

import jax
import jax.numpy as jnp
from jax import lax
from jax.experimental import pallas as pl
from jax.experimental.pallas import tpu as pltpu
from jax.sharding import PartitionSpec as P

norm_epsilon = 1e-05
f32 = jnp.float32
bf16 = jnp.bfloat16
S = 8
R = 64
B = 4
A = R // B
G = 8
H = 4
LANES = 128


def dot_nt(left, right):
    return lax.dot_general(left, right, (((1,), (1,)), ((), ())), preferred_element_type=f32)


def iota(shape, dim):
    return lax.broadcasted_iota(jnp.int32, shape, dim)


def factors_kernel(
    window,
    hbm_lengths,
    hbm_hidden,
    hbm_cot,
    hbm_gain,
    hbm_inp,
    hbm_outp,
    packed,
    lengths,
    hidden,
    cot,
    gain,
    inp,
    outp,
    in_acc,
    out_acc,
    sq_acc,
    out_t,
    sems,
):
    chunks, rows, columns = hidden.shape
    queries = lengths.shape[0]
    full = queries // G * G * S
    half = rows - full
    mid, low = full // 2, half // 2

    def start(source, target, at):
        copy = pltpu.make_async_copy(source, target, sems.at[at])
        copy.start()
        return copy

    def start_chunk(c):
        cut = pl.ds(c * columns, columns)
        return [
            start(hbm_inp.at[:, cut], inp.at[c], 4 + 2 * c),
            start(hbm_hidden.at[:, cut], hidden.at[c], 5 + 2 * c),
        ]

    copy_gain = start(hbm_gain, gain, 0)
    copies = [start_chunk(c) for c in range(window)]
    copy_gain.wait()
    tail = []
    for c in range(chunks):
        for copy in copies[c]:
            copy.wait()
        if c + window < chunks:
            copies.append(start_chunk(c + window))
        elif not tail:
            tail = [
                start(hbm_outp, outp, 1),
                start(hbm_cot, cot, 2),
                start(hbm_lengths, lengths, 3),
            ]
        scaled = inp[c].astype(f32) * gain[:, c * columns : (c + 1) * columns].astype(f32)
        high = scaled.astype(bf16)
        rest = (scaled - high.astype(f32)).astype(bf16)
        product = dot_nt(hidden[c], jnp.concatenate([high, rest], axis=0))
        in_acc[...] = product if c == 0 else in_acc[...] + product
        for r in range(0, rows, 16):
            total = None if c == 0 else sq_acc[r : r + 16, :]
            for at in range(0, columns, LANES):
                wide = hidden[c, r : r + 16, at : at + LANES].astype(f32)
                total = wide * wide if total is None else total + wide * wide
            sq_acc[r : r + 16, :] = total

    for copy in tail:
        copy.wait()
    odd = lax.rem(lax.axis_index("store"), 2)
    at_full = pl.multiple_of(odd * half, half)
    at_half = pl.multiple_of((1 - odd) * full, half)

    mean_square = jnp.sum(sq_acc[...], axis=1, keepdims=True) * (1.0 / (chunks * columns))
    factor = in_acc[:, :R] + in_acc[:, R:]
    factor = factor * lax.rsqrt(mean_square + norm_epsilon)
    position = iota((S, R), 0)
    for q in range(queries):
        in_acc[q * S : (q + 1) * S, :R] = jnp.where(
            position < lengths[q], factor[q * S : (q + 1) * S], 0.0
        )
    out_acc[...] = dot_nt(cot[...], outp[...])
    in_full = in_acc[pl.ds(at_full, full), :R]
    in_half = in_acc[pl.ds(at_half, half), :R]
    packed[:mid, :] = jnp.concatenate([in_full[:mid], in_full[mid:]], axis=1).astype(bf16)
    packed[mid : mid + low, :] = jnp.concatenate([in_half[:low], in_half[low:]], axis=1).astype(
        bf16
    )
    turned = out_acc[pl.ds(at_full, full), :].T
    for t in range(full // LANES):
        out_t[t * R : (t + 1) * R, :] = turned[:, t * LANES : (t + 1) * LANES]
    out_t[full // LANES * R :, :half] = out_acc[pl.ds(at_half, half), :].T

    def part(t, b):
        return out_t[pl.ds(t * R + b, A, stride=B), :]

    row = mid + low
    for m in range(full // (G * S)):
        t, at = divmod(m * G * S, LANES)
        for b in range(0, B, 2):
            both = [part(t, b + c)[:, at : at + G * S] for c in range(2)]
            packed[row : row + A, :] = jnp.concatenate(both, axis=1).astype(bf16)
            row += A
    packed[row : row + A, :] = jnp.concatenate(
        [part(full // LANES, b)[:, :half] for b in range(B)], axis=1
    ).astype(bf16)


def in_hbm(x):
    return pltpu.with_memory_space_constraint(x, pltpu.HBM)


def factors(lengths, hidden, cotangent, gain, in_projection, out_projection):
    rows, width = hidden.shape
    columns = 1024
    chunks = width // columns
    return pl.pallas_call(
        functools.partial(factors_kernel, 3),
        out_shape=jax.ShapeDtypeStruct((rows, 2 * R), bf16),
        in_specs=[pl.BlockSpec(memory_space=pl.ANY)] * 6,
        out_specs=pl.BlockSpec(memory_space=pltpu.VMEM),
        scratch_shapes=[
            pltpu.SMEM(lengths.shape, jnp.int32),
            pltpu.VMEM((chunks, rows, columns), bf16),
            pltpu.VMEM(cotangent.shape, bf16),
            pltpu.VMEM(gain.shape, bf16),
            pltpu.VMEM((chunks, R, columns), bf16),
            pltpu.VMEM(out_projection.shape, bf16),
            pltpu.VMEM((rows, 2 * R), f32),
            pltpu.VMEM((rows, R), f32),
            pltpu.VMEM((rows, LANES), f32),
            pltpu.VMEM((-(-rows // LANES) * R, LANES), f32),
            pltpu.SemaphoreType.DMA((4 + 2 * chunks,)),
        ],
        compiler_params=pltpu.CompilerParams(vmem_limit_bytes=24 * 2**20),
        name="factors",
    )(*[in_hbm(x) for x in (lengths, hidden, cotangent, gain, in_projection, out_projection)])


def fetch_kernel(n_layer, after, store, slab, sems):
    block = slab.shape[0] // n_layer
    rows = 16 if block % 16 == 0 else 8
    me = lax.axis_index("layer")
    copies = []
    for k in range(n_layer):
        at = pl.multiple_of(partner(me, k, n_layer) * block, rows)
        to = slab.at[pl.ds(k * block, block)]
        copies.append(pltpu.make_async_copy(store.at[pl.ds(at, block)], to, sems.at[k]))
        copies[-1].start()
    for copy in copies:
        copy.wait()


def fetch(after, store, n_layer):
    rows, features = store.shape
    return pl.pallas_call(
        functools.partial(fetch_kernel, n_layer),
        out_shape=jax.ShapeDtypeStruct((rows, features), bf16),
        in_specs=[pl.BlockSpec(memory_space=pl.ANY)] * 2,
        out_specs=pl.BlockSpec(memory_space=pltpu.VMEM),
        scratch_shapes=[pltpu.SemaphoreType.DMA((n_layer,))],
        compiler_params=pltpu.CompilerParams(vmem_limit_bytes=12 * 2**20),
        cost_estimate=pl.CostEstimate(
            flops=0, bytes_accessed=2 * rows * features, transcendentals=0
        ),
        name="fetch",
    )(after, in_hbm(store))


def spread_out(tile, owner):
    lanes = tile.shape[1]
    mine = (owner == iota((G, lanes), 0))[None]
    wide = jnp.where(mine, tile.astype(f32)[:, None, :], 0.0)
    return wide.reshape(A * G, lanes).astype(bf16)


def halves(tile):
    wide = tile.astype(f32)
    turned = jnp.concatenate([wide[:, R:], wide[:, :R]], axis=1)
    low = iota(wide.shape, 1) < R
    return [
        jnp.where(mask, x, 0.0).astype(bf16)
        for x in (wide, turned)
        for mask in (low, jnp.logical_not(low))
    ]


def diagonal(low, high):
    zero = jnp.zeros_like(low)
    left = jnp.concatenate([low, high, zero, zero], axis=0)
    right = jnp.concatenate([zero, zero, low, high], axis=0)
    return jnp.concatenate([left, right], axis=1)


def build_grads(shards, base, row0, full_groups, grads):
    mid = full_groups * G * S // 2
    low = H * S // 2
    lane = iota((G, 2 * 128), 1)
    whole_owner = lax.rem(lane, G * S) // S
    half_owner = lax.rem(lane, H * S) // S + H * (lane // 128)

    def whole(shard):
        found = []
        pairs = {}
        for m in range(full_groups):
            first = m % (full_groups // 2)
            if first not in pairs:
                pairs[first] = halves(
                    shards[base + shard, first * G * S : (first + 1) * G * S, :]
                )
            plain_low, plain_high, turned_low, turned_high = pairs[first]
            weights = (
                diagonal(plain_low, turned_high)
                if m < full_groups // 2
                else diagonal(turned_low, plain_high)
            )
            at = mid + low + m * 2 * A
            tile = jnp.concatenate(
                [shards[base + shard, at : at + A, :], shards[base + shard, at + A : at + 2 * A, :]],
                axis=1,
            )
            found.append((spread_out(tile, whole_owner), weights))
        return found

    def joined(shard):
        tiles, weights = [], []
        for s in (shard, shard + 1):
            plain_low, plain_high, turned_low, turned_high = halves(
                shards[base + s, mid : mid + low, :]
            )
            weights.append(
                diagonal(
                    jnp.concatenate([plain_low, turned_low], axis=0),
                    jnp.concatenate([turned_high, plain_high], axis=0),
                )
            )
            at = mid + low + full_groups * 2 * A
            tiles.append(shards[base + s, at : at + A, :])
        return [
            (
                spread_out(jnp.concatenate(tiles, axis=1), half_owner),
                jnp.concatenate(weights, axis=0),
            )
        ]

    groups = []
    for shard in (0, 2):
        groups += whole(shard) + joined(shard) + whole(shard + 1)
    for at in range(0, len(groups), 2):
        first, second = [jnp.dot(x, w, preferred_element_type=f32) for x, w in groups[at : at + 2]]
        for a in range(A):
            pair = [x[a * G : (a + 1) * G] for x in (first, second)]
            grads[pl.ds(row0 + at * G, 2 * G), a * 256 : (a + 1) * 256] = jnp.concatenate(
                pair, axis=0
            ).astype(bf16)


def grads_kernel(n_store, full_groups, k, *refs):
    gathered = refs[:n_store]
    slab, grads, out, shards = refs[n_store:]
    me_store = lax.axis_index("store")
    for at in range(n_store):
        shards[partner(me_store, at, n_store)] = gathered[at][...]
    four = 4 * (full_groups * G + H)
    if n_store == 4:
        build_grads(shards, 0, 0, full_groups, grads)
    else:

        @pl.loop(0, n_store // 4)
        def _(at):
            build_grads(shards, at * 4, pl.multiple_of(at * four, 16), full_groups, grads)

    scores_kernel(k, grads, slab, out)


def scores_kernel(k, grads, slab, *refs):
    *terms, out = refs
    block = out.shape[1]
    total = dot_nt(slab[k * block : (k + 1) * block, :], grads[...]).T
    for term in terms:
        total += term[...].astype(f32)
    out[...] = total.astype(out.dtype)


def partner(me, k, n):
    return jnp.bitwise_xor(me, k) if n & (n - 1) == 0 else lax.rem(n + k - me, n)


def swap(x, axis, n, k):
    pairs = [(i, i ^ k if n & (n - 1) == 0 else (n + k - i) % n) for i in range(n)]
    return lax.ppermute(x, axis, pairs)


def grads_and_scores(gathered, slab, n_store, n_layer, k):
    rows, features = slab.shape
    queries = n_store * gathered[0].shape[0] // S
    vmem = pl.BlockSpec(memory_space=pltpu.VMEM)
    return pl.pallas_call(
        functools.partial(grads_kernel, n_store, queries // n_store // G, k),
        out_shape=[
            jax.ShapeDtypeStruct((queries, features), bf16),
            jax.ShapeDtypeStruct((queries, rows // n_layer), bf16),
        ],
        in_specs=[vmem] * (n_store + 1),
        out_specs=[vmem] * 2,
        scratch_shapes=[pltpu.VMEM((n_store,) + gathered[0].shape, bf16)],
        compiler_params=pltpu.CompilerParams(vmem_limit_bytes=24 * 2**20),
        name="grads",
    )(*gathered, slab)


def scores(grads, slab, n_layer, k, terms=()):
    rows, features = slab.shape
    block = rows // n_layer
    queries = grads.shape[0]
    vmem = pl.BlockSpec(memory_space=pltpu.VMEM)
    return pl.pallas_call(
        functools.partial(scores_kernel, k),
        out_shape=jax.ShapeDtypeStruct((queries, block), bf16 if k else f32),
        in_specs=[vmem] * (2 + len(terms)),
        out_specs=vmem,
        compiler_params=pltpu.CompilerParams(vmem_limit_bytes=24 * 2**20),
        cost_estimate=pl.CostEstimate(
            flops=2 * queries * block * features,
            bytes_accessed=2 * (queries + block) * features,
            transcendentals=0,
        ),
        name="scores",
    )(grads, slab, *terms)


def on_device(n_store, n_layer, hidden, cotangent, lengths, norm_gain, in_proj, out_proj, store):
    queries, positions, width = hidden.shape[1:]
    packed = factors(
        lengths,
        hidden.reshape(queries * positions, width),
        cotangent.reshape(queries * positions, cotangent.shape[3]),
        norm_gain,
        in_proj[0],
        out_proj[0],
    )
    gathered = [packed] + [swap(packed, "store", n_store, k) for k in range(1, n_store)]
    slab = fetch(packed, store[0], n_layer)
    grads, partial = grads_and_scores(gathered, slab, n_store, n_layer, n_layer - 1)
    crossed = [swap(partial, "layer", n_layer, n_layer - 1)]
    for k in reversed(range(1, n_layer - 1)):
        crossed.append(swap(scores(grads, slab, n_layer, k), "layer", n_layer, k))
    total = scores(grads, slab, n_layer, 0, crossed[:1])
    for x in crossed[1:]:
        total = total + x.astype(f32)
    return total.T


def solution(mesh):
    placed = (
        P("layer", ("grp", "store"), None, None),
        P("layer", ("grp", "store"), None, None),
        P(("grp", "store")),
        P("layer", None),
        P("layer", None, None),
        P("layer", None, None),
        P("layer", ("grp", "store"), None),
    )
    return jax.shard_map(
        functools.partial(on_device, mesh.shape["store"], mesh.shape["layer"]),
        mesh=mesh,
        in_specs=placed,
        out_specs=P(("grp", "store", "layer"), None),
        check_vma=False,
    )
```

```python
import functools

import jax
import jax.numpy as jnp
from jax import lax
from jax.experimental import pallas as pl
from jax.experimental.pallas import tpu as pltpu
from jax.sharding import PartitionSpec as P

norm_epsilon = 1e-05
f32 = jnp.float32
bf16 = jnp.bfloat16
S = 8
R = 64
B = 4
A = R // B
G = 8
H = 4
LANES = 128


def dot_nt(left, right):
    return lax.dot_general(left, right, (((1,), (1,)), ((), ())), preferred_element_type=f32)


def iota(shape, dim):
    return lax.broadcasted_iota(jnp.int32, shape, dim)


def factors_kernel(
    window,
    hbm_lengths,
    hbm_hidden,
    hbm_cot,
    hbm_gain,
    hbm_inp,
    hbm_outp,
    packed,
    lengths,
    hidden,
    cot,
    gain,
    inp,
    outp,
    in_acc,
    out_acc,
    sq_acc,
    out_t,
    sems,
):
    chunks, rows, columns = hidden.shape
    queries = lengths.shape[0]
    full = queries // G * G * S
    half = rows - full
    mid, low = full // 2, half // 2

    def start(source, target, at):
        copy = pltpu.make_async_copy(source, target, sems.at[at])
        copy.start()
        return copy

    def start_chunk(c):
        cut = pl.ds(c * columns, columns)
        return [
            start(hbm_inp.at[:, cut], inp.at[c], 4 + 2 * c),
            start(hbm_hidden.at[:, cut], hidden.at[c], 5 + 2 * c),
        ]

    early = [
        start(hbm_outp, outp, 1),
        start(hbm_cot, cot, 2),
        start(hbm_gain, gain, 0),
        start(hbm_lengths, lengths, 3),
    ]
    copies = [start_chunk(c) for c in range(window)]
    for copy in early:
        copy.wait()
    odd = lax.rem(lax.axis_index("store"), 2)
    at_full = pl.multiple_of(odd * half, half)
    at_half = pl.multiple_of((1 - odd) * full, half)

    def pack(row, *parts):
        piece = jnp.concatenate(parts, axis=1).astype(bf16)
        for copy in range(packed.shape[0]):
            packed[copy, row : row + piece.shape[0], :] = piece

    out_acc[...] = dot_nt(cot[...], outp[...])
    turned = out_acc[pl.ds(at_full, full), :].T
    for t in range(full // LANES):
        out_t[t * R : (t + 1) * R, :] = turned[:, t * LANES : (t + 1) * LANES]
    out_t[full // LANES * R :, :half] = out_acc[pl.ds(at_half, half), :].T

    def part(t, b):
        return out_t[pl.ds(t * R + b, A, stride=B), :]

    row = mid + low
    for m in range(full // (G * S)):
        t, at = divmod(m * G * S, LANES)
        for b in range(0, B, 2):
            pack(row, *[part(t, b + c)[:, at : at + G * S] for c in range(2)])
            row += A
    pack(row, *[part(full // LANES, b)[:, :half] for b in range(B)])

    for c in range(chunks):
        for copy in copies[c]:
            copy.wait()
        if c + window < chunks:
            copies.append(start_chunk(c + window))
        scaled = inp[c].astype(f32) * gain[:, c * columns : (c + 1) * columns].astype(f32)
        high = scaled.astype(bf16)
        rest = (scaled - high.astype(f32)).astype(bf16)
        product = dot_nt(hidden[c], jnp.concatenate([high, rest], axis=0))
        in_acc[...] = product if c == 0 else in_acc[...] + product
        for r in range(0, rows, 48):
            wide = hidden[c, r : r + 48, :].astype(f32)
            square = wide * wide
            total = square[:, :LANES]
            for at in range(LANES, columns, LANES):
                total += square[:, at : at + LANES]
            sq_acc[r : r + 48, :] = total if c == 0 else sq_acc[r : r + 48, :] + total

    mean_square = jnp.sum(sq_acc[...], axis=1, keepdims=True) * (1.0 / (chunks * columns))
    factor = in_acc[:, :R] + in_acc[:, R:]
    factor = factor * lax.rsqrt(mean_square + norm_epsilon)
    position = iota((S, R), 0)
    for q in range(queries):
        out_acc[q * S : (q + 1) * S, :] = jnp.where(
            position < lengths[q], factor[q * S : (q + 1) * S], 0.0
        )
    in_full = out_acc[pl.ds(at_full, full), :]
    in_half = out_acc[pl.ds(at_half, half), :]
    pack(0, in_full[:mid], in_full[mid:])
    pack(mid, in_half[:low], in_half[low:])


def in_hbm(x):
    return pltpu.with_memory_space_constraint(x, pltpu.HBM)


def factors(copies, lengths, hidden, cotangent, gain, in_projection, out_projection):
    rows, width = hidden.shape
    columns = 1024
    chunks = width // columns
    return pl.pallas_call(
        functools.partial(factors_kernel, 3),
        out_shape=jax.ShapeDtypeStruct((copies, rows, 2 * R), bf16),
        in_specs=[pl.BlockSpec(memory_space=pl.ANY)] * 6,
        out_specs=pl.BlockSpec(memory_space=pltpu.VMEM),
        scratch_shapes=[
            pltpu.SMEM(lengths.shape, jnp.int32),
            pltpu.VMEM((chunks, rows, columns), bf16),
            pltpu.VMEM(cotangent.shape, bf16),
            pltpu.VMEM(gain.shape, bf16),
            pltpu.VMEM((chunks, R, columns), bf16),
            pltpu.VMEM(out_projection.shape, bf16),
            pltpu.VMEM((rows, 2 * R), f32),
            pltpu.VMEM((rows, R), f32),
            pltpu.VMEM((rows, LANES), f32),
            pltpu.VMEM((-(-rows // LANES) * R, LANES), f32),
            pltpu.SemaphoreType.DMA((4 + 2 * chunks,)),
        ],
        compiler_params=pltpu.CompilerParams(vmem_limit_bytes=24 * 2**20),
        name="factors",
    )(*[in_hbm(x) for x in (lengths, hidden, cotangent, gain, in_projection, out_projection)])


def fetch_kernel(n_layer, after, store, slab, sems):
    block = slab.shape[0] // n_layer
    rows = 16 if block % 16 == 0 else 8
    me = lax.axis_index("layer")
    copies = []
    for k in range(n_layer):
        at = pl.multiple_of(partner(me, k, n_layer) * block, rows)
        to = slab.at[pl.ds(k * block, block)]
        copies.append(pltpu.make_async_copy(store.at[pl.ds(at, block)], to, sems.at[k]))
        copies[-1].start()
    for copy in copies:
        copy.wait()


def fetch(after, store, n_layer):
    rows, features = store.shape
    return pl.pallas_call(
        functools.partial(fetch_kernel, n_layer),
        out_shape=jax.ShapeDtypeStruct((rows, features), bf16),
        in_specs=[pl.BlockSpec(memory_space=pl.ANY)] * 2,
        out_specs=pl.BlockSpec(memory_space=pltpu.VMEM),
        scratch_shapes=[pltpu.SemaphoreType.DMA((n_layer,))],
        compiler_params=pltpu.CompilerParams(vmem_limit_bytes=12 * 2**20),
        cost_estimate=pl.CostEstimate(
            flops=0, bytes_accessed=2 * rows * features, transcendentals=0
        ),
        name="fetch",
    )(after, in_hbm(store))


def spread_out(tile, owner):
    lanes = tile.shape[1]
    mine = (owner == iota((G, lanes), 0))[None]
    wide = jnp.where(mine, tile.astype(f32)[:, None, :], 0.0)
    return wide.reshape(A * G, lanes).astype(bf16)


def halves(tile):
    wide = tile.astype(f32)
    turned = jnp.concatenate([wide[:, R:], wide[:, :R]], axis=1)
    low = iota(wide.shape, 1) < R
    return [
        jnp.where(mask, x, 0.0).astype(bf16)
        for x in (wide, turned)
        for mask in (low, jnp.logical_not(low))
    ]


def diagonal(low, high):
    zero = jnp.zeros_like(low)
    left = jnp.concatenate([low, high, zero, zero], axis=0)
    right = jnp.concatenate([zero, zero, low, high], axis=0)
    return jnp.concatenate([left, right], axis=1)


def build_grads(shards, base, row0, full_groups, grads):
    mid = full_groups * G * S // 2
    low = H * S // 2
    lane = iota((G, 2 * 128), 1)
    whole_owner = lax.rem(lane, G * S) // S
    half_owner = lax.rem(lane, H * S) // S + H * (lane // 128)

    def whole(shard):
        found = []
        pairs = {}
        for m in range(full_groups):
            first = m % (full_groups // 2)
            if first not in pairs:
                pairs[first] = halves(
                    shards[base + shard, first * G * S : (first + 1) * G * S, :]
                )
            plain_low, plain_high, turned_low, turned_high = pairs[first]
            weights = (
                diagonal(plain_low, turned_high)
                if m < full_groups // 2
                else diagonal(turned_low, plain_high)
            )
            at = mid + low + m * 2 * A
            tile = jnp.concatenate(
                [shards[base + shard, at : at + A, :], shards[base + shard, at + A : at + 2 * A, :]],
                axis=1,
            )
            found.append((spread_out(tile, whole_owner), weights))
        return found

    def joined(shard):
        tiles, weights = [], []
        for s in (shard, shard + 1):
            plain_low, plain_high, turned_low, turned_high = halves(
                shards[base + s, mid : mid + low, :]
            )
            weights.append(
                diagonal(
                    jnp.concatenate([plain_low, turned_low], axis=0),
                    jnp.concatenate([turned_high, plain_high], axis=0),
                )
            )
            at = mid + low + full_groups * 2 * A
            tiles.append(shards[base + s, at : at + A, :])
        return [
            (
                spread_out(jnp.concatenate(tiles, axis=1), half_owner),
                jnp.concatenate(weights, axis=0),
            )
        ]

    groups = []
    for shard in (0, 2):
        groups += whole(shard) + joined(shard) + whole(shard + 1)
    for at in range(0, len(groups), 2):
        first, second = [jnp.dot(x, w, preferred_element_type=f32) for x, w in groups[at : at + 2]]
        for a in range(A):
            pair = [x[a * G : (a + 1) * G] for x in (first, second)]
            grads[pl.ds(row0 + at * G, 2 * G), a * 256 : (a + 1) * 256] = jnp.concatenate(
                pair, axis=0
            ).astype(bf16)


def grads_kernel(full_groups, k, shards, slab, grads, out):
    n_store = shards.shape[0]
    four = 4 * (full_groups * G + H)
    if n_store == 4:
        build_grads(shards, 0, 0, full_groups, grads)
    else:

        @pl.loop(0, n_store // 4)
        def _(at):
            build_grads(shards, at * 4, pl.multiple_of(at * four, 16), full_groups, grads)

    scores_kernel(k, grads, slab, out)


def scores_kernel(k, grads, slab, *refs, skip=0):
    *terms, out = refs[skip:]
    block = out.shape[1]
    total = dot_nt(slab[k * block : (k + 1) * block, :], grads[...]).T
    for term in terms:
        total += term[...].astype(f32)
    out[...] = total.astype(out.dtype)


def partner(me, k, n):
    return jnp.bitwise_xor(me, k) if n & (n - 1) == 0 else lax.rem(n + k - me, n)


def swap(x, axis, n, k):
    pairs = [(i, i ^ k if n & (n - 1) == 0 else (n + k - i) % n) for i in range(n)]
    return lax.ppermute(x, axis, pairs)


def grads_and_scores(shards, slab, n_layer, k):
    rows, features = slab.shape
    queries = shards.shape[1] // S
    vmem = pl.BlockSpec(memory_space=pltpu.VMEM)
    return pl.pallas_call(
        functools.partial(grads_kernel, queries // G, k),
        out_shape=[
            jax.ShapeDtypeStruct((shards.shape[0] * queries, features), bf16),
            jax.ShapeDtypeStruct((shards.shape[0] * queries, rows // n_layer), bf16),
        ],
        in_specs=[vmem] * 2,
        out_specs=[vmem] * 2,
        compiler_params=pltpu.CompilerParams(vmem_limit_bytes=24 * 2**20),
        name="grads",
    )(shards, slab)


def scores(grads, slab, n_layer, k, terms=(), after=()):
    rows, features = slab.shape
    block = rows // n_layer
    queries = grads.shape[0]
    vmem = pl.BlockSpec(memory_space=pltpu.VMEM)
    return pl.pallas_call(
        functools.partial(scores_kernel, k, skip=len(after)),
        out_shape=jax.ShapeDtypeStruct((queries, block), bf16 if k else f32),
        in_specs=[vmem] * 2
        + [pl.BlockSpec(memory_space=pl.ANY)] * len(after)
        + [vmem] * len(terms),
        out_specs=vmem,
        compiler_params=pltpu.CompilerParams(vmem_limit_bytes=24 * 2**20),
        cost_estimate=pl.CostEstimate(
            flops=2 * queries * block * features,
            bytes_accessed=2 * (queries + block) * features,
            transcendentals=0,
        ),
        name="scores",
    )(grads, slab, *after, *terms)


def on_device(n_store, n_layer, hidden, cotangent, lengths, norm_gain, in_proj, out_proj, store):
    queries, positions, width = hidden.shape[1:]
    packed = factors(
        n_store,
        lengths,
        hidden.reshape(queries * positions, width),
        cotangent.reshape(queries * positions, cotangent.shape[3]),
        norm_gain,
        in_proj[0],
        out_proj[0],
    )
    shards = lax.all_to_all(packed, "store", 0, 0)
    slab = fetch(packed, store[0], n_layer)
    grads, partial = grads_and_scores(shards, slab, n_layer, n_layer - 1)
    crossed = [swap(partial, "layer", n_layer, n_layer - 1)]
    for k in reversed(range(1, n_layer - 1)):
        after = crossed[:1] if k == 1 else []
        crossed.append(swap(scores(grads, slab, n_layer, k, after=after), "layer", n_layer, k))
    total = scores(grads, slab, n_layer, 0, terms=crossed[:1])
    for x in crossed[1:]:
        total = total + x.astype(f32)
    return total.T


def solution(mesh):
    placed = (
        P("layer", ("grp", "store"), None, None),
        P("layer", ("grp", "store"), None, None),
        P(("grp", "store")),
        P("layer", None),
        P("layer", None, None),
        P("layer", None, None),
        P("layer", ("grp", "store"), None),
    )
    return jax.shard_map(
        functools.partial(on_device, mesh.shape["store"], mesh.shape["layer"]),
        mesh=mesh,
        in_specs=placed,
        out_specs=P(("grp", "store", "layer"), None),
        check_vma=False,
    )
```

```python
import functools

import jax
import jax.numpy as jnp
from jax import lax
from jax.experimental import pallas as pl
from jax.experimental.pallas import tpu as pltpu
from jax.sharding import PartitionSpec as P

norm_epsilon = 1e-05
f32 = jnp.float32
bf16 = jnp.bfloat16
S = 8
R = 64
B = 4
A = R // B
G = 8
H = 4
LANES = 128


def dot_nt(left, right):
    return lax.dot_general(left, right, (((1,), (1,)), ((), ())), preferred_element_type=f32)


def iota(shape, dim):
    return lax.broadcasted_iota(jnp.int32, shape, dim)


def factors_kernel(
    hbm_lengths,
    hbm_hidden,
    hbm_cot,
    hbm_gain,
    hbm_inp,
    hbm_outp,
    packed,
    lengths,
    hidden,
    cot,
    gain,
    inp,
    outp,
    in_acc,
    out_acc,
    sq_acc,
    out_t,
    sems,
):
    chunks, rows, columns = hidden.shape
    queries = lengths.shape[0]
    full = queries // G * G * S
    half = rows - full
    mid, low = full // 2, half // 2

    def start(source, target, at):
        copy = pltpu.make_async_copy(source, target, sems.at[at])
        copy.start()
        return copy

    copies = []

    def start_chunks(upto):
        for c in range(len(copies), min(upto, chunks)):
            cut = pl.ds(c * columns, columns)
            copies.append(
                [
                    start(hbm_inp.at[:, cut], inp.at[c], 4 + 2 * c),
                    start(hbm_hidden.at[:, cut], hidden.at[c], 5 + 2 * c),
                ]
            )

    copy_gain = start(hbm_gain, gain, 0)
    early = [start(hbm_outp, outp, 1), start(hbm_cot, cot, 2), start(hbm_lengths, lengths, 3)]
    start_chunks(1)
    copy_gain.wait()
    start_chunks(3)
    for copy in early:
        copy.wait()
    start_chunks(4)
    odd = lax.rem(lax.axis_index("store"), 2)
    at_full = pl.multiple_of(odd * half, half)
    at_half = pl.multiple_of((1 - odd) * full, half)

    def pack(row, *parts):
        piece = jnp.concatenate(parts, axis=1).astype(bf16)
        packed[row : row + piece.shape[0], :] = piece

    out_acc[...] = dot_nt(cot[...], outp[...])
    turned = out_acc[pl.ds(at_full, full), :].T
    for t in range(full // LANES):
        out_t[t * R : (t + 1) * R, :] = turned[:, t * LANES : (t + 1) * LANES]
    out_t[full // LANES * R :, :half] = out_acc[pl.ds(at_half, half), :].T

    def part(t, b):
        return out_t[pl.ds(t * R + b, A, stride=B), :]

    row = mid + low
    for m in range(full // (G * S)):
        t, at = divmod(m * G * S, LANES)
        for b in range(0, B, 2):
            pack(row, *[part(t, b + c)[:, at : at + G * S] for c in range(2)])
            row += A
    pack(row, *[part(full // LANES, b)[:, :half] for b in range(B)])

    for c in range(chunks):
        for copy in copies[c]:
            copy.wait()
        start_chunks(c + 5)
        scaled = inp[c].astype(f32) * gain[:, c * columns : (c + 1) * columns].astype(f32)
        high = scaled.astype(bf16)
        rest = (scaled - high.astype(f32)).astype(bf16)
        product = dot_nt(hidden[c], jnp.concatenate([high, rest], axis=0))
        in_acc[...] = product if c == 0 else in_acc[...] + product
        for r in range(0, rows, 48):
            wide = hidden[c, r : r + 48, :].astype(f32)
            square = wide * wide
            total = square[:, :LANES]
            for at in range(LANES, columns, LANES):
                total += square[:, at : at + LANES]
            sq_acc[r : r + 48, :] = total if c == 0 else sq_acc[r : r + 48, :] + total

    mean_square = jnp.sum(sq_acc[...], axis=1, keepdims=True) * (1.0 / (chunks * columns))
    factor = in_acc[:, :R] + in_acc[:, R:]
    factor = factor * lax.rsqrt(mean_square + norm_epsilon)
    position = iota((S, R), 0)
    for q in range(queries):
        out_acc[q * S : (q + 1) * S, :] = jnp.where(
            position < lengths[q], factor[q * S : (q + 1) * S], 0.0
        )
    in_full = out_acc[pl.ds(at_full, full), :]
    in_half = out_acc[pl.ds(at_half, half), :]
    pack(0, in_full[:mid], in_full[mid:])
    pack(mid, in_half[:low], in_half[low:])


def in_hbm(x):
    return pltpu.with_memory_space_constraint(x, pltpu.HBM)


def factors(lengths, hidden, cotangent, gain, in_projection, out_projection):
    rows, width = hidden.shape
    columns = 1024
    chunks = width // columns
    return pl.pallas_call(
        factors_kernel,
        out_shape=jax.ShapeDtypeStruct((rows, 2 * R), bf16),
        in_specs=[pl.BlockSpec(memory_space=pl.ANY)] * 6,
        out_specs=pl.BlockSpec(memory_space=pltpu.VMEM),
        scratch_shapes=[
            pltpu.SMEM(lengths.shape, jnp.int32),
            pltpu.VMEM((chunks, rows, columns), bf16),
            pltpu.VMEM(cotangent.shape, bf16),
            pltpu.VMEM(gain.shape, bf16),
            pltpu.VMEM((chunks, R, columns), bf16),
            pltpu.VMEM(out_projection.shape, bf16),
            pltpu.VMEM((rows, 2 * R), f32),
            pltpu.VMEM((rows, R), f32),
            pltpu.VMEM((rows, LANES), f32),
            pltpu.VMEM((-(-rows // LANES) * R, LANES), f32),
            pltpu.SemaphoreType.DMA((4 + 2 * chunks,)),
        ],
        compiler_params=pltpu.CompilerParams(vmem_limit_bytes=24 * 2**20),
        name="factors",
    )(*[in_hbm(x) for x in (lengths, hidden, cotangent, gain, in_projection, out_projection)])


def fetch_kernel(n_layer, after, store, slab, sems):
    block = slab.shape[0] // n_layer
    rows = 16 if block % 16 == 0 else 8
    me = lax.axis_index("layer")
    copies = []
    for k in range(n_layer):
        at = pl.multiple_of(partner(me, k, n_layer) * block, rows)
        to = slab.at[pl.ds(k * block, block)]
        copies.append(pltpu.make_async_copy(store.at[pl.ds(at, block)], to, sems.at[k]))
        copies[-1].start()
    for copy in copies:
        copy.wait()


def fetch(after, store, n_layer):
    rows, features = store.shape
    return pl.pallas_call(
        functools.partial(fetch_kernel, n_layer),
        out_shape=jax.ShapeDtypeStruct((rows, features), bf16),
        in_specs=[pl.BlockSpec(memory_space=pl.ANY)] * 2,
        out_specs=pl.BlockSpec(memory_space=pltpu.VMEM),
        scratch_shapes=[pltpu.SemaphoreType.DMA((n_layer,))],
        compiler_params=pltpu.CompilerParams(vmem_limit_bytes=12 * 2**20),
        cost_estimate=pl.CostEstimate(
            flops=0, bytes_accessed=2 * rows * features, transcendentals=0
        ),
        name="fetch",
    )(after, in_hbm(store))


def spread_out(tile, owner):
    lanes = tile.shape[1]
    mine = (owner == iota((G, lanes), 0))[None]
    wide = jnp.where(mine, tile.astype(f32)[:, None, :], 0.0)
    return wide.reshape(A * G, lanes).astype(bf16)


def halves(tile):
    wide = tile.astype(f32)
    turned = jnp.concatenate([wide[:, R:], wide[:, :R]], axis=1)
    low = iota(wide.shape, 1) < R
    return [
        jnp.where(mask, x, 0.0).astype(bf16)
        for x in (wide, turned)
        for mask in (low, jnp.logical_not(low))
    ]


def diagonal(low, high):
    zero = jnp.zeros_like(low)
    left = jnp.concatenate([low, high, zero, zero], axis=0)
    right = jnp.concatenate([zero, zero, low, high], axis=0)
    return jnp.concatenate([left, right], axis=1)


def build_grads(shards, base, row0, full_groups, grads):
    mid = full_groups * G * S // 2
    low = H * S // 2
    lane = iota((G, 2 * 128), 1)
    whole_owner = lax.rem(lane, G * S) // S
    half_owner = lax.rem(lane, H * S) // S + H * (lane // 128)

    def whole(shard):
        found = []
        pairs = {}
        for m in range(full_groups):
            first = m % (full_groups // 2)
            if first not in pairs:
                pairs[first] = halves(
                    shards[base + shard, first * G * S : (first + 1) * G * S, :]
                )
            plain_low, plain_high, turned_low, turned_high = pairs[first]
            weights = (
                diagonal(plain_low, turned_high)
                if m < full_groups // 2
                else diagonal(turned_low, plain_high)
            )
            at = mid + low + m * 2 * A
            tile = jnp.concatenate(
                [shards[base + shard, at : at + A, :], shards[base + shard, at + A : at + 2 * A, :]],
                axis=1,
            )
            found.append((spread_out(tile, whole_owner), weights))
        return found

    def joined(shard):
        tiles, weights = [], []
        for s in (shard, shard + 1):
            plain_low, plain_high, turned_low, turned_high = halves(
                shards[base + s, mid : mid + low, :]
            )
            weights.append(
                diagonal(
                    jnp.concatenate([plain_low, turned_low], axis=0),
                    jnp.concatenate([turned_high, plain_high], axis=0),
                )
            )
            at = mid + low + full_groups * 2 * A
            tiles.append(shards[base + s, at : at + A, :])
        return [
            (
                spread_out(jnp.concatenate(tiles, axis=1), half_owner),
                jnp.concatenate(weights, axis=0),
            )
        ]

    groups = []
    for shard in (0, 2):
        groups += whole(shard) + joined(shard) + whole(shard + 1)
    for at in range(0, len(groups), 2):
        first, second = [jnp.dot(x, w, preferred_element_type=f32) for x, w in groups[at : at + 2]]
        for a in range(A):
            pair = [x[a * G : (a + 1) * G] for x in (first, second)]
            grads[pl.ds(row0 + at * G, 2 * G), a * 256 : (a + 1) * 256] = jnp.concatenate(
                pair, axis=0
            ).astype(bf16)


def grads_kernel(n_store, full_groups, k, *refs):
    gathered = refs[:n_store]
    slab, grads, out, shards = refs[n_store:]
    me_store = lax.axis_index("store")
    for at in range(n_store):
        shards[partner(me_store, at, n_store)] = gathered[at][...]
    four = 4 * (full_groups * G + H)
    if n_store == 4:
        build_grads(shards, 0, 0, full_groups, grads)
    else:

        @pl.loop(0, n_store // 4)
        def _(at):
            build_grads(shards, at * 4, pl.multiple_of(at * four, 16), full_groups, grads)

    scores_kernel(k, grads, slab, out)


def scores_kernel(k, grads, slab, *refs):
    *terms, out = refs
    block = out.shape[1]
    total = dot_nt(slab[k * block : (k + 1) * block, :], grads[...]).T
    for term in terms:
        total += term[...].astype(f32)
    out[...] = total.astype(out.dtype)


def partner(me, k, n):
    return jnp.bitwise_xor(me, k) if n & (n - 1) == 0 else lax.rem(n + k - me, n)


def swap(x, axis, n, k):
    pairs = [(i, i ^ k if n & (n - 1) == 0 else (n + k - i) % n) for i in range(n)]
    return lax.ppermute(x, axis, pairs)


def grads_and_scores(gathered, slab, n_store, n_layer, k):
    rows, features = slab.shape
    queries = n_store * gathered[0].shape[0] // S
    vmem = pl.BlockSpec(memory_space=pltpu.VMEM)
    return pl.pallas_call(
        functools.partial(grads_kernel, n_store, queries // n_store // G, k),
        out_shape=[
            jax.ShapeDtypeStruct((queries, features), bf16),
            jax.ShapeDtypeStruct((queries, rows // n_layer), bf16),
        ],
        in_specs=[vmem] * (n_store + 1),
        out_specs=[vmem] * 2,
        scratch_shapes=[pltpu.VMEM((n_store,) + gathered[0].shape, bf16)],
        compiler_params=pltpu.CompilerParams(vmem_limit_bytes=24 * 2**20),
        name="grads",
    )(*gathered, slab)


def scores(grads, slab, n_layer, k, terms=()):
    rows, features = slab.shape
    block = rows // n_layer
    queries = grads.shape[0]
    vmem = pl.BlockSpec(memory_space=pltpu.VMEM)
    return pl.pallas_call(
        functools.partial(scores_kernel, k),
        out_shape=jax.ShapeDtypeStruct((queries, block), bf16 if k else f32),
        in_specs=[vmem] * (2 + len(terms)),
        out_specs=vmem,
        compiler_params=pltpu.CompilerParams(vmem_limit_bytes=24 * 2**20),
        cost_estimate=pl.CostEstimate(
            flops=2 * queries * block * features,
            bytes_accessed=2 * (queries + block) * features,
            transcendentals=0,
        ),
        name="scores",
    )(grads, slab, *terms)


def on_device(n_store, n_layer, hidden, cotangent, lengths, norm_gain, in_proj, out_proj, store):
    queries, positions, width = hidden.shape[1:]
    packed = factors(
        lengths,
        hidden.reshape(queries * positions, width),
        cotangent.reshape(queries * positions, cotangent.shape[3]),
        norm_gain,
        in_proj[0],
        out_proj[0],
    )
    gathered = [packed] + [swap(packed, "store", n_store, k) for k in range(1, n_store)]
    slab = fetch(packed, store[0], n_layer)
    grads, partial = grads_and_scores(gathered, slab, n_store, n_layer, n_layer - 1)
    crossed = [swap(partial, "layer", n_layer, n_layer - 1)]
    for k in reversed(range(1, n_layer - 1)):
        crossed.append(swap(scores(grads, slab, n_layer, k), "layer", n_layer, k))
    total = scores(grads, slab, n_layer, 0, crossed[:1])
    for x in crossed[1:]:
        total = total + x.astype(f32)
    return total.T


def solution(mesh):
    placed = (
        P("layer", ("grp", "store"), None, None),
        P("layer", ("grp", "store"), None, None),
        P(("grp", "store")),
        P("layer", None),
        P("layer", None, None),
        P("layer", None, None),
        P("layer", ("grp", "store"), None),
    )
    return jax.shard_map(
        functools.partial(on_device, mesh.shape["store"], mesh.shape["layer"]),
        mesh=mesh,
        in_specs=placed,
        out_specs=P(("grp", "store", "layer"), None),
        check_vma=False,
    )
```

```python
import functools

import jax
import jax.numpy as jnp
from jax import lax
from jax.experimental import pallas as pl
from jax.experimental.pallas import tpu as pltpu
from jax.sharding import PartitionSpec as P

norm_epsilon = 1e-05
f32 = jnp.float32
bf16 = jnp.bfloat16
S = 8
R = 64
B = 4
A = R // B
G = 8
H = 4
LANES = 128


def dot_nt(left, right):
    return lax.dot_general(left, right, (((1,), (1,)), ((), ())), preferred_element_type=f32)


def iota(shape, dim):
    return lax.broadcasted_iota(jnp.int32, shape, dim)


def factors_kernel(
    window,
    hbm_lengths,
    hbm_hidden,
    hbm_cot,
    hbm_gain,
    hbm_inp,
    hbm_outp,
    packed,
    lengths,
    hidden,
    cot,
    gain,
    inp,
    outp,
    in_acc,
    out_acc,
    sq_acc,
    out_t,
    sems,
):
    chunks, rows, columns = hidden.shape
    queries = lengths.shape[0]
    full = queries // G * G * S
    half = rows - full
    mid, low = full // 2, half // 2

    def copy(source, target, at):
        return pltpu.make_async_copy(source, target, sems.at[at])

    def chunk(c):
        cut = pl.ds(pl.multiple_of(c * columns, columns), columns)
        return [
            copy(hbm_gain.at[:, cut], gain.at[c], 3 + c),
            copy(hbm_inp.at[:, cut], inp.at[c], 3 + chunks + c),
            copy(hbm_hidden.at[:, cut], hidden.at[c], 3 + 2 * chunks + c),
        ]

    def start_chunk(c):
        for piece in chunk(c):
            piece.start()

    early = [copy(hbm_outp, outp, 0), copy(hbm_cot, cot, 1), copy(hbm_lengths, lengths, 2)]
    for piece in early:
        piece.start()
    for c in range(window):
        start_chunk(c)
    in_acc[...] = jnp.zeros_like(in_acc)
    sq_acc[...] = jnp.zeros_like(sq_acc)
    for piece in early:
        piece.wait()
    odd = lax.rem(lax.axis_index("store"), 2)
    at_full = pl.multiple_of(odd * half, half)
    at_half = pl.multiple_of((1 - odd) * full, half)

    def pack(row, *parts):
        piece = jnp.concatenate(parts, axis=1).astype(bf16)
        packed[row : row + piece.shape[0], :] = piece

    out_acc[...] = dot_nt(cot[...], outp[...])
    turned = out_acc[pl.ds(at_full, full), :].T
    for t in range(full // LANES):
        out_t[t * R : (t + 1) * R, :] = turned[:, t * LANES : (t + 1) * LANES]
    out_t[full // LANES * R :, :half] = out_acc[pl.ds(at_half, half), :].T

    def part(t, b):
        return out_t[pl.ds(t * R + b, A, stride=B), :]

    row = mid + low
    for m in range(full // (G * S)):
        t, at = divmod(m * G * S, LANES)
        for b in range(0, B, 2):
            pack(row, *[part(t, b + c)[:, at : at + G * S] for c in range(2)])
            row += A
    pack(row, *[part(full // LANES, b)[:, :half] for b in range(B)])

    @pl.loop(0, chunks)
    def _(c):
        for piece in chunk(c):
            piece.wait()

        @pl.when(c + window < chunks)
        def _():
            start_chunk(c + window)

        scaled = inp[c].astype(f32) * gain[c].astype(f32)
        high = scaled.astype(bf16)
        rest = (scaled - high.astype(f32)).astype(bf16)
        in_acc[...] += dot_nt(hidden[c], jnp.concatenate([high, rest], axis=0))
        for r in range(0, rows, 48):
            wide = hidden[c, r : r + 48, :].astype(f32)
            square = wide * wide
            total = square[:, :LANES]
            for at in range(LANES, columns, LANES):
                total += square[:, at : at + LANES]
            sq_acc[r : r + 48, :] += total

    mean_square = jnp.sum(sq_acc[...], axis=1, keepdims=True) * (1.0 / (chunks * columns))
    factor = in_acc[:, :R] + in_acc[:, R:]
    factor = factor * lax.rsqrt(mean_square + norm_epsilon)
    position = iota((S, R), 0)
    for q in range(queries):
        out_acc[q * S : (q + 1) * S, :] = jnp.where(
            position < lengths[q], factor[q * S : (q + 1) * S], 0.0
        )
    in_full = out_acc[pl.ds(at_full, full), :]
    in_half = out_acc[pl.ds(at_half, half), :]
    pack(0, in_full[:mid], in_full[mid:])
    pack(mid, in_half[:low], in_half[low:])


def in_hbm(x):
    return pltpu.with_memory_space_constraint(x, pltpu.HBM)


def factors(lengths, hidden, cotangent, gain, in_projection, out_projection):
    rows, width = hidden.shape
    columns = 1024
    chunks = width // columns
    return pl.pallas_call(
        functools.partial(factors_kernel, 4),
        out_shape=jax.ShapeDtypeStruct((rows, 2 * R), bf16),
        in_specs=[pl.BlockSpec(memory_space=pl.ANY)] * 6,
        out_specs=pl.BlockSpec(memory_space=pltpu.VMEM),
        scratch_shapes=[
            pltpu.SMEM(lengths.shape, jnp.int32),
            pltpu.VMEM((chunks, rows, columns), bf16),
            pltpu.VMEM(cotangent.shape, bf16),
            pltpu.VMEM((chunks, 1, columns), bf16),
            pltpu.VMEM((chunks, R, columns), bf16),
            pltpu.VMEM(out_projection.shape, bf16),
            pltpu.VMEM((rows, 2 * R), f32),
            pltpu.VMEM((rows, R), f32),
            pltpu.VMEM((rows, LANES), f32),
            pltpu.VMEM((-(-rows // LANES) * R, LANES), f32),
            pltpu.SemaphoreType.DMA((3 + 3 * chunks,)),
        ],
        compiler_params=pltpu.CompilerParams(vmem_limit_bytes=24 * 2**20),
        name="factors",
    )(*[in_hbm(x) for x in (lengths, hidden, cotangent, gain, in_projection, out_projection)])


def fetch_kernel(n_layer, after, store, slab, sems):
    block = slab.shape[0] // n_layer
    rows = 16 if block % 16 == 0 else 8
    me = lax.axis_index("layer")
    copies = []
    for k in range(n_layer):
        at = pl.multiple_of(partner(me, k, n_layer) * block, rows)
        to = slab.at[pl.ds(k * block, block)]
        copies.append(pltpu.make_async_copy(store.at[pl.ds(at, block)], to, sems.at[k]))
        copies[-1].start()
    for copy in copies:
        copy.wait()


def fetch(after, store, n_layer):
    rows, features = store.shape
    return pl.pallas_call(
        functools.partial(fetch_kernel, n_layer),
        out_shape=jax.ShapeDtypeStruct((rows, features), bf16),
        in_specs=[pl.BlockSpec(memory_space=pl.ANY)] * 2,
        out_specs=pl.BlockSpec(memory_space=pltpu.VMEM),
        scratch_shapes=[pltpu.SemaphoreType.DMA((n_layer,))],
        compiler_params=pltpu.CompilerParams(vmem_limit_bytes=12 * 2**20),
        cost_estimate=pl.CostEstimate(
            flops=0, bytes_accessed=2 * rows * features, transcendentals=0
        ),
        name="fetch",
    )(after, in_hbm(store))


def spread_out(tile, owner):
    lanes = tile.shape[1]
    mine = (owner == iota((G, lanes), 0))[None]
    wide = jnp.where(mine, tile.astype(f32)[:, None, :], 0.0)
    return wide.reshape(A * G, lanes).astype(bf16)


def halves(tile):
    wide = tile.astype(f32)
    turned = jnp.concatenate([wide[:, R:], wide[:, :R]], axis=1)
    low = iota(wide.shape, 1) < R
    return [
        jnp.where(mask, x, 0.0).astype(bf16)
        for x in (wide, turned)
        for mask in (low, jnp.logical_not(low))
    ]


def diagonal(low, high):
    zero = jnp.zeros_like(low)
    left = jnp.concatenate([low, high, zero, zero], axis=0)
    right = jnp.concatenate([zero, zero, low, high], axis=0)
    return jnp.concatenate([left, right], axis=1)


def build_grads(shards, base, row0, full_groups, grads):
    mid = full_groups * G * S // 2
    low = H * S // 2
    lane = iota((G, 2 * 128), 1)
    whole_owner = lax.rem(lane, G * S) // S
    half_owner = lax.rem(lane, H * S) // S + H * (lane // 128)

    def whole(shard):
        found = []
        pairs = {}
        for m in range(full_groups):
            first = m % (full_groups // 2)
            if first not in pairs:
                pairs[first] = halves(
                    shards[base + shard, first * G * S : (first + 1) * G * S, :]
                )
            plain_low, plain_high, turned_low, turned_high = pairs[first]
            weights = (
                diagonal(plain_low, turned_high)
                if m < full_groups // 2
                else diagonal(turned_low, plain_high)
            )
            at = mid + low + m * 2 * A
            tile = jnp.concatenate(
                [shards[base + shard, at : at + A, :], shards[base + shard, at + A : at + 2 * A, :]],
                axis=1,
            )
            found.append((spread_out(tile, whole_owner), weights))
        return found

    def joined(shard):
        tiles, weights = [], []
        for s in (shard, shard + 1):
            plain_low, plain_high, turned_low, turned_high = halves(
                shards[base + s, mid : mid + low, :]
            )
            weights.append(
                diagonal(
                    jnp.concatenate([plain_low, turned_low], axis=0),
                    jnp.concatenate([turned_high, plain_high], axis=0),
                )
            )
            at = mid + low + full_groups * 2 * A
            tiles.append(shards[base + s, at : at + A, :])
        return [
            (
                spread_out(jnp.concatenate(tiles, axis=1), half_owner),
                jnp.concatenate(weights, axis=0),
            )
        ]

    groups = []
    for shard in (0, 2):
        groups += whole(shard) + joined(shard) + whole(shard + 1)
    for at in range(0, len(groups), 2):
        first, second = [jnp.dot(x, w, preferred_element_type=f32) for x, w in groups[at : at + 2]]
        for a in range(A):
            pair = [x[a * G : (a + 1) * G] for x in (first, second)]
            grads[pl.ds(row0 + at * G, 2 * G), a * 256 : (a + 1) * 256] = jnp.concatenate(
                pair, axis=0
            ).astype(bf16)


def grads_kernel(n_store, full_groups, k, *refs):
    gathered = refs[:n_store]
    slab, grads, out, shards = refs[n_store:]
    me_store = lax.axis_index("store")
    for at in range(n_store):
        shards[partner(me_store, at, n_store)] = gathered[at][...]
    four = 4 * (full_groups * G + H)
    if n_store == 4:
        build_grads(shards, 0, 0, full_groups, grads)
    else:

        @pl.loop(0, n_store // 4)
        def _(at):
            build_grads(shards, at * 4, pl.multiple_of(at * four, 16), full_groups, grads)

    scores_kernel(k, grads, slab, out)


def scores_kernel(k, grads, slab, *refs):
    *terms, out = refs
    block = out.shape[1]
    total = dot_nt(slab[k * block : (k + 1) * block, :], grads[...]).T
    for term in terms:
        total += term[...].astype(f32)
    out[...] = total.astype(out.dtype)


def partner(me, k, n):
    return jnp.bitwise_xor(me, k) if n & (n - 1) == 0 else lax.rem(n + k - me, n)


def swap(x, axis, n, k):
    pairs = [(i, i ^ k if n & (n - 1) == 0 else (n + k - i) % n) for i in range(n)]
    return lax.ppermute(x, axis, pairs)


def grads_and_scores(gathered, slab, n_store, n_layer, k):
    rows, features = slab.shape
    queries = n_store * gathered[0].shape[0] // S
    vmem = pl.BlockSpec(memory_space=pltpu.VMEM)
    return pl.pallas_call(
        functools.partial(grads_kernel, n_store, queries // n_store // G, k),
        out_shape=[
            jax.ShapeDtypeStruct((queries, features), bf16),
            jax.ShapeDtypeStruct((queries, rows // n_layer), bf16),
        ],
        in_specs=[vmem] * (n_store + 1),
        out_specs=[vmem] * 2,
        scratch_shapes=[pltpu.VMEM((n_store,) + gathered[0].shape, bf16)],
        compiler_params=pltpu.CompilerParams(vmem_limit_bytes=24 * 2**20),
        name="grads",
    )(*gathered, slab)


def scores(grads, slab, n_layer, k, terms=()):
    rows, features = slab.shape
    block = rows // n_layer
    queries = grads.shape[0]
    vmem = pl.BlockSpec(memory_space=pltpu.VMEM)
    return pl.pallas_call(
        functools.partial(scores_kernel, k),
        out_shape=jax.ShapeDtypeStruct((queries, block), bf16 if k else f32),
        in_specs=[vmem] * (2 + len(terms)),
        out_specs=vmem,
        compiler_params=pltpu.CompilerParams(vmem_limit_bytes=24 * 2**20),
        cost_estimate=pl.CostEstimate(
            flops=2 * queries * block * features,
            bytes_accessed=2 * (queries + block) * features,
            transcendentals=0,
        ),
        name="scores",
    )(grads, slab, *terms)


def on_device(n_store, n_layer, hidden, cotangent, lengths, norm_gain, in_proj, out_proj, store):
    queries, positions, width = hidden.shape[1:]
    packed = factors(
        lengths,
        hidden.reshape(queries * positions, width),
        cotangent.reshape(queries * positions, cotangent.shape[3]),
        norm_gain,
        in_proj[0],
        out_proj[0],
    )
    gathered = [packed] + [swap(packed, "store", n_store, k) for k in range(1, n_store)]
    slab = fetch(packed, store[0], n_layer)
    grads, partial = grads_and_scores(gathered, slab, n_store, n_layer, n_layer - 1)
    crossed = [swap(partial, "layer", n_layer, n_layer - 1)]
    for k in reversed(range(1, n_layer - 1)):
        crossed.append(swap(scores(grads, slab, n_layer, k), "layer", n_layer, k))
    total = scores(grads, slab, n_layer, 0, crossed[:1])
    for x in crossed[1:]:
        total = total + x.astype(f32)
    return total.T


def solution(mesh):
    placed = (
        P("layer", ("grp", "store"), None, None),
        P("layer", ("grp", "store"), None, None),
        P(("grp", "store")),
        P("layer", None),
        P("layer", None, None),
        P("layer", None, None),
        P("layer", ("grp", "store"), None),
    )
    return jax.shard_map(
        functools.partial(on_device, mesh.shape["store"], mesh.shape["layer"]),
        mesh=mesh,
        in_specs=placed,
        out_specs=P(("grp", "store", "layer"), None),
        check_vma=False,
    )
```

```python
import functools

import jax
import jax.numpy as jnp
from jax import lax
from jax.experimental import pallas as pl
from jax.experimental.pallas import tpu as pltpu
from jax.sharding import PartitionSpec as P

norm_epsilon = 1e-05
f32 = jnp.float32
bf16 = jnp.bfloat16
S = 8
R = 64
B = 4
A = R // B
G = 8
H = 4
LANES = 128


def dot_nt(left, right):
    return lax.dot_general(left, right, (((1,), (1,)), ((), ())), preferred_element_type=f32)


def iota(shape, dim):
    return lax.broadcasted_iota(jnp.int32, shape, dim)


def factors_kernel(
    window,
    hbm_lengths,
    hbm_hidden,
    hbm_cot,
    hbm_gain,
    hbm_inp,
    hbm_outp,
    packed,
    lengths,
    hidden,
    cot,
    gain,
    inp,
    outp,
    in_acc,
    sq_acc,
    out_t,
    sems,
):
    chunks, rows, columns = hidden.shape
    queries = lengths.shape[0]
    full = queries // G * G * S
    half = rows - full
    mid, low = full // 2, half // 2

    def copy(source, target, at):
        return pltpu.make_async_copy(source, target, sems.at[at])

    def chunk(c):
        cut = pl.ds(pl.multiple_of(c * columns, columns), columns)
        return [
            copy(hbm_gain.at[:, cut], gain.at[c], 3 + c),
            copy(hbm_inp.at[:, cut], inp.at[c], 3 + chunks + c),
            copy(hbm_hidden.at[:, cut], hidden.at[c], 3 + 2 * chunks + c),
        ]

    def start_chunk(c):
        for piece in chunk(c):
            piece.start()

    early = [copy(hbm_outp, outp, 0), copy(hbm_cot, cot, 1), copy(hbm_lengths, lengths, 2)]
    for c in range(window):
        start_chunk(c)
    for piece in early:
        piece.start()
    in_acc[...] = jnp.zeros_like(in_acc)
    sq_acc[...] = jnp.zeros_like(sq_acc)

    @pl.loop(0, chunks)
    def _(c):
        for piece in chunk(c):
            piece.wait()

        @pl.when(c + window < chunks)
        def _():
            start_chunk(c + window)

        scaled = inp[c].astype(f32) * gain[c].astype(f32)
        high = scaled.astype(bf16)
        rest = (scaled - high.astype(f32)).astype(bf16)
        in_acc[...] += dot_nt(hidden[c], jnp.concatenate([high, high, rest, rest], axis=0))
        for r in range(0, rows, 48):
            wide = hidden[c, r : r + 48, :].astype(f32)
            square = wide * wide
            total = square[:, :LANES]
            for at in range(LANES, columns, LANES):
                total += square[:, at : at + LANES]
            sq_acc[r : r + 48, :] += total

    for piece in early:
        piece.wait()
    odd = lax.rem(lax.axis_index("store"), 2)
    at_full = pl.multiple_of(odd * half, half)
    at_half = pl.multiple_of((1 - odd) * full, half)
    low_lanes = iota((S, LANES), 1) < R
    position = iota((S, LANES), 0)

    def in_rows(at, count):
        sums = in_acc[pl.ds(at, count), :]
        square = jnp.sum(sq_acc[pl.ds(at, count), :], axis=1, keepdims=True)
        scale = lax.rsqrt(square * (1.0 / (chunks * columns)) + norm_epsilon)
        factor = (sums[:, :LANES] + sums[:, LANES:]) * scale
        return [
            jnp.where(position < lengths[at // S + q], factor[q * S : (q + 1) * S], 0.0)
            for q in range(count // S)
        ]

    def side_by_side(tiles):
        both = zip(tiles[: len(tiles) // 2], tiles[len(tiles) // 2 :])
        return jnp.concatenate([jnp.where(low_lanes, x, y) for x, y in both], axis=0)

    packed[:mid, :] = side_by_side(in_rows(at_full, full)).astype(bf16)
    packed[mid : mid + low, :] = side_by_side(in_rows(at_half, half)).astype(bf16)

    whole = dot_nt(outp[...], cot[pl.ds(at_full, full), :])
    for t in range(full // LANES):
        out_t[t * R : (t + 1) * R, :] = whole[:, t * LANES : (t + 1) * LANES]
    out_t[full // LANES * R :, :half] = dot_nt(outp[...], cot[pl.ds(at_half, half), :])

    def part(t, b):
        return out_t[pl.ds(t * R + b, A, stride=B), :]

    row = mid + low
    for m in range(full // (G * S)):
        t, at = divmod(m * G * S, LANES)
        for b in range(0, B, 2):
            both = [part(t, b + c)[:, at : at + G * S] for c in range(2)]
            packed[row : row + A, :] = jnp.concatenate(both, axis=1).astype(bf16)
            row += A
    packed[row : row + A, :] = jnp.concatenate(
        [part(full // LANES, b)[:, :half] for b in range(B)], axis=1
    ).astype(bf16)


def in_hbm(x):
    return pltpu.with_memory_space_constraint(x, pltpu.HBM)


def factors(lengths, hidden, cotangent, gain, in_projection, out_projection):
    rows, width = hidden.shape
    columns = 2048
    chunks = width // columns
    return pl.pallas_call(
        functools.partial(factors_kernel, 2),
        out_shape=jax.ShapeDtypeStruct((rows, 2 * R), bf16),
        in_specs=[pl.BlockSpec(memory_space=pl.ANY)] * 6,
        out_specs=pl.BlockSpec(memory_space=pltpu.VMEM),
        scratch_shapes=[
            pltpu.SMEM(lengths.shape, jnp.int32),
            pltpu.VMEM((chunks, rows, columns), bf16),
            pltpu.VMEM(cotangent.shape, bf16),
            pltpu.VMEM((chunks, 1, columns), bf16),
            pltpu.VMEM((chunks, R, columns), bf16),
            pltpu.VMEM(out_projection.shape, bf16),
            pltpu.VMEM((rows, 4 * R), f32),
            pltpu.VMEM((rows, LANES), f32),
            pltpu.VMEM((-(-rows // LANES) * R, LANES), f32),
            pltpu.SemaphoreType.DMA((3 + 3 * chunks,)),
        ],
        compiler_params=pltpu.CompilerParams(vmem_limit_bytes=24 * 2**20),
        name="factors",
    )(*[in_hbm(x) for x in (lengths, hidden, cotangent, gain, in_projection, out_projection)])


def fetch_kernel(n_layer, after, store, slab, sems):
    block = slab.shape[0] // n_layer
    rows = 16 if block % 16 == 0 else 8
    me = lax.axis_index("layer")
    copies = []
    for k in range(n_layer):
        at = pl.multiple_of(partner(me, k, n_layer) * block, rows)
        to = slab.at[pl.ds(k * block, block)]
        copies.append(pltpu.make_async_copy(store.at[pl.ds(at, block)], to, sems.at[k]))
        copies[-1].start()
    for copy in copies:
        copy.wait()


def fetch(after, store, n_layer):
    rows, features = store.shape
    return pl.pallas_call(
        functools.partial(fetch_kernel, n_layer),
        out_shape=jax.ShapeDtypeStruct((rows, features), bf16),
        in_specs=[pl.BlockSpec(memory_space=pl.ANY)] * 2,
        out_specs=pl.BlockSpec(memory_space=pltpu.VMEM),
        scratch_shapes=[pltpu.SemaphoreType.DMA((n_layer,))],
        compiler_params=pltpu.CompilerParams(vmem_limit_bytes=12 * 2**20),
        cost_estimate=pl.CostEstimate(
            flops=0, bytes_accessed=2 * rows * features, transcendentals=0
        ),
        name="fetch",
    )(after, in_hbm(store))


def spread_out(tile, owner):
    lanes = tile.shape[1]
    mine = (owner == iota((G, lanes), 0))[None]
    wide = jnp.where(mine, tile.astype(f32)[:, None, :], 0.0)
    return wide.reshape(A * G, lanes).astype(bf16)


def halves(tile):
    wide = tile.astype(f32)
    turned = jnp.concatenate([wide[:, R:], wide[:, :R]], axis=1)
    low = iota(wide.shape, 1) < R
    return [
        jnp.where(mask, x, 0.0).astype(bf16)
        for x in (wide, turned)
        for mask in (low, jnp.logical_not(low))
    ]


def diagonal(low, high):
    zero = jnp.zeros_like(low)
    left = jnp.concatenate([low, high, zero, zero], axis=0)
    right = jnp.concatenate([zero, zero, low, high], axis=0)
    return jnp.concatenate([left, right], axis=1)


def build_grads(shards, base, row0, full_groups, grads):
    mid = full_groups * G * S // 2
    low = H * S // 2
    lane = iota((G, 2 * 128), 1)
    whole_owner = lax.rem(lane, G * S) // S
    half_owner = lax.rem(lane, H * S) // S + H * (lane // 128)

    def whole(shard):
        found = []
        pairs = {}
        for m in range(full_groups):
            first = m % (full_groups // 2)
            if first not in pairs:
                pairs[first] = halves(
                    shards[base + shard, first * G * S : (first + 1) * G * S, :]
                )
            plain_low, plain_high, turned_low, turned_high = pairs[first]
            weights = (
                diagonal(plain_low, turned_high)
                if m < full_groups // 2
                else diagonal(turned_low, plain_high)
            )
            at = mid + low + m * 2 * A
            tile = jnp.concatenate(
                [shards[base + shard, at : at + A, :], shards[base + shard, at + A : at + 2 * A, :]],
                axis=1,
            )
            found.append((spread_out(tile, whole_owner), weights))
        return found

    def joined(shard):
        tiles, weights = [], []
        for s in (shard, shard + 1):
            plain_low, plain_high, turned_low, turned_high = halves(
                shards[base + s, mid : mid + low, :]
            )
            weights.append(
                diagonal(
                    jnp.concatenate([plain_low, turned_low], axis=0),
                    jnp.concatenate([turned_high, plain_high], axis=0),
                )
            )
            at = mid + low + full_groups * 2 * A
            tiles.append(shards[base + s, at : at + A, :])
        return [
            (
                spread_out(jnp.concatenate(tiles, axis=1), half_owner),
                jnp.concatenate(weights, axis=0),
            )
        ]

    groups = []
    for shard in (0, 2):
        groups += whole(shard) + joined(shard) + whole(shard + 1)
    for at in range(0, len(groups), 2):
        first, second = [jnp.dot(x, w, preferred_element_type=f32) for x, w in groups[at : at + 2]]
        for a in range(A):
            pair = [x[a * G : (a + 1) * G] for x in (first, second)]
            grads[pl.ds(row0 + at * G, 2 * G), a * 256 : (a + 1) * 256] = jnp.concatenate(
                pair, axis=0
            ).astype(bf16)


def grads_kernel(n_store, full_groups, k, *refs):
    gathered = refs[:n_store]
    slab, grads, out, shards = refs[n_store:]
    me_store = lax.axis_index("store")
    for at in range(n_store):
        shards[partner(me_store, at, n_store)] = gathered[at][...]
    four = 4 * (full_groups * G + H)
    if n_store == 4:
        build_grads(shards, 0, 0, full_groups, grads)
    else:

        @pl.loop(0, n_store // 4)
        def _(at):
            build_grads(shards, at * 4, pl.multiple_of(at * four, 16), full_groups, grads)

    scores_kernel(k, grads, slab, out)


def scores_kernel(k, grads, slab, *refs):
    *terms, out = refs
    block = out.shape[1]
    total = dot_nt(slab[k * block : (k + 1) * block, :], grads[...]).T
    for term in terms:
        total += term[...].astype(f32)
    out[...] = total.astype(out.dtype)


def partner(me, k, n):
    return jnp.bitwise_xor(me, k) if n & (n - 1) == 0 else lax.rem(n + k - me, n)


def swap(x, axis, n, k):
    pairs = [(i, i ^ k if n & (n - 1) == 0 else (n + k - i) % n) for i in range(n)]
    return lax.ppermute(x, axis, pairs)


def grads_and_scores(gathered, slab, n_store, n_layer, k):
    rows, features = slab.shape
    queries = n_store * gathered[0].shape[0] // S
    vmem = pl.BlockSpec(memory_space=pltpu.VMEM)
    return pl.pallas_call(
        functools.partial(grads_kernel, n_store, queries // n_store // G, k),
        out_shape=[
            jax.ShapeDtypeStruct((queries, features), bf16),
            jax.ShapeDtypeStruct((queries, rows // n_layer), bf16),
        ],
        in_specs=[vmem] * (n_store + 1),
        out_specs=[vmem] * 2,
        scratch_shapes=[pltpu.VMEM((n_store,) + gathered[0].shape, bf16)],
        compiler_params=pltpu.CompilerParams(vmem_limit_bytes=24 * 2**20),
        name="grads",
    )(*gathered, slab)


def scores(grads, slab, n_layer, k, terms=()):
    rows, features = slab.shape
    block = rows // n_layer
    queries = grads.shape[0]
    vmem = pl.BlockSpec(memory_space=pltpu.VMEM)
    return pl.pallas_call(
        functools.partial(scores_kernel, k),
        out_shape=jax.ShapeDtypeStruct((queries, block), bf16 if k else f32),
        in_specs=[vmem] * (2 + len(terms)),
        out_specs=vmem,
        compiler_params=pltpu.CompilerParams(vmem_limit_bytes=24 * 2**20),
        cost_estimate=pl.CostEstimate(
            flops=2 * queries * block * features,
            bytes_accessed=2 * (queries + block) * features,
            transcendentals=0,
        ),
        name="scores",
    )(grads, slab, *terms)


def on_device(n_store, n_layer, hidden, cotangent, lengths, norm_gain, in_proj, out_proj, store):
    queries, positions, width = hidden.shape[1:]
    packed = factors(
        lengths,
        hidden.reshape(queries * positions, width),
        cotangent.reshape(queries * positions, cotangent.shape[3]),
        norm_gain,
        in_proj[0],
        out_proj[0],
    )
    gathered = [packed] + [swap(packed, "store", n_store, k) for k in range(1, n_store)]
    slab = fetch(packed, store[0], n_layer)
    grads, partial = grads_and_scores(gathered, slab, n_store, n_layer, n_layer - 1)
    crossed = [swap(partial, "layer", n_layer, n_layer - 1)]
    for k in reversed(range(1, n_layer - 1)):
        crossed.append(swap(scores(grads, slab, n_layer, k), "layer", n_layer, k))
    total = scores(grads, slab, n_layer, 0, crossed[:1])
    for x in crossed[1:]:
        total = total + x.astype(f32)
    return total.T


def solution(mesh):
    placed = (
        P("layer", ("grp", "store"), None, None),
        P("layer", ("grp", "store"), None, None),
        P(("grp", "store")),
        P("layer", None),
        P("layer", None, None),
        P("layer", None, None),
        P("layer", ("grp", "store"), None),
    )
    return jax.shard_map(
        functools.partial(on_device, mesh.shape["store"], mesh.shape["layer"]),
        mesh=mesh,
        in_specs=placed,
        out_specs=P(("grp", "store", "layer"), None),
        check_vma=False,
    )
```

```python
import functools

import jax
import jax.numpy as jnp
from jax import lax
from jax.experimental import pallas as pl
from jax.experimental.pallas import tpu as pltpu
from jax.sharding import PartitionSpec as P

norm_epsilon = 1e-05
f32 = jnp.float32
bf16 = jnp.bfloat16
S = 8
R = 64
B = 4
A = R // B
G = 8
H = 4
LANES = 128


def dot_nt(left, right):
    return lax.dot_general(left, right, (((1,), (1,)), ((), ())), preferred_element_type=f32)


def iota(shape, dim):
    return lax.broadcasted_iota(jnp.int32, shape, dim)


def factors_kernel(
    window,
    hbm_lengths,
    hbm_hidden,
    hbm_cot,
    hbm_gain,
    hbm_inp,
    hbm_outp,
    packed,
    lengths,
    hidden,
    cot,
    gain,
    inp,
    outp,
    in_acc,
    sq_acc,
    out_t,
    sems,
):
    chunks, rows, columns = hidden.shape
    queries = lengths.shape[0]
    full = queries // G * G * S
    half = rows - full
    mid, low = full // 2, half // 2

    def copy(source, target, at):
        return pltpu.make_async_copy(source, target, sems.at[at])

    def chunk(c):
        cut = pl.ds(pl.multiple_of(c * columns, columns), columns)
        return [
            copy(hbm_gain.at[:, cut], gain.at[c], 3 + c),
            copy(hbm_inp.at[:, cut], inp.at[c], 3 + chunks + c),
            copy(hbm_hidden.at[:, cut], hidden.at[c], 3 + 2 * chunks + c),
        ]

    def start_chunk(c):
        for piece in chunk(c):
            piece.start()

    early = [copy(hbm_outp, outp, 0), copy(hbm_cot, cot, 1), copy(hbm_lengths, lengths, 2)]
    for c in range(window):
        start_chunk(c)
    for piece in early:
        piece.start()
    in_acc[...] = jnp.zeros_like(in_acc)
    sq_acc[...] = jnp.zeros_like(sq_acc)

    @pl.loop(0, chunks)
    def _(c):
        for piece in chunk(c):
            piece.wait()

        @pl.when(c + window < chunks)
        def _():
            start_chunk(c + window)

        scaled = inp[c].astype(f32) * gain[c].astype(f32)
        high = scaled.astype(bf16)
        rest = (scaled - high.astype(f32)).astype(bf16)
        in_acc[...] += dot_nt(hidden[c], jnp.concatenate([high, high, rest, rest], axis=0))
        for r in range(0, rows, 48):
            wide = hidden[c, r : r + 48, :].astype(f32)
            square = wide * wide
            total = square[:, :LANES]
            for at in range(LANES, columns, LANES):
                total += square[:, at : at + LANES]
            sq_acc[r : r + 48, :] += total

    for piece in early:
        piece.wait()
    odd = lax.rem(lax.axis_index("store"), 2)
    at_full = pl.multiple_of(odd * half, half)
    at_half = pl.multiple_of((1 - odd) * full, half)
    low_lanes = iota((S, LANES), 1) < R
    position = iota((S, LANES), 0)

    def in_rows(at, count):
        sums = in_acc[pl.ds(at, count), :]
        square = jnp.sum(sq_acc[pl.ds(at, count), :], axis=1, keepdims=True)
        scale = lax.rsqrt(square * (1.0 / (chunks * columns)) + norm_epsilon)
        factor = (sums[:, :LANES] + sums[:, LANES:]) * scale
        return [
            jnp.where(position < lengths[at // S + q], factor[q * S : (q + 1) * S], 0.0)
            for q in range(count // S)
        ]

    def side_by_side(tiles):
        both = zip(tiles[: len(tiles) // 2], tiles[len(tiles) // 2 :])
        return jnp.concatenate([jnp.where(low_lanes, x, y) for x, y in both], axis=0)

    packed[:mid, :] = side_by_side(in_rows(at_full, full)).astype(bf16)
    packed[mid : mid + low, :] = side_by_side(in_rows(at_half, half)).astype(bf16)

    whole = dot_nt(outp[...], cot[pl.ds(at_full, full), :])
    for t in range(full // LANES):
        out_t[t * R : (t + 1) * R, :] = whole[:, t * LANES : (t + 1) * LANES]
    out_t[full // LANES * R :, :half] = dot_nt(outp[...], cot[pl.ds(at_half, half), :])

    def part(t, b):
        return out_t[pl.ds(t * R + b, A, stride=B), :]

    row = mid + low
    for m in range(full // (G * S)):
        t, at = divmod(m * G * S, LANES)
        for b in range(0, B, 2):
            both = [part(t, b + c)[:, at : at + G * S] for c in range(2)]
            packed[row : row + A, :] = jnp.concatenate(both, axis=1).astype(bf16)
            row += A
    packed[row : row + A, :] = jnp.concatenate(
        [part(full // LANES, b)[:, :half] for b in range(B)], axis=1
    ).astype(bf16)


def in_hbm(x):
    return pltpu.with_memory_space_constraint(x, pltpu.HBM)


def factors(lengths, hidden, cotangent, gain, in_projection, out_projection):
    rows, width = hidden.shape
    columns = 2048
    chunks = width // columns
    return pl.pallas_call(
        functools.partial(factors_kernel, 2),
        out_shape=jax.ShapeDtypeStruct((rows, 2 * R), bf16),
        in_specs=[pl.BlockSpec(memory_space=pl.ANY)] * 6,
        out_specs=pl.BlockSpec(memory_space=pltpu.VMEM),
        scratch_shapes=[
            pltpu.SMEM(lengths.shape, jnp.int32),
            pltpu.VMEM((chunks, rows, columns), bf16),
            pltpu.VMEM(cotangent.shape, bf16),
            pltpu.VMEM((chunks, 1, columns), bf16),
            pltpu.VMEM((chunks, R, columns), bf16),
            pltpu.VMEM(out_projection.shape, bf16),
            pltpu.VMEM((rows, 4 * R), f32),
            pltpu.VMEM((rows, LANES), f32),
            pltpu.VMEM((-(-rows // LANES) * R, LANES), f32),
            pltpu.SemaphoreType.DMA((3 + 3 * chunks,)),
        ],
        compiler_params=pltpu.CompilerParams(vmem_limit_bytes=24 * 2**20),
        name="factors",
    )(*[in_hbm(x) for x in (lengths, hidden, cotangent, gain, in_projection, out_projection)])


def fetch_kernel(n_layer, after, store, slab, sems):
    block = slab.shape[0] // n_layer
    rows = 16 if block % 16 == 0 else 8
    me = lax.axis_index("layer")
    copies = []
    for k in range(n_layer):
        at = pl.multiple_of(partner(me, k, n_layer) * block, rows)
        to = slab.at[pl.ds(k * block, block)]
        copies.append(pltpu.make_async_copy(store.at[pl.ds(at, block)], to, sems.at[k]))
        copies[-1].start()
    for copy in copies:
        copy.wait()


def fetch(after, store, n_layer):
    rows, features = store.shape
    return pl.pallas_call(
        functools.partial(fetch_kernel, n_layer),
        out_shape=jax.ShapeDtypeStruct((rows, features), bf16),
        in_specs=[pl.BlockSpec(memory_space=pl.ANY)] * 2,
        out_specs=pl.BlockSpec(memory_space=pltpu.VMEM),
        scratch_shapes=[pltpu.SemaphoreType.DMA((n_layer,))],
        compiler_params=pltpu.CompilerParams(vmem_limit_bytes=12 * 2**20),
        cost_estimate=pl.CostEstimate(
            flops=0, bytes_accessed=2 * rows * features, transcendentals=0
        ),
        name="fetch",
    )(after, in_hbm(store))


def spread_out(tile, owner):
    lanes = tile.shape[1]
    mine = (owner == iota((G, lanes), 0))[None]
    wide = jnp.where(mine, tile.astype(f32)[:, None, :], 0.0)
    return wide.reshape(A * G, lanes).astype(bf16)


def halves(tile):
    wide = tile.astype(f32)
    turned = jnp.concatenate([wide[:, R:], wide[:, :R]], axis=1)
    low = iota(wide.shape, 1) < R
    return [
        jnp.where(mask, x, 0.0).astype(bf16)
        for x in (wide, turned)
        for mask in (low, jnp.logical_not(low))
    ]


def diagonal(low, high):
    zero = jnp.zeros_like(low)
    left = jnp.concatenate([low, high, zero, zero], axis=0)
    right = jnp.concatenate([zero, zero, low, high], axis=0)
    return jnp.concatenate([left, right], axis=1)


def build_grads(shards, base, row0, full_groups, grads):
    mid = full_groups * G * S // 2
    low = H * S // 2
    lane = iota((G, 2 * 128), 1)
    whole_owner = lax.rem(lane, G * S) // S
    half_owner = lax.rem(lane, H * S) // S + H * (lane // 128)

    def whole(shard):
        found = []
        pairs = {}
        for m in range(full_groups):
            first = m % (full_groups // 2)
            if first not in pairs:
                pairs[first] = halves(
                    shards[base + shard, first * G * S : (first + 1) * G * S, :]
                )
            plain_low, plain_high, turned_low, turned_high = pairs[first]
            weights = (
                diagonal(plain_low, turned_high)
                if m < full_groups // 2
                else diagonal(turned_low, plain_high)
            )
            at = mid + low + m * 2 * A
            tile = jnp.concatenate(
                [shards[base + shard, at : at + A, :], shards[base + shard, at + A : at + 2 * A, :]],
                axis=1,
            )
            found.append((spread_out(tile, whole_owner), weights))
        return found

    def joined(shard):
        tiles, weights = [], []
        for s in (shard, shard + 1):
            plain_low, plain_high, turned_low, turned_high = halves(
                shards[base + s, mid : mid + low, :]
            )
            weights.append(
                diagonal(
                    jnp.concatenate([plain_low, turned_low], axis=0),
                    jnp.concatenate([turned_high, plain_high], axis=0),
                )
            )
            at = mid + low + full_groups * 2 * A
            tiles.append(shards[base + s, at : at + A, :])
        return [
            (
                spread_out(jnp.concatenate(tiles, axis=1), half_owner),
                jnp.concatenate(weights, axis=0),
            )
        ]

    groups = []
    for shard in (0, 2):
        groups += whole(shard) + joined(shard) + whole(shard + 1)
    for at in range(0, len(groups), 2):
        first, second = [jnp.dot(x, w, preferred_element_type=f32) for x, w in groups[at : at + 2]]
        for a in range(A):
            pair = [x[a * G : (a + 1) * G] for x in (first, second)]
            grads[pl.ds(row0 + at * G, 2 * G), a * 256 : (a + 1) * 256] = jnp.concatenate(
                pair, axis=0
            ).astype(bf16)


def grads_kernel(n_store, full_groups, k, *refs):
    gathered = refs[:n_store]
    slab, grads, out, shards = refs[n_store:]
    me_store = lax.axis_index("store")
    for at in range(n_store):
        shards[partner(me_store, at, n_store)] = gathered[at][...]
    four = 4 * (full_groups * G + H)
    if n_store == 4:
        build_grads(shards, 0, 0, full_groups, grads)
    else:

        @pl.loop(0, n_store // 4)
        def _(at):
            build_grads(shards, at * 4, pl.multiple_of(at * four, 16), full_groups, grads)

    scores_kernel(k, grads, slab, out)


def scores_kernel(k, grads, slab, *refs):
    *terms, out = refs
    block = out.shape[1]
    total = dot_nt(slab[k * block : (k + 1) * block, :], grads[...]).T
    for term in terms:
        total += term[...].astype(f32)
    out[...] = total.astype(out.dtype)


def partner(me, k, n):
    return jnp.bitwise_xor(me, k) if n & (n - 1) == 0 else lax.rem(n + k - me, n)


def swap(x, axis, n, k):
    pairs = [(i, i ^ k if n & (n - 1) == 0 else (n + k - i) % n) for i in range(n)]
    return lax.ppermute(x, axis, pairs)


def grads_and_scores(gathered, slab, n_store, n_layer, k):
    rows, features = slab.shape
    queries = n_store * gathered[0].shape[0] // S
    vmem = pl.BlockSpec(memory_space=pltpu.VMEM)
    return pl.pallas_call(
        functools.partial(grads_kernel, n_store, queries // n_store // G, k),
        out_shape=[
            jax.ShapeDtypeStruct((queries, features), bf16),
            jax.ShapeDtypeStruct((queries, rows // n_layer), bf16),
        ],
        in_specs=[vmem] * (n_store + 1),
        out_specs=[vmem] * 2,
        scratch_shapes=[pltpu.VMEM((n_store,) + gathered[0].shape, bf16)],
        compiler_params=pltpu.CompilerParams(vmem_limit_bytes=24 * 2**20),
        name="grads",
    )(*gathered, slab)


def scores(grads, slab, n_layer, k, terms=()):
    rows, features = slab.shape
    block = rows // n_layer
    queries = grads.shape[0]
    vmem = pl.BlockSpec(memory_space=pltpu.VMEM)
    return pl.pallas_call(
        functools.partial(scores_kernel, k),
        out_shape=jax.ShapeDtypeStruct((queries, block), bf16 if k else f32),
        in_specs=[vmem] * (2 + len(terms)),
        out_specs=vmem,
        compiler_params=pltpu.CompilerParams(vmem_limit_bytes=24 * 2**20),
        cost_estimate=pl.CostEstimate(
            flops=2 * queries * block * features,
            bytes_accessed=2 * (queries + block) * features,
            transcendentals=0,
        ),
        name="scores",
    )(grads, slab, *terms)


def on_device(n_store, n_layer, hidden, cotangent, lengths, norm_gain, in_proj, out_proj, store):
    queries, positions, width = hidden.shape[1:]
    packed = factors(
        lengths,
        hidden.reshape(queries * positions, width),
        cotangent.reshape(queries * positions, cotangent.shape[3]),
        norm_gain,
        in_proj[0],
        out_proj[0],
    )
    gathered = [packed] + [swap(packed, "store", n_store, k) for k in range(1, n_store)]
    slab = fetch(packed, store[0], n_layer)
    grads, partial = grads_and_scores(gathered, slab, n_store, n_layer, n_layer - 1)
    other = swap(partial, "layer", n_layer, 1)
    near = swap(scores(grads, slab, n_layer, 1), "layer", n_layer, 1)
    crossed = [near]
    for k in reversed(range(2, n_layer, 2)):
        if k < n_layer - 2:
            other = swap(scores(grads, slab, n_layer, k + 1), "layer", n_layer, 1)
        crossed.append(swap(scores(grads, slab, n_layer, k, [other]), "layer", n_layer, k))
    total = scores(grads, slab, n_layer, 0, crossed)
    return total.T


def solution(mesh):
    placed = (
        P("layer", ("grp", "store"), None, None),
        P("layer", ("grp", "store"), None, None),
        P(("grp", "store")),
        P("layer", None),
        P("layer", None, None),
        P("layer", None, None),
        P("layer", ("grp", "store"), None),
    )
    return jax.shard_map(
        functools.partial(on_device, mesh.shape["store"], mesh.shape["layer"]),
        mesh=mesh,
        in_specs=placed,
        out_specs=P(("grp", "store", "layer"), None),
        check_vma=False,
    )
```

```python
import functools

import jax
import jax.numpy as jnp
from jax import lax
from jax.experimental import pallas as pl
from jax.experimental.pallas import tpu as pltpu
from jax.sharding import PartitionSpec as P

norm_epsilon = 1e-05
f32 = jnp.float32
bf16 = jnp.bfloat16
S = 8
R = 64
B = 4
A = R // B
G = 8
H = 4
LANES = 128


def dot_nt(left, right):
    return lax.dot_general(left, right, (((1,), (1,)), ((), ())), preferred_element_type=f32)


def iota(shape, dim):
    return lax.broadcasted_iota(jnp.int32, shape, dim)


def factors_kernel(
    window,
    hbm_lengths,
    hbm_hidden,
    hbm_cot,
    hbm_gain,
    hbm_inp,
    hbm_outp,
    packed,
    lengths,
    hidden,
    cot,
    gain,
    inp,
    outp,
    in_acc,
    sq_acc,
    out_t,
    sems,
):
    chunks, rows, columns = hidden.shape
    queries = lengths.shape[0]
    full = queries // G * G * S
    half = rows - full
    mid, low = full // 2, half // 2

    def copy(source, target, at):
        return pltpu.make_async_copy(source, target, sems.at[at])

    def chunk(c):
        cut = pl.ds(pl.multiple_of(c * columns, columns), columns)
        return [
            copy(hbm_gain.at[:, cut], gain.at[c], 3 + c),
            copy(hbm_inp.at[:, cut], inp.at[c], 3 + chunks + c),
            copy(hbm_hidden.at[:, cut], hidden.at[c], 3 + 2 * chunks + c),
        ]

    def start_chunk(c):
        for piece in chunk(c):
            piece.start()

    early = [copy(hbm_outp, outp, 0), copy(hbm_cot, cot, 1), copy(hbm_lengths, lengths, 2)]
    for c in range(window):
        start_chunk(c)
    for piece in early:
        piece.start()
    in_acc[...] = jnp.zeros_like(in_acc)
    sq_acc[...] = jnp.zeros_like(sq_acc)

    @pl.loop(0, chunks)
    def _(c):
        for piece in chunk(c):
            piece.wait()

        @pl.when(c + window < chunks)
        def _():
            start_chunk(c + window)

        scaled = inp[c].astype(f32) * gain[c].astype(f32)
        high = scaled.astype(bf16)
        rest = (scaled - high.astype(f32)).astype(bf16)
        in_acc[...] += dot_nt(hidden[c], jnp.concatenate([high, high, rest, rest], axis=0))
        for r in range(0, rows, 48):
            wide = hidden[c, r : r + 48, :].astype(f32)
            square = wide * wide
            total = square[:, :LANES]
            for at in range(LANES, columns, LANES):
                total += square[:, at : at + LANES]
            sq_acc[r : r + 48, :] += total

    for piece in early:
        piece.wait()
    odd = lax.rem(lax.axis_index("store"), 2)
    at_full = pl.multiple_of(odd * half, half)
    at_half = pl.multiple_of((1 - odd) * full, half)
    low_lanes = iota((S, LANES), 1) < R
    position = iota((S, LANES), 0)

    def in_rows(at, count):
        sums = in_acc[pl.ds(at, count), :]
        square = jnp.sum(sq_acc[pl.ds(at, count), :], axis=1, keepdims=True)
        scale = lax.rsqrt(square * (1.0 / (chunks * columns)) + norm_epsilon)
        factor = (sums[:, :LANES] + sums[:, LANES:]) * scale
        return [
            jnp.where(position < lengths[at // S + q], factor[q * S : (q + 1) * S], 0.0)
            for q in range(count // S)
        ]

    def side_by_side(tiles):
        both = zip(tiles[: len(tiles) // 2], tiles[len(tiles) // 2 :])
        return jnp.concatenate([jnp.where(low_lanes, x, y) for x, y in both], axis=0)

    packed[:mid, :] = side_by_side(in_rows(at_full, full)).astype(bf16)
    packed[mid : mid + low, :] = side_by_side(in_rows(at_half, half)).astype(bf16)

    whole = dot_nt(outp[...], cot[pl.ds(at_full, full), :])
    for t in range(full // LANES):
        out_t[t * R : (t + 1) * R, :] = whole[:, t * LANES : (t + 1) * LANES]
    out_t[full // LANES * R :, :half] = dot_nt(outp[...], cot[pl.ds(at_half, half), :])

    def part(t, b):
        return out_t[pl.ds(t * R + b, A, stride=B), :]

    row = mid + low
    for m in range(full // (G * S)):
        t, at = divmod(m * G * S, LANES)
        for b in range(0, B, 2):
            both = [part(t, b + c)[:, at : at + G * S] for c in range(2)]
            packed[row : row + A, :] = jnp.concatenate(both, axis=1).astype(bf16)
            row += A
    packed[row : row + A, :] = jnp.concatenate(
        [part(full // LANES, b)[:, :half] for b in range(B)], axis=1
    ).astype(bf16)


def in_hbm(x):
    return pltpu.with_memory_space_constraint(x, pltpu.HBM)


def factors(lengths, hidden, cotangent, gain, in_projection, out_projection):
    rows, width = hidden.shape
    columns = 2048
    chunks = width // columns
    return pl.pallas_call(
        functools.partial(factors_kernel, 2),
        out_shape=jax.ShapeDtypeStruct((rows, 2 * R), bf16),
        in_specs=[pl.BlockSpec(memory_space=pl.ANY)] * 6,
        out_specs=pl.BlockSpec(memory_space=pltpu.VMEM),
        scratch_shapes=[
            pltpu.SMEM(lengths.shape, jnp.int32),
            pltpu.VMEM((chunks, rows, columns), bf16),
            pltpu.VMEM(cotangent.shape, bf16),
            pltpu.VMEM((chunks, 1, columns), bf16),
            pltpu.VMEM((chunks, R, columns), bf16),
            pltpu.VMEM(out_projection.shape, bf16),
            pltpu.VMEM((rows, 4 * R), f32),
            pltpu.VMEM((rows, LANES), f32),
            pltpu.VMEM((-(-rows // LANES) * R, LANES), f32),
            pltpu.SemaphoreType.DMA((3 + 3 * chunks,)),
        ],
        compiler_params=pltpu.CompilerParams(vmem_limit_bytes=24 * 2**20),
        name="factors",
    )(*[in_hbm(x) for x in (lengths, hidden, cotangent, gain, in_projection, out_projection)])


def fetch_kernel(n_layer, after, store, slab, sems):
    block = slab.shape[0] // n_layer
    rows = 16 if block % 16 == 0 else 8
    me = lax.axis_index("layer")
    copies = []
    for k in range(n_layer):
        at = pl.multiple_of(partner(me, k, n_layer) * block, rows)
        to = slab.at[pl.ds(k * block, block)]
        copies.append(pltpu.make_async_copy(store.at[pl.ds(at, block)], to, sems.at[k]))
        copies[-1].start()
    for copy in copies:
        copy.wait()


def fetch(after, store, n_layer):
    rows, features = store.shape
    return pl.pallas_call(
        functools.partial(fetch_kernel, n_layer),
        out_shape=jax.ShapeDtypeStruct((rows, features), bf16),
        in_specs=[pl.BlockSpec(memory_space=pl.ANY)] * 2,
        out_specs=pl.BlockSpec(memory_space=pltpu.VMEM),
        scratch_shapes=[pltpu.SemaphoreType.DMA((n_layer,))],
        compiler_params=pltpu.CompilerParams(vmem_limit_bytes=12 * 2**20),
        cost_estimate=pl.CostEstimate(
            flops=0, bytes_accessed=2 * rows * features, transcendentals=0
        ),
        name="fetch",
    )(after, in_hbm(store))


def spread_out(tile, owner):
    lanes = tile.shape[1]
    mine = (owner == iota((G, lanes), 0))[None]
    wide = jnp.where(mine, tile.astype(f32)[:, None, :], 0.0)
    return wide.reshape(A * G, lanes).astype(bf16)


def halves(tile):
    wide = tile.astype(f32)
    turned = jnp.concatenate([wide[:, R:], wide[:, :R]], axis=1)
    low = iota(wide.shape, 1) < R
    return [
        jnp.where(mask, x, 0.0).astype(bf16)
        for x in (wide, turned)
        for mask in (low, jnp.logical_not(low))
    ]


def diagonal(low, high):
    zero = jnp.zeros_like(low)
    left = jnp.concatenate([low, high, zero, zero], axis=0)
    right = jnp.concatenate([zero, zero, low, high], axis=0)
    return jnp.concatenate([left, right], axis=1)


def build_grads(shards, base, row0, full_groups, grads):
    mid = full_groups * G * S // 2
    low = H * S // 2
    lane = iota((G, 2 * 128), 1)
    whole_owner = lax.rem(lane, G * S) // S
    half_owner = lax.rem(lane, H * S) // S + H * (lane // 128)

    def whole(shard):
        found = []
        pairs = {}
        for m in range(full_groups):
            first = m % (full_groups // 2)
            if first not in pairs:
                pairs[first] = halves(
                    shards[base + shard, first * G * S : (first + 1) * G * S, :]
                )
            plain_low, plain_high, turned_low, turned_high = pairs[first]
            weights = (
                diagonal(plain_low, turned_high)
                if m < full_groups // 2
                else diagonal(turned_low, plain_high)
            )
            at = mid + low + m * 2 * A
            tile = jnp.concatenate(
                [shards[base + shard, at : at + A, :], shards[base + shard, at + A : at + 2 * A, :]],
                axis=1,
            )
            found.append((spread_out(tile, whole_owner), weights))
        return found

    def joined(shard):
        tiles, weights = [], []
        for s in (shard, shard + 1):
            plain_low, plain_high, turned_low, turned_high = halves(
                shards[base + s, mid : mid + low, :]
            )
            weights.append(
                diagonal(
                    jnp.concatenate([plain_low, turned_low], axis=0),
                    jnp.concatenate([turned_high, plain_high], axis=0),
                )
            )
            at = mid + low + full_groups * 2 * A
            tiles.append(shards[base + s, at : at + A, :])
        return [
            (
                spread_out(jnp.concatenate(tiles, axis=1), half_owner),
                jnp.concatenate(weights, axis=0),
            )
        ]

    groups = []
    for shard in (0, 2):
        groups += whole(shard) + joined(shard) + whole(shard + 1)
    for at in range(0, len(groups), 2):
        first, second = [jnp.dot(x, w, preferred_element_type=f32) for x, w in groups[at : at + 2]]
        for a in range(A):
            pair = [x[a * G : (a + 1) * G] for x in (first, second)]
            grads[pl.ds(row0 + at * G, 2 * G), a * 256 : (a + 1) * 256] = jnp.concatenate(
                pair, axis=0
            ).astype(bf16)


def grads_kernel(shifts, n_store, full_groups, k, packed, *refs):
    gathered = refs[: len(shifts)]
    slab, grads, out, shards = refs[len(shifts) :]
    me = lax.axis_index("store")
    shards[me] = packed[...]
    for (away, first, last), block in zip(shifts, gathered):

        @pl.when(jnp.logical_and(me >= first, me <= last))
        def _():
            shards[lax.rem(me + away, n_store)] = block[...]

    four = 4 * (full_groups * G + H)
    if n_store == 4:
        build_grads(shards, 0, 0, full_groups, grads)
    else:

        @pl.loop(0, n_store // 4)
        def _(at):
            build_grads(shards, at * 4, pl.multiple_of(at * four, 16), full_groups, grads)

    scores_kernel(k, grads, slab, out)


def scores_kernel(k, grads, slab, *refs):
    *terms, out = refs
    block = out.shape[1]
    total = dot_nt(slab[k * block : (k + 1) * block, :], grads[...]).T
    for term in terms:
        total += term[...].astype(f32)
    out[...] = total.astype(out.dtype)


def partner(me, k, n):
    return jnp.bitwise_xor(me, k) if n & (n - 1) == 0 else lax.rem(n + k - me, n)


def swap(x, axis, n, k):
    pairs = [(i, i ^ k if n & (n - 1) == 0 else (n + k - i) % n) for i in range(n)]
    return lax.ppermute(x, axis, pairs)


def store_shifts(n):
    if n == 4:
        return [(1, 3, 3), (2, 2, 3), (3, 0, 3), (2, 0, 1), (1, 0, 2)]
    return [(away, 0, n - 1) for away in range(1, n)]


def grads_and_scores(packed, slab, n_store, n_layer, k):
    rows, features = slab.shape
    queries = packed.shape[0] // S
    shifts = store_shifts(n_store)
    gathered = []
    for away, first, last in shifts:
        pairs = [((to + away) % n_store, to) for to in range(first, last + 1)]
        gathered.append(lax.ppermute(packed, "store", pairs))
    vmem = pl.BlockSpec(memory_space=pltpu.VMEM)
    return pl.pallas_call(
        functools.partial(grads_kernel, shifts, n_store, queries // G, k),
        out_shape=[
            jax.ShapeDtypeStruct((n_store * queries, features), bf16),
            jax.ShapeDtypeStruct((n_store * queries, rows // n_layer), bf16),
        ],
        in_specs=[vmem] * (len(shifts) + 2),
        out_specs=[vmem] * 2,
        scratch_shapes=[pltpu.VMEM((n_store,) + packed.shape, bf16)],
        compiler_params=pltpu.CompilerParams(vmem_limit_bytes=24 * 2**20),
        name="grads",
    )(packed, *gathered, slab)


def scores(grads, slab, n_layer, k, terms=()):
    rows, features = slab.shape
    block = rows // n_layer
    queries = grads.shape[0]
    vmem = pl.BlockSpec(memory_space=pltpu.VMEM)
    return pl.pallas_call(
        functools.partial(scores_kernel, k),
        out_shape=jax.ShapeDtypeStruct((queries, block), bf16 if k else f32),
        in_specs=[vmem] * (2 + len(terms)),
        out_specs=vmem,
        compiler_params=pltpu.CompilerParams(vmem_limit_bytes=24 * 2**20),
        cost_estimate=pl.CostEstimate(
            flops=2 * queries * block * features,
            bytes_accessed=2 * (queries + block) * features,
            transcendentals=0,
        ),
        name="scores",
    )(grads, slab, *terms)


def on_device(n_store, n_layer, hidden, cotangent, lengths, norm_gain, in_proj, out_proj, store):
    queries, positions, width = hidden.shape[1:]
    packed = factors(
        lengths,
        hidden.reshape(queries * positions, width),
        cotangent.reshape(queries * positions, cotangent.shape[3]),
        norm_gain,
        in_proj[0],
        out_proj[0],
    )
    slab = fetch(packed, store[0], n_layer)
    grads, partial = grads_and_scores(packed, slab, n_store, n_layer, n_layer - 1)
    other = swap(partial, "layer", n_layer, 1)
    near = swap(scores(grads, slab, n_layer, 1), "layer", n_layer, 1)
    crossed = [near]
    for k in reversed(range(2, n_layer, 2)):
        if k < n_layer - 2:
            other = swap(scores(grads, slab, n_layer, k + 1), "layer", n_layer, 1)
        crossed.append(swap(scores(grads, slab, n_layer, k, [other]), "layer", n_layer, k))
    total = scores(grads, slab, n_layer, 0)
    for x in crossed:
        total = total + x.astype(f32)
    return total.T


def solution(mesh):
    placed = (
        P("layer", ("grp", "store"), None, None),
        P("layer", ("grp", "store"), None, None),
        P(("grp", "store")),
        P("layer", None),
        P("layer", None, None),
        P("layer", None, None),
        P("layer", ("grp", "store"), None),
    )
    return jax.shard_map(
        functools.partial(on_device, mesh.shape["store"], mesh.shape["layer"]),
        mesh=mesh,
        in_specs=placed,
        out_specs=P(("grp", "store", "layer"), None),
        check_vma=False,
    )
```

```python
import functools

import jax
import jax.numpy as jnp
from jax import lax
from jax.experimental import pallas as pl
from jax.experimental.pallas import tpu as pltpu
from jax.sharding import PartitionSpec as P

norm_epsilon = 1e-05
f32 = jnp.float32
bf16 = jnp.bfloat16
S = 8
R = 64
B = 4
A = R // B
G = 8
H = 4
LANES = 128


def dot_nt(left, right):
    return lax.dot_general(left, right, (((1,), (1,)), ((), ())), preferred_element_type=f32)


def iota(shape, dim):
    return lax.broadcasted_iota(jnp.int32, shape, dim)


def factors_kernel(
    window,
    hbm_lengths,
    hbm_hidden,
    hbm_cot,
    hbm_gain,
    hbm_inp,
    hbm_outp,
    packed,
    lengths,
    hidden,
    cot,
    gain,
    inp,
    outp,
    in_acc,
    sq_acc,
    out_t,
    sems,
):
    chunks, rows, columns = hidden.shape
    queries = lengths.shape[0]
    full = queries // G * G * S
    half = rows - full
    mid, low = full // 2, half // 2

    def copy(source, target, at):
        return pltpu.make_async_copy(source, target, sems.at[at])

    def chunk(c):
        cut = pl.ds(pl.multiple_of(c * columns, columns), columns)
        return [
            copy(hbm_gain.at[:, cut], gain.at[c], 3 + c),
            copy(hbm_inp.at[:, cut], inp.at[c], 3 + chunks + c),
            copy(hbm_hidden.at[:, cut], hidden.at[c], 3 + 2 * chunks + c),
        ]

    def start_chunk(c):
        for piece in chunk(c):
            piece.start()

    early = [copy(hbm_outp, outp, 0), copy(hbm_cot, cot, 1), copy(hbm_lengths, lengths, 2)]
    for c in range(window):
        start_chunk(c)
    for piece in early:
        piece.start()
    in_acc[...] = jnp.zeros_like(in_acc)
    sq_acc[...] = jnp.zeros_like(sq_acc)

    @pl.loop(0, chunks)
    def _(c):
        for piece in chunk(c):
            piece.wait()

        @pl.when(c + window < chunks)
        def _():
            start_chunk(c + window)

        scaled = inp[c].astype(f32) * gain[c].astype(f32)
        high = scaled.astype(bf16)
        rest = (scaled - high.astype(f32)).astype(bf16)
        in_acc[...] += dot_nt(hidden[c], jnp.concatenate([high, high, rest, rest], axis=0))
        for r in range(0, rows, 48):
            wide = hidden[c, r : r + 48, :].astype(f32)
            square = wide * wide
            total = square[:, :LANES]
            for at in range(LANES, columns, LANES):
                total += square[:, at : at + LANES]
            sq_acc[r : r + 48, :] += total

    for piece in early:
        piece.wait()
    odd = lax.rem(lax.axis_index("store"), 2)
    at_full = pl.multiple_of(odd * half, half)
    at_half = pl.multiple_of((1 - odd) * full, half)
    low_lanes = iota((S, LANES), 1) < R
    position = iota((S, LANES), 0)

    def in_rows(at, count):
        sums = in_acc[pl.ds(at, count), :]
        square = jnp.sum(sq_acc[pl.ds(at, count), :], axis=1, keepdims=True)
        scale = lax.rsqrt(square * (1.0 / (chunks * columns)) + norm_epsilon)
        factor = (sums[:, :LANES] + sums[:, LANES:]) * scale
        return [
            jnp.where(position < lengths[at // S + q], factor[q * S : (q + 1) * S], 0.0)
            for q in range(count // S)
        ]

    def side_by_side(tiles):
        both = zip(tiles[: len(tiles) // 2], tiles[len(tiles) // 2 :])
        return jnp.concatenate([jnp.where(low_lanes, x, y) for x, y in both], axis=0)

    packed[:mid, :] = side_by_side(in_rows(at_full, full)).astype(bf16)
    packed[mid : mid + low, :] = side_by_side(in_rows(at_half, half)).astype(bf16)

    whole = dot_nt(outp[...], cot[pl.ds(at_full, full), :])
    for t in range(full // LANES):
        out_t[t * R : (t + 1) * R, :] = whole[:, t * LANES : (t + 1) * LANES]
    out_t[full // LANES * R :, :half] = dot_nt(outp[...], cot[pl.ds(at_half, half), :])

    def part(t, b):
        return out_t[pl.ds(t * R + b, A, stride=B), :]

    row = mid + low
    for m in range(full // (G * S)):
        t, at = divmod(m * G * S, LANES)
        for b in range(0, B, 2):
            both = [part(t, b + c)[:, at : at + G * S] for c in range(2)]
            packed[row : row + A, :] = jnp.concatenate(both, axis=1).astype(bf16)
            row += A
    packed[row : row + A, :] = jnp.concatenate(
        [part(full // LANES, b)[:, :half] for b in range(B)], axis=1
    ).astype(bf16)


def in_hbm(x):
    return pltpu.with_memory_space_constraint(x, pltpu.HBM)


def factors(lengths, hidden, cotangent, gain, in_projection, out_projection):
    rows, width = hidden.shape
    columns = 2048
    chunks = width // columns
    return pl.pallas_call(
        functools.partial(factors_kernel, 2),
        out_shape=jax.ShapeDtypeStruct((rows, 2 * R), bf16),
        in_specs=[pl.BlockSpec(memory_space=pl.ANY)] * 6,
        out_specs=pl.BlockSpec(memory_space=pltpu.VMEM),
        scratch_shapes=[
            pltpu.SMEM(lengths.shape, jnp.int32),
            pltpu.VMEM((chunks, rows, columns), bf16),
            pltpu.VMEM(cotangent.shape, bf16),
            pltpu.VMEM((chunks, 1, columns), bf16),
            pltpu.VMEM((chunks, R, columns), bf16),
            pltpu.VMEM(out_projection.shape, bf16),
            pltpu.VMEM((rows, 4 * R), f32),
            pltpu.VMEM((rows, LANES), f32),
            pltpu.VMEM((-(-rows // LANES) * R, LANES), f32),
            pltpu.SemaphoreType.DMA((3 + 3 * chunks,)),
        ],
        compiler_params=pltpu.CompilerParams(vmem_limit_bytes=24 * 2**20),
        name="factors",
    )(*[in_hbm(x) for x in (lengths, hidden, cotangent, gain, in_projection, out_projection)])


def fetch_kernel(n_layer, after, store, slab, sems):
    block = slab.shape[0] // n_layer
    rows = 16 if block % 16 == 0 else 8
    me = lax.axis_index("layer")
    copies = []
    for k in range(n_layer):
        at = pl.multiple_of(partner(me, k, n_layer) * block, rows)
        to = slab.at[pl.ds(k * block, block)]
        copies.append(pltpu.make_async_copy(store.at[pl.ds(at, block)], to, sems.at[k]))
        copies[-1].start()
    for copy in copies:
        copy.wait()


def fetch(after, store, n_layer):
    rows, features = store.shape
    return pl.pallas_call(
        functools.partial(fetch_kernel, n_layer),
        out_shape=jax.ShapeDtypeStruct((rows, features), bf16),
        in_specs=[pl.BlockSpec(memory_space=pl.ANY)] * 2,
        out_specs=pl.BlockSpec(memory_space=pltpu.VMEM),
        scratch_shapes=[pltpu.SemaphoreType.DMA((n_layer,))],
        compiler_params=pltpu.CompilerParams(vmem_limit_bytes=12 * 2**20),
        cost_estimate=pl.CostEstimate(
            flops=0, bytes_accessed=2 * rows * features, transcendentals=0
        ),
        name="fetch",
    )(after, in_hbm(store))


def spread_out(tile, owner):
    lanes = tile.shape[1]
    mine = (owner == iota((G, lanes), 0))[None]
    wide = jnp.where(mine, tile.astype(f32)[:, None, :], 0.0)
    return wide.reshape(A * G, lanes).astype(bf16)


def halves(tile):
    wide = tile.astype(f32)
    turned = jnp.concatenate([wide[:, R:], wide[:, :R]], axis=1)
    low = iota(wide.shape, 1) < R
    return [
        jnp.where(mask, x, 0.0).astype(bf16)
        for x in (wide, turned)
        for mask in (low, jnp.logical_not(low))
    ]


def diagonal(low, high):
    zero = jnp.zeros_like(low)
    left = jnp.concatenate([low, high, zero, zero], axis=0)
    right = jnp.concatenate([zero, zero, low, high], axis=0)
    return jnp.concatenate([left, right], axis=1)


def build_grads(shards, base, row0, full_groups, grads):
    mid = full_groups * G * S // 2
    low = H * S // 2
    lane = iota((G, 2 * 128), 1)
    whole_owner = lax.rem(lane, G * S) // S
    half_owner = lax.rem(lane, H * S) // S + H * (lane // 128)

    def whole(shard):
        found = []
        pairs = {}
        for m in range(full_groups):
            first = m % (full_groups // 2)
            if first not in pairs:
                pairs[first] = halves(
                    shards[base + shard, first * G * S : (first + 1) * G * S, :]
                )
            plain_low, plain_high, turned_low, turned_high = pairs[first]
            weights = (
                diagonal(plain_low, turned_high)
                if m < full_groups // 2
                else diagonal(turned_low, plain_high)
            )
            at = mid + low + m * 2 * A
            tile = jnp.concatenate(
                [shards[base + shard, at : at + A, :], shards[base + shard, at + A : at + 2 * A, :]],
                axis=1,
            )
            found.append((spread_out(tile, whole_owner), weights))
        return found

    def joined(shard):
        tiles, weights = [], []
        for s in (shard, shard + 1):
            plain_low, plain_high, turned_low, turned_high = halves(
                shards[base + s, mid : mid + low, :]
            )
            weights.append(
                diagonal(
                    jnp.concatenate([plain_low, turned_low], axis=0),
                    jnp.concatenate([turned_high, plain_high], axis=0),
                )
            )
            at = mid + low + full_groups * 2 * A
            tiles.append(shards[base + s, at : at + A, :])
        return [
            (
                spread_out(jnp.concatenate(tiles, axis=1), half_owner),
                jnp.concatenate(weights, axis=0),
            )
        ]

    groups = []
    for shard in (0, 2):
        groups += whole(shard) + joined(shard) + whole(shard + 1)
    for at in range(0, len(groups), 2):
        first, second = [jnp.dot(x, w, preferred_element_type=f32) for x, w in groups[at : at + 2]]
        for a in range(A):
            pair = [x[a * G : (a + 1) * G] for x in (first, second)]
            grads[pl.ds(row0 + at * G, 2 * G), a * 256 : (a + 1) * 256] = jnp.concatenate(
                pair, axis=0
            ).astype(bf16)


def grads_kernel(n_store, full_groups, k, *refs):
    gathered = refs[:n_store]
    slab, grads, out, shards = refs[n_store:]
    me_store = lax.axis_index("store")
    for at in range(n_store):
        shards[partner(me_store, n_store - 1 - at, n_store)] = gathered[at][...]
    four = 4 * (full_groups * G + H)
    if n_store == 4:
        build_grads(shards, 0, 0, full_groups, grads)
    else:

        @pl.loop(0, n_store // 4)
        def _(at):
            build_grads(shards, at * 4, pl.multiple_of(at * four, 16), full_groups, grads)

    scores_kernel(k, grads, slab, out)


def scores_kernel(k, grads, slab, *refs):
    *terms, out = refs
    block = out.shape[1]
    total = dot_nt(slab[k * block : (k + 1) * block, :], grads[...]).T
    for term in terms:
        total += term[...].astype(f32)
    out[...] = total.astype(out.dtype)


def partner(me, k, n):
    return jnp.bitwise_xor(me, k) if n & (n - 1) == 0 else lax.rem(n + k - me, n)


def swap(x, axis, n, k):
    pairs = [(i, i ^ k if n & (n - 1) == 0 else (n + k - i) % n) for i in range(n)]
    return lax.ppermute(x, axis, pairs)


def grads_and_scores(gathered, slab, n_store, n_layer, k):
    rows, features = slab.shape
    queries = n_store * gathered[0].shape[0] // S
    vmem = pl.BlockSpec(memory_space=pltpu.VMEM)
    return pl.pallas_call(
        functools.partial(grads_kernel, n_store, queries // n_store // G, k),
        out_shape=[
            jax.ShapeDtypeStruct((queries, features), bf16),
            jax.ShapeDtypeStruct((queries, rows // n_layer), bf16),
        ],
        in_specs=[vmem] * (n_store + 1),
        out_specs=[vmem] * 2,
        scratch_shapes=[pltpu.VMEM((n_store,) + gathered[0].shape, bf16)],
        compiler_params=pltpu.CompilerParams(vmem_limit_bytes=24 * 2**20),
        name="grads",
    )(*gathered, slab)


def scores(grads, slab, n_layer, k, terms=()):
    rows, features = slab.shape
    block = rows // n_layer
    queries = grads.shape[0]
    vmem = pl.BlockSpec(memory_space=pltpu.VMEM)
    return pl.pallas_call(
        functools.partial(scores_kernel, k),
        out_shape=jax.ShapeDtypeStruct((queries, block), bf16 if k else f32),
        in_specs=[vmem] * (2 + len(terms)),
        out_specs=vmem,
        compiler_params=pltpu.CompilerParams(vmem_limit_bytes=24 * 2**20),
        cost_estimate=pl.CostEstimate(
            flops=2 * queries * block * features,
            bytes_accessed=2 * (queries + block) * features,
            transcendentals=0,
        ),
        name="scores",
    )(grads, slab, *terms)


def on_device(n_store, n_layer, hidden, cotangent, lengths, norm_gain, in_proj, out_proj, store):
    queries, positions, width = hidden.shape[1:]
    packed = factors(
        lengths,
        hidden.reshape(queries * positions, width),
        cotangent.reshape(queries * positions, cotangent.shape[3]),
        norm_gain,
        in_proj[0],
        out_proj[0],
    )
    gathered = [swap(packed, "store", n_store, k) for k in reversed(range(1, n_store))] + [packed]
    slab = fetch(packed, store[0], n_layer)
    grads, partial = grads_and_scores(gathered, slab, n_store, n_layer, n_layer - 1)
    other = swap(partial, "layer", n_layer, 1)
    near = swap(scores(grads, slab, n_layer, 1), "layer", n_layer, 1)
    crossed = [near]
    for k in reversed(range(2, n_layer, 2)):
        if k < n_layer - 2:
            other = swap(scores(grads, slab, n_layer, k + 1), "layer", n_layer, 1)
        crossed.append(swap(scores(grads, slab, n_layer, k, [other]), "layer", n_layer, k))
    total = scores(grads, slab, n_layer, 0)
    for x in crossed:
        total = total + x.astype(f32)
    return total.T


def solution(mesh):
    placed = (
        P("layer", ("grp", "store"), None, None),
        P("layer", ("grp", "store"), None, None),
        P(("grp", "store")),
        P("layer", None),
        P("layer", None, None),
        P("layer", None, None),
        P("layer", ("grp", "store"), None),
    )
    return jax.shard_map(
        functools.partial(on_device, mesh.shape["store"], mesh.shape["layer"]),
        mesh=mesh,
        in_specs=placed,
        out_specs=P(("grp", "store", "layer"), None),
        check_vma=False,
    )
```

```python
import functools

import jax
import jax.numpy as jnp
from jax import lax
from jax.experimental import pallas as pl
from jax.experimental.pallas import tpu as pltpu
from jax.sharding import PartitionSpec as P

norm_epsilon = 1e-05
f32 = jnp.float32
bf16 = jnp.bfloat16
S = 8
R = 64
B = 4
A = R // B
G = 8
H = 4
LANES = 128


def dot_nt(left, right):
    return lax.dot_general(left, right, (((1,), (1,)), ((), ())), preferred_element_type=f32)


def iota(shape, dim):
    return lax.broadcasted_iota(jnp.int32, shape, dim)


def factors_kernel(
    window,
    hbm_lengths,
    hbm_hidden,
    hbm_cot,
    hbm_gain,
    hbm_inp,
    hbm_outp,
    packed,
    lengths,
    hidden,
    cot,
    gain,
    inp,
    outp,
    in_acc,
    sq_acc,
    out_t,
    sems,
):
    chunks, rows, columns = hidden.shape
    queries = lengths.shape[0]
    full = queries // G * G * S
    half = rows - full
    mid, low = full // 2, half // 2

    def copy(source, target, at):
        return pltpu.make_async_copy(source, target, sems.at[at])

    def chunk(c):
        cut = pl.ds(pl.multiple_of(c * columns, columns), columns)
        return [
            copy(hbm_gain.at[:, cut], gain.at[c], 3 + c),
            copy(hbm_inp.at[:, cut], inp.at[c], 3 + chunks + c),
            copy(hbm_hidden.at[:, cut], hidden.at[c], 3 + 2 * chunks + c),
        ]

    def start_chunk(c):
        for piece in chunk(c):
            piece.start()

    early = [copy(hbm_outp, outp, 0), copy(hbm_cot, cot, 1), copy(hbm_lengths, lengths, 2)]
    for c in range(window):
        start_chunk(c)
    for piece in early:
        piece.start()
    in_acc[...] = jnp.zeros_like(in_acc)
    sq_acc[...] = jnp.zeros_like(sq_acc)

    @pl.loop(0, chunks)
    def _(c):
        for piece in chunk(c):
            piece.wait()

        @pl.when(c + window < chunks)
        def _():
            start_chunk(c + window)

        scaled = inp[c].astype(f32) * gain[c].astype(f32)
        high = scaled.astype(bf16)
        rest = (scaled - high.astype(f32)).astype(bf16)
        in_acc[...] += dot_nt(hidden[c], jnp.concatenate([high, high, rest, rest], axis=0))
        for r in range(0, rows, 48):
            wide = hidden[c, r : r + 48, :].astype(f32)
            square = wide * wide
            total = square[:, :LANES]
            for at in range(LANES, columns, LANES):
                total += square[:, at : at + LANES]
            sq_acc[r : r + 48, :] += total

    for piece in early:
        piece.wait()
    odd = lax.rem(lax.axis_index("store"), 2)
    at_full = pl.multiple_of(odd * half, half)
    at_half = pl.multiple_of((1 - odd) * full, half)
    low_lanes = iota((S, LANES), 1) < R
    position = iota((S, LANES), 0)

    def in_rows(at, count):
        sums = in_acc[pl.ds(at, count), :]
        square = jnp.sum(sq_acc[pl.ds(at, count), :], axis=1, keepdims=True)
        scale = lax.rsqrt(square * (1.0 / (chunks * columns)) + norm_epsilon)
        factor = (sums[:, :LANES] + sums[:, LANES:]) * scale
        return [
            jnp.where(position < lengths[at // S + q], factor[q * S : (q + 1) * S], 0.0)
            for q in range(count // S)
        ]

    def side_by_side(tiles):
        both = zip(tiles[: len(tiles) // 2], tiles[len(tiles) // 2 :])
        return jnp.concatenate([jnp.where(low_lanes, x, y) for x, y in both], axis=0)

    packed[:mid, :] = side_by_side(in_rows(at_full, full)).astype(bf16)
    packed[mid : mid + low, :] = side_by_side(in_rows(at_half, half)).astype(bf16)

    whole = dot_nt(outp[...], cot[pl.ds(at_full, full), :])
    for t in range(full // LANES):
        out_t[t * R : (t + 1) * R, :] = whole[:, t * LANES : (t + 1) * LANES]
    out_t[full // LANES * R :, :half] = dot_nt(outp[...], cot[pl.ds(at_half, half), :])

    def part(t, b):
        return out_t[pl.ds(t * R + b, A, stride=B), :]

    row = mid + low
    for m in range(full // (G * S)):
        t, at = divmod(m * G * S, LANES)
        for b in range(0, B, 2):
            both = [part(t, b + c)[:, at : at + G * S] for c in range(2)]
            packed[row : row + A, :] = jnp.concatenate(both, axis=1).astype(bf16)
            row += A
    packed[row : row + A, :] = jnp.concatenate(
        [part(full // LANES, b)[:, :half] for b in range(B)], axis=1
    ).astype(bf16)


def in_hbm(x):
    return pltpu.with_memory_space_constraint(x, pltpu.HBM)


def factors(lengths, hidden, cotangent, gain, in_projection, out_projection):
    rows, width = hidden.shape
    columns = 2048
    chunks = width // columns
    return pl.pallas_call(
        functools.partial(factors_kernel, 2),
        out_shape=jax.ShapeDtypeStruct((rows, 2 * R), bf16),
        in_specs=[pl.BlockSpec(memory_space=pl.ANY)] * 6,
        out_specs=pl.BlockSpec(memory_space=pltpu.VMEM),
        scratch_shapes=[
            pltpu.SMEM(lengths.shape, jnp.int32),
            pltpu.VMEM((chunks, rows, columns), bf16),
            pltpu.VMEM(cotangent.shape, bf16),
            pltpu.VMEM((chunks, 1, columns), bf16),
            pltpu.VMEM((chunks, R, columns), bf16),
            pltpu.VMEM(out_projection.shape, bf16),
            pltpu.VMEM((rows, 4 * R), f32),
            pltpu.VMEM((rows, LANES), f32),
            pltpu.VMEM((-(-rows // LANES) * R, LANES), f32),
            pltpu.SemaphoreType.DMA((3 + 3 * chunks,)),
        ],
        compiler_params=pltpu.CompilerParams(vmem_limit_bytes=24 * 2**20),
        name="factors",
    )(*[in_hbm(x) for x in (lengths, hidden, cotangent, gain, in_projection, out_projection)])


def fetch_kernel(n_layer, after, store, slab, sems):
    block = slab.shape[0] // n_layer
    rows = 16 if block % 16 == 0 else 8
    me = lax.axis_index("layer")
    copies = []
    for k in range(n_layer):
        at = pl.multiple_of(partner(me, k, n_layer) * block, rows)
        to = slab.at[pl.ds(k * block, block)]
        copies.append(pltpu.make_async_copy(store.at[pl.ds(at, block)], to, sems.at[k]))
        copies[-1].start()
    for copy in copies:
        copy.wait()


def fetch(after, store, n_layer):
    rows, features = store.shape
    return pl.pallas_call(
        functools.partial(fetch_kernel, n_layer),
        out_shape=jax.ShapeDtypeStruct((rows, features), bf16),
        in_specs=[pl.BlockSpec(memory_space=pl.ANY)] * 2,
        out_specs=pl.BlockSpec(memory_space=pltpu.VMEM),
        scratch_shapes=[pltpu.SemaphoreType.DMA((n_layer,))],
        compiler_params=pltpu.CompilerParams(vmem_limit_bytes=12 * 2**20),
        cost_estimate=pl.CostEstimate(
            flops=0, bytes_accessed=2 * rows * features, transcendentals=0
        ),
        name="fetch",
    )(after, in_hbm(store))


def spread_out(tile, owner):
    lanes = tile.shape[1]
    mine = (owner == iota((G, lanes), 0))[None]
    wide = jnp.where(mine, tile.astype(f32)[:, None, :], 0.0)
    return wide.reshape(A * G, lanes).astype(bf16)


def halves(tile):
    wide = tile.astype(f32)
    turned = jnp.concatenate([wide[:, R:], wide[:, :R]], axis=1)
    low = iota(wide.shape, 1) < R
    return [
        jnp.where(mask, x, 0.0).astype(bf16)
        for x in (wide, turned)
        for mask in (low, jnp.logical_not(low))
    ]


def diagonal(low, high):
    zero = jnp.zeros_like(low)
    left = jnp.concatenate([low, high, zero, zero], axis=0)
    right = jnp.concatenate([zero, zero, low, high], axis=0)
    return jnp.concatenate([left, right], axis=1)


def build_grads(shards, base, row0, full_groups, grads):
    mid = full_groups * G * S // 2
    low = H * S // 2
    lane = iota((G, 2 * 128), 1)
    whole_owner = lax.rem(lane, G * S) // S
    half_owner = lax.rem(lane, H * S) // S + H * (lane // 128)

    def whole(shard):
        found = []
        pairs = {}
        for m in range(full_groups):
            first = m % (full_groups // 2)
            if first not in pairs:
                pairs[first] = halves(
                    shards[base + shard, first * G * S : (first + 1) * G * S, :]
                )
            plain_low, plain_high, turned_low, turned_high = pairs[first]
            weights = (
                diagonal(plain_low, turned_high)
                if m < full_groups // 2
                else diagonal(turned_low, plain_high)
            )
            at = mid + low + m * 2 * A
            tile = jnp.concatenate(
                [shards[base + shard, at : at + A, :], shards[base + shard, at + A : at + 2 * A, :]],
                axis=1,
            )
            found.append((spread_out(tile, whole_owner), weights))
        return found

    def joined(shard):
        tiles, weights = [], []
        for s in (shard, shard + 1):
            plain_low, plain_high, turned_low, turned_high = halves(
                shards[base + s, mid : mid + low, :]
            )
            weights.append(
                diagonal(
                    jnp.concatenate([plain_low, turned_low], axis=0),
                    jnp.concatenate([turned_high, plain_high], axis=0),
                )
            )
            at = mid + low + full_groups * 2 * A
            tiles.append(shards[base + s, at : at + A, :])
        return [
            (
                spread_out(jnp.concatenate(tiles, axis=1), half_owner),
                jnp.concatenate(weights, axis=0),
            )
        ]

    groups = []
    for shard in (0, 2):
        groups += whole(shard) + joined(shard) + whole(shard + 1)
    for at in range(0, len(groups), 2):
        first, second = [jnp.dot(x, w, preferred_element_type=f32) for x, w in groups[at : at + 2]]
        for a in range(A):
            pair = [x[a * G : (a + 1) * G] for x in (first, second)]
            grads[pl.ds(row0 + at * G, 2 * G), a * 256 : (a + 1) * 256] = jnp.concatenate(
                pair, axis=0
            ).astype(bf16)


def store_order(n):
    return [1, 3, 2] if n == 4 else list(range(1, n))


def grads_kernel(n_store, full_groups, k, *refs):
    gathered = refs[:n_store]
    slab, grads, out, shards = refs[n_store:]
    me_store = lax.axis_index("store")
    for block, away in zip(gathered, [0] + store_order(n_store)):
        shards[partner(me_store, away, n_store)] = block[...]
    four = 4 * (full_groups * G + H)
    if n_store == 4:
        build_grads(shards, 0, 0, full_groups, grads)
    else:

        @pl.loop(0, n_store // 4)
        def _(at):
            build_grads(shards, at * 4, pl.multiple_of(at * four, 16), full_groups, grads)

    scores_kernel(k, grads, slab, out)


def scores_kernel(k, grads, slab, *refs):
    *terms, out = refs
    block = out.shape[1]
    total = dot_nt(slab[k * block : (k + 1) * block, :], grads[...]).T
    for term in terms:
        total += term[...].astype(f32)
    out[...] = total.astype(out.dtype)


def partner(me, k, n):
    return jnp.bitwise_xor(me, k) if n & (n - 1) == 0 else lax.rem(n + k - me, n)


def swap(x, axis, n, k):
    pairs = [(i, i ^ k if n & (n - 1) == 0 else (n + k - i) % n) for i in range(n)]
    return lax.ppermute(x, axis, pairs)


def grads_and_scores(gathered, slab, n_store, n_layer, k):
    rows, features = slab.shape
    queries = n_store * gathered[0].shape[0] // S
    vmem = pl.BlockSpec(memory_space=pltpu.VMEM)
    return pl.pallas_call(
        functools.partial(grads_kernel, n_store, queries // n_store // G, k),
        out_shape=[
            jax.ShapeDtypeStruct((queries, features), bf16),
            jax.ShapeDtypeStruct((queries, rows // n_layer), bf16),
        ],
        in_specs=[vmem] * (n_store + 1),
        out_specs=[vmem] * 2,
        scratch_shapes=[pltpu.VMEM((n_store,) + gathered[0].shape, bf16)],
        compiler_params=pltpu.CompilerParams(vmem_limit_bytes=24 * 2**20),
        name="grads",
    )(*gathered, slab)


def scores(grads, slab, n_layer, k, terms=()):
    rows, features = slab.shape
    block = rows // n_layer
    queries = grads.shape[0]
    vmem = pl.BlockSpec(memory_space=pltpu.VMEM)
    return pl.pallas_call(
        functools.partial(scores_kernel, k),
        out_shape=jax.ShapeDtypeStruct((queries, block), bf16 if k else f32),
        in_specs=[vmem] * (2 + len(terms)),
        out_specs=vmem,
        compiler_params=pltpu.CompilerParams(vmem_limit_bytes=24 * 2**20),
        cost_estimate=pl.CostEstimate(
            flops=2 * queries * block * features,
            bytes_accessed=2 * (queries + block) * features,
            transcendentals=0,
        ),
        name="scores",
    )(grads, slab, *terms)


def on_device(n_store, n_layer, hidden, cotangent, lengths, norm_gain, in_proj, out_proj, store):
    queries, positions, width = hidden.shape[1:]
    packed = factors(
        lengths,
        hidden.reshape(queries * positions, width),
        cotangent.reshape(queries * positions, cotangent.shape[3]),
        norm_gain,
        in_proj[0],
        out_proj[0],
    )
    gathered = [packed] + [swap(packed, "store", n_store, k) for k in store_order(n_store)]
    slab = fetch(packed, store[0], n_layer)
    grads, partial = grads_and_scores(gathered, slab, n_store, n_layer, n_layer - 1)
    other = swap(partial, "layer", n_layer, 1)
    near = swap(scores(grads, slab, n_layer, 1), "layer", n_layer, 1)
    crossed = [near]
    for k in reversed(range(2, n_layer, 2)):
        if k < n_layer - 2:
            other = swap(scores(grads, slab, n_layer, k + 1), "layer", n_layer, 1)
        crossed.append(swap(scores(grads, slab, n_layer, k, [other]), "layer", n_layer, k))
    total = scores(grads, slab, n_layer, 0)
    for x in crossed:
        total = total + x.astype(f32)
    return total.T


def solution(mesh):
    placed = (
        P("layer", ("grp", "store"), None, None),
        P("layer", ("grp", "store"), None, None),
        P(("grp", "store")),
        P("layer", None),
        P("layer", None, None),
        P("layer", None, None),
        P("layer", ("grp", "store"), None),
    )
    return jax.shard_map(
        functools.partial(on_device, mesh.shape["store"], mesh.shape["layer"]),
        mesh=mesh,
        in_specs=placed,
        out_specs=P(("grp", "store", "layer"), None),
        check_vma=False,
    )
```

```python
import functools

import jax
import jax.numpy as jnp
from jax import lax
from jax.experimental import pallas as pl
from jax.experimental.pallas import tpu as pltpu
from jax.sharding import PartitionSpec as P

norm_epsilon = 1e-05
f32 = jnp.float32
bf16 = jnp.bfloat16
S = 8
R = 64
B = 4
A = R // B
G = 8
H = 4
LANES = 128


def dot_nt(left, right):
    return lax.dot_general(left, right, (((1,), (1,)), ((), ())), preferred_element_type=f32)


def iota(shape, dim):
    return lax.broadcasted_iota(jnp.int32, shape, dim)


def factors_kernel(
    cuts,
    hbm_lengths,
    hbm_hidden,
    hbm_cot,
    hbm_gain,
    hbm_inp,
    hbm_outp,
    packed,
    lengths,
    hidden,
    cot,
    gain,
    inp,
    outp,
    in_acc,
    sq_acc,
    out_t,
    sems,
):
    rows, width = hidden.shape
    queries = lengths.shape[0]
    full = queries // G * G * S
    half = rows - full
    mid, low = full // 2, half // 2
    chunks = len(cuts) - 1

    def copy(source, target, at):
        return pltpu.make_async_copy(source, target, sems.at[at])

    copy_gain = copy(hbm_gain, gain, 0)
    early = [copy(hbm_outp, outp, 1), copy(hbm_cot, cot, 2), copy(hbm_lengths, lengths, 3)]
    pieces = []
    for c in range(chunks):
        cut = pl.ds(cuts[c], cuts[c + 1] - cuts[c])
        pieces.append(
            [
                copy(hbm_inp.at[:, cut], inp.at[:, cut], 4 + 2 * c),
                copy(hbm_hidden.at[:, cut], hidden.at[:, cut], 5 + 2 * c),
            ]
        )

    def start(group):
        for piece in group:
            piece.start()

    copy_gain.start()
    for c in range(3):
        start(pieces[c])
    copy_gain.wait()
    start(pieces[3])
    for c in range(chunks):
        for piece in pieces[c]:
            piece.wait()
        if c + 4 < chunks:
            start(pieces[c + 4])
        if c + 4 == chunks:
            start(early)
        cut = slice(cuts[c], cuts[c + 1])
        scaled = inp[:, cut].astype(f32) * gain[:, cut].astype(f32)
        high = scaled.astype(bf16)
        rest = (scaled - high.astype(f32)).astype(bf16)
        product = dot_nt(hidden[:, cut], jnp.concatenate([high, rest], axis=0))
        in_acc[...] = product if c == 0 else in_acc[...] + product
        for r in range(0, rows, 48):
            wide = hidden[r : r + 48, cut].astype(f32)
            square = wide * wide
            total = square[:, :LANES]
            for at in range(LANES, cuts[c + 1] - cuts[c], LANES):
                total += square[:, at : at + LANES]
            sq_acc[r : r + 48, :] = total if c == 0 else sq_acc[r : r + 48, :] + total

    for piece in early:
        piece.wait()
    odd = lax.rem(lax.axis_index("store"), 2)
    at_full = pl.multiple_of(odd * half, half)
    at_half = pl.multiple_of((1 - odd) * full, half)
    low_lanes = iota((S, LANES), 1) < R
    position = iota((S, LANES), 0)

    def in_rows(at, count):
        sums = in_acc[pl.ds(at, count), :]
        square = jnp.sum(sq_acc[pl.ds(at, count), :], axis=1, keepdims=True)
        scale = lax.rsqrt(square * (1.0 / width) + norm_epsilon)
        factor = (sums + pltpu.roll(sums, R, 1)) * scale
        return [
            jnp.where(position < lengths[at // S + q], factor[q * S : (q + 1) * S], 0.0)
            for q in range(count // S)
        ]

    def side_by_side(tiles):
        both = zip(tiles[: len(tiles) // 2], tiles[len(tiles) // 2 :])
        return jnp.concatenate([jnp.where(low_lanes, x, y) for x, y in both], axis=0)

    packed[:mid, :] = side_by_side(in_rows(at_full, full)).astype(bf16)
    packed[mid : mid + low, :] = side_by_side(in_rows(at_half, half)).astype(bf16)

    whole = dot_nt(outp[...], cot[pl.ds(at_full, full), :])
    for t in range(full // LANES):
        out_t[t * R : (t + 1) * R, :] = whole[:, t * LANES : (t + 1) * LANES]
    out_t[full // LANES * R :, :half] = dot_nt(outp[...], cot[pl.ds(at_half, half), :])

    def part(t, b):
        return out_t[pl.ds(t * R + b, A, stride=B), :]

    row = mid + low
    for m in range(full // (G * S)):
        t, at = divmod(m * G * S, LANES)
        for b in range(0, B, 2):
            both = [part(t, b + c)[:, at : at + G * S] for c in range(2)]
            packed[row : row + A, :] = jnp.concatenate(both, axis=1).astype(bf16)
            row += A
    packed[row : row + A, :] = jnp.concatenate(
        [part(full // LANES, b)[:, :half] for b in range(B)], axis=1
    ).astype(bf16)


def in_hbm(x):
    return pltpu.with_memory_space_constraint(x, pltpu.HBM)


def factors(lengths, hidden, cotangent, gain, in_projection, out_projection):
    rows, width = hidden.shape
    cuts = [width * part // 16 for part in (0, 1, 2, 4, 8, 12, 16)]
    return pl.pallas_call(
        functools.partial(factors_kernel, cuts),
        out_shape=jax.ShapeDtypeStruct((rows, 2 * R), bf16),
        in_specs=[pl.BlockSpec(memory_space=pl.ANY)] * 6,
        out_specs=pl.BlockSpec(memory_space=pltpu.VMEM),
        scratch_shapes=[
            pltpu.SMEM(lengths.shape, jnp.int32),
            pltpu.VMEM(hidden.shape, bf16),
            pltpu.VMEM(cotangent.shape, bf16),
            pltpu.VMEM(gain.shape, bf16),
            pltpu.VMEM(in_projection.shape, bf16),
            pltpu.VMEM(out_projection.shape, bf16),
            pltpu.VMEM((rows, 2 * R), f32),
            pltpu.VMEM((rows, LANES), f32),
            pltpu.VMEM((-(-rows // LANES) * R, LANES), f32),
            pltpu.SemaphoreType.DMA((2 + 2 * len(cuts),)),
        ],
        compiler_params=pltpu.CompilerParams(vmem_limit_bytes=24 * 2**20),
        name="factors",
    )(*[in_hbm(x) for x in (lengths, hidden, cotangent, gain, in_projection, out_projection)])


def fetch_kernel(n_layer, after, store, slab, sems):
    block = slab.shape[0] // n_layer
    rows = 16 if block % 16 == 0 else 8
    me = lax.axis_index("layer")
    copies = []
    for k in range(n_layer):
        at = pl.multiple_of(partner(me, k, n_layer) * block, rows)
        to = slab.at[pl.ds(k * block, block)]
        copies.append(pltpu.make_async_copy(store.at[pl.ds(at, block)], to, sems.at[k]))
        copies[-1].start()
    for copy in copies:
        copy.wait()


def fetch(after, store, n_layer):
    rows, features = store.shape
    return pl.pallas_call(
        functools.partial(fetch_kernel, n_layer),
        out_shape=jax.ShapeDtypeStruct((rows, features), bf16),
        in_specs=[pl.BlockSpec(memory_space=pl.ANY)] * 2,
        out_specs=pl.BlockSpec(memory_space=pltpu.VMEM),
        scratch_shapes=[pltpu.SemaphoreType.DMA((n_layer,))],
        compiler_params=pltpu.CompilerParams(vmem_limit_bytes=12 * 2**20),
        cost_estimate=pl.CostEstimate(
            flops=0, bytes_accessed=2 * rows * features, transcendentals=0
        ),
        name="fetch",
    )(after, in_hbm(store))


def spread_out(tile, owner):
    lanes = tile.shape[1]
    mine = (owner == iota((G, lanes), 0))[None]
    wide = jnp.where(mine, tile.astype(f32)[:, None, :], 0.0)
    return wide.reshape(A * G, lanes).astype(bf16)


def halves(tile):
    wide = tile.astype(f32)
    turned = jnp.concatenate([wide[:, R:], wide[:, :R]], axis=1)
    low = iota(wide.shape, 1) < R
    return [
        jnp.where(mask, x, 0.0).astype(bf16)
        for x in (wide, turned)
        for mask in (low, jnp.logical_not(low))
    ]


def diagonal(low, high):
    zero = jnp.zeros_like(low)
    left = jnp.concatenate([low, high, zero, zero], axis=0)
    right = jnp.concatenate([zero, zero, low, high], axis=0)
    return jnp.concatenate([left, right], axis=1)


def build_grads(shards, base, row0, full_groups, grads):
    mid = full_groups * G * S // 2
    low = H * S // 2
    lane = iota((G, 2 * 128), 1)
    whole_owner = lax.rem(lane, G * S) // S
    half_owner = lax.rem(lane, H * S) // S + H * (lane // 128)

    def whole(shard):
        found = []
        pairs = {}
        for m in range(full_groups):
            first = m % (full_groups // 2)
            if first not in pairs:
                pairs[first] = halves(
                    shards[base + shard, first * G * S : (first + 1) * G * S, :]
                )
            plain_low, plain_high, turned_low, turned_high = pairs[first]
            weights = (
                diagonal(plain_low, turned_high)
                if m < full_groups // 2
                else diagonal(turned_low, plain_high)
            )
            at = mid + low + m * 2 * A
            tile = jnp.concatenate(
                [shards[base + shard, at : at + A, :], shards[base + shard, at + A : at + 2 * A, :]],
                axis=1,
            )
            found.append((spread_out(tile, whole_owner), weights))
        return found

    def joined(shard):
        tiles, weights = [], []
        for s in (shard, shard + 1):
            plain_low, plain_high, turned_low, turned_high = halves(
                shards[base + s, mid : mid + low, :]
            )
            weights.append(
                diagonal(
                    jnp.concatenate([plain_low, turned_low], axis=0),
                    jnp.concatenate([turned_high, plain_high], axis=0),
                )
            )
            at = mid + low + full_groups * 2 * A
            tiles.append(shards[base + s, at : at + A, :])
        return [
            (
                spread_out(jnp.concatenate(tiles, axis=1), half_owner),
                jnp.concatenate(weights, axis=0),
            )
        ]

    groups = []
    for shard in (0, 2):
        groups += whole(shard) + joined(shard) + whole(shard + 1)
    for at in range(0, len(groups), 2):
        first, second = [jnp.dot(x, w, preferred_element_type=f32) for x, w in groups[at : at + 2]]
        for a in range(A):
            pair = [x[a * G : (a + 1) * G] for x in (first, second)]
            grads[pl.ds(row0 + at * G, 2 * G), a * 256 : (a + 1) * 256] = jnp.concatenate(
                pair, axis=0
            ).astype(bf16)


def store_order(n):
    return [1, 3, 2] if n == 4 else list(range(1, n))


def grads_kernel(n_store, full_groups, k, *refs):
    gathered = refs[:n_store]
    slab, grads, out, shards = refs[n_store:]
    me_store = lax.axis_index("store")
    for block, away in zip(gathered, [0] + store_order(n_store)):
        shards[partner(me_store, away, n_store)] = block[...]
    four = 4 * (full_groups * G + H)
    if n_store == 4:
        build_grads(shards, 0, 0, full_groups, grads)
    else:

        @pl.loop(0, n_store // 4)
        def _(at):
            build_grads(shards, at * 4, pl.multiple_of(at * four, 16), full_groups, grads)

    scores_kernel(k, grads, slab, out)


def scores_kernel(k, grads, slab, *refs):
    *terms, out = refs
    block = out.shape[1]
    total = dot_nt(slab[k * block : (k + 1) * block, :], grads[...]).T
    for term in terms:
        total += term[...].astype(f32)
    out[...] = total.astype(out.dtype)


def partner(me, k, n):
    return jnp.bitwise_xor(me, k) if n & (n - 1) == 0 else lax.rem(n + k - me, n)


def swap(x, axis, n, k):
    pairs = [(i, i ^ k if n & (n - 1) == 0 else (n + k - i) % n) for i in range(n)]
    return lax.ppermute(x, axis, pairs)


def grads_and_scores(gathered, slab, n_store, n_layer, k):
    rows, features = slab.shape
    queries = n_store * gathered[0].shape[0] // S
    vmem = pl.BlockSpec(memory_space=pltpu.VMEM)
    return pl.pallas_call(
        functools.partial(grads_kernel, n_store, queries // n_store // G, k),
        out_shape=[
            jax.ShapeDtypeStruct((queries, features), bf16),
            jax.ShapeDtypeStruct((queries, rows // n_layer), bf16),
        ],
        in_specs=[vmem] * (n_store + 1),
        out_specs=[vmem] * 2,
        scratch_shapes=[pltpu.VMEM((n_store,) + gathered[0].shape, bf16)],
        compiler_params=pltpu.CompilerParams(vmem_limit_bytes=24 * 2**20),
        name="grads",
    )(*gathered, slab)


def scores(grads, slab, n_layer, k, terms=()):
    rows, features = slab.shape
    block = rows // n_layer
    queries = grads.shape[0]
    vmem = pl.BlockSpec(memory_space=pltpu.VMEM)
    return pl.pallas_call(
        functools.partial(scores_kernel, k),
        out_shape=jax.ShapeDtypeStruct((queries, block), bf16 if k else f32),
        in_specs=[vmem] * (2 + len(terms)),
        out_specs=vmem,
        compiler_params=pltpu.CompilerParams(vmem_limit_bytes=24 * 2**20),
        cost_estimate=pl.CostEstimate(
            flops=2 * queries * block * features,
            bytes_accessed=2 * (queries + block) * features,
            transcendentals=0,
        ),
        name="scores",
    )(grads, slab, *terms)


def on_device(n_store, n_layer, hidden, cotangent, lengths, norm_gain, in_proj, out_proj, store):
    queries, positions, width = hidden.shape[1:]
    packed = factors(
        lengths,
        hidden.reshape(queries * positions, width),
        cotangent.reshape(queries * positions, cotangent.shape[3]),
        norm_gain,
        in_proj[0],
        out_proj[0],
    )
    gathered = [packed] + [swap(packed, "store", n_store, k) for k in store_order(n_store)]
    slab = fetch(packed, store[0], n_layer)
    grads, partial = grads_and_scores(gathered, slab, n_store, n_layer, n_layer - 1)
    other = swap(partial, "layer", n_layer, 1)
    near = swap(scores(grads, slab, n_layer, 1), "layer", n_layer, 1)
    crossed = [near]
    for k in reversed(range(2, n_layer, 2)):
        if k < n_layer - 2:
            other = swap(scores(grads, slab, n_layer, k + 1), "layer", n_layer, 1)
        crossed.append(swap(scores(grads, slab, n_layer, k, [other]), "layer", n_layer, k))
    total = scores(grads, slab, n_layer, 0)
    for x in crossed:
        total = total + x.astype(f32)
    return total.T


def solution(mesh):
    placed = (
        P("layer", ("grp", "store"), None, None),
        P("layer", ("grp", "store"), None, None),
        P(("grp", "store")),
        P("layer", None),
        P("layer", None, None),
        P("layer", None, None),
        P("layer", ("grp", "store"), None),
    )
    return jax.shard_map(
        functools.partial(on_device, mesh.shape["store"], mesh.shape["layer"]),
        mesh=mesh,
        in_specs=placed,
        out_specs=P(("grp", "store", "layer"), None),
        check_vma=False,
    )
```

```python
import functools

import jax
import jax.numpy as jnp
from jax import lax
from jax.experimental import pallas as pl
from jax.experimental.pallas import tpu as pltpu
from jax.sharding import PartitionSpec as P

norm_epsilon = 1e-05
f32 = jnp.float32
bf16 = jnp.bfloat16
S = 8
R = 64
B = 4
A = R // B
G = 8
H = 4
LANES = 128


def dot_nt(left, right):
    return lax.dot_general(left, right, (((1,), (1,)), ((), ())), preferred_element_type=f32)


def iota(shape, dim):
    return lax.broadcasted_iota(jnp.int32, shape, dim)


def factors_kernel(
    hbm_lengths,
    hbm_hidden,
    hbm_cot,
    hbm_gain,
    hbm_inp,
    hbm_outp,
    packed,
    lengths,
    hidden,
    cot,
    gain,
    inp,
    outp,
    in_acc,
    sq_acc,
    out_t,
    sems,
):
    chunks, rows, columns = hidden.shape
    width = chunks * columns
    queries = lengths.shape[0]
    full = queries // G * G * S
    half = rows - full
    mid, low = full // 2, half // 2

    def copy(source, target, at):
        return pltpu.make_async_copy(source, target, sems.at[at])

    def pieces(c):
        cut = pl.ds(pl.multiple_of(c * columns, columns), columns)
        return [
            copy(hbm_inp.at[:, cut], inp.at[c], 4 + c),
            copy(hbm_hidden.at[:, cut], hidden.at[c], 4 + chunks + c),
        ]

    def start(group):
        for piece in group:
            piece.start()

    copy_gain = copy(hbm_gain, gain, 0)
    early = [copy(hbm_outp, outp, 1), copy(hbm_cot, cot, 2), copy(hbm_lengths, lengths, 3)]
    copy_gain.start()
    start(pieces(0))
    start(pieces(1))
    in_acc[...] = jnp.zeros_like(in_acc)
    sq_acc[...] = jnp.zeros_like(sq_acc)
    copy_gain.wait()
    start(pieces(2))

    @pl.loop(0, chunks)
    def _(c):
        for piece in pieces(c):
            piece.wait()

        @pl.when(c + 3 < chunks)
        def _():
            start(pieces(c + 3))

        @pl.when(c + 3 == chunks)
        def _():
            start(early)

        cut = pl.ds(pl.multiple_of(c * columns, columns), columns)
        scaled = inp[c].astype(f32) * gain[:, cut].astype(f32)
        high = scaled.astype(bf16)
        rest = (scaled - high.astype(f32)).astype(bf16)
        in_acc[...] += dot_nt(hidden[c], jnp.concatenate([high, rest], axis=0))
        for r in range(0, rows, 48):
            wide = hidden[c, r : r + 48, :].astype(f32)
            square = wide * wide
            total = square[:, :LANES]
            for at in range(LANES, columns, LANES):
                total += square[:, at : at + LANES]
            sq_acc[r : r + 48, :] += total

    for piece in early:
        piece.wait()
    odd = lax.rem(lax.axis_index("store"), 2)
    at_full = pl.multiple_of(odd * half, half)
    at_half = pl.multiple_of((1 - odd) * full, half)
    low_lanes = iota((S, LANES), 1) < R
    position = iota((S, LANES), 0)

    def in_rows(at, count):
        sums = in_acc[pl.ds(at, count), :]
        square = jnp.sum(sq_acc[pl.ds(at, count), :], axis=1, keepdims=True)
        scale = lax.rsqrt(square * (1.0 / width) + norm_epsilon)
        factor = (sums + pltpu.roll(sums, R, 1)) * scale
        return [
            jnp.where(position < lengths[at // S + q], factor[q * S : (q + 1) * S], 0.0)
            for q in range(count // S)
        ]

    def side_by_side(tiles):
        both = zip(tiles[: len(tiles) // 2], tiles[len(tiles) // 2 :])
        return jnp.concatenate([jnp.where(low_lanes, x, y) for x, y in both], axis=0)

    packed[:mid, :] = side_by_side(in_rows(at_full, full)).astype(bf16)
    packed[mid : mid + low, :] = side_by_side(in_rows(at_half, half)).astype(bf16)

    whole = dot_nt(outp[...], cot[pl.ds(at_full, full), :])
    for t in range(full // LANES):
        out_t[t * R : (t + 1) * R, :] = whole[:, t * LANES : (t + 1) * LANES]
    out_t[full // LANES * R :, :half] = dot_nt(outp[...], cot[pl.ds(at_half, half), :])

    def part(t, b):
        return out_t[pl.ds(t * R + b, A, stride=B), :]

    row = mid + low
    for m in range(full // (G * S)):
        t, at = divmod(m * G * S, LANES)
        for b in range(0, B, 2):
            both = [part(t, b + c)[:, at : at + G * S] for c in range(2)]
            packed[row : row + A, :] = jnp.concatenate(both, axis=1).astype(bf16)
            row += A
    packed[row : row + A, :] = jnp.concatenate(
        [part(full // LANES, b)[:, :half] for b in range(B)], axis=1
    ).astype(bf16)


def in_hbm(x):
    return pltpu.with_memory_space_constraint(x, pltpu.HBM)


def factors(lengths, hidden, cotangent, gain, in_projection, out_projection):
    rows, width = hidden.shape
    columns = 1024
    chunks = width // columns
    return pl.pallas_call(
        factors_kernel,
        out_shape=jax.ShapeDtypeStruct((rows, 2 * R), bf16),
        in_specs=[pl.BlockSpec(memory_space=pl.ANY)] * 6,
        out_specs=pl.BlockSpec(memory_space=pltpu.VMEM),
        scratch_shapes=[
            pltpu.SMEM(lengths.shape, jnp.int32),
            pltpu.VMEM((chunks, rows, columns), bf16),
            pltpu.VMEM(cotangent.shape, bf16),
            pltpu.VMEM(gain.shape, bf16),
            pltpu.VMEM((chunks, R, columns), bf16),
            pltpu.VMEM(out_projection.shape, bf16),
            pltpu.VMEM((rows, 2 * R), f32),
            pltpu.VMEM((rows, LANES), f32),
            pltpu.VMEM((-(-rows // LANES) * R, LANES), f32),
            pltpu.SemaphoreType.DMA((4 + 2 * chunks,)),
        ],
        compiler_params=pltpu.CompilerParams(vmem_limit_bytes=24 * 2**20),
        name="factors",
    )(*[in_hbm(x) for x in (lengths, hidden, cotangent, gain, in_projection, out_projection)])


def fetch_kernel(n_layer, after, store, slab, sems):
    block = slab.shape[0] // n_layer
    rows = 16 if block % 16 == 0 else 8
    me = lax.axis_index("layer")
    copies = []
    for k in range(n_layer):
        at = pl.multiple_of(partner(me, k, n_layer) * block, rows)
        to = slab.at[pl.ds(k * block, block)]
        copies.append(pltpu.make_async_copy(store.at[pl.ds(at, block)], to, sems.at[k]))
        copies[-1].start()
    for copy in copies:
        copy.wait()


def fetch(after, store, n_layer):
    rows, features = store.shape
    return pl.pallas_call(
        functools.partial(fetch_kernel, n_layer),
        out_shape=jax.ShapeDtypeStruct((rows, features), bf16),
        in_specs=[pl.BlockSpec(memory_space=pl.ANY)] * 2,
        out_specs=pl.BlockSpec(memory_space=pltpu.VMEM),
        scratch_shapes=[pltpu.SemaphoreType.DMA((n_layer,))],
        compiler_params=pltpu.CompilerParams(vmem_limit_bytes=12 * 2**20),
        cost_estimate=pl.CostEstimate(
            flops=0, bytes_accessed=2 * rows * features, transcendentals=0
        ),
        name="fetch",
    )(after, in_hbm(store))


def spread_out(tile, owner):
    lanes = tile.shape[1]
    mine = (owner == iota((G, lanes), 0))[None]
    wide = jnp.where(mine, tile.astype(f32)[:, None, :], 0.0)
    return wide.reshape(A * G, lanes).astype(bf16)


def halves(tile):
    wide = tile.astype(f32)
    turned = jnp.concatenate([wide[:, R:], wide[:, :R]], axis=1)
    low = iota(wide.shape, 1) < R
    return [
        jnp.where(mask, x, 0.0).astype(bf16)
        for x in (wide, turned)
        for mask in (low, jnp.logical_not(low))
    ]


def diagonal(low, high):
    zero = jnp.zeros_like(low)
    left = jnp.concatenate([low, high, zero, zero], axis=0)
    right = jnp.concatenate([zero, zero, low, high], axis=0)
    return jnp.concatenate([left, right], axis=1)


def build_grads(shards, base, row0, full_groups, grads):
    mid = full_groups * G * S // 2
    low = H * S // 2
    lane = iota((G, 2 * 128), 1)
    whole_owner = lax.rem(lane, G * S) // S
    half_owner = lax.rem(lane, H * S) // S + H * (lane // 128)

    def whole(shard):
        found = []
        pairs = {}
        for m in range(full_groups):
            first = m % (full_groups // 2)
            if first not in pairs:
                pairs[first] = halves(
                    shards[base + shard, first * G * S : (first + 1) * G * S, :]
                )
            plain_low, plain_high, turned_low, turned_high = pairs[first]
            weights = (
                diagonal(plain_low, turned_high)
                if m < full_groups // 2
                else diagonal(turned_low, plain_high)
            )
            at = mid + low + m * 2 * A
            tile = jnp.concatenate(
                [shards[base + shard, at : at + A, :], shards[base + shard, at + A : at + 2 * A, :]],
                axis=1,
            )
            found.append((spread_out(tile, whole_owner), weights))
        return found

    def joined(shard):
        tiles, weights = [], []
        for s in (shard, shard + 1):
            plain_low, plain_high, turned_low, turned_high = halves(
                shards[base + s, mid : mid + low, :]
            )
            weights.append(
                diagonal(
                    jnp.concatenate([plain_low, turned_low], axis=0),
                    jnp.concatenate([turned_high, plain_high], axis=0),
                )
            )
            at = mid + low + full_groups * 2 * A
            tiles.append(shards[base + s, at : at + A, :])
        return [
            (
                spread_out(jnp.concatenate(tiles, axis=1), half_owner),
                jnp.concatenate(weights, axis=0),
            )
        ]

    groups = []
    for shard in (0, 2):
        groups += whole(shard) + joined(shard) + whole(shard + 1)
    for at in range(0, len(groups), 2):
        first, second = [jnp.dot(x, w, preferred_element_type=f32) for x, w in groups[at : at + 2]]
        for a in range(A):
            pair = [x[a * G : (a + 1) * G] for x in (first, second)]
            grads[pl.ds(row0 + at * G, 2 * G), a * 256 : (a + 1) * 256] = jnp.concatenate(
                pair, axis=0
            ).astype(bf16)


def store_order(n):
    return [1, 3, 2] if n == 4 else list(range(1, n))


def grads_kernel(n_store, full_groups, k, *refs):
    gathered = refs[:n_store]
    slab, grads, out, shards = refs[n_store:]
    me_store = lax.axis_index("store")
    for block, away in zip(gathered, [0] + store_order(n_store)):
        shards[partner(me_store, away, n_store)] = block[...]
    four = 4 * (full_groups * G + H)
    if n_store == 4:
        build_grads(shards, 0, 0, full_groups, grads)
    else:

        @pl.loop(0, n_store // 4)
        def _(at):
            build_grads(shards, at * 4, pl.multiple_of(at * four, 16), full_groups, grads)

    scores_kernel(k, grads, slab, out)


def scores_kernel(k, grads, slab, *refs):
    *terms, out = refs
    block = out.shape[1]
    total = dot_nt(slab[k * block : (k + 1) * block, :], grads[...]).T
    for term in terms:
        total += term[...].astype(f32)
    out[...] = total.astype(out.dtype)


def partner(me, k, n):
    return jnp.bitwise_xor(me, k) if n & (n - 1) == 0 else lax.rem(n + k - me, n)


def swap(x, axis, n, k):
    pairs = [(i, i ^ k if n & (n - 1) == 0 else (n + k - i) % n) for i in range(n)]
    return lax.ppermute(x, axis, pairs)


def grads_and_scores(gathered, slab, n_store, n_layer, k):
    rows, features = slab.shape
    queries = n_store * gathered[0].shape[0] // S
    vmem = pl.BlockSpec(memory_space=pltpu.VMEM)
    return pl.pallas_call(
        functools.partial(grads_kernel, n_store, queries // n_store // G, k),
        out_shape=[
            jax.ShapeDtypeStruct((queries, features), bf16),
            jax.ShapeDtypeStruct((queries, rows // n_layer), bf16),
        ],
        in_specs=[vmem] * (n_store + 1),
        out_specs=[vmem] * 2,
        scratch_shapes=[pltpu.VMEM((n_store,) + gathered[0].shape, bf16)],
        compiler_params=pltpu.CompilerParams(vmem_limit_bytes=24 * 2**20),
        name="grads",
    )(*gathered, slab)


def scores(grads, slab, n_layer, k, terms=()):
    rows, features = slab.shape
    block = rows // n_layer
    queries = grads.shape[0]
    vmem = pl.BlockSpec(memory_space=pltpu.VMEM)
    return pl.pallas_call(
        functools.partial(scores_kernel, k),
        out_shape=jax.ShapeDtypeStruct((queries, block), bf16 if k else f32),
        in_specs=[vmem] * (2 + len(terms)),
        out_specs=vmem,
        compiler_params=pltpu.CompilerParams(vmem_limit_bytes=24 * 2**20),
        cost_estimate=pl.CostEstimate(
            flops=2 * queries * block * features,
            bytes_accessed=2 * (queries + block) * features,
            transcendentals=0,
        ),
        name="scores",
    )(grads, slab, *terms)


def on_device(n_store, n_layer, hidden, cotangent, lengths, norm_gain, in_proj, out_proj, store):
    queries, positions, width = hidden.shape[1:]
    packed = factors(
        lengths,
        hidden.reshape(queries * positions, width),
        cotangent.reshape(queries * positions, cotangent.shape[3]),
        norm_gain,
        in_proj[0],
        out_proj[0],
    )
    gathered = [packed] + [swap(packed, "store", n_store, k) for k in store_order(n_store)]
    slab = fetch(packed, store[0], n_layer)
    grads, partial = grads_and_scores(gathered, slab, n_store, n_layer, n_layer - 1)
    other = swap(partial, "layer", n_layer, 1)
    near = swap(scores(grads, slab, n_layer, 1), "layer", n_layer, 1)
    crossed = [near]
    for k in reversed(range(2, n_layer, 2)):
        if k < n_layer - 2:
            other = swap(scores(grads, slab, n_layer, k + 1), "layer", n_layer, 1)
        crossed.append(swap(scores(grads, slab, n_layer, k, [other]), "layer", n_layer, k))
    total = scores(grads, slab, n_layer, 0)
    for x in crossed:
        total = total + x.astype(f32)
    return total.T


def solution(mesh):
    placed = (
        P("layer", ("grp", "store"), None, None),
        P("layer", ("grp", "store"), None, None),
        P(("grp", "store")),
        P("layer", None),
        P("layer", None, None),
        P("layer", None, None),
        P("layer", ("grp", "store"), None),
    )
    return jax.shard_map(
        functools.partial(on_device, mesh.shape["store"], mesh.shape["layer"]),
        mesh=mesh,
        in_specs=placed,
        out_specs=P(("grp", "store", "layer"), None),
        check_vma=False,
    )
```

```python
import functools

import jax
import jax.numpy as jnp
from jax import lax
from jax.experimental import pallas as pl
from jax.experimental.pallas import tpu as pltpu
from jax.sharding import PartitionSpec as P

norm_epsilon = 1e-05
f32 = jnp.float32
bf16 = jnp.bfloat16
S = 8
R = 64
B = 4
A = R // B
G = 8
H = 4
LANES = 128


def dot_nt(left, right):
    return lax.dot_general(left, right, (((1,), (1,)), ((), ())), preferred_element_type=f32)


def iota(shape, dim):
    return lax.broadcasted_iota(jnp.int32, shape, dim)


def factors_kernel(
    hbm_lengths,
    hbm_hidden,
    hbm_cot,
    hbm_gain,
    hbm_inp,
    hbm_outp,
    packed,
    lengths,
    hidden,
    cot,
    gain,
    inp,
    outp,
    in_acc,
    sq_acc,
    out_t,
    sems,
):
    chunks, rows, columns = hidden.shape
    width = chunks * columns
    queries = lengths.shape[0]
    full = queries // G * G * S
    half = rows - full
    mid, low = full // 2, half // 2

    def copy(source, target, at):
        return pltpu.make_async_copy(source, target, sems.at[at])

    def pieces(c):
        cut = pl.ds(pl.multiple_of(c * columns, columns), columns)
        return [
            copy(hbm_inp.at[:, cut], inp.at[c], 4 + c),
            copy(hbm_hidden.at[:, cut], hidden.at[c], 4 + chunks + c),
        ]

    def start(group):
        for piece in group:
            piece.start()

    copy_gain = copy(hbm_gain, gain, 0)
    early = [copy(hbm_outp, outp, 1), copy(hbm_cot, cot, 2), copy(hbm_lengths, lengths, 3)]
    copy_gain.start()
    start(pieces(0))
    start(pieces(1))
    in_acc[...] = jnp.zeros_like(in_acc)
    sq_acc[...] = jnp.zeros_like(sq_acc)
    copy_gain.wait()
    start(pieces(2))

    @pl.loop(0, chunks)
    def _(c):
        for piece in pieces(c):
            piece.wait()

        @pl.when(c + 3 < chunks)
        def _():
            start(pieces(c + 3))

        @pl.when(c == 1)
        def _():
            start(early)

        cut = pl.ds(pl.multiple_of(c * columns, columns), columns)
        scaled = inp[c].astype(f32) * gain[:, cut].astype(f32)
        high = scaled.astype(bf16)
        rest = (scaled - high.astype(f32)).astype(bf16)
        in_acc[...] += dot_nt(hidden[c], jnp.concatenate([high, rest], axis=0))
        for r in range(0, rows, 48):
            wide = hidden[c, r : r + 48, :].astype(f32)
            square = wide * wide
            total = square[:, :LANES]
            for at in range(LANES, columns, LANES):
                total += square[:, at : at + LANES]
            sq_acc[r : r + 48, :] += total

    for piece in early:
        piece.wait()
    odd = lax.rem(lax.axis_index("store"), 2)
    at_full = pl.multiple_of(odd * half, half)
    at_half = pl.multiple_of((1 - odd) * full, half)
    low_lanes = iota((S, LANES), 1) < R
    position = iota((S, LANES), 0)

    def in_rows(at, count):
        sums = in_acc[pl.ds(at, count), :]
        square = jnp.sum(sq_acc[pl.ds(at, count), :], axis=1, keepdims=True)
        scale = lax.rsqrt(square * (1.0 / width) + norm_epsilon)
        factor = (sums + pltpu.roll(sums, R, 1)) * scale
        return [
            jnp.where(position < lengths[at // S + q], factor[q * S : (q + 1) * S], 0.0)
            for q in range(count // S)
        ]

    def side_by_side(tiles):
        both = zip(tiles[: len(tiles) // 2], tiles[len(tiles) // 2 :])
        return jnp.concatenate([jnp.where(low_lanes, x, y) for x, y in both], axis=0)

    packed[:mid, :] = side_by_side(in_rows(at_full, full)).astype(bf16)
    packed[mid : mid + low, :] = side_by_side(in_rows(at_half, half)).astype(bf16)

    whole = dot_nt(outp[...], cot[pl.ds(at_full, full), :])
    for t in range(full // LANES):
        out_t[t * R : (t + 1) * R, :] = whole[:, t * LANES : (t + 1) * LANES]
    out_t[full // LANES * R :, :half] = dot_nt(outp[...], cot[pl.ds(at_half, half), :])

    def part(t, b):
        return out_t[pl.ds(t * R + b, A, stride=B), :]

    row = mid + low
    for m in range(full // (G * S)):
        t, at = divmod(m * G * S, LANES)
        for b in range(0, B, 2):
            both = [part(t, b + c)[:, at : at + G * S] for c in range(2)]
            packed[row : row + A, :] = jnp.concatenate(both, axis=1).astype(bf16)
            row += A
    packed[row : row + A, :] = jnp.concatenate(
        [part(full // LANES, b)[:, :half] for b in range(B)], axis=1
    ).astype(bf16)


def in_hbm(x):
    return pltpu.with_memory_space_constraint(x, pltpu.HBM)


def factors(lengths, hidden, cotangent, gain, in_projection, out_projection):
    rows, width = hidden.shape
    columns = 2048
    chunks = width // columns
    return pl.pallas_call(
        factors_kernel,
        out_shape=jax.ShapeDtypeStruct((rows, 2 * R), bf16),
        in_specs=[pl.BlockSpec(memory_space=pl.ANY)] * 6,
        out_specs=pl.BlockSpec(memory_space=pltpu.VMEM),
        scratch_shapes=[
            pltpu.SMEM(lengths.shape, jnp.int32),
            pltpu.VMEM((chunks, rows, columns), bf16),
            pltpu.VMEM(cotangent.shape, bf16),
            pltpu.VMEM(gain.shape, bf16),
            pltpu.VMEM((chunks, R, columns), bf16),
            pltpu.VMEM(out_projection.shape, bf16),
            pltpu.VMEM((rows, 2 * R), f32),
            pltpu.VMEM((rows, LANES), f32),
            pltpu.VMEM((-(-rows // LANES) * R, LANES), f32),
            pltpu.SemaphoreType.DMA((4 + 2 * chunks,)),
        ],
        compiler_params=pltpu.CompilerParams(vmem_limit_bytes=24 * 2**20),
        name="factors",
    )(*[in_hbm(x) for x in (lengths, hidden, cotangent, gain, in_projection, out_projection)])


def fetch_kernel(n_layer, after, store, slab, sems):
    block = slab.shape[0] // n_layer
    rows = 16 if block % 16 == 0 else 8
    me = lax.axis_index("layer")
    copies = []
    for k in range(n_layer):
        at = pl.multiple_of(partner(me, k, n_layer) * block, rows)
        to = slab.at[pl.ds(k * block, block)]
        copies.append(pltpu.make_async_copy(store.at[pl.ds(at, block)], to, sems.at[k]))
        copies[-1].start()
    for copy in copies:
        copy.wait()


def fetch(after, store, n_layer):
    rows, features = store.shape
    return pl.pallas_call(
        functools.partial(fetch_kernel, n_layer),
        out_shape=jax.ShapeDtypeStruct((rows, features), bf16),
        in_specs=[pl.BlockSpec(memory_space=pl.ANY)] * 2,
        out_specs=pl.BlockSpec(memory_space=pltpu.VMEM),
        scratch_shapes=[pltpu.SemaphoreType.DMA((n_layer,))],
        compiler_params=pltpu.CompilerParams(vmem_limit_bytes=12 * 2**20),
        cost_estimate=pl.CostEstimate(
            flops=0, bytes_accessed=2 * rows * features, transcendentals=0
        ),
        name="fetch",
    )(after, in_hbm(store))


def spread_out(tile, owner):
    lanes = tile.shape[1]
    mine = (owner == iota((G, lanes), 0))[None]
    wide = jnp.where(mine, tile.astype(f32)[:, None, :], 0.0)
    return wide.reshape(A * G, lanes).astype(bf16)


def halves(tile):
    wide = tile.astype(f32)
    turned = jnp.concatenate([wide[:, R:], wide[:, :R]], axis=1)
    low = iota(wide.shape, 1) < R
    return [
        jnp.where(mask, x, 0.0).astype(bf16)
        for x in (wide, turned)
        for mask in (low, jnp.logical_not(low))
    ]


def diagonal(low, high):
    zero = jnp.zeros_like(low)
    left = jnp.concatenate([low, high, zero, zero], axis=0)
    right = jnp.concatenate([zero, zero, low, high], axis=0)
    return jnp.concatenate([left, right], axis=1)


def build_grads(shards, base, row0, full_groups, grads):
    mid = full_groups * G * S // 2
    low = H * S // 2
    lane = iota((G, 2 * 128), 1)
    whole_owner = lax.rem(lane, G * S) // S
    half_owner = lax.rem(lane, H * S) // S + H * (lane // 128)

    def whole(shard):
        found = []
        pairs = {}
        for m in range(full_groups):
            first = m % (full_groups // 2)
            if first not in pairs:
                pairs[first] = halves(
                    shards[base + shard, first * G * S : (first + 1) * G * S, :]
                )
            plain_low, plain_high, turned_low, turned_high = pairs[first]
            weights = (
                diagonal(plain_low, turned_high)
                if m < full_groups // 2
                else diagonal(turned_low, plain_high)
            )
            at = mid + low + m * 2 * A
            tile = jnp.concatenate(
                [shards[base + shard, at : at + A, :], shards[base + shard, at + A : at + 2 * A, :]],
                axis=1,
            )
            found.append((spread_out(tile, whole_owner), weights))
        return found

    def joined(shard):
        tiles, weights = [], []
        for s in (shard, shard + 1):
            plain_low, plain_high, turned_low, turned_high = halves(
                shards[base + s, mid : mid + low, :]
            )
            weights.append(
                diagonal(
                    jnp.concatenate([plain_low, turned_low], axis=0),
                    jnp.concatenate([turned_high, plain_high], axis=0),
                )
            )
            at = mid + low + full_groups * 2 * A
            tiles.append(shards[base + s, at : at + A, :])
        return [
            (
                spread_out(jnp.concatenate(tiles, axis=1), half_owner),
                jnp.concatenate(weights, axis=0),
            )
        ]

    groups = []
    for shard in (0, 2):
        groups += whole(shard) + joined(shard) + whole(shard + 1)
    for at in range(0, len(groups), 2):
        first, second = [jnp.dot(x, w, preferred_element_type=f32) for x, w in groups[at : at + 2]]
        for a in range(A):
            pair = [x[a * G : (a + 1) * G] for x in (first, second)]
            grads[pl.ds(row0 + at * G, 2 * G), a * 256 : (a + 1) * 256] = jnp.concatenate(
                pair, axis=0
            ).astype(bf16)


def store_order(n):
    return [1, 3, 2] if n == 4 else list(range(1, n))


def grads_kernel(n_store, full_groups, k, *refs):
    gathered = refs[:n_store]
    slab, grads, out, shards = refs[n_store:]
    me_store = lax.axis_index("store")
    for block, away in zip(gathered, [0] + store_order(n_store)):
        shards[partner(me_store, away, n_store)] = block[...]
    four = 4 * (full_groups * G + H)
    if n_store == 4:
        build_grads(shards, 0, 0, full_groups, grads)
    else:

        @pl.loop(0, n_store // 4)
        def _(at):
            build_grads(shards, at * 4, pl.multiple_of(at * four, 16), full_groups, grads)

    scores_kernel(k, grads, slab, out)


def scores_kernel(k, grads, slab, *refs):
    *terms, out = refs
    block = out.shape[1]
    total = dot_nt(slab[k * block : (k + 1) * block, :], grads[...]).T
    for term in terms:
        total += term[...].astype(f32)
    out[...] = total.astype(out.dtype)


def partner(me, k, n):
    return jnp.bitwise_xor(me, k) if n & (n - 1) == 0 else lax.rem(n + k - me, n)


def swap(x, axis, n, k):
    pairs = [(i, i ^ k if n & (n - 1) == 0 else (n + k - i) % n) for i in range(n)]
    return lax.ppermute(x, axis, pairs)


def grads_and_scores(gathered, slab, n_store, n_layer, k):
    rows, features = slab.shape
    queries = n_store * gathered[0].shape[0] // S
    vmem = pl.BlockSpec(memory_space=pltpu.VMEM)
    return pl.pallas_call(
        functools.partial(grads_kernel, n_store, queries // n_store // G, k),
        out_shape=[
            jax.ShapeDtypeStruct((queries, features), bf16),
            jax.ShapeDtypeStruct((queries, rows // n_layer), bf16),
        ],
        in_specs=[vmem] * (n_store + 1),
        out_specs=[vmem] * 2,
        scratch_shapes=[pltpu.VMEM((n_store,) + gathered[0].shape, bf16)],
        compiler_params=pltpu.CompilerParams(vmem_limit_bytes=24 * 2**20),
        name="grads",
    )(*gathered, slab)


def scores(grads, slab, n_layer, k, terms=()):
    rows, features = slab.shape
    block = rows // n_layer
    queries = grads.shape[0]
    vmem = pl.BlockSpec(memory_space=pltpu.VMEM)
    return pl.pallas_call(
        functools.partial(scores_kernel, k),
        out_shape=jax.ShapeDtypeStruct((queries, block), bf16 if k else f32),
        in_specs=[vmem] * (2 + len(terms)),
        out_specs=vmem,
        compiler_params=pltpu.CompilerParams(vmem_limit_bytes=24 * 2**20),
        cost_estimate=pl.CostEstimate(
            flops=2 * queries * block * features,
            bytes_accessed=2 * (queries + block) * features,
            transcendentals=0,
        ),
        name="scores",
    )(grads, slab, *terms)


def on_device(n_store, n_layer, hidden, cotangent, lengths, norm_gain, in_proj, out_proj, store):
    queries, positions, width = hidden.shape[1:]
    packed = factors(
        lengths,
        hidden.reshape(queries * positions, width),
        cotangent.reshape(queries * positions, cotangent.shape[3]),
        norm_gain,
        in_proj[0],
        out_proj[0],
    )
    gathered = [packed] + [swap(packed, "store", n_store, k) for k in store_order(n_store)]
    slab = fetch(packed, store[0], n_layer)
    grads, partial = grads_and_scores(gathered, slab, n_store, n_layer, n_layer - 1)
    other = swap(partial, "layer", n_layer, 1)
    near = swap(scores(grads, slab, n_layer, 1), "layer", n_layer, 1)
    crossed = [near]
    for k in reversed(range(2, n_layer, 2)):
        if k < n_layer - 2:
            other = swap(scores(grads, slab, n_layer, k + 1), "layer", n_layer, 1)
        crossed.append(swap(scores(grads, slab, n_layer, k, [other]), "layer", n_layer, k))
    total = scores(grads, slab, n_layer, 0)
    for x in crossed:
        total = total + x.astype(f32)
    return total.T


def solution(mesh):
    placed = (
        P("layer", ("grp", "store"), None, None),
        P("layer", ("grp", "store"), None, None),
        P(("grp", "store")),
        P("layer", None),
        P("layer", None, None),
        P("layer", None, None),
        P("layer", ("grp", "store"), None),
    )
    return jax.shard_map(
        functools.partial(on_device, mesh.shape["store"], mesh.shape["layer"]),
        mesh=mesh,
        in_specs=placed,
        out_specs=P(("grp", "store", "layer"), None),
        check_vma=False,
    )
```

```python
import functools

import jax
import jax.numpy as jnp
from jax import lax
from jax.experimental import pallas as pl
from jax.experimental.pallas import tpu as pltpu
from jax.sharding import PartitionSpec as P

norm_epsilon = 1e-05
f32 = jnp.float32
bf16 = jnp.bfloat16
S = 8
R = 64
B = 4
A = R // B
G = 8
H = 4
LANES = 128


def dot_nt(left, right):
    return lax.dot_general(left, right, (((1,), (1,)), ((), ())), preferred_element_type=f32)


def iota(shape, dim):
    return lax.broadcasted_iota(jnp.int32, shape, dim)


def factors_kernel(
    hbm_lengths,
    hbm_hidden,
    hbm_cot,
    hbm_gain,
    hbm_inp,
    hbm_outp,
    packed,
    lengths,
    hidden,
    cot,
    gain,
    inp,
    outp,
    in_acc,
    sq_acc,
    out_t,
    sems,
):
    chunks, rows, columns = hidden.shape
    width = chunks * columns
    queries = lengths.shape[0]
    full = queries // G * G * S
    half = rows - full
    mid, low = full // 2, half // 2

    def copy(source, target, at):
        return pltpu.make_async_copy(source, target, sems.at[at])

    def pieces(c):
        cut = pl.ds(pl.multiple_of(c * columns, columns), columns)
        return [
            copy(hbm_inp.at[:, cut], inp.at[c], 4 + c),
            copy(hbm_hidden.at[:, cut], hidden.at[c], 4 + chunks + c),
        ]

    def start(group):
        for piece in group:
            piece.start()

    copy_gain = copy(hbm_gain, gain, 0)
    early = [copy(hbm_outp, outp, 1), copy(hbm_cot, cot, 2), copy(hbm_lengths, lengths, 3)]
    copy_gain.start()
    for c in range(chunks):
        start(pieces(c))
    in_acc[...] = jnp.zeros_like(in_acc)
    sq_acc[...] = jnp.zeros_like(sq_acc)
    copy_gain.wait()

    @pl.loop(0, chunks)
    def _(c):
        for piece in pieces(c):
            piece.wait()

        @pl.when(c == 0)
        def _():
            start(early)

        cut = pl.ds(pl.multiple_of(c * columns, columns), columns)
        scaled = inp[c].astype(f32) * gain[:, cut].astype(f32)
        high = scaled.astype(bf16)
        rest = (scaled - high.astype(f32)).astype(bf16)
        in_acc[...] += dot_nt(hidden[c], jnp.concatenate([high, rest], axis=0))
        for r in range(0, rows, 48):
            wide = hidden[c, r : r + 48, :].astype(f32)
            square = wide * wide
            total = square[:, :LANES]
            for at in range(LANES, columns, LANES):
                total += square[:, at : at + LANES]
            sq_acc[r : r + 48, :] += total

    for piece in early:
        piece.wait()
    odd = lax.rem(lax.axis_index("store"), 2)
    at_full = pl.multiple_of(odd * half, half)
    at_half = pl.multiple_of((1 - odd) * full, half)
    low_lanes = iota((S, LANES), 1) < R
    position = iota((S, LANES), 0)

    def in_rows(at, count):
        sums = in_acc[pl.ds(at, count), :]
        square = jnp.sum(sq_acc[pl.ds(at, count), :], axis=1, keepdims=True)
        scale = lax.rsqrt(square * (1.0 / width) + norm_epsilon)
        factor = (sums + pltpu.roll(sums, R, 1)) * scale
        return [
            jnp.where(position < lengths[at // S + q], factor[q * S : (q + 1) * S], 0.0)
            for q in range(count // S)
        ]

    def side_by_side(tiles):
        both = zip(tiles[: len(tiles) // 2], tiles[len(tiles) // 2 :])
        return jnp.concatenate([jnp.where(low_lanes, x, y) for x, y in both], axis=0)

    packed[:mid, :] = side_by_side(in_rows(at_full, full)).astype(bf16)
    packed[mid : mid + low, :] = side_by_side(in_rows(at_half, half)).astype(bf16)

    whole = dot_nt(outp[...], cot[pl.ds(at_full, full), :])
    for t in range(full // LANES):
        out_t[t * R : (t + 1) * R, :] = whole[:, t * LANES : (t + 1) * LANES]
    out_t[full // LANES * R :, :half] = dot_nt(outp[...], cot[pl.ds(at_half, half), :])

    def part(t, b):
        return out_t[pl.ds(t * R + b, A, stride=B), :]

    row = mid + low
    for m in range(full // (G * S)):
        t, at = divmod(m * G * S, LANES)
        for b in range(0, B, 2):
            both = [part(t, b + c)[:, at : at + G * S] for c in range(2)]
            packed[row : row + A, :] = jnp.concatenate(both, axis=1).astype(bf16)
            row += A
    packed[row : row + A, :] = jnp.concatenate(
        [part(full // LANES, b)[:, :half] for b in range(B)], axis=1
    ).astype(bf16)


def in_hbm(x):
    return pltpu.with_memory_space_constraint(x, pltpu.HBM)


def factors(lengths, hidden, cotangent, gain, in_projection, out_projection):
    rows, width = hidden.shape
    columns = 2048
    chunks = width // columns
    return pl.pallas_call(
        factors_kernel,
        out_shape=jax.ShapeDtypeStruct((rows, 2 * R), bf16),
        in_specs=[pl.BlockSpec(memory_space=pl.ANY)] * 6,
        out_specs=pl.BlockSpec(memory_space=pltpu.VMEM),
        scratch_shapes=[
            pltpu.SMEM(lengths.shape, jnp.int32),
            pltpu.VMEM((chunks, rows, columns), bf16),
            pltpu.VMEM(cotangent.shape, bf16),
            pltpu.VMEM(gain.shape, bf16),
            pltpu.VMEM((chunks, R, columns), bf16),
            pltpu.VMEM(out_projection.shape, bf16),
            pltpu.VMEM((rows, 2 * R), f32),
            pltpu.VMEM((rows, LANES), f32),
            pltpu.VMEM((-(-rows // LANES) * R, LANES), f32),
            pltpu.SemaphoreType.DMA((4 + 2 * chunks,)),
        ],
        compiler_params=pltpu.CompilerParams(vmem_limit_bytes=24 * 2**20),
        name="factors",
    )(*[in_hbm(x) for x in (lengths, hidden, cotangent, gain, in_projection, out_projection)])


def fetch_kernel(n_layer, after, store, slab, sems):
    block = slab.shape[0] // n_layer
    rows = 16 if block % 16 == 0 else 8
    me = lax.axis_index("layer")
    copies = []
    for k in range(n_layer):
        at = pl.multiple_of(partner(me, k, n_layer) * block, rows)
        to = slab.at[pl.ds(k * block, block)]
        copies.append(pltpu.make_async_copy(store.at[pl.ds(at, block)], to, sems.at[k]))
        copies[-1].start()
    for copy in copies:
        copy.wait()


def fetch(after, store, n_layer):
    rows, features = store.shape
    return pl.pallas_call(
        functools.partial(fetch_kernel, n_layer),
        out_shape=jax.ShapeDtypeStruct((rows, features), bf16),
        in_specs=[pl.BlockSpec(memory_space=pl.ANY)] * 2,
        out_specs=pl.BlockSpec(memory_space=pltpu.VMEM),
        scratch_shapes=[pltpu.SemaphoreType.DMA((n_layer,))],
        compiler_params=pltpu.CompilerParams(vmem_limit_bytes=12 * 2**20),
        cost_estimate=pl.CostEstimate(
            flops=0, bytes_accessed=2 * rows * features, transcendentals=0
        ),
        name="fetch",
    )(after, in_hbm(store))


def spread_out(tile, owner):
    lanes = tile.shape[1]
    mine = (owner == iota((G, lanes), 0))[None]
    wide = jnp.where(mine, tile.astype(f32)[:, None, :], 0.0)
    return wide.reshape(A * G, lanes).astype(bf16)


def halves(tile):
    wide = tile.astype(f32)
    turned = jnp.concatenate([wide[:, R:], wide[:, :R]], axis=1)
    low = iota(wide.shape, 1) < R
    return [
        jnp.where(mask, x, 0.0).astype(bf16)
        for x in (wide, turned)
        for mask in (low, jnp.logical_not(low))
    ]


def diagonal(low, high):
    zero = jnp.zeros_like(low)
    left = jnp.concatenate([low, high, zero, zero], axis=0)
    right = jnp.concatenate([zero, zero, low, high], axis=0)
    return jnp.concatenate([left, right], axis=1)


def build_grads(shards, base, row0, full_groups, grads):
    mid = full_groups * G * S // 2
    low = H * S // 2
    lane = iota((G, 2 * 128), 1)
    whole_owner = lax.rem(lane, G * S) // S
    half_owner = lax.rem(lane, H * S) // S + H * (lane // 128)

    def whole(shard):
        found = []
        pairs = {}
        for m in range(full_groups):
            first = m % (full_groups // 2)
            if first not in pairs:
                pairs[first] = halves(
                    shards[base + shard, first * G * S : (first + 1) * G * S, :]
                )
            plain_low, plain_high, turned_low, turned_high = pairs[first]
            weights = (
                diagonal(plain_low, turned_high)
                if m < full_groups // 2
                else diagonal(turned_low, plain_high)
            )
            at = mid + low + m * 2 * A
            tile = jnp.concatenate(
                [shards[base + shard, at : at + A, :], shards[base + shard, at + A : at + 2 * A, :]],
                axis=1,
            )
            found.append((spread_out(tile, whole_owner), weights))
        return found

    def joined(shard):
        tiles, weights = [], []
        for s in (shard, shard + 1):
            plain_low, plain_high, turned_low, turned_high = halves(
                shards[base + s, mid : mid + low, :]
            )
            weights.append(
                diagonal(
                    jnp.concatenate([plain_low, turned_low], axis=0),
                    jnp.concatenate([turned_high, plain_high], axis=0),
                )
            )
            at = mid + low + full_groups * 2 * A
            tiles.append(shards[base + s, at : at + A, :])
        return [
            (
                spread_out(jnp.concatenate(tiles, axis=1), half_owner),
                jnp.concatenate(weights, axis=0),
            )
        ]

    groups = []
    for shard in (0, 2):
        groups += whole(shard) + joined(shard) + whole(shard + 1)
    for at in range(0, len(groups), 2):
        first, second = [jnp.dot(x, w, preferred_element_type=f32) for x, w in groups[at : at + 2]]
        for a in range(A):
            pair = [x[a * G : (a + 1) * G] for x in (first, second)]
            grads[pl.ds(row0 + at * G, 2 * G), a * 256 : (a + 1) * 256] = jnp.concatenate(
                pair, axis=0
            ).astype(bf16)


def store_order(n):
    return [1, 3, 2] if n == 4 else list(range(1, n))


def grads_kernel(n_store, full_groups, k, *refs):
    gathered = refs[:n_store]
    slab, grads, out, shards = refs[n_store:]
    me_store = lax.axis_index("store")
    for block, away in zip(gathered, [0] + store_order(n_store)):
        shards[partner(me_store, away, n_store)] = block[...]
    four = 4 * (full_groups * G + H)
    if n_store == 4:
        build_grads(shards, 0, 0, full_groups, grads)
    else:

        @pl.loop(0, n_store // 4)
        def _(at):
            build_grads(shards, at * 4, pl.multiple_of(at * four, 16), full_groups, grads)

    scores_kernel(k, grads, slab, out)


def scores_kernel(k, grads, slab, *refs, skip=0):
    outs = refs[skip:]
    block = outs[0].shape[1]
    total = dot_nt(slab[k * block : (k + 1) * block, :], grads[...]).T
    at = 0
    for out in outs:
        out[...] = total[at : at + out.shape[0]].astype(out.dtype)
        at += out.shape[0]


def partner(me, k, n):
    return jnp.bitwise_xor(me, k) if n & (n - 1) == 0 else lax.rem(n + k - me, n)


def swap(x, axis, n, k):
    pairs = [(i, i ^ k if n & (n - 1) == 0 else (n + k - i) % n) for i in range(n)]
    return lax.ppermute(x, axis, pairs)


def grads_and_scores(gathered, slab, n_store, n_layer, k):
    rows, features = slab.shape
    queries = n_store * gathered[0].shape[0] // S
    vmem = pl.BlockSpec(memory_space=pltpu.VMEM)
    return pl.pallas_call(
        functools.partial(grads_kernel, n_store, queries // n_store // G, k),
        out_shape=[
            jax.ShapeDtypeStruct((queries, features), bf16),
            jax.ShapeDtypeStruct((queries, rows // n_layer), bf16),
        ],
        in_specs=[vmem] * (n_store + 1),
        out_specs=[vmem] * 2,
        scratch_shapes=[pltpu.VMEM((n_store,) + gathered[0].shape, bf16)],
        compiler_params=pltpu.CompilerParams(vmem_limit_bytes=24 * 2**20),
        name="grads",
    )(*gathered, slab)


def scores(grads, slab, n_layer, k, pieces=1, after=()):
    rows, features = slab.shape
    block = rows // n_layer
    queries = grads.shape[0]
    vmem = pl.BlockSpec(memory_space=pltpu.VMEM)
    return pl.pallas_call(
        functools.partial(scores_kernel, k, skip=len(after)),
        out_shape=[jax.ShapeDtypeStruct((queries // pieces, block), bf16 if k % 2 else f32)] * pieces,
        in_specs=[vmem] * 2 + [pl.BlockSpec(memory_space=pl.ANY)] * len(after),
        out_specs=[vmem] * pieces,
        compiler_params=pltpu.CompilerParams(vmem_limit_bytes=24 * 2**20),
        cost_estimate=pl.CostEstimate(
            flops=2 * queries * block * features,
            bytes_accessed=2 * (queries + block) * features,
            transcendentals=0,
        ),
        name="scores",
    )(grads, slab, *after)


def on_device(n_store, n_layer, hidden, cotangent, lengths, norm_gain, in_proj, out_proj, store):
    queries, positions, width = hidden.shape[1:]
    packed = factors(
        lengths,
        hidden.reshape(queries * positions, width),
        cotangent.reshape(queries * positions, cotangent.shape[3]),
        norm_gain,
        in_proj[0],
        out_proj[0],
    )
    gathered = [packed] + [swap(packed, "store", n_store, k) for k in store_order(n_store)]
    slab = fetch(packed, store[0], n_layer)
    grads, partial = grads_and_scores(gathered, slab, n_store, n_layer, n_layer - 1)
    crossed = []
    for k in reversed(range(2, n_layer, 2)):
        if k < n_layer - 2:
            (partial,) = scores(grads, slab, n_layer, k + 1)
        other = swap(partial, "layer", n_layer, 1)
        (mine,) = scores(grads, slab, n_layer, k)
        joined = (mine + other.astype(f32)).astype(bf16)
        crossed.append(swap(joined, "layer", n_layer, k))
    near = [swap(x, "layer", n_layer, 1) for x in scores(grads, slab, n_layer, 1, 2, [joined])]
    (total,) = scores(grads, slab, n_layer, 0)
    total = total + jnp.concatenate(near, axis=0).astype(f32)
    for x in crossed:
        total = total + x.astype(f32)
    return total.T


def solution(mesh):
    placed = (
        P("layer", ("grp", "store"), None, None),
        P("layer", ("grp", "store"), None, None),
        P(("grp", "store")),
        P("layer", None),
        P("layer", None, None),
        P("layer", None, None),
        P("layer", ("grp", "store"), None),
    )
    return jax.shard_map(
        functools.partial(on_device, mesh.shape["store"], mesh.shape["layer"]),
        mesh=mesh,
        in_specs=placed,
        out_specs=P(("grp", "store", "layer"), None),
        check_vma=False,
    )
```

```python
import functools

import jax
import jax.numpy as jnp
from jax import lax
from jax.experimental import pallas as pl
from jax.experimental.pallas import tpu as pltpu
from jax.sharding import PartitionSpec as P

norm_epsilon = 1e-05
f32 = jnp.float32
bf16 = jnp.bfloat16
S = 8
R = 64
B = 4
A = R // B
G = 8
H = 4
LANES = 128


def dot_nt(left, right):
    return lax.dot_general(left, right, (((1,), (1,)), ((), ())), preferred_element_type=f32)


def iota(shape, dim):
    return lax.broadcasted_iota(jnp.int32, shape, dim)


def factors_kernel(
    hbm_lengths,
    hbm_hidden,
    hbm_cot,
    hbm_gain,
    hbm_inp,
    hbm_outp,
    packed,
    lengths,
    hidden,
    cot,
    gain,
    inp,
    outp,
    in_acc,
    sq_acc,
    out_t,
    sems,
):
    chunks, rows, columns = hidden.shape
    width = chunks * columns
    queries = lengths.shape[0]
    full = queries // G * G * S
    half = rows - full
    mid, low = full // 2, half // 2

    def copy(source, target, at):
        return pltpu.make_async_copy(source, target, sems.at[at])

    def pieces(c):
        cut = pl.ds(pl.multiple_of(c * columns, columns), columns)
        return [
            copy(hbm_inp.at[:, cut], inp.at[c], 4 + c),
            copy(hbm_hidden.at[:, cut], hidden.at[c], 4 + chunks + c),
        ]

    def start(group):
        for piece in group:
            piece.start()

    copy_gain = copy(hbm_gain, gain, 0)
    early = [copy(hbm_outp, outp, 1), copy(hbm_cot, cot, 2), copy(hbm_lengths, lengths, 3)]
    copy_gain.start()
    start(pieces(0))
    start(pieces(1))
    in_acc[...] = jnp.zeros_like(in_acc)
    sq_acc[...] = jnp.zeros_like(sq_acc)
    copy_gain.wait()
    start(pieces(2))

    @pl.loop(0, chunks)
    def _(c):
        for piece in pieces(c):
            piece.wait()

        @pl.when(c + 3 < chunks)
        def _():
            start(pieces(c + 3))

        @pl.when(c == 1)
        def _():
            start(early)

        cut = pl.ds(pl.multiple_of(c * columns, columns), columns)
        scaled = inp[c].astype(f32) * gain[:, cut].astype(f32)
        high = scaled.astype(bf16)
        rest = (scaled - high.astype(f32)).astype(bf16)
        in_acc[...] += dot_nt(hidden[c], jnp.concatenate([high, rest], axis=0))
        for r in range(0, rows, 48):
            wide = hidden[c, r : r + 48, :].astype(f32)
            square = wide * wide
            total = square[:, :LANES]
            for at in range(LANES, columns, LANES):
                total += square[:, at : at + LANES]
            sq_acc[r : r + 48, :] += total

    for piece in early:
        piece.wait()
    odd = lax.rem(lax.axis_index("store"), 2)
    at_full = pl.multiple_of(odd * half, half)
    at_half = pl.multiple_of((1 - odd) * full, half)
    low_lanes = iota((S, LANES), 1) < R
    position = iota((S, LANES), 0)

    def in_rows(at, count):
        sums = in_acc[pl.ds(at, count), :]
        square = jnp.sum(sq_acc[pl.ds(at, count), :], axis=1, keepdims=True)
        scale = lax.rsqrt(square * (1.0 / width) + norm_epsilon)
        factor = (sums + pltpu.roll(sums, R, 1)) * scale
        return [
            jnp.where(position < lengths[at // S + q], factor[q * S : (q + 1) * S], 0.0)
            for q in range(count // S)
        ]

    def side_by_side(tiles):
        both = zip(tiles[: len(tiles) // 2], tiles[len(tiles) // 2 :])
        return jnp.concatenate([jnp.where(low_lanes, x, y) for x, y in both], axis=0)

    packed[:mid, :] = side_by_side(in_rows(at_full, full)).astype(bf16)
    packed[mid : mid + low, :] = side_by_side(in_rows(at_half, half)).astype(bf16)

    whole = dot_nt(outp[...], cot[pl.ds(at_full, full), :])
    for t in range(full // LANES):
        out_t[t * R : (t + 1) * R, :] = whole[:, t * LANES : (t + 1) * LANES]
    out_t[full // LANES * R :, :half] = dot_nt(outp[...], cot[pl.ds(at_half, half), :])

    def part(t, b):
        return out_t[pl.ds(t * R + b, A, stride=B), :]

    row = mid + low
    for m in range(full // (G * S)):
        t, at = divmod(m * G * S, LANES)
        for b in range(0, B, 2):
            both = [part(t, b + c)[:, at : at + G * S] for c in range(2)]
            packed[row : row + A, :] = jnp.concatenate(both, axis=1).astype(bf16)
            row += A
    packed[row : row + A, :] = jnp.concatenate(
        [part(full // LANES, b)[:, :half] for b in range(B)], axis=1
    ).astype(bf16)


def in_hbm(x):
    return pltpu.with_memory_space_constraint(x, pltpu.HBM)


def factors(lengths, hidden, cotangent, gain, in_projection, out_projection):
    rows, width = hidden.shape
    columns = 2048
    chunks = width // columns
    return pl.pallas_call(
        factors_kernel,
        out_shape=jax.ShapeDtypeStruct((rows, 2 * R), bf16),
        in_specs=[pl.BlockSpec(memory_space=pl.ANY)] * 6,
        out_specs=pl.BlockSpec(memory_space=pltpu.VMEM),
        scratch_shapes=[
            pltpu.SMEM(lengths.shape, jnp.int32),
            pltpu.VMEM((chunks, rows, columns), bf16),
            pltpu.VMEM(cotangent.shape, bf16),
            pltpu.VMEM(gain.shape, bf16),
            pltpu.VMEM((chunks, R, columns), bf16),
            pltpu.VMEM(out_projection.shape, bf16),
            pltpu.VMEM((rows, 2 * R), f32),
            pltpu.VMEM((rows, LANES), f32),
            pltpu.VMEM((-(-rows // LANES) * R, LANES), f32),
            pltpu.SemaphoreType.DMA((4 + 2 * chunks,)),
        ],
        compiler_params=pltpu.CompilerParams(vmem_limit_bytes=24 * 2**20),
        name="factors",
    )(*[in_hbm(x) for x in (lengths, hidden, cotangent, gain, in_projection, out_projection)])


def block_copy(store, k, slab, sem, n_layer):
    block = slab.shape[0]
    rows = 16 if block % 16 == 0 else 8
    at = pl.multiple_of(partner(lax.axis_index("layer"), k, n_layer) * block, rows)
    return pltpu.make_async_copy(store.at[pl.ds(at, block)], slab, sem)


def fetch_kernel(n_layer, k, after, store, slab, sem):
    copy = block_copy(store, k, slab, sem, n_layer)
    copy.start()
    copy.wait()


def fetch(after, store, n_layer, k):
    rows, features = store.shape
    return pl.pallas_call(
        functools.partial(fetch_kernel, n_layer, k),
        out_shape=jax.ShapeDtypeStruct((rows // n_layer, features), bf16),
        in_specs=[pl.BlockSpec(memory_space=pl.ANY)] * 2,
        out_specs=pl.BlockSpec(memory_space=pltpu.VMEM),
        scratch_shapes=[pltpu.SemaphoreType.DMA],
        compiler_params=pltpu.CompilerParams(vmem_limit_bytes=12 * 2**20),
        cost_estimate=pl.CostEstimate(
            flops=0, bytes_accessed=2 * rows * features // n_layer, transcendentals=0
        ),
        name="fetch",
    )(after, in_hbm(store))


def spread_out(tile, owner):
    lanes = tile.shape[1]
    mine = (owner == iota((G, lanes), 0))[None]
    wide = jnp.where(mine, tile.astype(f32)[:, None, :], 0.0)
    return wide.reshape(A * G, lanes).astype(bf16)


def halves(tile):
    wide = tile.astype(f32)
    turned = jnp.concatenate([wide[:, R:], wide[:, :R]], axis=1)
    low = iota(wide.shape, 1) < R
    return [
        jnp.where(mask, x, 0.0).astype(bf16)
        for x in (wide, turned)
        for mask in (low, jnp.logical_not(low))
    ]


def diagonal(low, high):
    zero = jnp.zeros_like(low)
    left = jnp.concatenate([low, high, zero, zero], axis=0)
    right = jnp.concatenate([zero, zero, low, high], axis=0)
    return jnp.concatenate([left, right], axis=1)


def build_grads(shards, base, row0, full_groups, grads):
    mid = full_groups * G * S // 2
    low = H * S // 2
    lane = iota((G, 2 * 128), 1)
    whole_owner = lax.rem(lane, G * S) // S
    half_owner = lax.rem(lane, H * S) // S + H * (lane // 128)

    def whole(shard):
        found = []
        pairs = {}
        for m in range(full_groups):
            first = m % (full_groups // 2)
            if first not in pairs:
                pairs[first] = halves(
                    shards[base + shard, first * G * S : (first + 1) * G * S, :]
                )
            plain_low, plain_high, turned_low, turned_high = pairs[first]
            weights = (
                diagonal(plain_low, turned_high)
                if m < full_groups // 2
                else diagonal(turned_low, plain_high)
            )
            at = mid + low + m * 2 * A
            tile = jnp.concatenate(
                [shards[base + shard, at : at + A, :], shards[base + shard, at + A : at + 2 * A, :]],
                axis=1,
            )
            found.append((spread_out(tile, whole_owner), weights))
        return found

    def joined(shard):
        tiles, weights = [], []
        for s in (shard, shard + 1):
            plain_low, plain_high, turned_low, turned_high = halves(
                shards[base + s, mid : mid + low, :]
            )
            weights.append(
                diagonal(
                    jnp.concatenate([plain_low, turned_low], axis=0),
                    jnp.concatenate([turned_high, plain_high], axis=0),
                )
            )
            at = mid + low + full_groups * 2 * A
            tiles.append(shards[base + s, at : at + A, :])
        return [
            (
                spread_out(jnp.concatenate(tiles, axis=1), half_owner),
                jnp.concatenate(weights, axis=0),
            )
        ]

    groups = []
    for shard in (0, 2):
        groups += whole(shard) + joined(shard) + whole(shard + 1)
    for at in range(0, len(groups), 2):
        first, second = [jnp.dot(x, w, preferred_element_type=f32) for x, w in groups[at : at + 2]]
        for a in range(A):
            pair = [x[a * G : (a + 1) * G] for x in (first, second)]
            grads[pl.ds(row0 + at * G, 2 * G), a * 256 : (a + 1) * 256] = jnp.concatenate(
                pair, axis=0
            ).astype(bf16)


def grads_kernel(n_store, n_layer, full_groups, k, *refs):
    gathered = refs[:n_store]
    slab, store, grads, out, following, shards, sem = refs[n_store:]
    copy = block_copy(store, k - 1, following, sem, n_layer)
    copy.start()
    me_store = lax.axis_index("store")
    for away in range(n_store):
        shards[lax.rem(me_store + away, n_store)] = gathered[away][...]
    four = 4 * (full_groups * G + H)
    if n_store == 4:
        build_grads(shards, 0, 0, full_groups, grads)
    else:

        @pl.loop(0, n_store // 4)
        def _(at):
            build_grads(shards, at * 4, pl.multiple_of(at * four, 16), full_groups, grads)

    score(grads, slab, [out])
    copy.wait()


def score(grads, slab, outs):
    total = dot_nt(slab[...], grads[...]).T
    at = 0
    for out in outs:
        out[...] = total[at : at + out.shape[0]].astype(out.dtype)
        at += out.shape[0]


def scores_kernel(n_layer, k, pieces, grads, slab, store, *refs):
    if k == 0:
        score(grads, slab, refs[-pieces:])
        return
    following, sem = refs[-2:]
    copy = block_copy(store, k - 1, following, sem, n_layer)
    copy.start()
    score(grads, slab, refs[-2 - pieces : -2])
    copy.wait()


def partner(me, k, n):
    return jnp.bitwise_xor(me, k) if n & (n - 1) == 0 else lax.rem(n + k - me, n)


def swap(x, axis, n, k):
    pairs = [(i, i ^ k if n & (n - 1) == 0 else (n + k - i) % n) for i in range(n)]
    return lax.ppermute(x, axis, pairs)


def grads_and_scores(packed, slab, store, n_store, n_layer, k):
    block, features = slab.shape
    queries = packed.shape[0] // S
    gathered = [packed]
    for away in range(1, n_store):
        pairs = [((to + away) % n_store, to) for to in range(n_store)]
        gathered.append(lax.ppermute(packed, "store", pairs))
    vmem = pl.BlockSpec(memory_space=pltpu.VMEM)
    return pl.pallas_call(
        functools.partial(grads_kernel, n_store, n_layer, queries // G, k),
        out_shape=[
            jax.ShapeDtypeStruct((n_store * queries, features), bf16),
            jax.ShapeDtypeStruct((n_store * queries, block), bf16),
            jax.ShapeDtypeStruct(slab.shape, bf16),
        ],
        in_specs=[vmem] * (n_store + 1) + [pl.BlockSpec(memory_space=pl.ANY)],
        out_specs=[vmem] * 3,
        scratch_shapes=[pltpu.VMEM((n_store,) + packed.shape, bf16), pltpu.SemaphoreType.DMA],
        compiler_params=pltpu.CompilerParams(vmem_limit_bytes=24 * 2**20),
        name="grads",
    )(*gathered, slab, in_hbm(store))


def scores(grads, slab, store, n_layer, k, pieces=1, after=()):
    block, features = slab.shape
    queries = grads.shape[0]
    vmem = pl.BlockSpec(memory_space=pltpu.VMEM)
    piece = jax.ShapeDtypeStruct((queries // pieces, block), bf16 if k % 2 else f32)
    following = [jax.ShapeDtypeStruct(slab.shape, bf16)] if k else []
    return pl.pallas_call(
        functools.partial(scores_kernel, n_layer, k, pieces),
        out_shape=[piece] * pieces + following,
        in_specs=[vmem] * 2 + [pl.BlockSpec(memory_space=pl.ANY)] * (1 + len(after)),
        out_specs=[vmem] * (pieces + len(following)),
        scratch_shapes=[pltpu.SemaphoreType.DMA] * len(following),
        compiler_params=pltpu.CompilerParams(vmem_limit_bytes=24 * 2**20),
        cost_estimate=pl.CostEstimate(
            flops=2 * queries * block * features,
            bytes_accessed=2 * (queries + 2 * block) * features,
            transcendentals=0,
        ),
        name="scores",
    )(grads, slab, in_hbm(store), *after)


def on_device(n_store, n_layer, hidden, cotangent, lengths, norm_gain, in_proj, out_proj, store):
    queries, positions, width = hidden.shape[1:]
    packed = factors(
        lengths,
        hidden.reshape(queries * positions, width),
        cotangent.reshape(queries * positions, cotangent.shape[3]),
        norm_gain,
        in_proj[0],
        out_proj[0],
    )
    rows = store[0]
    slab = fetch(packed, rows, n_layer, n_layer - 1)
    grads, partial, slab = grads_and_scores(packed, slab, rows, n_store, n_layer, n_layer - 1)
    crossed = []
    for k in reversed(range(2, n_layer, 2)):
        if k < n_layer - 2:
            partial, slab = scores(grads, slab, rows, n_layer, k + 1)
        other = swap(partial, "layer", n_layer, 1)
        mine, slab = scores(grads, slab, rows, n_layer, k)
        joined = (mine + other.astype(f32)).astype(bf16)
        crossed.append(swap(joined, "layer", n_layer, k))
    *near, slab = scores(grads, slab, rows, n_layer, 1, 2, [joined])
    (total,) = scores(grads, slab, rows, n_layer, 0)
    near = [swap(x, "layer", n_layer, 1) for x in near]
    total = total + jnp.concatenate(near, axis=0).astype(f32)
    for x in crossed:
        total = total + x.astype(f32)
    return total.T


def solution(mesh):
    placed = (
        P("layer", ("grp", "store"), None, None),
        P("layer", ("grp", "store"), None, None),
        P(("grp", "store")),
        P("layer", None),
        P("layer", None, None),
        P("layer", None, None),
        P("layer", ("grp", "store"), None),
    )
    return jax.shard_map(
        functools.partial(on_device, mesh.shape["store"], mesh.shape["layer"]),
        mesh=mesh,
        in_specs=placed,
        out_specs=P(("grp", "store", "layer"), None),
        check_vma=False,
    )
```

```python
import functools

import jax
import jax.numpy as jnp
from jax import lax
from jax.experimental import pallas as pl
from jax.experimental.pallas import tpu as pltpu
from jax.sharding import PartitionSpec as P

norm_epsilon = 1e-05
f32 = jnp.float32
bf16 = jnp.bfloat16
S = 8
R = 64
B = 4
A = R // B
G = 8
H = 4
LANES = 128


def dot_nt(left, right):
    return lax.dot_general(left, right, (((1,), (1,)), ((), ())), preferred_element_type=f32)


def iota(shape, dim):
    return lax.broadcasted_iota(jnp.int32, shape, dim)


def factors_kernel(
    hbm_lengths,
    hbm_hidden,
    hbm_cot,
    hbm_gain,
    hbm_inp,
    hbm_outp,
    packed,
    lengths,
    hidden,
    cot,
    gain,
    inp,
    outp,
    weights,
    in_acc,
    out_t,
    sems,
):
    blocks, step, width = hidden.shape
    rows = blocks * step
    queries = lengths.shape[0]
    full = queries // G * G * S
    half = rows - full
    mid, low = full // 2, half // 2

    def copy(source, target, at):
        return pltpu.make_async_copy(source, target, sems.at[at])

    def block_rows(r):
        at = pl.ds(pl.multiple_of(r * step, step), step)
        return copy(hbm_hidden.at[at, :], hidden.at[r], 5 + r)

    first = [copy(hbm_outp, outp, 0), copy(hbm_cot, cot, 1)]
    then = [copy(hbm_gain, gain, 2), copy(hbm_inp, inp, 3), copy(hbm_lengths, lengths, 4)]
    for piece in first + then + [block_rows(r) for r in range(blocks)]:
        piece.start()
    odd = lax.rem(lax.axis_index("store"), 2)
    at_full = pl.multiple_of(odd * half, half)
    at_half = pl.multiple_of((1 - odd) * full, half)
    for piece in first:
        piece.wait()

    whole = dot_nt(outp[...], cot[pl.ds(at_full, full), :])
    for t in range(full // LANES):
        out_t[t * R : (t + 1) * R, :] = whole[:, t * LANES : (t + 1) * LANES]
    out_t[full // LANES * R :, :half] = dot_nt(outp[...], cot[pl.ds(at_half, half), :])

    def part(t, b):
        return out_t[pl.ds(t * R + b, A, stride=B), :]

    row = mid + low
    for m in range(full // (G * S)):
        t, at = divmod(m * G * S, LANES)
        for b in range(0, B, 2):
            both = [part(t, b + c)[:, at : at + G * S] for c in range(2)]
            packed[row : row + A, :] = jnp.concatenate(both, axis=1).astype(bf16)
            row += A
    packed[row : row + A, :] = jnp.concatenate(
        [part(full // LANES, b)[:, :half] for b in range(B)], axis=1
    ).astype(bf16)

    for piece in then:
        piece.wait()
    weights[...] = inp[...] * gain[...]

    @pl.loop(0, blocks)
    def _(r):
        block_rows(r).wait()
        product = dot_nt(hidden[r], weights[...])
        total = jnp.zeros((step, LANES), f32)
        for at in range(0, width, LANES):
            wide = hidden[r, :, at : at + LANES].astype(f32)
            total += wide * wide
        mean_square = jnp.sum(total, axis=1, keepdims=True) * (1.0 / width)
        factor = product * lax.rsqrt(mean_square + norm_epsilon)
        at = pl.ds(pl.multiple_of(r * step, step), step)
        in_acc[at, :] = jnp.concatenate([factor, factor], axis=1)

    low_lanes = iota((S, LANES), 1) < R
    position = iota((S, LANES), 0)

    def in_rows(at, count):
        factor = in_acc[pl.ds(at, count), :]
        return [
            jnp.where(position < lengths[at // S + q], factor[q * S : (q + 1) * S], 0.0)
            for q in range(count // S)
        ]

    def side_by_side(tiles):
        both = zip(tiles[: len(tiles) // 2], tiles[len(tiles) // 2 :])
        return jnp.concatenate([jnp.where(low_lanes, x, y) for x, y in both], axis=0)

    packed[:mid, :] = side_by_side(in_rows(at_full, full)).astype(bf16)
    packed[mid : mid + low, :] = side_by_side(in_rows(at_half, half)).astype(bf16)


def in_hbm(x):
    return pltpu.with_memory_space_constraint(x, pltpu.HBM)


def factors(lengths, hidden, cotangent, gain, in_projection, out_projection):
    rows, width = hidden.shape
    blocks = 3
    return pl.pallas_call(
        factors_kernel,
        out_shape=jax.ShapeDtypeStruct((rows, 2 * R), bf16),
        in_specs=[pl.BlockSpec(memory_space=pl.ANY)] * 6,
        out_specs=pl.BlockSpec(memory_space=pltpu.VMEM),
        scratch_shapes=[
            pltpu.SMEM(lengths.shape, jnp.int32),
            pltpu.VMEM((blocks, rows // blocks, width), bf16),
            pltpu.VMEM(cotangent.shape, bf16),
            pltpu.VMEM(gain.shape, bf16),
            pltpu.VMEM(in_projection.shape, bf16),
            pltpu.VMEM(out_projection.shape, bf16),
            pltpu.VMEM(in_projection.shape, bf16),
            pltpu.VMEM((rows, 2 * R), f32),
            pltpu.VMEM((-(-rows // LANES) * R, LANES), f32),
            pltpu.SemaphoreType.DMA((5 + blocks,)),
        ],
        compiler_params=pltpu.CompilerParams(vmem_limit_bytes=24 * 2**20),
        name="factors",
    )(*[in_hbm(x) for x in (lengths, hidden, cotangent, gain, in_projection, out_projection)])


def fetch_kernel(n_layer, after, store, slab, sems):
    block = slab.shape[0] // n_layer
    rows = 16 if block % 16 == 0 else 8
    me = lax.axis_index("layer")
    copies = []
    for k in range(n_layer):
        at = pl.multiple_of(partner(me, k, n_layer) * block, rows)
        to = slab.at[pl.ds(k * block, block)]
        copies.append(pltpu.make_async_copy(store.at[pl.ds(at, block)], to, sems.at[k]))
        copies[-1].start()
    for copy in copies:
        copy.wait()


def fetch(after, store, n_layer):
    rows, features = store.shape
    return pl.pallas_call(
        functools.partial(fetch_kernel, n_layer),
        out_shape=jax.ShapeDtypeStruct((rows, features), bf16),
        in_specs=[pl.BlockSpec(memory_space=pl.ANY)] * 2,
        out_specs=pl.BlockSpec(memory_space=pltpu.VMEM),
        scratch_shapes=[pltpu.SemaphoreType.DMA((n_layer,))],
        compiler_params=pltpu.CompilerParams(vmem_limit_bytes=12 * 2**20),
        cost_estimate=pl.CostEstimate(
            flops=0, bytes_accessed=2 * rows * features, transcendentals=0
        ),
        name="fetch",
    )(after, in_hbm(store))


def spread_out(tile, owner):
    lanes = tile.shape[1]
    mine = (owner == iota((G, lanes), 0))[None]
    wide = jnp.where(mine, tile.astype(f32)[:, None, :], 0.0)
    return wide.reshape(A * G, lanes).astype(bf16)


def halves(tile):
    wide = tile.astype(f32)
    turned = jnp.concatenate([wide[:, R:], wide[:, :R]], axis=1)
    low = iota(wide.shape, 1) < R
    return [
        jnp.where(mask, x, 0.0).astype(bf16)
        for x in (wide, turned)
        for mask in (low, jnp.logical_not(low))
    ]


def diagonal(low, high):
    zero = jnp.zeros_like(low)
    left = jnp.concatenate([low, high, zero, zero], axis=0)
    right = jnp.concatenate([zero, zero, low, high], axis=0)
    return jnp.concatenate([left, right], axis=1)


def build_grads(shards, base, row0, full_groups, grads):
    mid = full_groups * G * S // 2
    low = H * S // 2
    lane = iota((G, 2 * 128), 1)
    whole_owner = lax.rem(lane, G * S) // S
    half_owner = lax.rem(lane, H * S) // S + H * (lane // 128)

    def whole(shard):
        found = []
        pairs = {}
        for m in range(full_groups):
            first = m % (full_groups // 2)
            if first not in pairs:
                pairs[first] = halves(
                    shards[base + shard, first * G * S : (first + 1) * G * S, :]
                )
            plain_low, plain_high, turned_low, turned_high = pairs[first]
            weights = (
                diagonal(plain_low, turned_high)
                if m < full_groups // 2
                else diagonal(turned_low, plain_high)
            )
            at = mid + low + m * 2 * A
            tile = jnp.concatenate(
                [shards[base + shard, at : at + A, :], shards[base + shard, at + A : at + 2 * A, :]],
                axis=1,
            )
            found.append((spread_out(tile, whole_owner), weights))
        return found

    def joined(shard):
        tiles, weights = [], []
        for s in (shard, shard + 1):
            plain_low, plain_high, turned_low, turned_high = halves(
                shards[base + s, mid : mid + low, :]
            )
            weights.append(
                diagonal(
                    jnp.concatenate([plain_low, turned_low], axis=0),
                    jnp.concatenate([turned_high, plain_high], axis=0),
                )
            )
            at = mid + low + full_groups * 2 * A
            tiles.append(shards[base + s, at : at + A, :])
        return [
            (
                spread_out(jnp.concatenate(tiles, axis=1), half_owner),
                jnp.concatenate(weights, axis=0),
            )
        ]

    groups = []
    for shard in (0, 2):
        groups += whole(shard) + joined(shard) + whole(shard + 1)
    for at in range(0, len(groups), 2):
        first, second = [jnp.dot(x, w, preferred_element_type=f32) for x, w in groups[at : at + 2]]
        for a in range(A):
            pair = [x[a * G : (a + 1) * G] for x in (first, second)]
            grads[pl.ds(row0 + at * G, 2 * G), a * 256 : (a + 1) * 256] = jnp.concatenate(
                pair, axis=0
            ).astype(bf16)


def store_order(n):
    return [1, 3, 2] if n == 4 else list(range(1, n))


def grads_kernel(n_store, full_groups, k, *refs):
    gathered = refs[:n_store]
    slab, grads, out, shards = refs[n_store:]
    me_store = lax.axis_index("store")
    for block, away in zip(gathered, [0] + store_order(n_store)):
        shards[partner(me_store, away, n_store)] = block[...]
    four = 4 * (full_groups * G + H)
    if n_store == 4:
        build_grads(shards, 0, 0, full_groups, grads)
    else:

        @pl.loop(0, n_store // 4)
        def _(at):
            build_grads(shards, at * 4, pl.multiple_of(at * four, 16), full_groups, grads)

    scores_kernel(k, grads, slab, out)


def scores_kernel(k, grads, slab, *refs, skip=0):
    outs = refs[skip:]
    block = outs[0].shape[1]
    total = dot_nt(slab[k * block : (k + 1) * block, :], grads[...]).T
    at = 0
    for out in outs:
        out[...] = total[at : at + out.shape[0]].astype(out.dtype)
        at += out.shape[0]


def partner(me, k, n):
    return jnp.bitwise_xor(me, k) if n & (n - 1) == 0 else lax.rem(n + k - me, n)


def swap(x, axis, n, k):
    pairs = [(i, i ^ k if n & (n - 1) == 0 else (n + k - i) % n) for i in range(n)]
    return lax.ppermute(x, axis, pairs)


def grads_and_scores(gathered, slab, n_store, n_layer, k):
    rows, features = slab.shape
    queries = n_store * gathered[0].shape[0] // S
    vmem = pl.BlockSpec(memory_space=pltpu.VMEM)
    return pl.pallas_call(
        functools.partial(grads_kernel, n_store, queries // n_store // G, k),
        out_shape=[
            jax.ShapeDtypeStruct((queries, features), bf16),
            jax.ShapeDtypeStruct((queries, rows // n_layer), bf16),
        ],
        in_specs=[vmem] * (n_store + 1),
        out_specs=[vmem] * 2,
        scratch_shapes=[pltpu.VMEM((n_store,) + gathered[0].shape, bf16)],
        compiler_params=pltpu.CompilerParams(vmem_limit_bytes=24 * 2**20),
        name="grads",
    )(*gathered, slab)


def scores(grads, slab, n_layer, k, pieces=1, after=()):
    rows, features = slab.shape
    block = rows // n_layer
    queries = grads.shape[0]
    vmem = pl.BlockSpec(memory_space=pltpu.VMEM)
    return pl.pallas_call(
        functools.partial(scores_kernel, k, skip=len(after)),
        out_shape=[jax.ShapeDtypeStruct((queries // pieces, block), bf16 if k % 2 else f32)] * pieces,
        in_specs=[vmem] * 2 + [pl.BlockSpec(memory_space=pl.ANY)] * len(after),
        out_specs=[vmem] * pieces,
        compiler_params=pltpu.CompilerParams(vmem_limit_bytes=24 * 2**20),
        cost_estimate=pl.CostEstimate(
            flops=2 * queries * block * features,
            bytes_accessed=2 * (queries + block) * features,
            transcendentals=0,
        ),
        name="scores",
    )(grads, slab, *after)


def on_device(n_store, n_layer, hidden, cotangent, lengths, norm_gain, in_proj, out_proj, store):
    queries, positions, width = hidden.shape[1:]
    packed = factors(
        lengths,
        hidden.reshape(queries * positions, width),
        cotangent.reshape(queries * positions, cotangent.shape[3]),
        norm_gain,
        in_proj[0],
        out_proj[0],
    )
    gathered = [packed] + [swap(packed, "store", n_store, k) for k in store_order(n_store)]
    slab = fetch(packed, store[0], n_layer)
    grads, partial = grads_and_scores(gathered, slab, n_store, n_layer, n_layer - 1)
    crossed = []
    for k in reversed(range(2, n_layer, 2)):
        if k < n_layer - 2:
            (partial,) = scores(grads, slab, n_layer, k + 1)
        other = swap(partial, "layer", n_layer, 1)
        (mine,) = scores(grads, slab, n_layer, k)
        joined = (mine + other.astype(f32)).astype(bf16)
        crossed.append(swap(joined, "layer", n_layer, k))
    near = [swap(x, "layer", n_layer, 1) for x in scores(grads, slab, n_layer, 1, 2, [joined])]
    (total,) = scores(grads, slab, n_layer, 0)
    total = total + jnp.concatenate(near, axis=0).astype(f32)
    for x in crossed:
        total = total + x.astype(f32)
    return total.T


def solution(mesh):
    placed = (
        P("layer", ("grp", "store"), None, None),
        P("layer", ("grp", "store"), None, None),
        P(("grp", "store")),
        P("layer", None),
        P("layer", None, None),
        P("layer", None, None),
        P("layer", ("grp", "store"), None),
    )
    return jax.shard_map(
        functools.partial(on_device, mesh.shape["store"], mesh.shape["layer"]),
        mesh=mesh,
        in_specs=placed,
        out_specs=P(("grp", "store", "layer"), None),
        check_vma=False,
    )
```

```python
import functools

import jax
import jax.numpy as jnp
from jax import lax
from jax.experimental import pallas as pl
from jax.experimental.pallas import tpu as pltpu
from jax.sharding import PartitionSpec as P

norm_epsilon = 1e-05
f32 = jnp.float32
bf16 = jnp.bfloat16
S = 8
R = 64
B = 4
A = R // B
G = 8
H = 4
LANES = 128


def dot_nt(left, right):
    return lax.dot_general(left, right, (((1,), (1,)), ((), ())), preferred_element_type=f32)


def iota(shape, dim):
    return lax.broadcasted_iota(jnp.int32, shape, dim)


def factors_kernel(
    hbm_lengths,
    hbm_hidden,
    hbm_cot,
    hbm_gain,
    hbm_inp,
    hbm_outp,
    packed,
    lengths,
    hidden,
    cot,
    gain,
    inp,
    outp,
    weights,
    in_acc,
    out_t,
    sems,
):
    blocks, step, width = hidden.shape
    rows = blocks * step
    queries = lengths.shape[0]
    full = queries // G * G * S
    half = rows - full
    mid, low = full // 2, half // 2

    def copy(source, target, at):
        return pltpu.make_async_copy(source, target, sems.at[at])

    def block_rows(r):
        at = pl.ds(pl.multiple_of(r * step, step), step)
        return copy(hbm_hidden.at[at, :], hidden.at[r], 5 + r)

    first = [copy(hbm_outp, outp, 0), copy(hbm_cot, cot, 1)]
    then = [copy(hbm_gain, gain, 2), copy(hbm_inp, inp, 3), copy(hbm_lengths, lengths, 4)]
    for piece in first + then + [block_rows(0)]:
        piece.start()
    odd = lax.rem(lax.axis_index("store"), 2)
    at_full = pl.multiple_of(odd * half, half)
    at_half = pl.multiple_of((1 - odd) * full, half)
    for piece in first:
        piece.wait()

    @pl.when(odd >= 0)
    def _():
        for r in range(1, blocks):
            block_rows(r).start()

    whole = dot_nt(outp[...], cot[pl.ds(at_full, full), :])
    for t in range(full // LANES):
        out_t[t * R : (t + 1) * R, :] = whole[:, t * LANES : (t + 1) * LANES]
    out_t[full // LANES * R :, :half] = dot_nt(outp[...], cot[pl.ds(at_half, half), :])

    def part(t, b):
        return out_t[pl.ds(t * R + b, A, stride=B), :]

    row = mid + low
    for m in range(full // (G * S)):
        t, at = divmod(m * G * S, LANES)
        for b in range(0, B, 2):
            both = [part(t, b + c)[:, at : at + G * S] for c in range(2)]
            packed[row : row + A, :] = jnp.concatenate(both, axis=1).astype(bf16)
            row += A
    packed[row : row + A, :] = jnp.concatenate(
        [part(full // LANES, b)[:, :half] for b in range(B)], axis=1
    ).astype(bf16)

    for piece in then:
        piece.wait()
    weights[...] = inp[...] * gain[...]

    @pl.loop(0, blocks)
    def _(r):
        block_rows(r).wait()
        product = dot_nt(hidden[r], weights[...])
        total = jnp.zeros((step, LANES), f32)
        for at in range(0, width, LANES):
            wide = hidden[r, :, at : at + LANES].astype(f32)
            total += wide * wide
        mean_square = jnp.sum(total, axis=1, keepdims=True) * (1.0 / width)
        factor = product * lax.rsqrt(mean_square + norm_epsilon)
        at = pl.ds(pl.multiple_of(r * step, step), step)
        in_acc[at, :] = jnp.concatenate([factor, factor], axis=1)

    low_lanes = iota((S, LANES), 1) < R
    position = iota((S, LANES), 0)

    def in_rows(at, count):
        factor = in_acc[pl.ds(at, count), :]
        return [
            jnp.where(position < lengths[at // S + q], factor[q * S : (q + 1) * S], 0.0)
            for q in range(count // S)
        ]

    def side_by_side(tiles):
        both = zip(tiles[: len(tiles) // 2], tiles[len(tiles) // 2 :])
        return jnp.concatenate([jnp.where(low_lanes, x, y) for x, y in both], axis=0)

    packed[:mid, :] = side_by_side(in_rows(at_full, full)).astype(bf16)
    packed[mid : mid + low, :] = side_by_side(in_rows(at_half, half)).astype(bf16)


def in_hbm(x):
    return pltpu.with_memory_space_constraint(x, pltpu.HBM)


def factors(lengths, hidden, cotangent, gain, in_projection, out_projection):
    rows, width = hidden.shape
    blocks = 3
    return pl.pallas_call(
        factors_kernel,
        out_shape=jax.ShapeDtypeStruct((rows, 2 * R), bf16),
        in_specs=[pl.BlockSpec(memory_space=pl.ANY)] * 6,
        out_specs=pl.BlockSpec(memory_space=pltpu.VMEM),
        scratch_shapes=[
            pltpu.SMEM(lengths.shape, jnp.int32),
            pltpu.VMEM((blocks, rows // blocks, width), bf16),
            pltpu.VMEM(cotangent.shape, bf16),
            pltpu.VMEM(gain.shape, bf16),
            pltpu.VMEM(in_projection.shape, bf16),
            pltpu.VMEM(out_projection.shape, bf16),
            pltpu.VMEM(in_projection.shape, bf16),
            pltpu.VMEM((rows, 2 * R), f32),
            pltpu.VMEM((-(-rows // LANES) * R, LANES), f32),
            pltpu.SemaphoreType.DMA((5 + blocks,)),
        ],
        compiler_params=pltpu.CompilerParams(vmem_limit_bytes=24 * 2**20),
        name="factors",
    )(*[in_hbm(x) for x in (lengths, hidden, cotangent, gain, in_projection, out_projection)])


def fetch_kernel(n_layer, after, store, slab, sems):
    block = slab.shape[0] // n_layer
    rows = 16 if block % 16 == 0 else 8
    me = lax.axis_index("layer")
    copies = []
    for k in range(n_layer):
        at = pl.multiple_of(partner(me, k, n_layer) * block, rows)
        to = slab.at[pl.ds(k * block, block)]
        copies.append(pltpu.make_async_copy(store.at[pl.ds(at, block)], to, sems.at[k]))
        copies[-1].start()
    for copy in copies:
        copy.wait()


def fetch(after, store, n_layer):
    rows, features = store.shape
    return pl.pallas_call(
        functools.partial(fetch_kernel, n_layer),
        out_shape=jax.ShapeDtypeStruct((rows, features), bf16),
        in_specs=[pl.BlockSpec(memory_space=pl.ANY)] * 2,
        out_specs=pl.BlockSpec(memory_space=pltpu.VMEM),
        scratch_shapes=[pltpu.SemaphoreType.DMA((n_layer,))],
        compiler_params=pltpu.CompilerParams(vmem_limit_bytes=12 * 2**20),
        cost_estimate=pl.CostEstimate(
            flops=0, bytes_accessed=2 * rows * features, transcendentals=0
        ),
        name="fetch",
    )(after, in_hbm(store))


def spread_out(tile, owner):
    lanes = tile.shape[1]
    mine = (owner == iota((G, lanes), 0))[None]
    wide = jnp.where(mine, tile.astype(f32)[:, None, :], 0.0)
    return wide.reshape(A * G, lanes).astype(bf16)


def halves(tile):
    wide = tile.astype(f32)
    turned = jnp.concatenate([wide[:, R:], wide[:, :R]], axis=1)
    low = iota(wide.shape, 1) < R
    return [
        jnp.where(mask, x, 0.0).astype(bf16)
        for x in (wide, turned)
        for mask in (low, jnp.logical_not(low))
    ]


def diagonal(low, high):
    zero = jnp.zeros_like(low)
    left = jnp.concatenate([low, high, zero, zero], axis=0)
    right = jnp.concatenate([zero, zero, low, high], axis=0)
    return jnp.concatenate([left, right], axis=1)


def build_grads(shards, base, row0, full_groups, grads):
    mid = full_groups * G * S // 2
    low = H * S // 2
    lane = iota((G, 2 * 128), 1)
    whole_owner = lax.rem(lane, G * S) // S
    half_owner = lax.rem(lane, H * S) // S + H * (lane // 128)

    def whole(shard):
        found = []
        pairs = {}
        for m in range(full_groups):
            first = m % (full_groups // 2)
            if first not in pairs:
                pairs[first] = halves(
                    shards[base + shard, first * G * S : (first + 1) * G * S, :]
                )
            plain_low, plain_high, turned_low, turned_high = pairs[first]
            weights = (
                diagonal(plain_low, turned_high)
                if m < full_groups // 2
                else diagonal(turned_low, plain_high)
            )
            at = mid + low + m * 2 * A
            tile = jnp.concatenate(
                [shards[base + shard, at : at + A, :], shards[base + shard, at + A : at + 2 * A, :]],
                axis=1,
            )
            found.append((spread_out(tile, whole_owner), weights))
        return found

    def joined(shard):
        tiles, weights = [], []
        for s in (shard, shard + 1):
            plain_low, plain_high, turned_low, turned_high = halves(
                shards[base + s, mid : mid + low, :]
            )
            weights.append(
                diagonal(
                    jnp.concatenate([plain_low, turned_low], axis=0),
                    jnp.concatenate([turned_high, plain_high], axis=0),
                )
            )
            at = mid + low + full_groups * 2 * A
            tiles.append(shards[base + s, at : at + A, :])
        return [
            (
                spread_out(jnp.concatenate(tiles, axis=1), half_owner),
                jnp.concatenate(weights, axis=0),
            )
        ]

    groups = []
    for shard in (0, 2):
        groups += whole(shard) + joined(shard) + whole(shard + 1)
    for at in range(0, len(groups), 2):
        first, second = [jnp.dot(x, w, preferred_element_type=f32) for x, w in groups[at : at + 2]]
        for a in range(A):
            pair = [x[a * G : (a + 1) * G] for x in (first, second)]
            grads[pl.ds(row0 + at * G, 2 * G), a * 256 : (a + 1) * 256] = jnp.concatenate(
                pair, axis=0
            ).astype(bf16)


def source(to, away, n):
    if n != 4:
        return (to + away) % n
    place = ((to ^ to // 2) + away) % n
    return place ^ place // 2


def grads_kernel(n_store, full_groups, k, *refs):
    gathered = refs[:n_store]
    slab, grads, out, shards = refs[n_store:]
    me_store = lax.axis_index("store")
    for away, block in enumerate(gathered):
        shards[source(me_store, away, n_store)] = block[...]
    four = 4 * (full_groups * G + H)
    if n_store == 4:
        build_grads(shards, 0, 0, full_groups, grads)
    else:

        @pl.loop(0, n_store // 4)
        def _(at):
            build_grads(shards, at * 4, pl.multiple_of(at * four, 16), full_groups, grads)

    scores_kernel(k, grads, slab, out)


def scores_kernel(k, grads, slab, *refs, skip=0):
    outs = refs[skip:]
    block = outs[0].shape[1]
    total = dot_nt(slab[k * block : (k + 1) * block, :], grads[...]).T
    at = 0
    for out in outs:
        out[...] = total[at : at + out.shape[0]].astype(out.dtype)
        at += out.shape[0]


def partner(me, k, n):
    return jnp.bitwise_xor(me, k) if n & (n - 1) == 0 else lax.rem(n + k - me, n)


def swap(x, axis, n, k):
    pairs = [(i, i ^ k if n & (n - 1) == 0 else (n + k - i) % n) for i in range(n)]
    return lax.ppermute(x, axis, pairs)


def grads_and_scores(gathered, slab, n_store, n_layer, k):
    rows, features = slab.shape
    queries = n_store * gathered[0].shape[0] // S
    vmem = pl.BlockSpec(memory_space=pltpu.VMEM)
    return pl.pallas_call(
        functools.partial(grads_kernel, n_store, queries // n_store // G, k),
        out_shape=[
            jax.ShapeDtypeStruct((queries, features), bf16),
            jax.ShapeDtypeStruct((queries, rows // n_layer), bf16),
        ],
        in_specs=[vmem] * (n_store + 1),
        out_specs=[vmem] * 2,
        scratch_shapes=[pltpu.VMEM((n_store,) + gathered[0].shape, bf16)],
        compiler_params=pltpu.CompilerParams(vmem_limit_bytes=24 * 2**20),
        name="grads",
    )(*gathered, slab)


def scores(grads, slab, n_layer, k, pieces=1, after=()):
    rows, features = slab.shape
    block = rows // n_layer
    queries = grads.shape[0]
    vmem = pl.BlockSpec(memory_space=pltpu.VMEM)
    return pl.pallas_call(
        functools.partial(scores_kernel, k, skip=len(after)),
        out_shape=[jax.ShapeDtypeStruct((queries // pieces, block), bf16 if k % 2 else f32)] * pieces,
        in_specs=[vmem] * 2 + [pl.BlockSpec(memory_space=pl.ANY)] * len(after),
        out_specs=[vmem] * pieces,
        compiler_params=pltpu.CompilerParams(vmem_limit_bytes=24 * 2**20),
        cost_estimate=pl.CostEstimate(
            flops=2 * queries * block * features,
            bytes_accessed=2 * (queries + block) * features,
            transcendentals=0,
        ),
        name="scores",
    )(grads, slab, *after)


def on_device(n_store, n_layer, hidden, cotangent, lengths, norm_gain, in_proj, out_proj, store):
    queries, positions, width = hidden.shape[1:]
    packed = factors(
        lengths,
        hidden.reshape(queries * positions, width),
        cotangent.reshape(queries * positions, cotangent.shape[3]),
        norm_gain,
        in_proj[0],
        out_proj[0],
    )
    gathered = [packed]
    for away in range(1, n_store):
        pairs = [(source(to, away, n_store), to) for to in range(n_store)]
        gathered.append(lax.ppermute(packed, "store", pairs))
    slab = fetch(packed, store[0], n_layer)
    grads, partial = grads_and_scores(gathered, slab, n_store, n_layer, n_layer - 1)
    crossed = []
    for k in reversed(range(2, n_layer, 2)):
        if k < n_layer - 2:
            (partial,) = scores(grads, slab, n_layer, k + 1)
        other = swap(partial, "layer", n_layer, 1)
        (mine,) = scores(grads, slab, n_layer, k)
        joined = (mine + other.astype(f32)).astype(bf16)
        crossed.append(swap(joined, "layer", n_layer, k))
    near = [swap(x, "layer", n_layer, 1) for x in scores(grads, slab, n_layer, 1, 2, [joined])]
    (total,) = scores(grads, slab, n_layer, 0)
    total = total + jnp.concatenate(near, axis=0).astype(f32)
    for x in crossed:
        total = total + x.astype(f32)
    return total.T


def solution(mesh):
    placed = (
        P("layer", ("grp", "store"), None, None),
        P("layer", ("grp", "store"), None, None),
        P(("grp", "store")),
        P("layer", None),
        P("layer", None, None),
        P("layer", None, None),
        P("layer", ("grp", "store"), None),
    )
    return jax.shard_map(
        functools.partial(on_device, mesh.shape["store"], mesh.shape["layer"]),
        mesh=mesh,
        in_specs=placed,
        out_specs=P(("grp", "store", "layer"), None),
        check_vma=False,
    )
```

```python
import functools

import jax
import jax.numpy as jnp
from jax import lax
from jax.experimental import pallas as pl
from jax.experimental.pallas import tpu as pltpu
from jax.sharding import PartitionSpec as P

norm_epsilon = 1e-05
f32 = jnp.float32
bf16 = jnp.bfloat16
S = 8
R = 64
B = 4
A = R // B
G = 8
H = 4
LANES = 128


def dot_nt(left, right):
    return lax.dot_general(left, right, (((1,), (1,)), ((), ())), preferred_element_type=f32)


def iota(shape, dim):
    return lax.broadcasted_iota(jnp.int32, shape, dim)


def factors_kernel(
    n_layer,
    hbm_lengths,
    hbm_hidden,
    hbm_cot,
    hbm_gain,
    hbm_inp,
    hbm_outp,
    hbm_store,
    packed,
    far,
    lengths,
    hidden,
    cot,
    gain,
    inp,
    outp,
    weights,
    in_acc,
    out_t,
    sems,
):
    blocks, step, width = hidden.shape
    rows = blocks * step
    queries = lengths.shape[0]
    full = queries // G * G * S
    half = rows - full
    mid, low = full // 2, half // 2

    def copy(source, target, at):
        return pltpu.make_async_copy(source, target, sems.at[at])

    def block_rows(r):
        at = pl.ds(pl.multiple_of(r * step, step), step)
        return copy(hbm_hidden.at[at, :], hidden.at[r], 5 + r)

    first = [copy(hbm_outp, outp, 0), copy(hbm_cot, cot, 1)]
    then = [copy(hbm_gain, gain, 2), copy(hbm_inp, inp, 3), copy(hbm_lengths, lengths, 4)]
    for piece in first + then + [block_rows(0)]:
        piece.start()
    odd = lax.rem(lax.axis_index("store"), 2)
    at_full = pl.multiple_of(odd * half, half)
    at_half = pl.multiple_of((1 - odd) * full, half)
    slab = store_copies(hbm_store, far, range(2, n_layer), sems, 5 + blocks, n_layer)
    for piece in first:
        piece.wait()

    @pl.when(odd >= 0)
    def _():
        for r in range(1, blocks):
            block_rows(r).start()
        for piece in slab:
            piece.start()

    whole = dot_nt(outp[...], cot[pl.ds(at_full, full), :])
    for t in range(full // LANES):
        out_t[t * R : (t + 1) * R, :] = whole[:, t * LANES : (t + 1) * LANES]
    out_t[full // LANES * R :, :half] = dot_nt(outp[...], cot[pl.ds(at_half, half), :])

    def part(t, b):
        return out_t[pl.ds(t * R + b, A, stride=B), :]

    row = mid + low
    for m in range(full // (G * S)):
        t, at = divmod(m * G * S, LANES)
        for b in range(0, B, 2):
            both = [part(t, b + c)[:, at : at + G * S] for c in range(2)]
            packed[row : row + A, :] = jnp.concatenate(both, axis=1).astype(bf16)
            row += A
    packed[row : row + A, :] = jnp.concatenate(
        [part(full // LANES, b)[:, :half] for b in range(B)], axis=1
    ).astype(bf16)

    for piece in then:
        piece.wait()
    weights[...] = inp[...] * gain[...]

    @pl.loop(0, blocks)
    def _(r):
        block_rows(r).wait()
        product = dot_nt(hidden[r], weights[...])
        total = jnp.zeros((step, LANES), f32)
        for at in range(0, width, LANES):
            wide = hidden[r, :, at : at + LANES].astype(f32)
            total += wide * wide
        mean_square = jnp.sum(total, axis=1, keepdims=True) * (1.0 / width)
        factor = product * lax.rsqrt(mean_square + norm_epsilon)
        at = pl.ds(pl.multiple_of(r * step, step), step)
        in_acc[at, :] = jnp.concatenate([factor, factor], axis=1)

    low_lanes = iota((S, LANES), 1) < R
    position = iota((S, LANES), 0)

    def in_rows(at, count):
        factor = in_acc[pl.ds(at, count), :]
        return [
            jnp.where(position < lengths[at // S + q], factor[q * S : (q + 1) * S], 0.0)
            for q in range(count // S)
        ]

    def side_by_side(tiles):
        both = zip(tiles[: len(tiles) // 2], tiles[len(tiles) // 2 :])
        return jnp.concatenate([jnp.where(low_lanes, x, y) for x, y in both], axis=0)

    packed[:mid, :] = side_by_side(in_rows(at_full, full)).astype(bf16)
    packed[mid : mid + low, :] = side_by_side(in_rows(at_half, half)).astype(bf16)
    for piece in slab:
        piece.wait()


def in_hbm(x):
    return pltpu.with_memory_space_constraint(x, pltpu.HBM)


def factors(n_layer, lengths, hidden, cotangent, gain, in_projection, out_projection, store):
    rows, width = hidden.shape
    blocks = 3
    far = (store.shape[0] // n_layer * (n_layer - 2), store.shape[1])
    args = (lengths, hidden, cotangent, gain, in_projection, out_projection, store)
    return pl.pallas_call(
        functools.partial(factors_kernel, n_layer),
        out_shape=[
            jax.ShapeDtypeStruct((rows, 2 * R), bf16),
            jax.ShapeDtypeStruct(far, bf16),
        ],
        in_specs=[pl.BlockSpec(memory_space=pl.ANY)] * len(args),
        out_specs=[pl.BlockSpec(memory_space=pltpu.VMEM)] * 2,
        scratch_shapes=[
            pltpu.SMEM(lengths.shape, jnp.int32),
            pltpu.VMEM((blocks, rows // blocks, width), bf16),
            pltpu.VMEM(cotangent.shape, bf16),
            pltpu.VMEM(gain.shape, bf16),
            pltpu.VMEM(in_projection.shape, bf16),
            pltpu.VMEM(out_projection.shape, bf16),
            pltpu.VMEM(in_projection.shape, bf16),
            pltpu.VMEM((rows, 2 * R), f32),
            pltpu.VMEM((-(-rows // LANES) * R, LANES), f32),
            pltpu.SemaphoreType.DMA((5 + blocks + n_layer - 2,)),
        ],
        compiler_params=pltpu.CompilerParams(vmem_limit_bytes=24 * 2**20),
        name="factors",
    )(*[in_hbm(x) for x in args])


def store_copies(store, slab, places, sems, at, n_layer):
    block = store.shape[0] // n_layer
    rows = 16 if block % 16 == 0 else 8
    me = lax.axis_index("layer")
    copies = []
    for to, k in enumerate(places):
        start = pl.multiple_of(partner(me, k, n_layer) * block, rows)
        target = slab.at[pl.ds(to * block, block)]
        copies.append(
            pltpu.make_async_copy(store.at[pl.ds(start, block)], target, sems.at[at + to])
        )
    return copies


def fetch_kernel(n_layer, after, store, near, sems):
    copies = store_copies(store, near, range(2), sems, 0, n_layer)
    for copy in copies:
        copy.start()
    for copy in copies:
        copy.wait()


def fetch(after, store, n_layer):
    rows, features = store.shape
    return pl.pallas_call(
        functools.partial(fetch_kernel, n_layer),
        out_shape=jax.ShapeDtypeStruct((rows // n_layer * 2, features), bf16),
        in_specs=[pl.BlockSpec(memory_space=pl.ANY)] * 2,
        out_specs=pl.BlockSpec(memory_space=pltpu.VMEM),
        scratch_shapes=[pltpu.SemaphoreType.DMA((2,))],
        compiler_params=pltpu.CompilerParams(vmem_limit_bytes=12 * 2**20),
        cost_estimate=pl.CostEstimate(
            flops=0, bytes_accessed=4 * rows * features // n_layer, transcendentals=0
        ),
        name="fetch",
    )(after, in_hbm(store))


def spread_out(tile, owner):
    lanes = tile.shape[1]
    mine = (owner == iota((G, lanes), 0))[None]
    wide = jnp.where(mine, tile.astype(f32)[:, None, :], 0.0)
    return wide.reshape(A * G, lanes).astype(bf16)


def halves(tile):
    wide = tile.astype(f32)
    turned = jnp.concatenate([wide[:, R:], wide[:, :R]], axis=1)
    low = iota(wide.shape, 1) < R
    return [
        jnp.where(mask, x, 0.0).astype(bf16)
        for x in (wide, turned)
        for mask in (low, jnp.logical_not(low))
    ]


def diagonal(low, high):
    zero = jnp.zeros_like(low)
    left = jnp.concatenate([low, high, zero, zero], axis=0)
    right = jnp.concatenate([zero, zero, low, high], axis=0)
    return jnp.concatenate([left, right], axis=1)


def build_grads(shards, base, row0, full_groups, grads):
    mid = full_groups * G * S // 2
    low = H * S // 2
    lane = iota((G, 2 * 128), 1)
    whole_owner = lax.rem(lane, G * S) // S
    half_owner = lax.rem(lane, H * S) // S + H * (lane // 128)

    def whole(shard):
        found = []
        pairs = {}
        for m in range(full_groups):
            first = m % (full_groups // 2)
            if first not in pairs:
                pairs[first] = halves(
                    shards[base + shard, first * G * S : (first + 1) * G * S, :]
                )
            plain_low, plain_high, turned_low, turned_high = pairs[first]
            weights = (
                diagonal(plain_low, turned_high)
                if m < full_groups // 2
                else diagonal(turned_low, plain_high)
            )
            at = mid + low + m * 2 * A
            tile = jnp.concatenate(
                [shards[base + shard, at : at + A, :], shards[base + shard, at + A : at + 2 * A, :]],
                axis=1,
            )
            found.append((spread_out(tile, whole_owner), weights))
        return found

    def joined(shard):
        tiles, weights = [], []
        for s in (shard, shard + 1):
            plain_low, plain_high, turned_low, turned_high = halves(
                shards[base + s, mid : mid + low, :]
            )
            weights.append(
                diagonal(
                    jnp.concatenate([plain_low, turned_low], axis=0),
                    jnp.concatenate([turned_high, plain_high], axis=0),
                )
            )
            at = mid + low + full_groups * 2 * A
            tiles.append(shards[base + s, at : at + A, :])
        return [
            (
                spread_out(jnp.concatenate(tiles, axis=1), half_owner),
                jnp.concatenate(weights, axis=0),
            )
        ]

    groups = []
    for shard in (0, 2):
        groups += whole(shard) + joined(shard) + whole(shard + 1)
    for at in range(0, len(groups), 2):
        first, second = [jnp.dot(x, w, preferred_element_type=f32) for x, w in groups[at : at + 2]]
        for a in range(A):
            pair = [x[a * G : (a + 1) * G] for x in (first, second)]
            grads[pl.ds(row0 + at * G, 2 * G), a * 256 : (a + 1) * 256] = jnp.concatenate(
                pair, axis=0
            ).astype(bf16)


def source(to, away, n):
    if n != 4:
        return (to + away) % n
    place = ((to ^ to // 2) + away) % n
    return place ^ place // 2


def grads_kernel(n_store, full_groups, k, *refs):
    gathered = refs[:n_store]
    slab, _, grads, out, shards = refs[n_store:]
    me_store = lax.axis_index("store")
    for away, block in enumerate(gathered):
        shards[source(me_store, away, n_store)] = block[...]
    four = 4 * (full_groups * G + H)
    if n_store == 4:
        build_grads(shards, 0, 0, full_groups, grads)
    else:

        @pl.loop(0, n_store // 4)
        def _(at):
            build_grads(shards, at * 4, pl.multiple_of(at * four, 16), full_groups, grads)

    scores_kernel(k, grads, slab, out)


def scores_kernel(k, grads, slab, *refs, skip=0):
    outs = refs[skip:]
    block = outs[0].shape[1]
    total = dot_nt(slab[k * block : (k + 1) * block, :], grads[...]).T
    at = 0
    for out in outs:
        out[...] = total[at : at + out.shape[0]].astype(out.dtype)
        at += out.shape[0]


def partner(me, k, n):
    return jnp.bitwise_xor(me, k) if n & (n - 1) == 0 else lax.rem(n + k - me, n)


def swap(x, axis, n, k):
    pairs = [(i, i ^ k if n & (n - 1) == 0 else (n + k - i) % n) for i in range(n)]
    return lax.ppermute(x, axis, pairs)


def grads_and_scores(gathered, slab, block, at, after):
    n_store = len(gathered)
    queries = gathered[0].shape[0] // S
    vmem = pl.BlockSpec(memory_space=pltpu.VMEM)
    return pl.pallas_call(
        functools.partial(grads_kernel, n_store, queries // G, at),
        out_shape=[
            jax.ShapeDtypeStruct((n_store * queries, slab.shape[1]), bf16),
            jax.ShapeDtypeStruct((n_store * queries, block), bf16),
        ],
        in_specs=[vmem] * (n_store + 1) + [pl.BlockSpec(memory_space=pl.ANY)],
        out_specs=[vmem] * 2,
        scratch_shapes=[pltpu.VMEM((n_store,) + gathered[0].shape, bf16)],
        compiler_params=pltpu.CompilerParams(vmem_limit_bytes=24 * 2**20),
        name="grads",
    )(*gathered, slab, after)


def scores(grads, slab, block, at, kind, pieces=1, after=()):
    queries, features = grads.shape
    vmem = pl.BlockSpec(memory_space=pltpu.VMEM)
    return pl.pallas_call(
        functools.partial(scores_kernel, at, skip=len(after)),
        out_shape=[jax.ShapeDtypeStruct((queries // pieces, block), kind)] * pieces,
        in_specs=[vmem] * 2 + [pl.BlockSpec(memory_space=pl.ANY)] * len(after),
        out_specs=[vmem] * pieces,
        compiler_params=pltpu.CompilerParams(vmem_limit_bytes=24 * 2**20),
        cost_estimate=pl.CostEstimate(
            flops=2 * queries * block * features,
            bytes_accessed=2 * (queries + block) * features,
            transcendentals=0,
        ),
        name="scores",
    )(grads, slab, *after)


def on_device(n_store, n_layer, hidden, cotangent, lengths, norm_gain, in_proj, out_proj, store):
    queries, positions, width = hidden.shape[1:]
    block = store.shape[1] // n_layer
    packed, far = factors(
        n_layer,
        lengths,
        hidden.reshape(queries * positions, width),
        cotangent.reshape(queries * positions, cotangent.shape[3]),
        norm_gain,
        in_proj[0],
        out_proj[0],
        store[0],
    )
    gathered = [packed]
    for away in range(1, n_store):
        pairs = [(source(to, away, n_store), to) for to in range(n_store)]
        gathered.append(lax.ppermute(packed, "store", pairs))
    near = fetch(packed, store[0], n_layer)
    last = n_layer - 3
    grads, partial = grads_and_scores(gathered, far, block, last, near)
    crossed = []
    for at in reversed(range(0, last, 2)):
        if at + 1 < last:
            (partial,) = scores(grads, far, block, at + 1, bf16)
        other = swap(partial, "layer", n_layer, 1)
        (mine,) = scores(grads, far, block, at, f32)
        joined = (mine + other.astype(f32)).astype(bf16)
        crossed.append(swap(joined, "layer", n_layer, at + 2))
    halves_of_other = scores(grads, near, block, 1, bf16, 2, [joined])
    (total,) = scores(grads, near, block, 0, f32)
    other = [swap(x, "layer", n_layer, 1) for x in halves_of_other]
    total = total + jnp.concatenate(other, axis=0).astype(f32)
    for x in crossed:
        total = total + x.astype(f32)
    return total.T


def solution(mesh):
    placed = (
        P("layer", ("grp", "store"), None, None),
        P("layer", ("grp", "store"), None, None),
        P(("grp", "store")),
        P("layer", None),
        P("layer", None, None),
        P("layer", None, None),
        P("layer", ("grp", "store"), None),
    )
    return jax.shard_map(
        functools.partial(on_device, mesh.shape["store"], mesh.shape["layer"]),
        mesh=mesh,
        in_specs=placed,
        out_specs=P(("grp", "store", "layer"), None),
        check_vma=False,
    )
```

```python
import functools

import jax
import jax.numpy as jnp
from jax import lax
from jax.experimental import pallas as pl
from jax.experimental.pallas import tpu as pltpu
from jax.sharding import PartitionSpec as P

norm_epsilon = 1e-05
f32 = jnp.float32
bf16 = jnp.bfloat16
S = 8
R = 64
B = 4
A = R // B
G = 8
H = 4
LANES = 128


def dot_nt(left, right):
    return lax.dot_general(left, right, (((1,), (1,)), ((), ())), preferred_element_type=f32)


def iota(shape, dim):
    return lax.broadcasted_iota(jnp.int32, shape, dim)


def factors_kernel(
    n_layer,
    hbm_lengths,
    hbm_hidden,
    hbm_cot,
    hbm_gain,
    hbm_inp,
    hbm_outp,
    hbm_store,
    packed,
    far,
    lengths,
    hidden,
    cot,
    gain,
    inp,
    outp,
    weights,
    in_acc,
    out_t,
    sems,
):
    blocks, step, width = hidden.shape
    rows = blocks * step
    queries = lengths.shape[0]
    full = queries // G * G * S
    half = rows - full
    mid, low = full // 2, half // 2

    def copy(source, target, at):
        return pltpu.make_async_copy(source, target, sems.at[at])

    def block_rows(r):
        at = pl.ds(pl.multiple_of(r * step, step), step)
        return copy(hbm_hidden.at[at, :], hidden.at[r], 5 + r)

    first = [copy(hbm_outp, outp, 0), copy(hbm_cot, cot, 1)]
    then = [copy(hbm_gain, gain, 2), copy(hbm_inp, inp, 3), copy(hbm_lengths, lengths, 4)]
    for piece in first + then + [block_rows(0)]:
        piece.start()
    odd = lax.rem(lax.axis_index("store"), 2)
    at_full = pl.multiple_of(odd * half, half)
    at_half = pl.multiple_of((1 - odd) * full, half)
    slab = store_copies(hbm_store, far, range(2, n_layer), sems, 5 + blocks, n_layer)
    for piece in first:
        piece.wait()

    @pl.when(odd >= 0)
    def _():
        for r in range(1, blocks):
            block_rows(r).start()
        for piece in slab:
            piece.start()

    whole = dot_nt(outp[...], cot[pl.ds(at_full, full), :])
    for t in range(full // LANES):
        out_t[t * R : (t + 1) * R, :] = whole[:, t * LANES : (t + 1) * LANES]
    out_t[full // LANES * R :, :half] = dot_nt(outp[...], cot[pl.ds(at_half, half), :])

    def part(t, b):
        return out_t[pl.ds(t * R + b, A, stride=B), :]

    row = mid + low
    for m in range(full // (G * S)):
        t, at = divmod(m * G * S, LANES)
        for b in range(0, B, 2):
            both = [part(t, b + c)[:, at : at + G * S] for c in range(2)]
            packed[row : row + A, :] = jnp.concatenate(both, axis=1).astype(bf16)
            row += A
    packed[row : row + A, :] = jnp.concatenate(
        [part(full // LANES, b)[:, :half] for b in range(B)], axis=1
    ).astype(bf16)

    for piece in then:
        piece.wait()
    weights[...] = inp[...] * gain[...]

    @pl.loop(0, blocks)
    def _(r):
        block_rows(r).wait()
        product = dot_nt(hidden[r], weights[...])
        total = jnp.zeros((step, LANES), f32)
        for at in range(0, width, LANES):
            wide = hidden[r, :, at : at + LANES].astype(f32)
            total += wide * wide
        mean_square = jnp.sum(total, axis=1, keepdims=True) * (1.0 / width)
        factor = product * lax.rsqrt(mean_square + norm_epsilon)
        at = pl.ds(pl.multiple_of(r * step, step), step)
        in_acc[at, :] = jnp.concatenate([factor, factor], axis=1)

    low_lanes = iota((S, LANES), 1) < R
    position = iota((S, LANES), 0)

    def in_rows(at, count):
        factor = in_acc[pl.ds(at, count), :]
        return [
            jnp.where(position < lengths[at // S + q], factor[q * S : (q + 1) * S], 0.0)
            for q in range(count // S)
        ]

    def side_by_side(tiles):
        both = zip(tiles[: len(tiles) // 2], tiles[len(tiles) // 2 :])
        return jnp.concatenate([jnp.where(low_lanes, x, y) for x, y in both], axis=0)

    packed[:mid, :] = side_by_side(in_rows(at_full, full)).astype(bf16)
    packed[mid : mid + low, :] = side_by_side(in_rows(at_half, half)).astype(bf16)
    for piece in slab:
        piece.wait()


def in_hbm(x):
    return pltpu.with_memory_space_constraint(x, pltpu.HBM)


def factors(n_layer, lengths, hidden, cotangent, gain, in_projection, out_projection, store):
    rows, width = hidden.shape
    blocks = 2
    far = (store.shape[0] // n_layer * (n_layer - 2), store.shape[1])
    args = (lengths, hidden, cotangent, gain, in_projection, out_projection, store)
    return pl.pallas_call(
        functools.partial(factors_kernel, n_layer),
        out_shape=[
            jax.ShapeDtypeStruct((rows, 2 * R), bf16),
            jax.ShapeDtypeStruct(far, bf16),
        ],
        in_specs=[pl.BlockSpec(memory_space=pl.ANY)] * len(args),
        out_specs=[pl.BlockSpec(memory_space=pltpu.VMEM)] * 2,
        scratch_shapes=[
            pltpu.SMEM(lengths.shape, jnp.int32),
            pltpu.VMEM((blocks, rows // blocks, width), bf16),
            pltpu.VMEM(cotangent.shape, bf16),
            pltpu.VMEM(gain.shape, bf16),
            pltpu.VMEM(in_projection.shape, bf16),
            pltpu.VMEM(out_projection.shape, bf16),
            pltpu.VMEM(in_projection.shape, bf16),
            pltpu.VMEM((rows, 2 * R), f32),
            pltpu.VMEM((-(-rows // LANES) * R, LANES), f32),
            pltpu.SemaphoreType.DMA((5 + blocks + n_layer - 2,)),
        ],
        compiler_params=pltpu.CompilerParams(vmem_limit_bytes=24 * 2**20),
        name="factors",
    )(*[in_hbm(x) for x in args])


def store_copies(store, slab, places, sems, at, n_layer):
    block = store.shape[0] // n_layer
    rows = 16 if block % 16 == 0 else 8
    me = lax.axis_index("layer")
    copies = []
    for to, k in enumerate(places):
        start = pl.multiple_of(partner(me, k, n_layer) * block, rows)
        target = slab.at[pl.ds(to * block, block)]
        copies.append(
            pltpu.make_async_copy(store.at[pl.ds(start, block)], target, sems.at[at + to])
        )
    return copies


def fetch_kernel(n_layer, after, store, near, sems):
    copies = store_copies(store, near, range(2), sems, 0, n_layer)
    for copy in copies:
        copy.start()
    for copy in copies:
        copy.wait()


def fetch(after, store, n_layer):
    rows, features = store.shape
    return pl.pallas_call(
        functools.partial(fetch_kernel, n_layer),
        out_shape=jax.ShapeDtypeStruct((rows // n_layer * 2, features), bf16),
        in_specs=[pl.BlockSpec(memory_space=pl.ANY)] * 2,
        out_specs=pl.BlockSpec(memory_space=pltpu.VMEM),
        scratch_shapes=[pltpu.SemaphoreType.DMA((2,))],
        compiler_params=pltpu.CompilerParams(vmem_limit_bytes=12 * 2**20),
        cost_estimate=pl.CostEstimate(
            flops=0, bytes_accessed=4 * rows * features // n_layer, transcendentals=0
        ),
        name="fetch",
    )(after, in_hbm(store))


def spread_out(tile, owner):
    lanes = tile.shape[1]
    mine = (owner == iota((G, lanes), 0))[None]
    wide = jnp.where(mine, tile.astype(f32)[:, None, :], 0.0)
    return wide.reshape(A * G, lanes).astype(bf16)


def halves(tile):
    wide = tile.astype(f32)
    turned = jnp.concatenate([wide[:, R:], wide[:, :R]], axis=1)
    low = iota(wide.shape, 1) < R
    return [
        jnp.where(mask, x, 0.0).astype(bf16)
        for x in (wide, turned)
        for mask in (low, jnp.logical_not(low))
    ]


def diagonal(low, high):
    zero = jnp.zeros_like(low)
    left = jnp.concatenate([low, high, zero, zero], axis=0)
    right = jnp.concatenate([zero, zero, low, high], axis=0)
    return jnp.concatenate([left, right], axis=1)


def build_grads(shards, base, row0, full_groups, grads):
    mid = full_groups * G * S // 2
    low = H * S // 2
    lane = iota((G, 2 * 128), 1)
    whole_owner = lax.rem(lane, G * S) // S
    half_owner = lax.rem(lane, H * S) // S + H * (lane // 128)

    def whole(shard):
        found = []
        pairs = {}
        for m in range(full_groups):
            first = m % (full_groups // 2)
            if first not in pairs:
                pairs[first] = halves(
                    shards[base + shard, first * G * S : (first + 1) * G * S, :]
                )
            plain_low, plain_high, turned_low, turned_high = pairs[first]
            weights = (
                diagonal(plain_low, turned_high)
                if m < full_groups // 2
                else diagonal(turned_low, plain_high)
            )
            at = mid + low + m * 2 * A
            tile = jnp.concatenate(
                [shards[base + shard, at : at + A, :], shards[base + shard, at + A : at + 2 * A, :]],
                axis=1,
            )
            found.append((spread_out(tile, whole_owner), weights))
        return found

    def joined(shard):
        tiles, weights = [], []
        for s in (shard, shard + 1):
            plain_low, plain_high, turned_low, turned_high = halves(
                shards[base + s, mid : mid + low, :]
            )
            weights.append(
                diagonal(
                    jnp.concatenate([plain_low, turned_low], axis=0),
                    jnp.concatenate([turned_high, plain_high], axis=0),
                )
            )
            at = mid + low + full_groups * 2 * A
            tiles.append(shards[base + s, at : at + A, :])
        return [
            (
                spread_out(jnp.concatenate(tiles, axis=1), half_owner),
                jnp.concatenate(weights, axis=0),
            )
        ]

    groups = []
    for shard in (0, 2):
        groups += whole(shard) + joined(shard) + whole(shard + 1)
    for at in range(0, len(groups), 2):
        first, second = [jnp.dot(x, w, preferred_element_type=f32) for x, w in groups[at : at + 2]]
        for a in range(A):
            pair = [x[a * G : (a + 1) * G] for x in (first, second)]
            grads[pl.ds(row0 + at * G, 2 * G), a * 256 : (a + 1) * 256] = jnp.concatenate(
                pair, axis=0
            ).astype(bf16)


def source(to, away, n):
    if n != 4:
        return (to + away) % n
    place = ((to ^ to // 2) + away) % n
    return place ^ place // 2


def grads_kernel(n_store, full_groups, k, *refs):
    gathered = refs[:n_store]
    slab, _, grads, out, shards = refs[n_store:]
    me_store = lax.axis_index("store")
    for away, block in enumerate(gathered):
        shards[source(me_store, away, n_store)] = block[...]
    four = 4 * (full_groups * G + H)
    if n_store == 4:
        build_grads(shards, 0, 0, full_groups, grads)
    else:

        @pl.loop(0, n_store // 4)
        def _(at):
            build_grads(shards, at * 4, pl.multiple_of(at * four, 16), full_groups, grads)

    scores_kernel(k, grads, slab, out)


def scores_kernel(k, grads, slab, *refs, skip=0):
    outs = refs[skip:]
    block = outs[0].shape[1]
    total = dot_nt(slab[k * block : (k + 1) * block, :], grads[...]).T
    at = 0
    for out in outs:
        out[...] = total[at : at + out.shape[0]].astype(out.dtype)
        at += out.shape[0]


def partner(me, k, n):
    return jnp.bitwise_xor(me, k) if n & (n - 1) == 0 else lax.rem(n + k - me, n)


def swap(x, axis, n, k):
    pairs = [(i, i ^ k if n & (n - 1) == 0 else (n + k - i) % n) for i in range(n)]
    return lax.ppermute(x, axis, pairs)


def grads_and_scores(gathered, slab, block, at, after):
    n_store = len(gathered)
    queries = gathered[0].shape[0] // S
    vmem = pl.BlockSpec(memory_space=pltpu.VMEM)
    return pl.pallas_call(
        functools.partial(grads_kernel, n_store, queries // G, at),
        out_shape=[
            jax.ShapeDtypeStruct((n_store * queries, slab.shape[1]), bf16),
            jax.ShapeDtypeStruct((n_store * queries, block), bf16),
        ],
        in_specs=[vmem] * (n_store + 1) + [pl.BlockSpec(memory_space=pl.ANY)],
        out_specs=[vmem] * 2,
        scratch_shapes=[pltpu.VMEM((n_store,) + gathered[0].shape, bf16)],
        compiler_params=pltpu.CompilerParams(vmem_limit_bytes=24 * 2**20),
        name="grads",
    )(*gathered, slab, after)


def scores(grads, slab, block, at, kind, pieces=1, after=()):
    queries, features = grads.shape
    vmem = pl.BlockSpec(memory_space=pltpu.VMEM)
    return pl.pallas_call(
        functools.partial(scores_kernel, at, skip=len(after)),
        out_shape=[jax.ShapeDtypeStruct((queries // pieces, block), kind)] * pieces,
        in_specs=[vmem] * 2 + [pl.BlockSpec(memory_space=pl.ANY)] * len(after),
        out_specs=[vmem] * pieces,
        compiler_params=pltpu.CompilerParams(vmem_limit_bytes=24 * 2**20),
        cost_estimate=pl.CostEstimate(
            flops=2 * queries * block * features,
            bytes_accessed=2 * (queries + block) * features,
            transcendentals=0,
        ),
        name="scores",
    )(grads, slab, *after)


def on_device(n_store, n_layer, hidden, cotangent, lengths, norm_gain, in_proj, out_proj, store):
    queries, positions, width = hidden.shape[1:]
    block = store.shape[1] // n_layer
    packed, far = factors(
        n_layer,
        lengths,
        hidden.reshape(queries * positions, width),
        cotangent.reshape(queries * positions, cotangent.shape[3]),
        norm_gain,
        in_proj[0],
        out_proj[0],
        store[0],
    )
    gathered = [packed]
    for away in range(1, n_store):
        pairs = [(source(to, away, n_store), to) for to in range(n_store)]
        gathered.append(lax.ppermute(packed, "store", pairs))
    near = fetch(packed, store[0], n_layer)
    last = n_layer - 3
    grads, partial = grads_and_scores(gathered, far, block, last, near)
    crossed = []
    for at in reversed(range(0, last, 2)):
        if at + 1 < last:
            (partial,) = scores(grads, far, block, at + 1, bf16)
        other = swap(partial, "layer", n_layer, 1)
        (mine,) = scores(grads, far, block, at, f32)
        joined = (mine + other.astype(f32)).astype(bf16)
        crossed.append(swap(joined, "layer", n_layer, at + 2))
    halves_of_other = scores(grads, near, block, 1, bf16, 2, [joined])
    (total,) = scores(grads, near, block, 0, f32)
    other = [swap(x, "layer", n_layer, 1) for x in halves_of_other]
    total = total + jnp.concatenate(other, axis=0).astype(f32)
    for x in crossed:
        total = total + x.astype(f32)
    return total.T


def solution(mesh):
    placed = (
        P("layer", ("grp", "store"), None, None),
        P("layer", ("grp", "store"), None, None),
        P(("grp", "store")),
        P("layer", None),
        P("layer", None, None),
        P("layer", None, None),
        P("layer", ("grp", "store"), None),
    )
    return jax.shard_map(
        functools.partial(on_device, mesh.shape["store"], mesh.shape["layer"]),
        mesh=mesh,
        in_specs=placed,
        out_specs=P(("grp", "store", "layer"), None),
        check_vma=False,
    )
```

```python
import functools

import jax
import jax.numpy as jnp
from jax import lax
from jax.experimental import pallas as pl
from jax.experimental.pallas import tpu as pltpu
from jax.sharding import PartitionSpec as P

norm_epsilon = 1e-05
f32 = jnp.float32
bf16 = jnp.bfloat16
S = 8
R = 64
B = 4
A = R // B
G = 8
H = 4
LANES = 128


def dot_nt(left, right):
    return lax.dot_general(left, right, (((1,), (1,)), ((), ())), preferred_element_type=f32)


def iota(shape, dim):
    return lax.broadcasted_iota(jnp.int32, shape, dim)


def factors_kernel(
    n_layer,
    hbm_lengths,
    hbm_hidden,
    hbm_cot,
    hbm_gain,
    hbm_inp,
    hbm_outp,
    hbm_store,
    packed,
    far,
    lengths,
    hidden,
    cot,
    gain,
    inp,
    outp,
    weights,
    in_acc,
    out_t,
    sems,
):
    blocks, step, width = hidden.shape
    rows = blocks * step
    queries = lengths.shape[0]
    full = queries // G * G * S
    half = rows - full
    mid, low = full // 2, half // 2

    def copy(source, target, at):
        return pltpu.make_async_copy(source, target, sems.at[at])

    def block_rows(r):
        at = pl.ds(pl.multiple_of(r * step, step), step)
        return copy(hbm_hidden.at[at, :], hidden.at[r], 5 + r)

    first = [copy(hbm_outp, outp, 0), copy(hbm_cot, cot, 1)]
    then = [copy(hbm_gain, gain, 2), copy(hbm_inp, inp, 3), copy(hbm_lengths, lengths, 4)]
    for piece in first + then + [block_rows(0)]:
        piece.start()
    odd = lax.rem(lax.axis_index("store"), 2)
    at_full = pl.multiple_of(odd * half, half)
    at_half = pl.multiple_of((1 - odd) * full, half)
    slab = store_copies(hbm_store, far, range(2, n_layer), sems, 5 + blocks, n_layer)
    for piece in first:
        piece.wait()

    @pl.when(odd >= 0)
    def _():
        for r in range(1, blocks):
            block_rows(r).start()
        for piece in slab:
            piece.start()

    whole = dot_nt(outp[...], cot[pl.ds(at_full, full), :])
    for t in range(full // LANES):
        out_t[t * R : (t + 1) * R, :] = whole[:, t * LANES : (t + 1) * LANES]
    out_t[full // LANES * R :, :half] = dot_nt(outp[...], cot[pl.ds(at_half, half), :])

    def part(t, b):
        return out_t[pl.ds(t * R + b, A, stride=B), :]

    row = mid + low
    for m in range(full // (G * S)):
        t, at = divmod(m * G * S, LANES)
        for b in range(0, B, 2):
            both = [part(t, b + c)[:, at : at + G * S] for c in range(2)]
            packed[row : row + A, :] = jnp.concatenate(both, axis=1).astype(bf16)
            row += A
    packed[row : row + A, :] = jnp.concatenate(
        [part(full // LANES, b)[:, :half] for b in range(B)], axis=1
    ).astype(bf16)

    for piece in then:
        piece.wait()
    weights[...] = inp[...] * gain[...]

    @pl.loop(0, blocks)
    def _(r):
        block_rows(r).wait()
        product = dot_nt(hidden[r], weights[...])
        total = jnp.zeros((step, LANES), f32)
        for at in range(0, width, LANES):
            wide = hidden[r, :, at : at + LANES].astype(f32)
            total += wide * wide
        mean_square = jnp.sum(total, axis=1, keepdims=True) * (1.0 / width)
        factor = product * lax.rsqrt(mean_square + norm_epsilon)
        at = pl.ds(pl.multiple_of(r * step, step), step)
        in_acc[at, :] = jnp.concatenate([factor, factor], axis=1)

    low_lanes = iota((S, LANES), 1) < R
    position = iota((S, LANES), 0)

    def in_rows(at, count):
        factor = in_acc[pl.ds(at, count), :]
        return [
            jnp.where(position < lengths[at // S + q], factor[q * S : (q + 1) * S], 0.0)
            for q in range(count // S)
        ]

    def side_by_side(tiles):
        both = zip(tiles[: len(tiles) // 2], tiles[len(tiles) // 2 :])
        return jnp.concatenate([jnp.where(low_lanes, x, y) for x, y in both], axis=0)

    packed[:mid, :] = side_by_side(in_rows(at_full, full)).astype(bf16)
    packed[mid : mid + low, :] = side_by_side(in_rows(at_half, half)).astype(bf16)
    for piece in slab:
        piece.wait()


def in_hbm(x):
    return pltpu.with_memory_space_constraint(x, pltpu.HBM)


def factors(n_layer, lengths, hidden, cotangent, gain, in_projection, out_projection, store):
    rows, width = hidden.shape
    blocks = 6
    far = (store.shape[0] // n_layer * (n_layer - 2), store.shape[1])
    args = (lengths, hidden, cotangent, gain, in_projection, out_projection, store)
    return pl.pallas_call(
        functools.partial(factors_kernel, n_layer),
        out_shape=[
            jax.ShapeDtypeStruct((rows, 2 * R), bf16),
            jax.ShapeDtypeStruct(far, bf16),
        ],
        in_specs=[pl.BlockSpec(memory_space=pl.ANY)] * len(args),
        out_specs=[pl.BlockSpec(memory_space=pltpu.VMEM)] * 2,
        scratch_shapes=[
            pltpu.SMEM(lengths.shape, jnp.int32),
            pltpu.VMEM((blocks, rows // blocks, width), bf16),
            pltpu.VMEM(cotangent.shape, bf16),
            pltpu.VMEM(gain.shape, bf16),
            pltpu.VMEM(in_projection.shape, bf16),
            pltpu.VMEM(out_projection.shape, bf16),
            pltpu.VMEM(in_projection.shape, bf16),
            pltpu.VMEM((rows, 2 * R), f32),
            pltpu.VMEM((-(-rows // LANES) * R, LANES), f32),
            pltpu.SemaphoreType.DMA((5 + blocks + n_layer - 2,)),
        ],
        compiler_params=pltpu.CompilerParams(vmem_limit_bytes=24 * 2**20),
        name="factors",
    )(*[in_hbm(x) for x in args])


def store_copies(store, slab, places, sems, at, n_layer):
    block = store.shape[0] // n_layer
    rows = 16 if block % 16 == 0 else 8
    me = lax.axis_index("layer")
    copies = []
    for to, k in enumerate(places):
        start = pl.multiple_of(partner(me, k, n_layer) * block, rows)
        target = slab.at[pl.ds(to * block, block)]
        copies.append(
            pltpu.make_async_copy(store.at[pl.ds(start, block)], target, sems.at[at + to])
        )
    return copies


def fetch_kernel(n_layer, after, store, near, sems):
    copies = store_copies(store, near, range(2), sems, 0, n_layer)
    for copy in copies:
        copy.start()
    for copy in copies:
        copy.wait()


def fetch(after, store, n_layer):
    rows, features = store.shape
    return pl.pallas_call(
        functools.partial(fetch_kernel, n_layer),
        out_shape=jax.ShapeDtypeStruct((rows // n_layer * 2, features), bf16),
        in_specs=[pl.BlockSpec(memory_space=pl.ANY)] * 2,
        out_specs=pl.BlockSpec(memory_space=pltpu.VMEM),
        scratch_shapes=[pltpu.SemaphoreType.DMA((2,))],
        compiler_params=pltpu.CompilerParams(vmem_limit_bytes=12 * 2**20),
        cost_estimate=pl.CostEstimate(
            flops=0, bytes_accessed=4 * rows * features // n_layer, transcendentals=0
        ),
        name="fetch",
    )(after, in_hbm(store))


def spread_out(tile, owner):
    lanes = tile.shape[1]
    mine = (owner == iota((G, lanes), 0))[None]
    wide = jnp.where(mine, tile.astype(f32)[:, None, :], 0.0)
    return wide.reshape(A * G, lanes).astype(bf16)


def halves(tile):
    wide = tile.astype(f32)
    turned = jnp.concatenate([wide[:, R:], wide[:, :R]], axis=1)
    low = iota(wide.shape, 1) < R
    return [
        jnp.where(mask, x, 0.0).astype(bf16)
        for x in (wide, turned)
        for mask in (low, jnp.logical_not(low))
    ]


def diagonal(low, high):
    zero = jnp.zeros_like(low)
    left = jnp.concatenate([low, high, zero, zero], axis=0)
    right = jnp.concatenate([zero, zero, low, high], axis=0)
    return jnp.concatenate([left, right], axis=1)


def build_grads(shards, base, row0, full_groups, grads):
    mid = full_groups * G * S // 2
    low = H * S // 2
    lane = iota((G, 2 * 128), 1)
    whole_owner = lax.rem(lane, G * S) // S
    half_owner = lax.rem(lane, H * S) // S + H * (lane // 128)

    def whole(shard):
        found = []
        pairs = {}
        for m in range(full_groups):
            first = m % (full_groups // 2)
            if first not in pairs:
                pairs[first] = halves(
                    shards[base + shard, first * G * S : (first + 1) * G * S, :]
                )
            plain_low, plain_high, turned_low, turned_high = pairs[first]
            weights = (
                diagonal(plain_low, turned_high)
                if m < full_groups // 2
                else diagonal(turned_low, plain_high)
            )
            at = mid + low + m * 2 * A
            tile = jnp.concatenate(
                [shards[base + shard, at : at + A, :], shards[base + shard, at + A : at + 2 * A, :]],
                axis=1,
            )
            found.append((spread_out(tile, whole_owner), weights))
        return found

    def joined(shard):
        tiles, weights = [], []
        for s in (shard, shard + 1):
            plain_low, plain_high, turned_low, turned_high = halves(
                shards[base + s, mid : mid + low, :]
            )
            weights.append(
                diagonal(
                    jnp.concatenate([plain_low, turned_low], axis=0),
                    jnp.concatenate([turned_high, plain_high], axis=0),
                )
            )
            at = mid + low + full_groups * 2 * A
            tiles.append(shards[base + s, at : at + A, :])
        return [
            (
                spread_out(jnp.concatenate(tiles, axis=1), half_owner),
                jnp.concatenate(weights, axis=0),
            )
        ]

    groups = []
    for shard in (0, 2):
        groups += whole(shard) + joined(shard) + whole(shard + 1)
    for at in range(0, len(groups), 2):
        first, second = [jnp.dot(x, w, preferred_element_type=f32) for x, w in groups[at : at + 2]]
        for a in range(A):
            pair = [x[a * G : (a + 1) * G] for x in (first, second)]
            grads[pl.ds(row0 + at * G, 2 * G), a * 256 : (a + 1) * 256] = jnp.concatenate(
                pair, axis=0
            ).astype(bf16)


def source(to, away, n):
    if n != 4:
        return (to + away) % n
    place = ((to ^ to // 2) + away) % n
    return place ^ place // 2


def grads_kernel(n_store, full_groups, k, *refs):
    gathered = refs[:n_store]
    slab, _, grads, out, shards = refs[n_store:]
    me_store = lax.axis_index("store")
    for away, block in enumerate(gathered):
        shards[source(me_store, away, n_store)] = block[...]
    four = 4 * (full_groups * G + H)
    if n_store == 4:
        build_grads(shards, 0, 0, full_groups, grads)
    else:

        @pl.loop(0, n_store // 4)
        def _(at):
            build_grads(shards, at * 4, pl.multiple_of(at * four, 16), full_groups, grads)

    scores_kernel(k, grads, slab, out)


def scores_kernel(k, grads, slab, *refs, skip=0):
    outs = refs[skip:]
    block = outs[0].shape[1]
    total = dot_nt(slab[k * block : (k + 1) * block, :], grads[...]).T
    at = 0
    for out in outs:
        out[...] = total[at : at + out.shape[0]].astype(out.dtype)
        at += out.shape[0]


def partner(me, k, n):
    return jnp.bitwise_xor(me, k) if n & (n - 1) == 0 else lax.rem(n + k - me, n)


def swap(x, axis, n, k):
    pairs = [(i, i ^ k if n & (n - 1) == 0 else (n + k - i) % n) for i in range(n)]
    return lax.ppermute(x, axis, pairs)


def grads_and_scores(gathered, slab, block, at, after):
    n_store = len(gathered)
    queries = gathered[0].shape[0] // S
    vmem = pl.BlockSpec(memory_space=pltpu.VMEM)
    return pl.pallas_call(
        functools.partial(grads_kernel, n_store, queries // G, at),
        out_shape=[
            jax.ShapeDtypeStruct((n_store * queries, slab.shape[1]), bf16),
            jax.ShapeDtypeStruct((n_store * queries, block), bf16),
        ],
        in_specs=[vmem] * (n_store + 1) + [pl.BlockSpec(memory_space=pl.ANY)],
        out_specs=[vmem] * 2,
        scratch_shapes=[pltpu.VMEM((n_store,) + gathered[0].shape, bf16)],
        compiler_params=pltpu.CompilerParams(vmem_limit_bytes=24 * 2**20),
        name="grads",
    )(*gathered, slab, after)


def scores(grads, slab, block, at, kind, pieces=1, after=()):
    queries, features = grads.shape
    vmem = pl.BlockSpec(memory_space=pltpu.VMEM)
    return pl.pallas_call(
        functools.partial(scores_kernel, at, skip=len(after)),
        out_shape=[jax.ShapeDtypeStruct((queries // pieces, block), kind)] * pieces,
        in_specs=[vmem] * 2 + [pl.BlockSpec(memory_space=pl.ANY)] * len(after),
        out_specs=[vmem] * pieces,
        compiler_params=pltpu.CompilerParams(vmem_limit_bytes=24 * 2**20),
        cost_estimate=pl.CostEstimate(
            flops=2 * queries * block * features,
            bytes_accessed=2 * (queries + block) * features,
            transcendentals=0,
        ),
        name="scores",
    )(grads, slab, *after)


def on_device(n_store, n_layer, hidden, cotangent, lengths, norm_gain, in_proj, out_proj, store):
    queries, positions, width = hidden.shape[1:]
    block = store.shape[1] // n_layer
    packed, far = factors(
        n_layer,
        lengths,
        hidden.reshape(queries * positions, width),
        cotangent.reshape(queries * positions, cotangent.shape[3]),
        norm_gain,
        in_proj[0],
        out_proj[0],
        store[0],
    )
    gathered = [packed]
    for away in range(1, n_store):
        pairs = [(source(to, away, n_store), to) for to in range(n_store)]
        gathered.append(lax.ppermute(packed, "store", pairs))
    near = fetch(packed, store[0], n_layer)
    last = n_layer - 3
    grads, partial = grads_and_scores(gathered, far, block, last, near)
    crossed = []
    for at in reversed(range(0, last, 2)):
        if at + 1 < last:
            (partial,) = scores(grads, far, block, at + 1, bf16)
        other = swap(partial, "layer", n_layer, 1)
        (mine,) = scores(grads, far, block, at, f32)
        joined = (mine + other.astype(f32)).astype(bf16)
        crossed.append(swap(joined, "layer", n_layer, at + 2))
    halves_of_other = scores(grads, near, block, 1, bf16, 2, [joined])
    (total,) = scores(grads, near, block, 0, f32)
    other = [swap(x, "layer", n_layer, 1) for x in halves_of_other]
    total = total + jnp.concatenate(other, axis=0).astype(f32)
    for x in crossed:
        total = total + x.astype(f32)
    return total.T


def solution(mesh):
    placed = (
        P("layer", ("grp", "store"), None, None),
        P("layer", ("grp", "store"), None, None),
        P(("grp", "store")),
        P("layer", None),
        P("layer", None, None),
        P("layer", None, None),
        P("layer", ("grp", "store"), None),
    )
    return jax.shard_map(
        functools.partial(on_device, mesh.shape["store"], mesh.shape["layer"]),
        mesh=mesh,
        in_specs=placed,
        out_specs=P(("grp", "store", "layer"), None),
        check_vma=False,
    )
```

```python
import functools

import jax
import jax.numpy as jnp
from jax import lax
from jax.experimental import pallas as pl
from jax.experimental.pallas import tpu as pltpu
from jax.sharding import PartitionSpec as P

norm_epsilon = 1e-05
f32 = jnp.float32
bf16 = jnp.bfloat16
S = 8
R = 64
B = 4
A = R // B
G = 8
H = 4
LANES = 128


def dot_nt(left, right):
    return lax.dot_general(left, right, (((1,), (1,)), ((), ())), preferred_element_type=f32)


def iota(shape, dim):
    return lax.broadcasted_iota(jnp.int32, shape, dim)


def factors_kernel(
    n_layer,
    hbm_lengths,
    hbm_hidden,
    hbm_cot,
    hbm_gain,
    hbm_inp,
    hbm_outp,
    hbm_store,
    packed,
    far,
    lengths,
    hidden,
    cot,
    gain,
    inp,
    outp,
    weights,
    in_acc,
    out_t,
    sems,
):
    blocks, step, width = hidden.shape
    rows = blocks * step
    queries = lengths.shape[0]
    full = queries // G * G * S
    half = rows - full
    mid, low = full // 2, half // 2

    def copy(source, target, at):
        return pltpu.make_async_copy(source, target, sems.at[at])

    def block_rows(r):
        at = pl.ds(pl.multiple_of(r * step, step), step)
        return copy(hbm_hidden.at[at, :], hidden.at[r], 5 + r)

    first = [copy(hbm_outp, outp, 0), copy(hbm_cot, cot, 1)]
    then = [copy(hbm_gain, gain, 2), copy(hbm_inp, inp, 3), copy(hbm_lengths, lengths, 4)]
    for piece in first + then + [block_rows(0)]:
        piece.start()
    odd = lax.rem(lax.axis_index("store"), 2)
    at_full = pl.multiple_of(odd * half, half)
    at_half = pl.multiple_of((1 - odd) * full, half)
    slab = store_copies(hbm_store, far, range(2, n_layer), sems, 5 + blocks, n_layer)
    for piece in first:
        piece.wait()

    @pl.when(odd >= 0)
    def _():
        for r in range(1, blocks):
            block_rows(r).start()
        for piece in slab:
            piece.start()

    whole = dot_nt(outp[...], cot[pl.ds(at_full, full), :])
    for t in range(full // LANES):
        out_t[t * R : (t + 1) * R, :] = whole[:, t * LANES : (t + 1) * LANES]
    out_t[full // LANES * R :, :half] = dot_nt(outp[...], cot[pl.ds(at_half, half), :])

    def part(t, b):
        return out_t[pl.ds(t * R + b, A, stride=B), :]

    row = mid + low
    for m in range(full // (G * S)):
        t, at = divmod(m * G * S, LANES)
        for b in range(0, B, 2):
            both = [part(t, b + c)[:, at : at + G * S] for c in range(2)]
            packed[row : row + A, :] = jnp.concatenate(both, axis=1).astype(bf16)
            row += A
    packed[row : row + A, :] = jnp.concatenate(
        [part(full // LANES, b)[:, :half] for b in range(B)], axis=1
    ).astype(bf16)

    for piece in then:
        piece.wait()
    weights[...] = inp[...] * gain[...]

    @pl.loop(0, blocks)
    def _(r):
        block_rows(r).wait()
        product = dot_nt(hidden[r], weights[...])
        total = jnp.zeros((step, LANES), f32)
        for at in range(0, width, LANES):
            wide = hidden[r, :, at : at + LANES].astype(f32)
            total += wide * wide
        mean_square = jnp.sum(total, axis=1, keepdims=True) * (1.0 / width)
        factor = product * lax.rsqrt(mean_square + norm_epsilon)
        at = pl.ds(pl.multiple_of(r * step, step), step)
        in_acc[at, :] = jnp.concatenate([factor, factor], axis=1)

    low_lanes = iota((S, LANES), 1) < R
    position = iota((S, LANES), 0)

    def in_rows(at, count):
        factor = in_acc[pl.ds(at, count), :]
        return [
            jnp.where(position < lengths[at // S + q], factor[q * S : (q + 1) * S], 0.0)
            for q in range(count // S)
        ]

    def side_by_side(tiles):
        both = zip(tiles[: len(tiles) // 2], tiles[len(tiles) // 2 :])
        return jnp.concatenate([jnp.where(low_lanes, x, y) for x, y in both], axis=0)

    packed[:mid, :] = side_by_side(in_rows(at_full, full)).astype(bf16)
    packed[mid : mid + low, :] = side_by_side(in_rows(at_half, half)).astype(bf16)
    for piece in slab:
        piece.wait()


def in_hbm(x):
    return pltpu.with_memory_space_constraint(x, pltpu.HBM)


def factors(n_layer, lengths, hidden, cotangent, gain, in_projection, out_projection, store):
    rows, width = hidden.shape
    blocks = 3
    far = (store.shape[0] // n_layer * (n_layer - 2), store.shape[1])
    args = (lengths, hidden, cotangent, gain, in_projection, out_projection, store)
    return pl.pallas_call(
        functools.partial(factors_kernel, n_layer),
        out_shape=[
            jax.ShapeDtypeStruct((rows, 2 * R), bf16),
            jax.ShapeDtypeStruct(far, bf16),
        ],
        in_specs=[pl.BlockSpec(memory_space=pl.ANY)] * len(args),
        out_specs=[pl.BlockSpec(memory_space=pltpu.VMEM)] * 2,
        scratch_shapes=[
            pltpu.SMEM(lengths.shape, jnp.int32),
            pltpu.VMEM((blocks, rows // blocks, width), bf16),
            pltpu.VMEM(cotangent.shape, bf16),
            pltpu.VMEM(gain.shape, bf16),
            pltpu.VMEM(in_projection.shape, bf16),
            pltpu.VMEM(out_projection.shape, bf16),
            pltpu.VMEM(in_projection.shape, bf16),
            pltpu.VMEM((rows, 2 * R), f32),
            pltpu.VMEM((-(-rows // LANES) * R, LANES), f32),
            pltpu.SemaphoreType.DMA((5 + blocks + n_layer - 2,)),
        ],
        compiler_params=pltpu.CompilerParams(vmem_limit_bytes=24 * 2**20),
        name="factors",
    )(*[in_hbm(x) for x in args])


def store_copies(store, slab, places, sems, at, n_layer):
    block = store.shape[0] // n_layer
    rows = 16 if block % 16 == 0 else 8
    me = lax.axis_index("layer")
    copies = []
    for to, k in enumerate(places):
        start = pl.multiple_of(partner(me, k, n_layer) * block, rows)
        target = slab.at[pl.ds(to * block, block)]
        copies.append(
            pltpu.make_async_copy(store.at[pl.ds(start, block)], target, sems.at[at + to])
        )
    return copies


def fetch_kernel(n_layer, packed, store, near, again, sems):
    copies = store_copies(store, near, range(2), sems, 0, n_layer)
    for copy in copies:
        copy.start()
    again[...] = packed[...]
    for copy in copies:
        copy.wait()


def fetch(packed, store, n_layer):
    rows, features = store.shape
    return pl.pallas_call(
        functools.partial(fetch_kernel, n_layer),
        out_shape=[
            jax.ShapeDtypeStruct((rows // n_layer * 2, features), bf16),
            jax.ShapeDtypeStruct(packed.shape, bf16),
        ],
        in_specs=[
            pl.BlockSpec(memory_space=pltpu.VMEM),
            pl.BlockSpec(memory_space=pl.ANY),
        ],
        out_specs=[pl.BlockSpec(memory_space=pltpu.VMEM)] * 2,
        scratch_shapes=[pltpu.SemaphoreType.DMA((2,))],
        compiler_params=pltpu.CompilerParams(vmem_limit_bytes=12 * 2**20),
        cost_estimate=pl.CostEstimate(
            flops=0, bytes_accessed=4 * rows * features // n_layer, transcendentals=0
        ),
        name="fetch",
    )(packed, in_hbm(store))


def spread_out(tile, owner):
    lanes = tile.shape[1]
    mine = (owner == iota((G, lanes), 0))[None]
    wide = jnp.where(mine, tile.astype(f32)[:, None, :], 0.0)
    return wide.reshape(A * G, lanes).astype(bf16)


def halves(tile):
    wide = tile.astype(f32)
    turned = jnp.concatenate([wide[:, R:], wide[:, :R]], axis=1)
    low = iota(wide.shape, 1) < R
    return [
        jnp.where(mask, x, 0.0).astype(bf16)
        for x in (wide, turned)
        for mask in (low, jnp.logical_not(low))
    ]


def diagonal(low, high):
    zero = jnp.zeros_like(low)
    left = jnp.concatenate([low, high, zero, zero], axis=0)
    right = jnp.concatenate([zero, zero, low, high], axis=0)
    return jnp.concatenate([left, right], axis=1)


def build_grads(shards, base, row0, full_groups, grads):
    mid = full_groups * G * S // 2
    low = H * S // 2
    lane = iota((G, 2 * 128), 1)
    whole_owner = lax.rem(lane, G * S) // S
    half_owner = lax.rem(lane, H * S) // S + H * (lane // 128)

    def whole(shard):
        found = []
        pairs = {}
        for m in range(full_groups):
            first = m % (full_groups // 2)
            if first not in pairs:
                pairs[first] = halves(
                    shards[base + shard, first * G * S : (first + 1) * G * S, :]
                )
            plain_low, plain_high, turned_low, turned_high = pairs[first]
            weights = (
                diagonal(plain_low, turned_high)
                if m < full_groups // 2
                else diagonal(turned_low, plain_high)
            )
            at = mid + low + m * 2 * A
            tile = jnp.concatenate(
                [shards[base + shard, at : at + A, :], shards[base + shard, at + A : at + 2 * A, :]],
                axis=1,
            )
            found.append((spread_out(tile, whole_owner), weights))
        return found

    def joined(shard):
        tiles, weights = [], []
        for s in (shard, shard + 1):
            plain_low, plain_high, turned_low, turned_high = halves(
                shards[base + s, mid : mid + low, :]
            )
            weights.append(
                diagonal(
                    jnp.concatenate([plain_low, turned_low], axis=0),
                    jnp.concatenate([turned_high, plain_high], axis=0),
                )
            )
            at = mid + low + full_groups * 2 * A
            tiles.append(shards[base + s, at : at + A, :])
        return [
            (
                spread_out(jnp.concatenate(tiles, axis=1), half_owner),
                jnp.concatenate(weights, axis=0),
            )
        ]

    groups = []
    for shard in (0, 2):
        groups += whole(shard) + joined(shard) + whole(shard + 1)
    for at in range(0, len(groups), 2):
        first, second = [jnp.dot(x, w, preferred_element_type=f32) for x, w in groups[at : at + 2]]
        for a in range(A):
            pair = [x[a * G : (a + 1) * G] for x in (first, second)]
            grads[pl.ds(row0 + at * G, 2 * G), a * 256 : (a + 1) * 256] = jnp.concatenate(
                pair, axis=0
            ).astype(bf16)


def source(to, away, n):
    if n != 4:
        return (to + away) % n
    place = ((to ^ to // 2) + away) % n
    return place ^ place // 2


def grads_kernel(n_store, full_groups, k, *refs):
    gathered = refs[:n_store]
    slab, _, grads, out, shards = refs[n_store:]
    me_store = lax.axis_index("store")
    for away, block in enumerate(gathered):
        shards[source(me_store, away, n_store)] = block[...]
    four = 4 * (full_groups * G + H)
    if n_store == 4:
        build_grads(shards, 0, 0, full_groups, grads)
    else:

        @pl.loop(0, n_store // 4)
        def _(at):
            build_grads(shards, at * 4, pl.multiple_of(at * four, 16), full_groups, grads)

    scores_kernel(k, grads, slab, out)


def scores_kernel(k, grads, slab, *refs, skip=0):
    outs = refs[skip:]
    block = outs[0].shape[1]
    total = dot_nt(slab[k * block : (k + 1) * block, :], grads[...]).T
    at = 0
    for out in outs:
        out[...] = total[at : at + out.shape[0]].astype(out.dtype)
        at += out.shape[0]


def partner(me, k, n):
    return jnp.bitwise_xor(me, k) if n & (n - 1) == 0 else lax.rem(n + k - me, n)


def swap(x, axis, n, k):
    pairs = [(i, i ^ k if n & (n - 1) == 0 else (n + k - i) % n) for i in range(n)]
    return lax.ppermute(x, axis, pairs)


def grads_and_scores(gathered, slab, block, at, after):
    n_store = len(gathered)
    queries = gathered[0].shape[0] // S
    vmem = pl.BlockSpec(memory_space=pltpu.VMEM)
    return pl.pallas_call(
        functools.partial(grads_kernel, n_store, queries // G, at),
        out_shape=[
            jax.ShapeDtypeStruct((n_store * queries, slab.shape[1]), bf16),
            jax.ShapeDtypeStruct((n_store * queries, block), bf16),
        ],
        in_specs=[vmem] * (n_store + 1) + [pl.BlockSpec(memory_space=pl.ANY)],
        out_specs=[vmem] * 2,
        scratch_shapes=[pltpu.VMEM((n_store,) + gathered[0].shape, bf16)],
        compiler_params=pltpu.CompilerParams(vmem_limit_bytes=24 * 2**20),
        name="grads",
    )(*gathered, slab, after)


def scores(grads, slab, block, at, kind, pieces=1, after=()):
    queries, features = grads.shape
    vmem = pl.BlockSpec(memory_space=pltpu.VMEM)
    return pl.pallas_call(
        functools.partial(scores_kernel, at, skip=len(after)),
        out_shape=[jax.ShapeDtypeStruct((queries // pieces, block), kind)] * pieces,
        in_specs=[vmem] * 2 + [pl.BlockSpec(memory_space=pl.ANY)] * len(after),
        out_specs=[vmem] * pieces,
        compiler_params=pltpu.CompilerParams(vmem_limit_bytes=24 * 2**20),
        cost_estimate=pl.CostEstimate(
            flops=2 * queries * block * features,
            bytes_accessed=2 * (queries + block) * features,
            transcendentals=0,
        ),
        name="scores",
    )(grads, slab, *after)


def on_device(n_store, n_layer, hidden, cotangent, lengths, norm_gain, in_proj, out_proj, store):
    queries, positions, width = hidden.shape[1:]
    block = store.shape[1] // n_layer
    packed, far = factors(
        n_layer,
        lengths,
        hidden.reshape(queries * positions, width),
        cotangent.reshape(queries * positions, cotangent.shape[3]),
        norm_gain,
        in_proj[0],
        out_proj[0],
        store[0],
    )
    near, again = fetch(packed, store[0], n_layer)
    gathered = [packed]
    for away in range(1, n_store):
        pairs = [(source(to, away, n_store), to) for to in range(n_store)]
        gathered.append(lax.ppermute(again if away == 1 else packed, "store", pairs))
    last = n_layer - 3
    grads, partial = grads_and_scores(gathered, far, block, last, near)
    crossed = []
    for at in reversed(range(0, last, 2)):
        if at + 1 < last:
            (partial,) = scores(grads, far, block, at + 1, bf16)
        other = swap(partial, "layer", n_layer, 1)
        (mine,) = scores(grads, far, block, at, f32)
        joined = (mine + other.astype(f32)).astype(bf16)
        crossed.append(swap(joined, "layer", n_layer, at + 2))
    halves_of_other = scores(grads, near, block, 1, bf16, 2, [joined])
    (total,) = scores(grads, near, block, 0, f32)
    other = [swap(x, "layer", n_layer, 1) for x in halves_of_other]
    total = total + jnp.concatenate(other, axis=0).astype(f32)
    for x in crossed:
        total = total + x.astype(f32)
    return total.T


def solution(mesh):
    placed = (
        P("layer", ("grp", "store"), None, None),
        P("layer", ("grp", "store"), None, None),
        P(("grp", "store")),
        P("layer", None),
        P("layer", None, None),
        P("layer", None, None),
        P("layer", ("grp", "store"), None),
    )
    return jax.shard_map(
        functools.partial(on_device, mesh.shape["store"], mesh.shape["layer"]),
        mesh=mesh,
        in_specs=placed,
        out_specs=P(("grp", "store", "layer"), None),
        check_vma=False,
    )
```

```python
import functools

import jax
import jax.numpy as jnp
from jax import lax
from jax.experimental import pallas as pl
from jax.experimental.pallas import tpu as pltpu
from jax.sharding import PartitionSpec as P

norm_epsilon = 1e-05
f32 = jnp.float32
bf16 = jnp.bfloat16
S = 8
R = 64
B = 4
A = R // B
G = 8
H = 4
LANES = 128


def dot_nt(left, right):
    return lax.dot_general(left, right, (((1,), (1,)), ((), ())), preferred_element_type=f32)


def iota(shape, dim):
    return lax.broadcasted_iota(jnp.int32, shape, dim)


def factors_kernel(
    n_layer,
    hbm_lengths,
    hbm_hidden,
    hbm_cot,
    hbm_gain,
    hbm_inp,
    hbm_outp,
    hbm_store,
    packed,
    far,
    lengths,
    hidden,
    cot,
    gain,
    inp,
    outp,
    weights,
    in_acc,
    out_t,
    sems,
):
    blocks, step, width = hidden.shape
    rows = blocks * step
    queries = lengths.shape[0]
    full = queries // G * G * S
    half = rows - full
    mid, low = full // 2, half // 2

    def copy(source, target, at):
        return pltpu.make_async_copy(source, target, sems.at[at])

    def block_rows(r):
        at = pl.ds(pl.multiple_of(r * step, step), step)
        return copy(hbm_hidden.at[at, :], hidden.at[r], 5 + r)

    first = [copy(hbm_outp, outp, 0), copy(hbm_cot, cot, 1)]
    then = [copy(hbm_gain, gain, 2), copy(hbm_inp, inp, 3), copy(hbm_lengths, lengths, 4)]
    for piece in first + then + [block_rows(0)]:
        piece.start()
    odd = lax.rem(lax.axis_index("store"), 2)
    at_full = pl.multiple_of(odd * half, half)
    at_half = pl.multiple_of((1 - odd) * full, half)
    slab = store_copies(hbm_store, far, range(2, n_layer), sems, 5 + blocks, n_layer)
    for piece in first:
        piece.wait()

    @pl.when(odd >= 0)
    def _():
        for r in range(1, blocks):
            block_rows(r).start()
        for piece in slab:
            piece.start()

    whole = dot_nt(outp[...], cot[pl.ds(at_full, full), :])
    for t in range(full // LANES):
        out_t[t * R : (t + 1) * R, :] = whole[:, t * LANES : (t + 1) * LANES]
    out_t[full // LANES * R :, :half] = dot_nt(outp[...], cot[pl.ds(at_half, half), :])

    def part(t, b):
        return out_t[pl.ds(t * R + b, A, stride=B), :]

    row = mid + low
    for m in range(full // (G * S)):
        t, at = divmod(m * G * S, LANES)
        for b in range(0, B, 2):
            both = [part(t, b + c)[:, at : at + G * S] for c in range(2)]
            packed[row : row + A, :] = jnp.concatenate(both, axis=1).astype(bf16)
            row += A
    packed[row : row + A, :] = jnp.concatenate(
        [part(full // LANES, b)[:, :half] for b in range(B)], axis=1
    ).astype(bf16)

    for piece in then:
        piece.wait()
    weights[...] = inp[...] * gain[...]

    @pl.loop(0, blocks)
    def _(r):
        block_rows(r).wait()
        product = dot_nt(hidden[r], weights[...])
        total = jnp.zeros((step, LANES), f32)
        for at in range(0, width, LANES):
            wide = hidden[r, :, at : at + LANES].astype(f32)
            total += wide * wide
        mean_square = jnp.sum(total, axis=1, keepdims=True) * (1.0 / width)
        factor = product * lax.rsqrt(mean_square + norm_epsilon)
        at = pl.ds(pl.multiple_of(r * step, step), step)
        in_acc[at, :] = jnp.concatenate([factor, factor], axis=1)

    low_lanes = iota((S, LANES), 1) < R
    position = iota((S, LANES), 0)

    def in_rows(at, count):
        factor = in_acc[pl.ds(at, count), :]
        return [
            jnp.where(position < lengths[at // S + q], factor[q * S : (q + 1) * S], 0.0)
            for q in range(count // S)
        ]

    def side_by_side(tiles):
        both = zip(tiles[: len(tiles) // 2], tiles[len(tiles) // 2 :])
        return jnp.concatenate([jnp.where(low_lanes, x, y) for x, y in both], axis=0)

    packed[:mid, :] = side_by_side(in_rows(at_full, full)).astype(bf16)
    packed[mid : mid + low, :] = side_by_side(in_rows(at_half, half)).astype(bf16)
    for piece in slab:
        piece.wait()


def in_hbm(x):
    return pltpu.with_memory_space_constraint(x, pltpu.HBM)


def factors(n_layer, lengths, hidden, cotangent, gain, in_projection, out_projection, store):
    rows, width = hidden.shape
    blocks = 3
    far = (store.shape[0] // n_layer * (n_layer - 2), store.shape[1])
    args = (lengths, hidden, cotangent, gain, in_projection, out_projection, store)
    return pl.pallas_call(
        functools.partial(factors_kernel, n_layer),
        out_shape=[
            jax.ShapeDtypeStruct((rows, 2 * R), bf16),
            jax.ShapeDtypeStruct(far, bf16),
        ],
        in_specs=[pl.BlockSpec(memory_space=pl.ANY)] * len(args),
        out_specs=[pl.BlockSpec(memory_space=pltpu.VMEM)] * 2,
        scratch_shapes=[
            pltpu.SMEM(lengths.shape, jnp.int32),
            pltpu.VMEM((blocks, rows // blocks, width), bf16),
            pltpu.VMEM(cotangent.shape, bf16),
            pltpu.VMEM(gain.shape, bf16),
            pltpu.VMEM(in_projection.shape, bf16),
            pltpu.VMEM(out_projection.shape, bf16),
            pltpu.VMEM(in_projection.shape, bf16),
            pltpu.VMEM((rows, 2 * R), f32),
            pltpu.VMEM((-(-rows // LANES) * R, LANES), f32),
            pltpu.SemaphoreType.DMA((5 + blocks + n_layer - 2,)),
        ],
        compiler_params=pltpu.CompilerParams(vmem_limit_bytes=24 * 2**20),
        name="factors",
    )(*[in_hbm(x) for x in args])


def store_copies(store, slab, places, sems, at, n_layer):
    block = store.shape[0] // n_layer
    rows = 16 if block % 16 == 0 else 8
    me = lax.axis_index("layer")
    copies = []
    for to, k in enumerate(places):
        start = pl.multiple_of(partner(me, k, n_layer) * block, rows)
        target = slab.at[pl.ds(to * block, block)]
        copies.append(
            pltpu.make_async_copy(store.at[pl.ds(start, block)], target, sems.at[at + to])
        )
    return copies


def fetch_kernel(n_layer, after, store, near, sems):
    copies = store_copies(store, near, range(2), sems, 0, n_layer)
    for copy in copies:
        copy.start()
    for copy in copies:
        copy.wait()


def fetch(after, store, n_layer):
    rows, features = store.shape
    return pl.pallas_call(
        functools.partial(fetch_kernel, n_layer),
        out_shape=jax.ShapeDtypeStruct((rows // n_layer * 2, features), bf16),
        in_specs=[pl.BlockSpec(memory_space=pl.ANY)] * 2,
        out_specs=pl.BlockSpec(memory_space=pltpu.VMEM),
        scratch_shapes=[pltpu.SemaphoreType.DMA((2,))],
        compiler_params=pltpu.CompilerParams(vmem_limit_bytes=12 * 2**20),
        cost_estimate=pl.CostEstimate(
            flops=0, bytes_accessed=4 * rows * features // n_layer, transcendentals=0
        ),
        name="fetch",
    )(after, in_hbm(store))


def spread_out(tile, owner):
    lanes = tile.shape[1]
    mine = (owner == iota((G, lanes), 0))[None]
    wide = jnp.where(mine, tile.astype(f32)[:, None, :], 0.0)
    return wide.reshape(A * G, lanes).astype(bf16)


def halves(tile):
    wide = tile.astype(f32)
    turned = jnp.concatenate([wide[:, R:], wide[:, :R]], axis=1)
    low = iota(wide.shape, 1) < R
    return [
        jnp.where(mask, x, 0.0).astype(bf16)
        for x in (wide, turned)
        for mask in (low, jnp.logical_not(low))
    ]


def diagonal(low, high):
    zero = jnp.zeros_like(low)
    left = jnp.concatenate([low, high, zero, zero], axis=0)
    right = jnp.concatenate([zero, zero, low, high], axis=0)
    return jnp.concatenate([left, right], axis=1)


def build_grads(shards, base, row0, full_groups, grads):
    mid = full_groups * G * S // 2
    low = H * S // 2
    lane = iota((G, 2 * 128), 1)
    whole_owner = lax.rem(lane, G * S) // S
    half_owner = lax.rem(lane, H * S) // S + H * (lane // 128)

    def whole(shard):
        found = []
        pairs = {}
        for m in range(full_groups):
            first = m % (full_groups // 2)
            if first not in pairs:
                pairs[first] = halves(
                    shards[base + shard, first * G * S : (first + 1) * G * S, :]
                )
            plain_low, plain_high, turned_low, turned_high = pairs[first]
            weights = (
                diagonal(plain_low, turned_high)
                if m < full_groups // 2
                else diagonal(turned_low, plain_high)
            )
            at = mid + low + m * 2 * A
            tile = jnp.concatenate(
                [shards[base + shard, at : at + A, :], shards[base + shard, at + A : at + 2 * A, :]],
                axis=1,
            )
            found.append((spread_out(tile, whole_owner), weights))
        return found

    def joined(shard):
        tiles, weights = [], []
        for s in (shard, shard + 1):
            plain_low, plain_high, turned_low, turned_high = halves(
                shards[base + s, mid : mid + low, :]
            )
            weights.append(
                diagonal(
                    jnp.concatenate([plain_low, turned_low], axis=0),
                    jnp.concatenate([turned_high, plain_high], axis=0),
                )
            )
            at = mid + low + full_groups * 2 * A
            tiles.append(shards[base + s, at : at + A, :])
        return [
            (
                spread_out(jnp.concatenate(tiles, axis=1), half_owner),
                jnp.concatenate(weights, axis=0),
            )
        ]

    groups = []
    for shard in (0, 2):
        groups += whole(shard) + joined(shard) + whole(shard + 1)
    for at in range(0, len(groups), 2):
        first, second = [jnp.dot(x, w, preferred_element_type=f32) for x, w in groups[at : at + 2]]
        for a in range(A):
            pair = [x[a * G : (a + 1) * G] for x in (first, second)]
            grads[pl.ds(row0 + at * G, 2 * G), a * 256 : (a + 1) * 256] = jnp.concatenate(
                pair, axis=0
            ).astype(bf16)


def source(to, away, n):
    if n != 4:
        return (to + away) % n
    place = ((to ^ to // 2) + away) % n
    return place ^ place // 2


def shift_order(n):
    return [2, 1, 3] if n == 4 else list(range(1, n))


def grads_kernel(n_store, full_groups, k, *refs):
    gathered = refs[:n_store]
    slab, _, grads, *outs, shards = refs[n_store:]
    me_store = lax.axis_index("store")
    for away, block in zip([0] + shift_order(n_store), gathered):
        shards[source(me_store, away, n_store)] = block[...]
    four = 4 * (full_groups * G + H)
    if n_store == 4:
        build_grads(shards, 0, 0, full_groups, grads)
    else:

        @pl.loop(0, n_store // 4)
        def _(at):
            build_grads(shards, at * 4, pl.multiple_of(at * four, 16), full_groups, grads)

    scores_kernel(k, grads, slab, *outs)


def scores_kernel(k, grads, slab, *refs, skip=0):
    outs = refs[skip:]
    block = outs[0].shape[1]
    total = dot_nt(slab[k * block : (k + 1) * block, :], grads[...]).T
    at = 0
    for out in outs:
        out[...] = total[at : at + out.shape[0]].astype(out.dtype)
        at += out.shape[0]


def partner(me, k, n):
    return jnp.bitwise_xor(me, k) if n & (n - 1) == 0 else lax.rem(n + k - me, n)


def swap(x, axis, n, k):
    pairs = [(i, i ^ k if n & (n - 1) == 0 else (n + k - i) % n) for i in range(n)]
    return lax.ppermute(x, axis, pairs)


def grads_and_scores(gathered, slab, block, at, after):
    n_store = len(gathered)
    queries = gathered[0].shape[0] // S
    vmem = pl.BlockSpec(memory_space=pltpu.VMEM)
    return pl.pallas_call(
        functools.partial(grads_kernel, n_store, queries // G, at),
        out_shape=[
            jax.ShapeDtypeStruct((n_store * queries, slab.shape[1]), bf16),
        ]
        + [jax.ShapeDtypeStruct((n_store * queries // 2, block), bf16)] * 2,
        in_specs=[vmem] * (n_store + 1) + [pl.BlockSpec(memory_space=pl.ANY)],
        out_specs=[vmem] * 3,
        scratch_shapes=[pltpu.VMEM((n_store,) + gathered[0].shape, bf16)],
        compiler_params=pltpu.CompilerParams(vmem_limit_bytes=24 * 2**20),
        name="grads",
    )(*gathered, slab, after)


def scores(grads, slab, block, at, kind, pieces=1, after=()):
    queries, features = grads.shape
    vmem = pl.BlockSpec(memory_space=pltpu.VMEM)
    return pl.pallas_call(
        functools.partial(scores_kernel, at, skip=len(after)),
        out_shape=[jax.ShapeDtypeStruct((queries // pieces, block), kind)] * pieces,
        in_specs=[vmem] * 2 + [pl.BlockSpec(memory_space=pl.ANY)] * len(after),
        out_specs=[vmem] * pieces,
        compiler_params=pltpu.CompilerParams(vmem_limit_bytes=24 * 2**20),
        cost_estimate=pl.CostEstimate(
            flops=2 * queries * block * features,
            bytes_accessed=2 * (queries + block) * features,
            transcendentals=0,
        ),
        name="scores",
    )(grads, slab, *after)


def on_device(n_store, n_layer, hidden, cotangent, lengths, norm_gain, in_proj, out_proj, store):
    queries, positions, width = hidden.shape[1:]
    block = store.shape[1] // n_layer
    packed, far = factors(
        n_layer,
        lengths,
        hidden.reshape(queries * positions, width),
        cotangent.reshape(queries * positions, cotangent.shape[3]),
        norm_gain,
        in_proj[0],
        out_proj[0],
        store[0],
    )
    gathered = [packed]
    for away in shift_order(n_store):
        pairs = [(source(to, away, n_store), to) for to in range(n_store)]
        gathered.append(lax.ppermute(packed, "store", pairs))
    near = fetch(packed, store[0], n_layer)
    last = n_layer - 3
    grads, *partial = grads_and_scores(gathered, far, block, last, near)
    crossed = []
    for at in reversed(range(0, last, 2)):
        if at + 1 < last:
            partial = scores(grads, far, block, at + 1, bf16)
        other = jnp.concatenate([swap(x, "layer", n_layer, 1) for x in partial], axis=0)
        (mine,) = scores(grads, far, block, at, f32)
        joined = (mine + other.astype(f32)).astype(bf16)
        crossed.append(swap(joined, "layer", n_layer, at + 2))
    halves_of_other = scores(grads, near, block, 1, bf16, 2, [joined])
    (total,) = scores(grads, near, block, 0, f32)
    other = [swap(x, "layer", n_layer, 1) for x in halves_of_other]
    total = total + jnp.concatenate(other, axis=0).astype(f32)
    for x in crossed:
        total = total + x.astype(f32)
    return total.T


def solution(mesh):
    placed = (
        P("layer", ("grp", "store"), None, None),
        P("layer", ("grp", "store"), None, None),
        P(("grp", "store")),
        P("layer", None),
        P("layer", None, None),
        P("layer", None, None),
        P("layer", ("grp", "store"), None),
    )
    return jax.shard_map(
        functools.partial(on_device, mesh.shape["store"], mesh.shape["layer"]),
        mesh=mesh,
        in_specs=placed,
        out_specs=P(("grp", "store", "layer"), None),
        check_vma=False,
    )
```

```python
import functools

import jax
import jax.numpy as jnp
from jax import lax
from jax.experimental import pallas as pl
from jax.experimental.pallas import tpu as pltpu
from jax.sharding import PartitionSpec as P

norm_epsilon = 1e-05
f32 = jnp.float32
bf16 = jnp.bfloat16
S = 8
R = 64
B = 4
A = R // B
G = 8
H = 4
LANES = 128


def dot_nt(left, right):
    return lax.dot_general(left, right, (((1,), (1,)), ((), ())), preferred_element_type=f32)


def iota(shape, dim):
    return lax.broadcasted_iota(jnp.int32, shape, dim)


def factors_kernel(
    n_layer,
    hbm_lengths,
    hbm_hidden,
    hbm_cot,
    hbm_gain,
    hbm_inp,
    hbm_outp,
    hbm_store,
    packed,
    far,
    lengths,
    hidden,
    cot,
    gain,
    inp,
    outp,
    weights,
    in_acc,
    out_t,
    sems,
):
    blocks, step, width = hidden.shape
    rows = blocks * step
    queries = lengths.shape[0]
    full = queries // G * G * S
    half = rows - full
    mid, low = full // 2, half // 2

    def copy(source, target, at):
        return pltpu.make_async_copy(source, target, sems.at[at])

    def block_rows(r):
        at = pl.ds(pl.multiple_of(r * step, step), step)
        return copy(hbm_hidden.at[at, :], hidden.at[r], 5 + r)

    first = [copy(hbm_outp, outp, 0), copy(hbm_cot, cot, 1)]
    then = [copy(hbm_gain, gain, 2), copy(hbm_inp, inp, 3), copy(hbm_lengths, lengths, 4)]
    for piece in first + then + [block_rows(0)]:
        piece.start()
    odd = lax.rem(lax.axis_index("store"), 2)
    at_full = pl.multiple_of(odd * half, half)
    at_half = pl.multiple_of((1 - odd) * full, half)
    slab = store_copies(hbm_store, far, range(2, n_layer), sems, 5 + blocks, n_layer)
    for piece in first:
        piece.wait()

    @pl.when(odd >= 0)
    def _():
        for r in range(1, blocks):
            block_rows(r).start()
        for piece in slab:
            piece.start()

    whole = dot_nt(outp[...], cot[pl.ds(at_full, full), :])
    for t in range(full // LANES):
        out_t[t * R : (t + 1) * R, :] = whole[:, t * LANES : (t + 1) * LANES]
    out_t[full // LANES * R :, :half] = dot_nt(outp[...], cot[pl.ds(at_half, half), :])

    def part(t, b):
        return out_t[pl.ds(t * R + b, A, stride=B), :]

    row = mid + low
    for m in range(full // (G * S)):
        t, at = divmod(m * G * S, LANES)
        for b in range(0, B, 2):
            both = [part(t, b + c)[:, at : at + G * S] for c in range(2)]
            packed[row : row + A, :] = jnp.concatenate(both, axis=1).astype(bf16)
            row += A
    packed[row : row + A, :] = jnp.concatenate(
        [part(full // LANES, b)[:, :half] for b in range(B)], axis=1
    ).astype(bf16)

    for piece in then:
        piece.wait()
    weights[...] = inp[...] * gain[...]
    position = iota((S, R), 0)

    @pl.loop(0, blocks)
    def _(r):
        block_rows(r).wait()
        product = dot_nt(hidden[r], weights[...])
        total = jnp.zeros((step, LANES), f32)
        for at in range(0, width, LANES):
            wide = hidden[r, :, at : at + LANES].astype(f32)
            total += wide * wide
        mean_square = jnp.sum(total, axis=1, keepdims=True) * (1.0 / width)
        factor = product * lax.rsqrt(mean_square + norm_epsilon)
        at = pl.ds(pl.multiple_of(r * step, step), step)
        live = [
            jnp.where(position < lengths[r * (step // S) + q], factor[q * S : (q + 1) * S], 0.0)
            for q in range(step // S)
        ]
        factor = jnp.concatenate(live, axis=0)
        in_acc[at, :] = jnp.concatenate([factor, factor], axis=1)

    low_lanes = iota((1, LANES), 1) < R

    def side_by_side(at, count):
        left = in_acc[pl.ds(at, count // 2), :]
        right = in_acc[pl.ds(at + count // 2, count // 2), :]
        return jnp.where(low_lanes, left, right).astype(bf16)

    packed[:mid, :] = side_by_side(at_full, full)
    packed[mid : mid + low, :] = side_by_side(at_half, half)
    for piece in slab:
        piece.wait()


def in_hbm(x):
    return pltpu.with_memory_space_constraint(x, pltpu.HBM)


def factors(n_layer, lengths, hidden, cotangent, gain, in_projection, out_projection, store):
    rows, width = hidden.shape
    blocks = 3
    far = (store.shape[0] // n_layer * (n_layer - 2), store.shape[1])
    args = (lengths, hidden, cotangent, gain, in_projection, out_projection, store)
    return pl.pallas_call(
        functools.partial(factors_kernel, n_layer),
        out_shape=[
            jax.ShapeDtypeStruct((rows, 2 * R), bf16),
            jax.ShapeDtypeStruct(far, bf16),
        ],
        in_specs=[pl.BlockSpec(memory_space=pl.ANY)] * len(args),
        out_specs=[pl.BlockSpec(memory_space=pltpu.VMEM)] * 2,
        scratch_shapes=[
            pltpu.SMEM(lengths.shape, jnp.int32),
            pltpu.VMEM((blocks, rows // blocks, width), bf16),
            pltpu.VMEM(cotangent.shape, bf16),
            pltpu.VMEM(gain.shape, bf16),
            pltpu.VMEM(in_projection.shape, bf16),
            pltpu.VMEM(out_projection.shape, bf16),
            pltpu.VMEM(in_projection.shape, bf16),
            pltpu.VMEM((rows, 2 * R), f32),
            pltpu.VMEM((-(-rows // LANES) * R, LANES), f32),
            pltpu.SemaphoreType.DMA((5 + blocks + n_layer - 2,)),
        ],
        compiler_params=pltpu.CompilerParams(vmem_limit_bytes=24 * 2**20),
        name="factors",
    )(*[in_hbm(x) for x in args])


def store_copies(store, slab, places, sems, at, n_layer):
    block = store.shape[0] // n_layer
    rows = 16 if block % 16 == 0 else 8
    me = lax.axis_index("layer")
    copies = []
    for to, k in enumerate(places):
        start = pl.multiple_of(partner(me, k, n_layer) * block, rows)
        target = slab.at[pl.ds(to * block, block)]
        copies.append(
            pltpu.make_async_copy(store.at[pl.ds(start, block)], target, sems.at[at + to])
        )
    return copies


def fetch_kernel(n_layer, after, store, near, sems):
    copies = store_copies(store, near, range(2), sems, 0, n_layer)
    for copy in copies:
        copy.start()
    for copy in copies:
        copy.wait()


def fetch(after, store, n_layer):
    rows, features = store.shape
    return pl.pallas_call(
        functools.partial(fetch_kernel, n_layer),
        out_shape=jax.ShapeDtypeStruct((rows // n_layer * 2, features), bf16),
        in_specs=[pl.BlockSpec(memory_space=pl.ANY)] * 2,
        out_specs=pl.BlockSpec(memory_space=pltpu.VMEM),
        scratch_shapes=[pltpu.SemaphoreType.DMA((2,))],
        compiler_params=pltpu.CompilerParams(vmem_limit_bytes=12 * 2**20),
        cost_estimate=pl.CostEstimate(
            flops=0, bytes_accessed=4 * rows * features // n_layer, transcendentals=0
        ),
        name="fetch",
    )(after, in_hbm(store))


def spread_out(tile, owner):
    lanes = tile.shape[1]
    mine = (owner == iota((G, lanes), 0))[None]
    wide = jnp.where(mine, tile.astype(f32)[:, None, :], 0.0)
    return wide.reshape(A * G, lanes).astype(bf16)


def halves(tile):
    wide = tile.astype(f32)
    turned = jnp.concatenate([wide[:, R:], wide[:, :R]], axis=1)
    low = iota(wide.shape, 1) < R
    return [
        jnp.where(mask, x, 0.0).astype(bf16)
        for x in (wide, turned)
        for mask in (low, jnp.logical_not(low))
    ]


def diagonal(low, high):
    zero = jnp.zeros_like(low)
    left = jnp.concatenate([low, high, zero, zero], axis=0)
    right = jnp.concatenate([zero, zero, low, high], axis=0)
    return jnp.concatenate([left, right], axis=1)


def build_grads(shards, base, row0, full_groups, grads):
    mid = full_groups * G * S // 2
    low = H * S // 2
    lane = iota((G, 2 * 128), 1)
    whole_owner = lax.rem(lane, G * S) // S
    half_owner = lax.rem(lane, H * S) // S + H * (lane // 128)

    def whole(shard):
        found = []
        pairs = {}
        for m in range(full_groups):
            first = m % (full_groups // 2)
            if first not in pairs:
                pairs[first] = halves(
                    shards[base + shard, first * G * S : (first + 1) * G * S, :]
                )
            plain_low, plain_high, turned_low, turned_high = pairs[first]
            weights = (
                diagonal(plain_low, turned_high)
                if m < full_groups // 2
                else diagonal(turned_low, plain_high)
            )
            at = mid + low + m * 2 * A
            tile = jnp.concatenate(
                [shards[base + shard, at : at + A, :], shards[base + shard, at + A : at + 2 * A, :]],
                axis=1,
            )
            found.append((spread_out(tile, whole_owner), weights))
        return found

    def joined(shard):
        tiles, weights = [], []
        for s in (shard, shard + 1):
            plain_low, plain_high, turned_low, turned_high = halves(
                shards[base + s, mid : mid + low, :]
            )
            weights.append(
                diagonal(
                    jnp.concatenate([plain_low, turned_low], axis=0),
                    jnp.concatenate([turned_high, plain_high], axis=0),
                )
            )
            at = mid + low + full_groups * 2 * A
            tiles.append(shards[base + s, at : at + A, :])
        return [
            (
                spread_out(jnp.concatenate(tiles, axis=1), half_owner),
                jnp.concatenate(weights, axis=0),
            )
        ]

    groups = []
    for shard in (0, 2):
        groups += whole(shard) + joined(shard) + whole(shard + 1)
    for at in range(0, len(groups), 2):
        first, second = [jnp.dot(x, w, preferred_element_type=f32) for x, w in groups[at : at + 2]]
        for a in range(A):
            pair = [x[a * G : (a + 1) * G] for x in (first, second)]
            grads[pl.ds(row0 + at * G, 2 * G), a * 256 : (a + 1) * 256] = jnp.concatenate(
                pair, axis=0
            ).astype(bf16)


def source(to, away, n):
    if n != 4:
        return (to + away) % n
    place = ((to ^ to // 2) + away) % n
    return place ^ place // 2


def grads_kernel(n_store, full_groups, k, *refs):
    gathered = refs[:n_store]
    slab, _, grads, out, shards = refs[n_store:]
    me_store = lax.axis_index("store")
    for away, block in enumerate(gathered):
        shards[source(me_store, away, n_store)] = block[...]
    four = 4 * (full_groups * G + H)
    if n_store == 4:
        build_grads(shards, 0, 0, full_groups, grads)
    else:

        @pl.loop(0, n_store // 4)
        def _(at):
            build_grads(shards, at * 4, pl.multiple_of(at * four, 16), full_groups, grads)

    scores_kernel(k, grads, slab, out)


def scores_kernel(k, grads, slab, *refs, skip=0):
    outs = refs[skip:]
    block = outs[0].shape[1]
    total = dot_nt(slab[k * block : (k + 1) * block, :], grads[...]).T
    at = 0
    for out in outs:
        out[...] = total[at : at + out.shape[0]].astype(out.dtype)
        at += out.shape[0]


def partner(me, k, n):
    return jnp.bitwise_xor(me, k) if n & (n - 1) == 0 else lax.rem(n + k - me, n)


def swap(x, axis, n, k):
    pairs = [(i, i ^ k if n & (n - 1) == 0 else (n + k - i) % n) for i in range(n)]
    return lax.ppermute(x, axis, pairs)


def grads_and_scores(gathered, slab, block, at, after):
    n_store = len(gathered)
    queries = gathered[0].shape[0] // S
    vmem = pl.BlockSpec(memory_space=pltpu.VMEM)
    return pl.pallas_call(
        functools.partial(grads_kernel, n_store, queries // G, at),
        out_shape=[
            jax.ShapeDtypeStruct((n_store * queries, slab.shape[1]), bf16),
            jax.ShapeDtypeStruct((n_store * queries, block), bf16),
        ],
        in_specs=[vmem] * (n_store + 1) + [pl.BlockSpec(memory_space=pl.ANY)],
        out_specs=[vmem] * 2,
        scratch_shapes=[pltpu.VMEM((n_store,) + gathered[0].shape, bf16)],
        compiler_params=pltpu.CompilerParams(vmem_limit_bytes=24 * 2**20),
        name="grads",
    )(*gathered, slab, after)


def scores(grads, slab, block, at, kind, pieces=1, after=()):
    queries, features = grads.shape
    vmem = pl.BlockSpec(memory_space=pltpu.VMEM)
    return pl.pallas_call(
        functools.partial(scores_kernel, at, skip=len(after)),
        out_shape=[jax.ShapeDtypeStruct((queries // pieces, block), kind)] * pieces,
        in_specs=[vmem] * 2 + [pl.BlockSpec(memory_space=pl.ANY)] * len(after),
        out_specs=[vmem] * pieces,
        compiler_params=pltpu.CompilerParams(vmem_limit_bytes=24 * 2**20),
        cost_estimate=pl.CostEstimate(
            flops=2 * queries * block * features,
            bytes_accessed=2 * (queries + block) * features,
            transcendentals=0,
        ),
        name="scores",
    )(grads, slab, *after)


def on_device(n_store, n_layer, hidden, cotangent, lengths, norm_gain, in_proj, out_proj, store):
    queries, positions, width = hidden.shape[1:]
    block = store.shape[1] // n_layer
    packed, far = factors(
        n_layer,
        lengths,
        hidden.reshape(queries * positions, width),
        cotangent.reshape(queries * positions, cotangent.shape[3]),
        norm_gain,
        in_proj[0],
        out_proj[0],
        store[0],
    )
    gathered = [packed]
    for away in range(1, n_store):
        pairs = [(source(to, away, n_store), to) for to in range(n_store)]
        gathered.append(lax.ppermute(packed, "store", pairs))
    near = fetch(packed, store[0], n_layer)
    last = n_layer - 3
    grads, partial = grads_and_scores(gathered, far, block, last, near)
    crossed = []
    for at in reversed(range(0, last, 2)):
        if at + 1 < last:
            (partial,) = scores(grads, far, block, at + 1, bf16)
        other = swap(partial, "layer", n_layer, 1)
        (mine,) = scores(grads, far, block, at, f32)
        joined = (mine + other.astype(f32)).astype(bf16)
        crossed.append(swap(joined, "layer", n_layer, at + 2))
    halves_of_other = scores(grads, near, block, 1, bf16, 2, [joined])
    (total,) = scores(grads, near, block, 0, f32)
    other = [swap(x, "layer", n_layer, 1) for x in halves_of_other]
    total = total + jnp.concatenate(other, axis=0).astype(f32)
    for x in crossed:
        total = total + x.astype(f32)
    return total.T


def solution(mesh):
    placed = (
        P("layer", ("grp", "store"), None, None),
        P("layer", ("grp", "store"), None, None),
        P(("grp", "store")),
        P("layer", None),
        P("layer", None, None),
        P("layer", None, None),
        P("layer", ("grp", "store"), None),
    )
    return jax.shard_map(
        functools.partial(on_device, mesh.shape["store"], mesh.shape["layer"]),
        mesh=mesh,
        in_specs=placed,
        out_specs=P(("grp", "store", "layer"), None),
        check_vma=False,
    )
```

```python
import functools

import jax
import jax.numpy as jnp
from jax import lax
from jax.experimental import pallas as pl
from jax.experimental.pallas import tpu as pltpu
from jax.sharding import PartitionSpec as P

norm_epsilon = 1e-05
f32 = jnp.float32
bf16 = jnp.bfloat16
S = 8
R = 64
B = 4
A = R // B
G = 8
H = 4
LANES = 128


def dot_nt(left, right):
    return lax.dot_general(left, right, (((1,), (1,)), ((), ())), preferred_element_type=f32)


def iota(shape, dim):
    return lax.broadcasted_iota(jnp.int32, shape, dim)


def factors_kernel(
    n_layer,
    hbm_lengths,
    hbm_hidden,
    hbm_cot,
    hbm_gain,
    hbm_inp,
    hbm_outp,
    hbm_store,
    packed,
    far,
    lengths,
    hidden,
    cot,
    gain,
    inp,
    outp,
    weights,
    in_acc,
    out_t,
    sems,
):
    blocks, step, width = hidden.shape
    rows = blocks * step
    queries = lengths.shape[0]
    full = queries // G * G * S
    half = rows - full
    mid, low = full // 2, half // 2

    def copy(source, target, at):
        return pltpu.make_async_copy(source, target, sems.at[at])

    def block_rows(r):
        at = pl.ds(pl.multiple_of(r * step, step), step)
        return copy(hbm_hidden.at[at, :], hidden.at[r], 5 + r)

    first = [copy(hbm_outp, outp, 0), copy(hbm_cot, cot, 1)]
    then = [copy(hbm_gain, gain, 2), copy(hbm_inp, inp, 3), copy(hbm_lengths, lengths, 4)]
    for piece in first + then + [block_rows(0)]:
        piece.start()
    odd = lax.rem(lax.axis_index("store"), 2)
    at_full = pl.multiple_of(odd * half, half)
    at_half = pl.multiple_of((1 - odd) * full, half)
    slab = store_copies(hbm_store, far, range(2, n_layer), sems, 5 + blocks, n_layer)
    for piece in first:
        piece.wait()

    @pl.when(odd >= 0)
    def _():
        for r in range(1, blocks):
            block_rows(r).start()
        for piece in slab:
            piece.start()

    whole = dot_nt(outp[...], cot[pl.ds(at_full, full), :])
    for t in range(full // LANES):
        out_t[t * R : (t + 1) * R, :] = whole[:, t * LANES : (t + 1) * LANES]
    out_t[full // LANES * R :, :half] = dot_nt(outp[...], cot[pl.ds(at_half, half), :])

    def part(t, b):
        return out_t[pl.ds(t * R + b, A, stride=B), :]

    row = mid + low
    for m in range(full // (G * S)):
        t, at = divmod(m * G * S, LANES)
        for b in range(0, B, 2):
            both = [part(t, b + c)[:, at : at + G * S] for c in range(2)]
            packed[row : row + A, :] = jnp.concatenate(both, axis=1).astype(bf16)
            row += A
    packed[row : row + A, :] = jnp.concatenate(
        [part(full // LANES, b)[:, :half] for b in range(B)], axis=1
    ).astype(bf16)

    for piece in then:
        piece.wait()
    weights[...] = inp[...] * gain[...]

    @pl.loop(0, blocks)
    def _(r):
        block_rows(r).wait()
        product = dot_nt(hidden[r], weights[...])
        total = jnp.zeros((step, LANES), f32)
        for at in range(0, width, LANES):
            wide = hidden[r, :, at : at + LANES].astype(f32)
            total += wide * wide
        mean_square = jnp.sum(total, axis=1, keepdims=True) * (1.0 / width)
        factor = product * lax.rsqrt(mean_square + norm_epsilon)
        at = pl.ds(pl.multiple_of(r * step, step), step)
        in_acc[at, :] = jnp.concatenate([factor, factor], axis=1)

    low_lanes = iota((S, LANES), 1) < R
    position = iota((S, LANES), 0)

    def in_rows(at, count):
        factor = in_acc[pl.ds(at, count), :]
        return [
            jnp.where(position < lengths[at // S + q], factor[q * S : (q + 1) * S], 0.0)
            for q in range(count // S)
        ]

    def side_by_side(tiles):
        both = zip(tiles[: len(tiles) // 2], tiles[len(tiles) // 2 :])
        return jnp.concatenate([jnp.where(low_lanes, x, y) for x, y in both], axis=0)

    packed[:mid, :] = side_by_side(in_rows(at_full, full)).astype(bf16)
    packed[mid : mid + low, :] = side_by_side(in_rows(at_half, half)).astype(bf16)
    for piece in slab:
        piece.wait()


def in_hbm(x):
    return pltpu.with_memory_space_constraint(x, pltpu.HBM)


def factors(n_layer, lengths, hidden, cotangent, gain, in_projection, out_projection, store):
    rows, width = hidden.shape
    blocks = 3
    far = (store.shape[0] // n_layer * (n_layer - 2), store.shape[1])
    args = (lengths, hidden, cotangent, gain, in_projection, out_projection, store)
    return pl.pallas_call(
        functools.partial(factors_kernel, n_layer),
        out_shape=[
            jax.ShapeDtypeStruct((rows, 2 * R), bf16),
            jax.ShapeDtypeStruct(far, bf16),
        ],
        in_specs=[pl.BlockSpec(memory_space=pl.ANY)] * len(args),
        out_specs=[pl.BlockSpec(memory_space=pltpu.VMEM)] * 2,
        scratch_shapes=[
            pltpu.SMEM(lengths.shape, jnp.int32),
            pltpu.VMEM((blocks, rows // blocks, width), bf16),
            pltpu.VMEM(cotangent.shape, bf16),
            pltpu.VMEM(gain.shape, bf16),
            pltpu.VMEM(in_projection.shape, bf16),
            pltpu.VMEM(out_projection.shape, bf16),
            pltpu.VMEM(in_projection.shape, bf16),
            pltpu.VMEM((rows, 2 * R), f32),
            pltpu.VMEM((-(-rows // LANES) * R, LANES), f32),
            pltpu.SemaphoreType.DMA((5 + blocks + n_layer - 2,)),
        ],
        compiler_params=pltpu.CompilerParams(vmem_limit_bytes=24 * 2**20),
        name="factors",
    )(*[in_hbm(x) for x in args])


def store_copies(store, slab, places, sems, at, n_layer):
    block = store.shape[0] // n_layer
    rows = 16 if block % 16 == 0 else 8
    me = lax.axis_index("layer")
    copies = []
    for to, k in enumerate(places):
        start = pl.multiple_of(partner(me, k, n_layer) * block, rows)
        target = slab.at[pl.ds(to * block, block)]
        copies.append(
            pltpu.make_async_copy(store.at[pl.ds(start, block)], target, sems.at[at + to])
        )
    return copies


def fetch_kernel(n_layer, after, store, near, sems):
    copies = store_copies(store, near, range(2), sems, 0, n_layer)
    for copy in copies:
        copy.start()
    for copy in copies:
        copy.wait()


def fetch(after, store, n_layer):
    rows, features = store.shape
    return pl.pallas_call(
        functools.partial(fetch_kernel, n_layer),
        out_shape=jax.ShapeDtypeStruct((rows // n_layer * 2, features), bf16),
        in_specs=[pl.BlockSpec(memory_space=pl.ANY)] * 2,
        out_specs=pl.BlockSpec(memory_space=pltpu.VMEM),
        scratch_shapes=[pltpu.SemaphoreType.DMA((2,))],
        compiler_params=pltpu.CompilerParams(vmem_limit_bytes=12 * 2**20),
        cost_estimate=pl.CostEstimate(
            flops=0, bytes_accessed=4 * rows * features // n_layer, transcendentals=0
        ),
        name="fetch",
    )(after, in_hbm(store))


def spread_out(tile, owner):
    lanes = tile.shape[1]
    mine = (owner == iota((G, lanes), 0))[None]
    wide = jnp.where(mine, tile.astype(f32)[:, None, :], 0.0)
    return wide.reshape(A * G, lanes).astype(bf16)


def halves(tile):
    wide = tile.astype(f32)
    turned = jnp.concatenate([wide[:, R:], wide[:, :R]], axis=1)
    low = iota(wide.shape, 1) < R
    return [
        jnp.where(mask, x, 0.0).astype(bf16)
        for x in (wide, turned)
        for mask in (low, jnp.logical_not(low))
    ]


def diagonal(low, high):
    zero = jnp.zeros_like(low)
    left = jnp.concatenate([low, high, zero, zero], axis=0)
    right = jnp.concatenate([zero, zero, low, high], axis=0)
    return jnp.concatenate([left, right], axis=1)


def build_grads(shards, base, row0, full_groups, grads):
    mid = full_groups * G * S // 2
    low = H * S // 2
    lane = iota((G, 2 * 128), 1)
    whole_owner = lax.rem(lane, G * S) // S
    half_owner = lax.rem(lane, H * S) // S + H * (lane // 128)

    def whole(shard):
        found = []
        pairs = {}
        for m in range(full_groups):
            first = m % (full_groups // 2)
            if first not in pairs:
                pairs[first] = halves(
                    shards[base + shard, first * G * S : (first + 1) * G * S, :]
                )
            plain_low, plain_high, turned_low, turned_high = pairs[first]
            weights = (
                diagonal(plain_low, turned_high)
                if m < full_groups // 2
                else diagonal(turned_low, plain_high)
            )
            at = mid + low + m * 2 * A
            tile = jnp.concatenate(
                [shards[base + shard, at : at + A, :], shards[base + shard, at + A : at + 2 * A, :]],
                axis=1,
            )
            found.append((spread_out(tile, whole_owner), weights))
        return found

    def joined(shard):
        tiles, weights = [], []
        for s in (shard, shard + 1):
            plain_low, plain_high, turned_low, turned_high = halves(
                shards[base + s, mid : mid + low, :]
            )
            weights.append(
                diagonal(
                    jnp.concatenate([plain_low, turned_low], axis=0),
                    jnp.concatenate([turned_high, plain_high], axis=0),
                )
            )
            at = mid + low + full_groups * 2 * A
            tiles.append(shards[base + s, at : at + A, :])
        return [
            (
                spread_out(jnp.concatenate(tiles, axis=1), half_owner),
                jnp.concatenate(weights, axis=0),
            )
        ]

    groups = []
    for shard in (0, 2):
        groups += whole(shard) + joined(shard) + whole(shard + 1)
    for at in range(0, len(groups), 2):
        first, second = [jnp.dot(x, w, preferred_element_type=f32) for x, w in groups[at : at + 2]]
        for a in range(A):
            pair = [x[a * G : (a + 1) * G] for x in (first, second)]
            grads[pl.ds(row0 + at * G, 2 * G), a * 256 : (a + 1) * 256] = jnp.concatenate(
                pair, axis=0
            ).astype(bf16)


def source(to, away, n):
    if n != 4:
        return (to + away) % n
    place = (to % 2 * 2 + to // 2 + away) % n
    return place % 2 * 2 + place // 2


def shift_order(n):
    return [2, 1, 3] if n == 4 else list(range(1, n))


def grads_kernel(n_store, full_groups, k, *refs):
    gathered = refs[:n_store]
    slab, _, grads, out, shards = refs[n_store:]
    me_store = lax.axis_index("store")
    for away, block in zip([0] + shift_order(n_store), gathered):
        shards[source(me_store, away, n_store)] = block[...]
    four = 4 * (full_groups * G + H)
    if n_store == 4:
        build_grads(shards, 0, 0, full_groups, grads)
    else:

        @pl.loop(0, n_store // 4)
        def _(at):
            build_grads(shards, at * 4, pl.multiple_of(at * four, 16), full_groups, grads)

    scores_kernel(k, grads, slab, out)


def scores_kernel(k, grads, slab, *refs, skip=0):
    outs = refs[skip:]
    block = outs[0].shape[1]
    total = dot_nt(slab[k * block : (k + 1) * block, :], grads[...]).T
    at = 0
    for out in outs:
        out[...] = total[at : at + out.shape[0]].astype(out.dtype)
        at += out.shape[0]


def partner(me, k, n):
    return jnp.bitwise_xor(me, k) if n & (n - 1) == 0 else lax.rem(n + k - me, n)


def swap(x, axis, n, k):
    pairs = [(i, i ^ k if n & (n - 1) == 0 else (n + k - i) % n) for i in range(n)]
    return lax.ppermute(x, axis, pairs)


def grads_and_scores(gathered, slab, block, at, after):
    n_store = len(gathered)
    queries = gathered[0].shape[0] // S
    vmem = pl.BlockSpec(memory_space=pltpu.VMEM)
    return pl.pallas_call(
        functools.partial(grads_kernel, n_store, queries // G, at),
        out_shape=[
            jax.ShapeDtypeStruct((n_store * queries, slab.shape[1]), bf16),
            jax.ShapeDtypeStruct((n_store * queries, block), bf16),
        ],
        in_specs=[vmem] * (n_store + 1) + [pl.BlockSpec(memory_space=pl.ANY)],
        out_specs=[vmem] * 2,
        scratch_shapes=[pltpu.VMEM((n_store,) + gathered[0].shape, bf16)],
        compiler_params=pltpu.CompilerParams(vmem_limit_bytes=24 * 2**20),
        name="grads",
    )(*gathered, slab, after)


def scores(grads, slab, block, at, kind, pieces=1, after=()):
    queries, features = grads.shape
    vmem = pl.BlockSpec(memory_space=pltpu.VMEM)
    return pl.pallas_call(
        functools.partial(scores_kernel, at, skip=len(after)),
        out_shape=[jax.ShapeDtypeStruct((queries // pieces, block), kind)] * pieces,
        in_specs=[vmem] * 2 + [pl.BlockSpec(memory_space=pl.ANY)] * len(after),
        out_specs=[vmem] * pieces,
        compiler_params=pltpu.CompilerParams(vmem_limit_bytes=24 * 2**20),
        cost_estimate=pl.CostEstimate(
            flops=2 * queries * block * features,
            bytes_accessed=2 * (queries + block) * features,
            transcendentals=0,
        ),
        name="scores",
    )(grads, slab, *after)


def on_device(n_store, n_layer, hidden, cotangent, lengths, norm_gain, in_proj, out_proj, store):
    queries, positions, width = hidden.shape[1:]
    block = store.shape[1] // n_layer
    packed, far = factors(
        n_layer,
        lengths,
        hidden.reshape(queries * positions, width),
        cotangent.reshape(queries * positions, cotangent.shape[3]),
        norm_gain,
        in_proj[0],
        out_proj[0],
        store[0],
    )
    gathered = [packed]
    for away in shift_order(n_store):
        pairs = [(source(to, away, n_store), to) for to in range(n_store)]
        gathered.append(lax.ppermute(packed, "store", pairs))
    near = fetch(packed, store[0], n_layer)
    last = n_layer - 3
    grads, partial = grads_and_scores(gathered, far, block, last, near)
    crossed = []
    for at in reversed(range(0, last, 2)):
        if at + 1 < last:
            (partial,) = scores(grads, far, block, at + 1, bf16)
        other = swap(partial, "layer", n_layer, 1)
        (mine,) = scores(grads, far, block, at, f32)
        joined = (mine + other.astype(f32)).astype(bf16)
        crossed.append(swap(joined, "layer", n_layer, at + 2))
    halves_of_other = scores(grads, near, block, 1, bf16, 2, [joined])
    (total,) = scores(grads, near, block, 0, f32)
    other = [swap(x, "layer", n_layer, 1) for x in halves_of_other]
    total = total + jnp.concatenate(other, axis=0).astype(f32)
    for x in crossed:
        total = total + x.astype(f32)
    return total.T


def solution(mesh):
    placed = (
        P("layer", ("grp", "store"), None, None),
        P("layer", ("grp", "store"), None, None),
        P(("grp", "store")),
        P("layer", None),
        P("layer", None, None),
        P("layer", None, None),
        P("layer", ("grp", "store"), None),
    )
    return jax.shard_map(
        functools.partial(on_device, mesh.shape["store"], mesh.shape["layer"]),
        mesh=mesh,
        in_specs=placed,
        out_specs=P(("grp", "store", "layer"), None),
        check_vma=False,
    )
```

```python
import functools

import jax
import jax.numpy as jnp
from jax import lax
from jax.experimental import pallas as pl
from jax.experimental.pallas import tpu as pltpu
from jax.sharding import PartitionSpec as P

norm_epsilon = 1e-05
f32 = jnp.float32
bf16 = jnp.bfloat16
S = 8
R = 64
B = 4
A = R // B
G = 8
H = 4
LANES = 128


def dot_nt(left, right):
    return lax.dot_general(left, right, (((1,), (1,)), ((), ())), preferred_element_type=f32)


def iota(shape, dim):
    return lax.broadcasted_iota(jnp.int32, shape, dim)


def factors_kernel(
    n_layer,
    hbm_lengths,
    hbm_hidden,
    hbm_cot,
    hbm_gain,
    hbm_inp,
    hbm_outp,
    hbm_store,
    packed,
    far,
    lengths,
    hidden,
    cot,
    gain,
    inp,
    outp,
    weights,
    in_acc,
    out_t,
    sems,
):
    blocks, step, width = hidden.shape
    rows = blocks * step
    queries = lengths.shape[0]
    full = queries // G * G * S
    half = rows - full
    mid, low = full // 2, half // 2

    def copy(source, target, at):
        return pltpu.make_async_copy(source, target, sems.at[at])

    def block_rows(r):
        at = pl.ds(pl.multiple_of(r * step, step), step)
        return copy(hbm_hidden.at[at, :], hidden.at[r], 5 + r)

    first = [copy(hbm_outp, outp, 0), copy(hbm_cot, cot, 1)]
    then = [copy(hbm_gain, gain, 2), copy(hbm_inp, inp, 3), copy(hbm_lengths, lengths, 4)]
    for piece in first + then + [block_rows(r) for r in range(blocks)]:
        piece.start()
    odd = lax.rem(lax.axis_index("store"), 2)
    at_full = pl.multiple_of(odd * half, half)
    at_half = pl.multiple_of((1 - odd) * full, half)
    slab = store_copies(hbm_store, far, range(2, n_layer), sems, 5 + blocks, n_layer)
    for piece in first:
        piece.wait()

    @pl.when(odd >= 0)
    def _():
        for piece in slab:
            piece.start()

    whole = dot_nt(outp[...], cot[pl.ds(at_full, full), :])
    for t in range(full // LANES):
        out_t[t * R : (t + 1) * R, :] = whole[:, t * LANES : (t + 1) * LANES]
    out_t[full // LANES * R :, :half] = dot_nt(outp[...], cot[pl.ds(at_half, half), :])

    def part(t, b):
        return out_t[pl.ds(t * R + b, A, stride=B), :]

    row = mid + low
    for m in range(full // (G * S)):
        t, at = divmod(m * G * S, LANES)
        for b in range(0, B, 2):
            both = [part(t, b + c)[:, at : at + G * S] for c in range(2)]
            packed[row : row + A, :] = jnp.concatenate(both, axis=1).astype(bf16)
            row += A
    packed[row : row + A, :] = jnp.concatenate(
        [part(full // LANES, b)[:, :half] for b in range(B)], axis=1
    ).astype(bf16)

    for piece in then:
        piece.wait()
    weights[...] = inp[...] * gain[...]

    @pl.loop(0, blocks)
    def _(r):
        block_rows(r).wait()
        product = dot_nt(hidden[r], weights[...])
        total = jnp.zeros((step, LANES), f32)
        for at in range(0, width, LANES):
            wide = hidden[r, :, at : at + LANES].astype(f32)
            total += wide * wide
        mean_square = jnp.sum(total, axis=1, keepdims=True) * (1.0 / width)
        factor = product * lax.rsqrt(mean_square + norm_epsilon)
        at = pl.ds(pl.multiple_of(r * step, step), step)
        in_acc[at, :] = jnp.concatenate([factor, factor], axis=1)

    low_lanes = iota((S, LANES), 1) < R
    position = iota((S, LANES), 0)

    def in_rows(at, count):
        factor = in_acc[pl.ds(at, count), :]
        return [
            jnp.where(position < lengths[at // S + q], factor[q * S : (q + 1) * S], 0.0)
            for q in range(count // S)
        ]

    def side_by_side(tiles):
        both = zip(tiles[: len(tiles) // 2], tiles[len(tiles) // 2 :])
        return jnp.concatenate([jnp.where(low_lanes, x, y) for x, y in both], axis=0)

    packed[:mid, :] = side_by_side(in_rows(at_full, full)).astype(bf16)
    packed[mid : mid + low, :] = side_by_side(in_rows(at_half, half)).astype(bf16)
    for piece in slab:
        piece.wait()


def in_hbm(x):
    return pltpu.with_memory_space_constraint(x, pltpu.HBM)


def factors(n_layer, lengths, hidden, cotangent, gain, in_projection, out_projection, store):
    rows, width = hidden.shape
    blocks = 3
    far = (store.shape[0] // n_layer * (n_layer - 2), store.shape[1])
    args = (lengths, hidden, cotangent, gain, in_projection, out_projection, store)
    return pl.pallas_call(
        functools.partial(factors_kernel, n_layer),
        out_shape=[
            jax.ShapeDtypeStruct((rows, 2 * R), bf16),
            jax.ShapeDtypeStruct(far, bf16),
        ],
        in_specs=[pl.BlockSpec(memory_space=pl.ANY)] * len(args),
        out_specs=[pl.BlockSpec(memory_space=pltpu.VMEM)] * 2,
        scratch_shapes=[
            pltpu.SMEM(lengths.shape, jnp.int32),
            pltpu.VMEM((blocks, rows // blocks, width), bf16),
            pltpu.VMEM(cotangent.shape, bf16),
            pltpu.VMEM(gain.shape, bf16),
            pltpu.VMEM(in_projection.shape, bf16),
            pltpu.VMEM(out_projection.shape, bf16),
            pltpu.VMEM(in_projection.shape, bf16),
            pltpu.VMEM((rows, 2 * R), f32),
            pltpu.VMEM((-(-rows // LANES) * R, LANES), f32),
            pltpu.SemaphoreType.DMA((5 + blocks + n_layer - 2,)),
        ],
        compiler_params=pltpu.CompilerParams(vmem_limit_bytes=24 * 2**20),
        name="factors",
    )(*[in_hbm(x) for x in args])


def store_copies(store, slab, places, sems, at, n_layer):
    block = store.shape[0] // n_layer
    rows = 16 if block % 16 == 0 else 8
    me = lax.axis_index("layer")
    copies = []
    for to, k in enumerate(places):
        start = pl.multiple_of(partner(me, k, n_layer) * block, rows)
        target = slab.at[pl.ds(to * block, block)]
        copies.append(
            pltpu.make_async_copy(store.at[pl.ds(start, block)], target, sems.at[at + to])
        )
    return copies


def fetch_kernel(n_layer, after, store, near, sems):
    copies = store_copies(store, near, range(2), sems, 0, n_layer)
    for copy in copies:
        copy.start()
    for copy in copies:
        copy.wait()


def fetch(after, store, n_layer):
    rows, features = store.shape
    return pl.pallas_call(
        functools.partial(fetch_kernel, n_layer),
        out_shape=jax.ShapeDtypeStruct((rows // n_layer * 2, features), bf16),
        in_specs=[pl.BlockSpec(memory_space=pl.ANY)] * 2,
        out_specs=pl.BlockSpec(memory_space=pltpu.VMEM),
        scratch_shapes=[pltpu.SemaphoreType.DMA((2,))],
        compiler_params=pltpu.CompilerParams(vmem_limit_bytes=12 * 2**20),
        cost_estimate=pl.CostEstimate(
            flops=0, bytes_accessed=4 * rows * features // n_layer, transcendentals=0
        ),
        name="fetch",
    )(after, in_hbm(store))


def spread_out(tile, owner):
    lanes = tile.shape[1]
    mine = (owner == iota((G, lanes), 0))[None]
    wide = jnp.where(mine, tile.astype(f32)[:, None, :], 0.0)
    return wide.reshape(A * G, lanes).astype(bf16)


def halves(tile):
    wide = tile.astype(f32)
    turned = jnp.concatenate([wide[:, R:], wide[:, :R]], axis=1)
    low = iota(wide.shape, 1) < R
    return [
        jnp.where(mask, x, 0.0).astype(bf16)
        for x in (wide, turned)
        for mask in (low, jnp.logical_not(low))
    ]


def diagonal(low, high):
    zero = jnp.zeros_like(low)
    left = jnp.concatenate([low, high, zero, zero], axis=0)
    right = jnp.concatenate([zero, zero, low, high], axis=0)
    return jnp.concatenate([left, right], axis=1)


def build_grads(shards, base, row0, full_groups, grads):
    mid = full_groups * G * S // 2
    low = H * S // 2
    lane = iota((G, 2 * 128), 1)
    whole_owner = lax.rem(lane, G * S) // S
    half_owner = lax.rem(lane, H * S) // S + H * (lane // 128)

    def whole(shard):
        found = []
        pairs = {}
        for m in range(full_groups):
            first = m % (full_groups // 2)
            if first not in pairs:
                pairs[first] = halves(
                    shards[base + shard, first * G * S : (first + 1) * G * S, :]
                )
            plain_low, plain_high, turned_low, turned_high = pairs[first]
            weights = (
                diagonal(plain_low, turned_high)
                if m < full_groups // 2
                else diagonal(turned_low, plain_high)
            )
            at = mid + low + m * 2 * A
            tile = jnp.concatenate(
                [shards[base + shard, at : at + A, :], shards[base + shard, at + A : at + 2 * A, :]],
                axis=1,
            )
            found.append((spread_out(tile, whole_owner), weights))
        return found

    def joined(shard):
        tiles, weights = [], []
        for s in (shard, shard + 1):
            plain_low, plain_high, turned_low, turned_high = halves(
                shards[base + s, mid : mid + low, :]
            )
            weights.append(
                diagonal(
                    jnp.concatenate([plain_low, turned_low], axis=0),
                    jnp.concatenate([turned_high, plain_high], axis=0),
                )
            )
            at = mid + low + full_groups * 2 * A
            tiles.append(shards[base + s, at : at + A, :])
        return [
            (
                spread_out(jnp.concatenate(tiles, axis=1), half_owner),
                jnp.concatenate(weights, axis=0),
            )
        ]

    groups = []
    for shard in (0, 2):
        groups += whole(shard) + joined(shard) + whole(shard + 1)
    for at in range(0, len(groups), 2):
        first, second = [jnp.dot(x, w, preferred_element_type=f32) for x, w in groups[at : at + 2]]
        for a in range(A):
            pair = [x[a * G : (a + 1) * G] for x in (first, second)]
            grads[pl.ds(row0 + at * G, 2 * G), a * 256 : (a + 1) * 256] = jnp.concatenate(
                pair, axis=0
            ).astype(bf16)


def source(to, away, n):
    if n != 4:
        return (to + away) % n
    place = ((to ^ to // 2) + away) % n
    return place ^ place // 2


def grads_kernel(n_store, full_groups, k, *refs):
    gathered = refs[:n_store]
    slab, _, grads, out, shards = refs[n_store:]
    me_store = lax.axis_index("store")
    for away, block in enumerate(gathered):
        shards[source(me_store, away, n_store)] = block[...]
    four = 4 * (full_groups * G + H)
    if n_store == 4:
        build_grads(shards, 0, 0, full_groups, grads)
    else:

        @pl.loop(0, n_store // 4)
        def _(at):
            build_grads(shards, at * 4, pl.multiple_of(at * four, 16), full_groups, grads)

    scores_kernel(k, grads, slab, out)


def scores_kernel(k, grads, slab, *refs, skip=0):
    outs = refs[skip:]
    block = outs[0].shape[1]
    total = dot_nt(slab[k * block : (k + 1) * block, :], grads[...]).T
    at = 0
    for out in outs:
        out[...] = total[at : at + out.shape[0]].astype(out.dtype)
        at += out.shape[0]


def partner(me, k, n):
    return jnp.bitwise_xor(me, k) if n & (n - 1) == 0 else lax.rem(n + k - me, n)


def swap(x, axis, n, k):
    pairs = [(i, i ^ k if n & (n - 1) == 0 else (n + k - i) % n) for i in range(n)]
    return lax.ppermute(x, axis, pairs)


def grads_and_scores(gathered, slab, block, at, after):
    n_store = len(gathered)
    queries = gathered[0].shape[0] // S
    vmem = pl.BlockSpec(memory_space=pltpu.VMEM)
    return pl.pallas_call(
        functools.partial(grads_kernel, n_store, queries // G, at),
        out_shape=[
            jax.ShapeDtypeStruct((n_store * queries, slab.shape[1]), bf16),
            jax.ShapeDtypeStruct((n_store * queries, block), bf16),
        ],
        in_specs=[vmem] * (n_store + 1) + [pl.BlockSpec(memory_space=pl.ANY)],
        out_specs=[vmem] * 2,
        scratch_shapes=[pltpu.VMEM((n_store,) + gathered[0].shape, bf16)],
        compiler_params=pltpu.CompilerParams(vmem_limit_bytes=24 * 2**20),
        name="grads",
    )(*gathered, slab, after)


def scores(grads, slab, block, at, kind, pieces=1, after=()):
    queries, features = grads.shape
    vmem = pl.BlockSpec(memory_space=pltpu.VMEM)
    return pl.pallas_call(
        functools.partial(scores_kernel, at, skip=len(after)),
        out_shape=[jax.ShapeDtypeStruct((queries // pieces, block), kind)] * pieces,
        in_specs=[vmem] * 2 + [pl.BlockSpec(memory_space=pl.ANY)] * len(after),
        out_specs=[vmem] * pieces,
        compiler_params=pltpu.CompilerParams(vmem_limit_bytes=24 * 2**20),
        cost_estimate=pl.CostEstimate(
            flops=2 * queries * block * features,
            bytes_accessed=2 * (queries + block) * features,
            transcendentals=0,
        ),
        name="scores",
    )(grads, slab, *after)


def on_device(n_store, n_layer, hidden, cotangent, lengths, norm_gain, in_proj, out_proj, store):
    queries, positions, width = hidden.shape[1:]
    block = store.shape[1] // n_layer
    packed, far = factors(
        n_layer,
        lengths,
        hidden.reshape(queries * positions, width),
        cotangent.reshape(queries * positions, cotangent.shape[3]),
        norm_gain,
        in_proj[0],
        out_proj[0],
        store[0],
    )
    gathered = [packed]
    for away in range(1, n_store):
        pairs = [(source(to, away, n_store), to) for to in range(n_store)]
        gathered.append(lax.ppermute(packed, "store", pairs))
    near = fetch(packed, store[0], n_layer)
    last = n_layer - 3
    grads, partial = grads_and_scores(gathered, far, block, last, near)
    crossed = []
    for at in reversed(range(0, last, 2)):
        if at + 1 < last:
            (partial,) = scores(grads, far, block, at + 1, bf16)
        other = swap(partial, "layer", n_layer, 1)
        (mine,) = scores(grads, far, block, at, f32)
        joined = (mine + other.astype(f32)).astype(bf16)
        crossed.append(swap(joined, "layer", n_layer, at + 2))
    halves_of_other = scores(grads, near, block, 1, bf16, 2, [joined])
    (total,) = scores(grads, near, block, 0, f32)
    other = [swap(x, "layer", n_layer, 1) for x in halves_of_other]
    total = total + jnp.concatenate(other, axis=0).astype(f32)
    for x in crossed:
        total = total + x.astype(f32)
    return total.T


def solution(mesh):
    placed = (
        P("layer", ("grp", "store"), None, None),
        P("layer", ("grp", "store"), None, None),
        P(("grp", "store")),
        P("layer", None),
        P("layer", None, None),
        P("layer", None, None),
        P("layer", ("grp", "store"), None),
    )
    return jax.shard_map(
        functools.partial(on_device, mesh.shape["store"], mesh.shape["layer"]),
        mesh=mesh,
        in_specs=placed,
        out_specs=P(("grp", "store", "layer"), None),
        check_vma=False,
    )
```
